32 devices in a mesh: groups: 2 (over x), dp: 16 (over z, y, core).
Axes of the slice: x: 2, y: 2, z: 4, core: 2. Of those that a mesh axis runs over, the one named last changes fastest.
Arguments:
- token_ids: int32 [64, 64], P(('groups', 'dp')), parts along dimension 0, may hold values from 0 to 3839, as said below
- lengths: int32 [64], P(('groups', 'dp')), parts along dimension 0, may hold values from 16 to 64
- word_table: bfloat16 [3840, 1024], P('dp'), may hold values from -6 to 6
- pos_table: bfloat16 [64, 1024], replicated, may hold values from -3 to 3
- emb_gain: float32 [1024], replicated, may hold values from 0.25 to 1.75
- emb_bias: float32 [1024], replicated, may hold values from -1.75 to 1.75
- w_qkv: bfloat16 [1024, 1536], replicated, may hold values from -0.1875 to 0.1875
- w_out: bfloat16 [512, 1024], replicated, may hold values from -0.25 to 0.25
- out_bias: float32 [1024], replicated, may hold values from -3 to 3
- norm_gain: float32 [1024], replicated, may hold values from 0.25 to 1.75
- norm_bias: float32 [1024], replicated, may hold values from -1.75 to 1.75
- stored_rows: bfloat16 [8128, 1024], P(('groups', 'dp')), parts along dimension 0, may hold values from -6 to 6
- row_owner: int32 [8192, 1], P(('groups', 'dp')), parts along dimension 0, may hold values from 0 to 15; in each aligned block of 256 rows (0 to 255, 256 to 511, ...) at most 48 rows name the same one
- row_slot: int32 [8192], P(('groups', 'dp')), parts along dimension 0, may hold values from 0 to 511
- centroids: float32 [16384, 1024], P(('groups', 'dp')), parts along dimension 0, may hold values from -6 to 6
Outputs:
- passage_embed: bfloat16 [64, 1024], P(('groups', 'dp')), parts along dimension 0
- new_centroids: float32 [16384, 1024], P(('groups', 'dp')), parts along dimension 0
The draws below stay inside these ranges and needn't reach their ends.
There are 2 independent parts, one for each index of `groups`. The reference program is written for one: setup_inputs(seed, part) draws one part's arguments, and reference() takes and returns one part's arrays. A program takes and returns all parts, laid end to end along the dimension named above; an argument that names none is the same for every part. Nothing has to cross between parts.
Inputs may be any that keep to these rules, and one draw needn't show every extreme that they name: `token_ids`: token ids of device o's vocabulary rows are o * 240 to (o + 1) * 240 - 1. Among the 128 tokens of one index of dp, at most 24 have ids of one index's rows, and in every such block some index has exactly 24. `row_owner`: among the 256 rows of one index of dp, at most 48 name one index; some index is named 48 times.
All inputs are finite; a program needn't handle non-finite values.
Results may differ from the reference program's by a relative error of at most 0.0038.
Values may be sent and summed in bfloat16 or wider, within the bound.
No kernel may reach another device: no remote copies, remote signals or barrier semaphores. Data moves between devices by JAX's collectives and lax.ppermute only.
A program may use at most 64 MiB of HBM per device.

```python
import math
import jax
import jax.numpy as jnp
import numpy as np
from jax import lax

D = 1024
HEADS = 8
HD = 64
SEQ = 64
PASS_DEV = 2
V_DEV = 240
CENT_DEV = 512
KROWS_DEV = 256
TOK_DEV = 128
STORE_DEV = 254
PASSAGES = 32
VOCAB = 3840
CLUSTERS = 8192
STORED = 4064
KROWS = 4096
TCAP = 24
KCAP = 48
N_DP = 16


def draw_token_ids(key, part):
    key = jax.random.fold_in(key, 11)
    key_place, key_owner, key_offset = jax.random.split(key, 3)
    places = jax.vmap(lambda subkey: jax.random.permutation(subkey, TOK_DEV))(jax.random.split(key_place, N_DP))
    places = places.astype(jnp.int32)
    layout = jnp.where(places < TCAP, 0, 1 + (places - TCAP) % (N_DP - 1))
    orders = jax.vmap(lambda subkey: jax.random.permutation(subkey, N_DP))(jax.random.split(key_owner, N_DP))
    owners = jnp.take_along_axis(orders.astype(jnp.int32), layout, axis=1)
    offsets = jax.random.randint(key_offset, (N_DP, TOK_DEV), 0, V_DEV, dtype=jnp.int32)
    return (owners * V_DEV + offsets).reshape(PASSAGES, SEQ)


def with_ends(entries, own_key, least, top_value):
    index_at = [jax.random.randint(jax.random.fold_in(own_key, axis), (), 0, length) for axis, length in enumerate(entries.shape)]
    longest = entries.shape.index(max(entries.shape))
    next_to = index_at[:longest] + [(index_at[longest] + 1) % entries.shape[longest]] + index_at[longest + 1:]
    return entries.at[tuple(index_at)].set(least).at[tuple(next_to)].set(top_value)


def levels(rng, dims, pieces, smallest, largest):
    level, own = 1.0, jax.random.fold_in(rng, 6)
    for axis_at, shards_of in pieces:
        steps = jnp.exp(jax.random.uniform(jax.random.fold_in(own, axis_at), (shards_of,), jnp.float32, smallest / len(pieces), largest / len(pieces)))
        level = level * jnp.repeat(steps, dims[axis_at] // shards_of).reshape([-1 if axis == axis_at else 1 for axis in range(len(dims))])
    return level


def cumulative_ranks(amount, slope):
    loads = [(1 << 20) // math.isqrt(grade ** slope) + 1 for grade in range(1, amount + 1)]
    scale = 1 + sum(loads) // (1 << 30)
    return np.cumsum(np.array([max(1, weight // scale) for weight in loads]))


def skewed_ids(own_key, shape, count, slope):
    listing = cumulative_ranks(count, slope)
    pick = jax.random.randint(jax.random.fold_in(own_key, 1), shape, 0, int(listing[count - 1]))
    standing = jnp.searchsorted(jnp.asarray(listing, jnp.int32), pick, side="right")
    return jax.random.permutation(jax.random.fold_in(own_key, 2), count)[standing].astype(jnp.int32)


def routed_block(own_key, own, number, rows, count, top, bound, slope):
    sequence = jax.random.permutation(own_key, count)
    heavy_load, usual = portions_of(count, rows * top, bound, slope, True), portions_of(count, rows * top, bound, slope, False)
    places = jnp.arange(count)

    def named(sizes, offset_by):
        used = int((sizes > 0).sum())
        fixed = max(1, used // 4)
        passed = fixed + (places - fixed + offset_by * (used - fixed)) % max(1, count - fixed)
        return jnp.zeros((count,), jnp.int32).at[sequence[jnp.where(places < fixed, places, passed)]].set(jnp.asarray(sizes, jnp.int32))

    sizes = jnp.where(number % 4 == 0, named(heavy_load, number // 4), named(usual, number - number // 4 - 1))
    mixed = jax.random.permutation(jax.random.fold_in(own, 3), count)
    source_of, taker = mixed[0:count // 2 * 2:2], mixed[1:count // 2 * 2:2]
    slack = jnp.minimum(sizes[source_of] - 1, bound - sizes[taker]) // 2
    slack = jnp.where((source_of == sequence[0]) | (taker == sequence[0]) | (sizes[taker] == 0), 0, jnp.maximum(slack, 0))
    passed = jax.random.randint(jax.random.fold_in(own, 4), (count // 2,), 0, 1 << 20) % (slack + 1)
    sizes = sizes.at[source_of].add(-passed).at[taker].add(passed)
    labels = jnp.searchsorted(jnp.cumsum(sizes), jnp.arange(rows * top), side="right").astype(jnp.int32)
    listing = labels.reshape(top, rows).T
    listing = listing[jax.random.permutation(jax.random.fold_in(own, 1), rows)]
    offset_by = jax.random.randint(jax.random.fold_in(own, 2), (rows, 1), 0, top)
    return jnp.take_along_axis(listing, (jnp.arange(top)[None, :] + offset_by) % top, axis=1)


def portions_of(amount, total, most, slope, full):
    weights = [(1 << 20) // math.isqrt(rank ** slope) + 1 for rank in range(1, amount + 1)]
    largest = most if full else min(most, max(-(-total // amount), total * weights[0] // sum(weights)))
    least = 1 if total - largest >= amount - 1 else 0
    given, surplus = [largest] + [least] * (amount - 1), total - largest - least * (amount - 1)
    while surplus > 0:
        free = [i for i in range(1, amount) if given[i] < largest] or [i for i in range(1, amount) if given[i] < most]
        whole, remaining = sum([weights[i] for i in free]), surplus
        for i in free:
            addition = min(most - given[i], max(1, remaining * weights[i] // whole), surplus)
            given[i] = given[i] + addition
            surplus = surplus - addition
    return np.array(given)


def normal_values(own_key, dims, scale, bound, shards=(), kind=jnp.bfloat16):
    array = scale * jax.random.normal(own_key, dims, jnp.float32)
    if shards:
        array = array * levels(own_key, dims, shards, -0.22, 0.18)
    return jnp.clip(array, -bound, bound).astype(kind)


def setup_inputs(seed: int = 0, part: int = 0) -> dict:
    splits = jax.random.split(jax.random.key(seed), 16)
    part_splits = jax.random.split(jax.random.fold_in(splits[15], part), 16)
    token_ids = draw_token_ids(jax.random.fold_in(jax.random.fold_in(splits[15], part), 71), part)
    lengths = with_ends(jax.random.randint(part_splits[1], (PASSAGES,), SEQ // 4, SEQ + 1), jax.random.fold_in(part_splits[1], 1), SEQ // 4, SEQ).astype(jnp.int32)
    word_table = normal_values(splits[2], (VOCAB, D), 1.0, 6.0, ((0, 16),))
    pos_table = normal_values(splits[3], (SEQ, D), 0.5, 3.0)
    emb_gain = jnp.clip(1.0 + 0.15 * jax.random.normal(splits[4], (D,), jnp.float32), 0.25, 1.75)
    emb_bias = normal_values(splits[5], (D,), 0.3, 1.75, (), jnp.float32)
    w_qkv = normal_values(splits[6], (D, 3 * HEADS * HD), D ** -0.5, 0.1875)
    w_out = normal_values(splits[7], (HEADS * HD, D), (HEADS * HD) ** -0.5, 0.25)
    out_bias = normal_values(splits[8], (D,), 0.5, 3.0, (), jnp.float32)
    norm_gain = jnp.clip(1.0 + 0.15 * jax.random.normal(splits[9], (D,), jnp.float32), 0.25, 1.75)
    norm_bias = normal_values(splits[10], (D,), 0.3, 1.75, (), jnp.float32)
    stored_rows = normal_values(part_splits[11], (STORED, D), 1.0, 6.0, ((0, 16),))
    row_owner_keys = jax.random.split(jax.random.fold_in(part_splits[12], 1), KROWS // KROWS_DEV)
    row_owner_turns = jax.random.permutation(jax.random.fold_in(part_splits[12], 3), KROWS // KROWS_DEV)
    row_owner = jax.vmap(lambda own, number: routed_block(jax.random.fold_in(part_splits[12], 2), own, number, KROWS_DEV, N_DP, 1, KCAP, 2))(row_owner_keys, row_owner_turns).reshape((KROWS, 1))
    row_slot = with_ends(skewed_ids(part_splits[13], (KROWS,), CENT_DEV, 2), jax.random.fold_in(part_splits[13], 3), 0, CENT_DEV - 1).astype(jnp.int32)
    centroids = normal_values(part_splits[14], (CLUSTERS, D), 1.0, 6.0, ((0, 16),), jnp.float32)
    return {"token_ids": token_ids, "lengths": lengths, "word_table": word_table, "pos_table": pos_table, "emb_gain": emb_gain, "emb_bias": emb_bias, "w_qkv": w_qkv, "w_out": w_out, "out_bias": out_bias, "norm_gain": norm_gain, "norm_bias": norm_bias, "stored_rows": stored_rows, "row_owner": row_owner, "row_slot": row_slot, "centroids": centroids}


def layer_norm(values, gain, shift):
    center = values - lax.optimization_barrier(jnp.mean(values, axis=-1, keepdims=True))
    spread = lax.optimization_barrier(jnp.mean(center * center, axis=-1, keepdims=True))
    return center * lax.rsqrt(spread + 1e-12) * gain + shift

def encode(tok_rows, lengths, pos_table, emb_gain, emb_bias, w_qkv, w_out, out_bias, norm_gain, norm_bias):
    passes, seq_len, width = tok_rows.shape
    summed = tok_rows.astype(jnp.float32) + pos_table.astype(jnp.float32)[None]
    embedded = layer_norm(summed, emb_gain, emb_bias).astype(jnp.bfloat16)
    flat = embedded.reshape(passes * seq_len, width)
    projected = jnp.dot(flat, w_qkv, preferred_element_type=jnp.float32).astype(jnp.bfloat16)
    projected = projected.reshape(passes, seq_len, 3, HEADS, HD)
    query = projected[:, :, 0].astype(jnp.float32)
    keyset = projected[:, :, 1].astype(jnp.float32)
    valueset = projected[:, :, 2].astype(jnp.float32)
    scores = jnp.einsum('pqhd,pkhd->phqk', query, keyset) * HD ** (-0.5)
    valid = (jnp.arange(seq_len, dtype=jnp.int32)[None, :] < lengths[:, None]).astype(jnp.float32)
    weights = jnp.exp(scores) * valid[:, None, None, :]
    probs = (weights / lax.optimization_barrier(jnp.sum(weights, axis=-1, keepdims=True))).astype(jnp.bfloat16)
    context = jnp.einsum('phqk,pkhd->pqhd', probs.astype(jnp.float32), valueset).astype(jnp.bfloat16)
    context = context.reshape(passes * seq_len, HEADS * HD)
    attended = jnp.dot(context, w_out, preferred_element_type=jnp.float32) + out_bias
    hidden = layer_norm(flat.astype(jnp.float32) + attended, norm_gain, norm_bias).reshape(passes, seq_len, width)
    pooled = lax.optimization_barrier(jnp.sum(hidden * valid[:, :, None], axis=1)) / lax.optimization_barrier(jnp.sum(valid, axis=1, keepdims=True))
    scaled = pooled * lax.rsqrt(lax.optimization_barrier(jnp.mean(pooled * pooled, axis=-1, keepdims=True)) + 1e-06)
    return scaled.astype(jnp.bfloat16)

def reference(token_ids, lengths, word_table, pos_table, emb_gain, emb_bias, w_qkv, w_out, out_bias, norm_gain, norm_bias, stored_rows, row_owner, row_slot, centroids):
    id_blocks = token_ids.reshape(N_DP, PASS_DEV, SEQ)
    len_blocks = lengths.reshape(N_DP, PASS_DEV)

    def one_block(block):
        block_ids, block_len = block
        tok_rows = word_table[block_ids]
        return encode(tok_rows, block_len, pos_table, emb_gain, emb_bias, w_qkv, w_out, out_bias, norm_gain, norm_bias)
    passage_embed = lax.map(one_block, (id_blocks, len_blocks)).reshape(PASSAGES, D)
    rows = jnp.concatenate([stored_rows.reshape(N_DP, STORE_DEV, D), passage_embed.reshape(N_DP, PASS_DEV, D)], axis=1).reshape(KROWS, D)
    cluster = (row_owner[:, 0] * CENT_DEV + row_slot).astype(jnp.int32)
    sums = jax.ops.segment_sum(rows.astype(jnp.float32), cluster, num_segments=CLUSTERS)
    counts = jax.ops.segment_sum(jnp.ones((KROWS,), jnp.float32), cluster, num_segments=CLUSTERS)
    new_centroids = jnp.where(counts[:, None] > 0, sums / jnp.maximum(counts, 1.0)[:, None], centroids)
    return (passage_embed, new_centroids)
```

```python
import jax
import jax.numpy as jnp
from jax import lax
from jax.sharding import PartitionSpec as P

HEADS = 8
HD = 64


def layer_norm(values, gain, shift):
    center = values - jnp.mean(values, axis=-1, keepdims=True)
    spread = jnp.mean(center * center, axis=-1, keepdims=True)
    return center * lax.rsqrt(spread + 1e-12) * gain + shift


def encode(
    tok_rows, lengths, pos_table, emb_gain, emb_bias, w_qkv, w_out, out_bias, norm_gain, norm_bias
):
    passes, seq_len, width = tok_rows.shape
    summed = tok_rows.astype(jnp.float32) + pos_table.astype(jnp.float32)[None]
    embedded = layer_norm(summed, emb_gain, emb_bias).astype(jnp.bfloat16)
    flat = embedded.reshape(passes * seq_len, width)
    projected = jnp.dot(flat, w_qkv, preferred_element_type=jnp.float32).astype(jnp.bfloat16)
    projected = projected.reshape(passes, seq_len, 3, HEADS, HD)
    query = projected[:, :, 0]
    keyset = projected[:, :, 1]
    valueset = projected[:, :, 2]
    scores = jnp.einsum(
        "pqhd,pkhd->phqk", query, keyset, preferred_element_type=jnp.float32
    ) * HD ** (-0.5)
    valid = (jnp.arange(seq_len, dtype=jnp.int32)[None, :] < lengths[:, None]).astype(jnp.float32)
    weights = jnp.exp(scores) * valid[:, None, None, :]
    probs = (weights / jnp.sum(weights, axis=-1, keepdims=True)).astype(jnp.bfloat16)
    context = jnp.einsum(
        "phqk,pkhd->pqhd", probs, valueset, preferred_element_type=jnp.float32
    ).astype(jnp.bfloat16)
    context = context.reshape(passes * seq_len, HEADS * HD)
    attended = jnp.dot(context, w_out, preferred_element_type=jnp.float32) + out_bias
    hidden = layer_norm(flat.astype(jnp.float32) + attended, norm_gain, norm_bias).reshape(
        passes, seq_len, width
    )
    pooled = jnp.sum(hidden * valid[:, :, None], axis=1) / jnp.sum(valid, axis=1, keepdims=True)
    scaled = pooled * lax.rsqrt(jnp.mean(pooled * pooled, axis=-1, keepdims=True) + 1e-06)
    return scaled.astype(jnp.bfloat16)


def slot_rank(target):
    positions = jnp.arange(target.shape[0], dtype=jnp.int32)
    earlier = (target[:, None] == target[None, :]) & (positions[None, :] < positions[:, None])
    return jnp.sum(earlier.astype(jnp.int32), axis=1)


def slot_table(target, peer_count, capacity):
    slot = target * capacity + slot_rank(target)
    return slot[None, :] == jnp.arange(peer_count * capacity, dtype=jnp.int32)[:, None]


def arrivals(mine, values, capacity):
    count = mine.shape[1]
    positions = jnp.arange(count, dtype=jnp.int32)
    before = (positions[:, None] < positions[None, :]).astype(jnp.bfloat16)
    rank = jnp.dot(mine.astype(jnp.bfloat16), before, preferred_element_type=jnp.float32)
    rank = jnp.where(mine, rank.astype(jnp.int32), capacity)
    places = jnp.arange(capacity, dtype=jnp.int32)
    hit = rank[:, None, :] == places[None, :, None]
    return jnp.sum(jnp.where(hit, values[:, None, :] + 1, 0), axis=2) - 1


def shards(
    token_ids,
    lengths,
    word_table,
    pos_table,
    emb_gain,
    emb_bias,
    w_qkv,
    w_out,
    out_bias,
    norm_gain,
    norm_bias,
    stored_rows,
    row_owner,
    row_slot,
    centroids,
):
    peer_count = lax.axis_size("dp")
    me = lax.axis_index("dp")
    width = word_table.shape[1]
    vocab_rows = word_table.shape[0]
    centre_count = centroids.shape[0]
    passes, seq_len = token_ids.shape
    token_list = token_ids.reshape(passes * seq_len)
    token_count = token_list.shape[0]
    row_count = row_slot.shape[0]
    store_count = stored_rows.shape[0]
    owners = row_owner[:, 0]
    token_cap = max(2, 3 * token_count // peer_count)
    row_cap = max(2, 3 * row_count // peer_count)

    plan = lax.all_gather(
        jnp.concatenate([token_list, owners, row_slot]), "dp", axis=0, tiled=False
    )
    all_ids = plan[:, :token_count]
    all_owners = plan[:, token_count : token_count + row_count]
    all_slots = plan[:, token_count + row_count :]

    row_table = slot_table(owners, peer_count, row_cap)
    buffer = jnp.dot(
        row_table[:, :store_count].astype(jnp.bfloat16),
        stored_rows,
        preferred_element_type=jnp.float32,
    ).astype(jnp.bfloat16)
    got_rows = lax.all_to_all(
        buffer.reshape(peer_count, row_cap, width), "dp", split_axis=0, concat_axis=0, tiled=True
    )

    wanted = arrivals(all_ids // vocab_rows == me, all_ids - me * vocab_rows, token_cap)
    wanted = wanted.reshape(peer_count * token_cap)
    chosen = wanted[:, None] == jnp.arange(vocab_rows, dtype=jnp.int32)[None, :]
    found = jnp.dot(
        chosen.astype(jnp.bfloat16), word_table, preferred_element_type=jnp.float32
    ).astype(jnp.bfloat16)
    fetched = lax.all_to_all(
        found.reshape(peer_count, token_cap, width), "dp", split_axis=0, concat_axis=0, tiled=True
    )
    picker = slot_table(token_list // vocab_rows, peer_count, token_cap).T.astype(jnp.bfloat16)
    tok_flat = jnp.dot(
        picker, fetched.reshape(peer_count * token_cap, width), preferred_element_type=jnp.float32
    )
    tok_rows = tok_flat.astype(jnp.bfloat16).reshape(passes, seq_len, width)
    passage_embed = encode(
        tok_rows,
        lengths,
        pos_table,
        emb_gain,
        emb_bias,
        w_qkv,
        w_out,
        out_bias,
        norm_gain,
        norm_bias,
    )
    all_embeds = lax.all_gather(passage_embed, "dp", axis=0, tiled=True)

    centres = jnp.arange(centre_count, dtype=jnp.int32)[:, None]
    places = arrivals(all_owners == me, all_slots, row_cap).reshape(peer_count * row_cap)
    onehot = (centres == places[None, :]).astype(jnp.bfloat16)
    counts = jnp.sum(onehot, axis=1, dtype=jnp.float32)
    sums = jnp.dot(
        onehot, got_rows.reshape(peer_count * row_cap, width), preferred_element_type=jnp.float32
    )
    late = jnp.where(all_owners[:, store_count:] == me, all_slots[:, store_count:], -1)
    late_onehot = (centres == late.reshape(-1)[None, :]).astype(jnp.bfloat16)
    sums = sums + jnp.dot(late_onehot, all_embeds, preferred_element_type=jnp.float32)
    new_centroids = jnp.where(
        counts[:, None] > 0, sums / jnp.maximum(counts, 1.0)[:, None], centroids
    )
    return (passage_embed, new_centroids)


def solution(mesh):
    return jax.shard_map(
        shards,
        mesh=mesh,
        in_specs=(
            P(("groups", "dp"), None),
            P(("groups", "dp")),
            P("dp", None),
            P(),
            P(),
            P(),
            P(),
            P(),
            P(),
            P(),
            P(),
            P(("groups", "dp"), None),
            P(("groups", "dp"), None),
            P(("groups", "dp")),
            P(("groups", "dp"), None),
        ),
        out_specs=(P(("groups", "dp"), None), P(("groups", "dp"), None)),
        check_vma=False,
    )
```

```python
import jax
import jax.numpy as jnp
from jax import lax
from jax.sharding import PartitionSpec as P

HEADS = 8
HD = 64


def layer_norm(values, gain, shift):
    center = values - jnp.mean(values, axis=-1, keepdims=True)
    spread = jnp.mean(center * center, axis=-1, keepdims=True)
    return center * lax.rsqrt(spread + 1e-12) * gain + shift


def encode(
    tok_rows, lengths, pos_table, emb_gain, emb_bias, w_qkv, w_out, out_bias, norm_gain, norm_bias
):
    passes, seq_len, width = tok_rows.shape
    summed = tok_rows.astype(jnp.float32) + pos_table.astype(jnp.float32)[None]
    embedded = layer_norm(summed, emb_gain, emb_bias).astype(jnp.bfloat16)
    flat = embedded.reshape(passes * seq_len, width)
    projected = jnp.dot(flat, w_qkv, preferred_element_type=jnp.float32).astype(jnp.bfloat16)
    projected = projected.reshape(passes, seq_len, 3, HEADS, HD)
    query = projected[:, :, 0]
    keyset = projected[:, :, 1]
    valueset = projected[:, :, 2]
    scores = jnp.einsum(
        "pqhd,pkhd->phqk", query, keyset, preferred_element_type=jnp.float32
    ) * HD ** (-0.5)
    valid = (jnp.arange(seq_len, dtype=jnp.int32)[None, :] < lengths[:, None]).astype(jnp.float32)
    weights = jnp.exp(scores) * valid[:, None, None, :]
    probs = (weights / jnp.sum(weights, axis=-1, keepdims=True)).astype(jnp.bfloat16)
    context = jnp.einsum(
        "phqk,pkhd->pqhd", probs, valueset, preferred_element_type=jnp.float32
    ).astype(jnp.bfloat16)
    context = context.reshape(passes * seq_len, HEADS * HD)
    attended = jnp.dot(context, w_out, preferred_element_type=jnp.float32) + out_bias
    hidden = layer_norm(flat.astype(jnp.float32) + attended, norm_gain, norm_bias).reshape(
        passes, seq_len, width
    )
    pooled = jnp.sum(hidden * valid[:, :, None], axis=1) / jnp.sum(valid, axis=1, keepdims=True)
    scaled = pooled * lax.rsqrt(jnp.mean(pooled * pooled, axis=-1, keepdims=True) + 1e-06)
    return scaled.astype(jnp.bfloat16)


def slot_rank(target):
    positions = jnp.arange(target.shape[0], dtype=jnp.int32)
    earlier = (target[:, None] == target[None, :]) & (positions[None, :] < positions[:, None])
    return jnp.sum(earlier.astype(jnp.int32), axis=1)


def slot_table(target, peer_count, capacity):
    slot = target * capacity + slot_rank(target)
    return slot[None, :] == jnp.arange(peer_count * capacity, dtype=jnp.int32)[:, None]


def place_ints(table, values, empty_value):
    filled = jnp.any(table, axis=1)
    picked = jnp.sum(jnp.where(table, values[None, :], 0), axis=1)
    return jnp.where(filled, picked, empty_value)


def swap_blocks(blocks, axis):
    peers = blocks.shape[0]
    me = lax.axis_index(axis)
    got = [blocks[me]]
    for step in range(1, peers):
        moves = [(i, (i + step) % peers) for i in range(peers)]
        got.append(lax.ppermute(blocks[(me + step) % peers], axis, moves))
    return got


def shards(
    token_ids,
    lengths,
    word_table,
    pos_table,
    emb_gain,
    emb_bias,
    w_qkv,
    w_out,
    out_bias,
    norm_gain,
    norm_bias,
    stored_rows,
    row_owner,
    row_slot,
    centroids,
):
    peer_count = lax.axis_size("dp")
    width = word_table.shape[1]
    vocab_rows = word_table.shape[0]
    centre_count = centroids.shape[0]
    passes, seq_len = token_ids.shape
    token_list = token_ids.reshape(passes * seq_len)
    token_count = token_list.shape[0]
    row_count = row_slot.shape[0]
    store_count = stored_rows.shape[0]
    owners = row_owner[:, 0]
    token_cap = max(2, 3 * token_count // peer_count)
    row_cap = max(2, 3 * row_count // peer_count)

    target = token_list // vocab_rows
    token_table = slot_table(target, peer_count, token_cap)
    requests = place_ints(token_table, token_list - target * vocab_rows, -1)
    row_table = slot_table(owners, peer_count, row_cap)
    places = place_ints(row_table, row_slot, -1)
    late = jnp.where(
        owners[None, store_count:] == jnp.arange(peer_count, dtype=jnp.int32)[:, None],
        row_slot[None, store_count:],
        -1,
    )
    plan = lax.all_to_all(
        jnp.concatenate(
            [requests.reshape(peer_count, token_cap), places.reshape(peer_count, row_cap), late],
            axis=1,
        ),
        "dp",
        split_axis=0,
        concat_axis=0,
        tiled=True,
    )

    buffer = jnp.dot(
        row_table[:, :store_count].astype(jnp.bfloat16),
        stored_rows,
        preferred_element_type=jnp.float32,
    ).astype(jnp.bfloat16)
    got_rows = swap_blocks(buffer.reshape(peer_count, row_cap, width), "dp")

    wanted = plan[:, :token_cap].reshape(peer_count * token_cap)
    chosen = wanted[:, None] == jnp.arange(vocab_rows, dtype=jnp.int32)[None, :]
    found = jnp.dot(
        chosen.astype(jnp.bfloat16), word_table, preferred_element_type=jnp.float32
    ).astype(jnp.bfloat16)
    fetched = lax.all_to_all(
        found.reshape(peer_count, token_cap, width), "dp", split_axis=0, concat_axis=0, tiled=True
    )
    tok_flat = jnp.dot(
        token_table.T.astype(jnp.bfloat16),
        fetched.reshape(peer_count * token_cap, width),
        preferred_element_type=jnp.float32,
    )
    tok_rows = tok_flat.astype(jnp.bfloat16).reshape(passes, seq_len, width)
    passage_embed = encode(
        tok_rows,
        lengths,
        pos_table,
        emb_gain,
        emb_bias,
        w_qkv,
        w_out,
        out_bias,
        norm_gain,
        norm_bias,
    )
    all_embeds = lax.all_to_all(
        jnp.broadcast_to(passage_embed[None], (peer_count, passes, width)),
        "dp",
        split_axis=0,
        concat_axis=0,
        tiled=True,
    ).reshape(peer_count * passes, width)

    centres = jnp.arange(centre_count, dtype=jnp.int32)[:, None]
    got_places = plan[:, token_cap : token_cap + row_cap]
    onehot = (centres == got_places.reshape(peer_count * row_cap)[None, :]).astype(jnp.bfloat16)
    counts = jnp.sum(onehot, axis=1, dtype=jnp.float32)
    order = (lax.axis_index("dp") - jnp.arange(peer_count, dtype=jnp.int32)) % peer_count
    onehot = (centres == got_places[order].reshape(peer_count * row_cap)[None, :]).astype(jnp.bfloat16)
    sums = jnp.dot(onehot, jnp.concatenate(got_rows, axis=0), preferred_element_type=jnp.float32)
    late_onehot = (centres == plan[:, token_cap + row_cap :].reshape(-1)[None, :]).astype(jnp.bfloat16)
    sums = sums + jnp.dot(late_onehot, all_embeds, preferred_element_type=jnp.float32)
    new_centroids = jnp.where(
        counts[:, None] > 0, sums / jnp.maximum(counts, 1.0)[:, None], centroids
    )
    return (passage_embed, new_centroids)


def solution(mesh):
    return jax.shard_map(
        shards,
        mesh=mesh,
        in_specs=(
            P(("groups", "dp"), None),
            P(("groups", "dp")),
            P("dp", None),
            P(),
            P(),
            P(),
            P(),
            P(),
            P(),
            P(),
            P(),
            P(("groups", "dp"), None),
            P(("groups", "dp"), None),
            P(("groups", "dp")),
            P(("groups", "dp"), None),
        ),
        out_specs=(P(("groups", "dp"), None), P(("groups", "dp"), None)),
        check_vma=False,
    )
```

```python
import jax
import jax.numpy as jnp
from jax import lax
from jax.experimental import pallas as pl
from jax.experimental.pallas import tpu as pltpu
from jax.sharding import PartitionSpec as P

HEADS = 8
HD = 64


def normed(values, gain, shift):
    center = values - jnp.mean(values, axis=-1, keepdims=True)
    spread = jnp.mean(center * center, axis=-1, keepdims=True)
    return center * lax.rsqrt(spread + 1e-12) * gain + shift


def head_sums(weights, seq):
    rows, columns = weights.shape
    lane = lax.broadcasted_iota(jnp.int32, (rows, 2 * seq), 1)
    sums = []
    for start in range(0, columns, 2 * seq):
        pair = weights[:, start : start + 2 * seq]
        first = jnp.sum(jnp.where(lane < seq, pair, 0.0), axis=1, keepdims=True)
        second = jnp.sum(jnp.where(lane < seq, 0.0, pair), axis=1, keepdims=True)
        sums.append(jnp.where(lane < seq, first, second))
    return jnp.concatenate(sums, axis=1)


def encode_kernel(
    lengths, slots, fetched, pos, emb_gain, emb_bias, w_qkv, w_out, out_bias, norm_gain, norm_bias, out
):
    tokens, slot_count = slots.shape[0], fetched.shape[0]
    passes = out.shape[0]
    seq = tokens // passes
    inner = HEADS * HD
    spot = lax.broadcasted_iota(jnp.int32, (tokens, slot_count), 1)
    picker = jnp.where(slots[...] == spot, 1.0, 0.0).astype(jnp.bfloat16)
    tok = jnp.dot(picker, fetched[...], preferred_element_type=jnp.float32)
    where_at = pos[...].astype(jnp.float32)
    summed = tok + jnp.concatenate([where_at] * passes, axis=0)
    embedded = normed(summed, emb_gain[...], emb_bias[...]).astype(jnp.bfloat16)
    projected = jnp.dot(embedded, w_qkv[...], preferred_element_type=jnp.float32)
    projected = projected.astype(jnp.bfloat16)

    block_row = lax.broadcasted_iota(jnp.int32, (HEADS * seq, inner), 0) // seq
    block_col = lax.broadcasted_iota(jnp.int32, (HEADS * seq, inner), 1) // HD
    same = block_row == block_col
    lane = lax.broadcasted_iota(jnp.int32, (seq, HEADS * seq), 1) % seq
    contexts = []
    for p in range(passes):
        part = projected[p * seq : (p + 1) * seq]
        query, keys, vals = part[:, :inner], part[:, inner : 2 * inner], part[:, 2 * inner :]
        zero = jnp.zeros((), jnp.bfloat16)
        keys = jnp.where(same, jnp.concatenate([keys] * HEADS, axis=0), zero)
        vals = jnp.where(same, jnp.concatenate([vals] * HEADS, axis=0), zero)
        scores = lax.dot_general(
            query, keys, (((1,), (1,)), ((), ())), preferred_element_type=jnp.float32
        ) * HD ** (-0.5)
        weights = jnp.where(lane < lengths[p], jnp.exp(scores), 0.0)
        probs = (weights / head_sums(weights, seq)).astype(jnp.bfloat16)
        contexts.append(jnp.dot(probs, vals, preferred_element_type=jnp.float32))
    context = jnp.concatenate(contexts, axis=0).astype(jnp.bfloat16)
    attended = jnp.dot(context, w_out[...], preferred_element_type=jnp.float32) + out_bias[...]
    hidden = normed(embedded.astype(jnp.float32) + attended, norm_gain[...], norm_bias[...])
    row = lax.broadcasted_iota(jnp.int32, (seq, 1), 0)
    for p in range(passes):
        kept = jnp.where(row < lengths[p], hidden[p * seq : (p + 1) * seq], 0.0)
        pooled = jnp.sum(kept, axis=0, keepdims=True) / lengths[p].astype(jnp.float32)
        scale = lax.rsqrt(jnp.mean(pooled * pooled, axis=-1, keepdims=True) + 1e-06)
        out[p : p + 1, :] = (pooled * scale).astype(jnp.bfloat16)


def encode(
    slots, fetched, lengths, pos_table, emb_gain, emb_bias, w_qkv, w_out, out_bias, norm_gain, norm_bias
):
    width = fetched.shape[1]
    tokens = slots.shape[0]
    passes = lengths.shape[0]
    macs = tokens * width * (fetched.shape[0] + 4 * HEADS * HD)
    return pl.pallas_call(
        encode_kernel,
        out_shape=jax.ShapeDtypeStruct((passes, width), jnp.bfloat16),
        in_specs=[pl.BlockSpec(memory_space=pltpu.SMEM)]
        + [pl.BlockSpec(memory_space=pltpu.VMEM)] * 10,
        out_specs=pl.BlockSpec(memory_space=pltpu.VMEM),
        compiler_params=pltpu.CompilerParams(vmem_limit_bytes=32 * 1024 * 1024),
        cost_estimate=pl.CostEstimate(
            flops=2 * macs, bytes_accessed=6 * 1024 * 1024, transcendentals=0
        ),
        name="encode",
    )(
        lengths,
        slots[:, None],
        fetched,
        pos_table,
        emb_gain[None],
        emb_bias[None],
        w_qkv,
        w_out,
        out_bias[None],
        norm_gain[None],
        norm_bias[None],
    )


def slot_rank(target):
    positions = jnp.arange(target.shape[0], dtype=jnp.int32)
    earlier = (target[:, None] == target[None, :]) & (positions[None, :] < positions[:, None])
    return jnp.sum(earlier.astype(jnp.int32), axis=1)


def place_ints(slot, values, slot_count):
    table = slot[None, :] == jnp.arange(slot_count, dtype=jnp.int32)[:, None]
    return jnp.sum(jnp.where(table, values[None, :] + 1, 0), axis=1) - 1


def pack_rows(slot, rows, slot_count):
    table = slot[None, :] == jnp.arange(slot_count, dtype=jnp.int32)[:, None]
    packed = jnp.dot(table.astype(jnp.bfloat16), rows, preferred_element_type=jnp.float32)
    return packed.astype(jnp.bfloat16)


def gather_doubling(block, axis):
    peers = lax.axis_size(axis)
    reach = 1
    while reach < peers:
        moves = [(i, i ^ reach) for i in range(peers)]
        block = jnp.concatenate([block, lax.ppermute(block, axis, moves)], axis=0)
        reach *= 2
    return block


def update_kernel(places, late, rows, embeds, centroids, out):
    count = out.shape[0]
    first = pl.program_id(0) * count

    def onehot(where_to):
        centre = lax.broadcasted_iota(jnp.int32, (count, where_to.shape[1]), 0) + first
        return jnp.where(centre == where_to[...], 1.0, 0.0)

    early_hot, late_hot = onehot(places), onehot(late)
    sums = jnp.dot(
        early_hot.astype(jnp.bfloat16), rows[...], preferred_element_type=jnp.float32
    ) + jnp.dot(late_hot.astype(jnp.bfloat16), embeds[...], preferred_element_type=jnp.float32)
    counts = jnp.sum(early_hot, axis=1, keepdims=True)
    out[...] = jnp.where(counts > 0, sums / jnp.maximum(counts, 1.0), centroids[...])


def update(places, late, rows, embeds, centroids):
    centre_count, width = centroids.shape
    block = 128
    whole = lambda array: pl.BlockSpec(array.shape, lambda i: (0, 0))
    part = pl.BlockSpec((block, width), lambda i: (i, 0))
    return pl.pallas_call(
        update_kernel,
        grid=(centre_count // block,),
        out_shape=jax.ShapeDtypeStruct(centroids.shape, jnp.float32),
        in_specs=[whole(places), whole(late), whole(rows), whole(embeds), part],
        out_specs=part,
        compiler_params=pltpu.CompilerParams(vmem_limit_bytes=32 * 1024 * 1024),
        cost_estimate=pl.CostEstimate(
            flops=2 * centre_count * width * rows.shape[0],
            bytes_accessed=8 * centre_count * width,
            transcendentals=0,
        ),
        name="update",
    )(places, late, rows, embeds, centroids)


def shards(
    token_ids,
    lengths,
    word_table,
    pos_table,
    emb_gain,
    emb_bias,
    w_qkv,
    w_out,
    out_bias,
    norm_gain,
    norm_bias,
    stored_rows,
    row_owner,
    row_slot,
    centroids,
):
    peer_count = lax.axis_size("dp")
    half = peer_count // 2
    me = lax.axis_index("dp")
    base = me // half * half
    peers = jnp.arange(peer_count, dtype=jnp.int32)
    width = word_table.shape[1]
    vocab_rows = word_table.shape[0]
    passes, seq_len = token_ids.shape
    token_list = token_ids.reshape(passes * seq_len)
    token_count = token_list.shape[0]
    row_count = row_slot.shape[0]
    store_count = stored_rows.shape[0]
    owners = row_owner[:, 0]
    token_cap = max(2, 3 * token_count // peer_count)
    row_cap = max(2, 3 * row_count // peer_count)

    across = [(i, (i + half) % peer_count) for i in range(peer_count)]
    partner_owners = lax.ppermute(owners, "dp", across)
    partner_rows = lax.ppermute(stored_rows, "dp", across)

    target = token_list // vocab_rows
    token_slot = target * token_cap + slot_rank(target)
    requests = place_ints(token_slot, token_list - target * vocab_rows, peer_count * token_cap)
    row_rank = slot_rank(owners)
    places = place_ints(owners * row_cap + row_rank, row_slot, peer_count * row_cap)
    late = jnp.where(owners[None, store_count:] == peers[:, None], row_slot[None, store_count:], -1)
    plan = lax.all_to_all(
        jnp.concatenate(
            [requests.reshape(peer_count, token_cap), places.reshape(peer_count, row_cap), late],
            axis=1,
        ),
        "dp",
        split_axis=0,
        concat_axis=0,
        tiled=True,
    )
    wanted = plan[:, :token_cap].reshape(peer_count * token_cap)
    chosen = wanted[:, None] == jnp.arange(vocab_rows, dtype=jnp.int32)[None, :]
    found = jnp.dot(
        chosen.astype(jnp.bfloat16), word_table, preferred_element_type=jnp.float32
    ).astype(jnp.bfloat16)
    fetched = lax.all_to_all(
        found.reshape(peer_count, token_cap, width), "dp", split_axis=0, concat_axis=0, tiled=True
    ).reshape(peer_count * token_cap, width)

    def half_pack(row_block, row_owners, ranks):
        inside = (row_owners >= base) & (row_owners < base + half)
        slot = jnp.where(inside, (row_owners - base) * row_cap + ranks, -1)[:store_count]
        return pack_rows(slot, row_block, half * row_cap).reshape(half, row_cap, width)

    own_pack = half_pack(stored_rows, owners, row_rank)
    partner_pack = half_pack(partner_rows, partner_owners, slot_rank(partner_owners))
    groups = [list(range(half)), list(range(half, peer_count))]
    got_rows = lax.all_to_all(
        jnp.concatenate([own_pack, partner_pack], axis=1),
        "dp",
        split_axis=0,
        concat_axis=0,
        tiled=True,
        axis_index_groups=groups,
    ).reshape(peer_count * row_cap, width)
    got_places = plan[:, token_cap : token_cap + row_cap].reshape(2, half, row_cap)
    got_places = jnp.where(base == 0, got_places, got_places[::-1])
    got_places = got_places.transpose(1, 0, 2).reshape(1, peer_count * row_cap)

    passage_embed = encode(
        token_slot,
        fetched,
        lengths,
        pos_table,
        emb_gain,
        emb_bias,
        w_qkv,
        w_out,
        out_bias,
        norm_gain,
        norm_bias,
    )
    all_embeds = gather_doubling(passage_embed, "dp")
    late_places = plan[:, token_cap + row_cap :][me ^ peers].reshape(1, -1)
    new_centroids = update(got_places, late_places, got_rows, all_embeds, centroids)
    return (passage_embed, new_centroids)


def solution(mesh):
    return jax.shard_map(
        shards,
        mesh=mesh,
        in_specs=(
            P(("groups", "dp"), None),
            P(("groups", "dp")),
            P("dp", None),
            P(),
            P(),
            P(),
            P(),
            P(),
            P(),
            P(),
            P(),
            P(("groups", "dp"), None),
            P(("groups", "dp"), None),
            P(("groups", "dp")),
            P(("groups", "dp"), None),
        ),
        out_specs=(P(("groups", "dp"), None), P(("groups", "dp"), None)),
        check_vma=False,
    )
```

```python
import functools

import jax
import jax.numpy as jnp
from jax import lax
from jax.experimental import pallas as pl
from jax.experimental.pallas import tpu as pltpu
from jax.sharding import PartitionSpec as P

HEADS = 8
HD = 64


def normed(values, gain, shift):
    center = values - jnp.mean(values, axis=-1, keepdims=True)
    spread = jnp.mean(center * center, axis=-1, keepdims=True)
    return center * lax.rsqrt(spread + 1e-12) * gain + shift


def head_sums(weights, seq):
    rows, columns = weights.shape
    lane = lax.broadcasted_iota(jnp.int32, (rows, 2 * seq), 1)
    sums = []
    for start in range(0, columns, 2 * seq):
        pair = weights[:, start : start + 2 * seq]
        first = jnp.sum(jnp.where(lane < seq, pair, 0.0), axis=1, keepdims=True)
        second = jnp.sum(jnp.where(lane < seq, 0.0, pair), axis=1, keepdims=True)
        sums.append(jnp.where(lane < seq, first, second))
    return jnp.concatenate(sums, axis=1)


def encode_kernel(
    lengths, slots, fetched, pos, emb_gain, emb_bias, w_qkv, w_out, out_bias, norm_gain, norm_bias, out
):
    tokens, slot_count = slots.shape[0], fetched.shape[0]
    passes = out.shape[0]
    seq = tokens // passes
    inner = HEADS * HD
    spot = lax.broadcasted_iota(jnp.int32, (tokens, slot_count), 1)
    picker = jnp.where(slots[...] == spot, 1.0, 0.0).astype(jnp.bfloat16)
    tok = jnp.dot(picker, fetched[...], preferred_element_type=jnp.float32)
    where_at = pos[...].astype(jnp.float32)
    summed = tok + jnp.concatenate([where_at] * passes, axis=0)
    embedded = normed(summed, emb_gain[...], emb_bias[...]).astype(jnp.bfloat16)
    projected = jnp.dot(embedded, w_qkv[...], preferred_element_type=jnp.float32)
    projected = projected.astype(jnp.bfloat16)

    block_row = lax.broadcasted_iota(jnp.int32, (HEADS * seq, inner), 0) // seq
    block_col = lax.broadcasted_iota(jnp.int32, (HEADS * seq, inner), 1) // HD
    same = block_row == block_col
    lane = lax.broadcasted_iota(jnp.int32, (seq, HEADS * seq), 1) % seq
    contexts = []
    for p in range(passes):
        part = projected[p * seq : (p + 1) * seq]
        query, keys, vals = part[:, :inner], part[:, inner : 2 * inner], part[:, 2 * inner :]
        zero = jnp.zeros((), jnp.bfloat16)
        keys = jnp.where(same, jnp.concatenate([keys] * HEADS, axis=0), zero)
        vals = jnp.where(same, jnp.concatenate([vals] * HEADS, axis=0), zero)
        scores = lax.dot_general(
            query, keys, (((1,), (1,)), ((), ())), preferred_element_type=jnp.float32
        ) * HD ** (-0.5)
        weights = jnp.where(lane < lengths[p], jnp.exp(scores), 0.0)
        probs = (weights / head_sums(weights, seq)).astype(jnp.bfloat16)
        contexts.append(jnp.dot(probs, vals, preferred_element_type=jnp.float32))
    context = jnp.concatenate(contexts, axis=0).astype(jnp.bfloat16)
    attended = jnp.dot(context, w_out[...], preferred_element_type=jnp.float32) + out_bias[...]
    hidden = normed(embedded.astype(jnp.float32) + attended, norm_gain[...], norm_bias[...])
    row = lax.broadcasted_iota(jnp.int32, (seq, 1), 0)
    for p in range(passes):
        kept = jnp.where(row < lengths[p], hidden[p * seq : (p + 1) * seq], 0.0)
        pooled = jnp.sum(kept, axis=0, keepdims=True) / lengths[p].astype(jnp.float32)
        scale = lax.rsqrt(jnp.mean(pooled * pooled, axis=-1, keepdims=True) + 1e-06)
        out[p : p + 1, :] = (pooled * scale).astype(jnp.bfloat16)


def encode(
    slots, fetched, lengths, pos_table, emb_gain, emb_bias, w_qkv, w_out, out_bias, norm_gain, norm_bias
):
    width = fetched.shape[1]
    tokens = slots.shape[0]
    passes = lengths.shape[0]
    macs = tokens * width * (fetched.shape[0] + 4 * HEADS * HD)
    return pl.pallas_call(
        encode_kernel,
        out_shape=jax.ShapeDtypeStruct((passes, width), jnp.bfloat16),
        in_specs=[pl.BlockSpec(memory_space=pltpu.SMEM)]
        + [pl.BlockSpec(memory_space=pltpu.VMEM)] * 10,
        out_specs=pl.BlockSpec(memory_space=pltpu.VMEM),
        compiler_params=pltpu.CompilerParams(vmem_limit_bytes=32 * 1024 * 1024),
        cost_estimate=pl.CostEstimate(
            flops=2 * macs, bytes_accessed=6 * 1024 * 1024, transcendentals=0
        ),
        name="encode",
    )(
        lengths,
        slots[:, None],
        fetched,
        pos_table,
        emb_gain[None],
        emb_bias[None],
        w_qkv,
        w_out,
        out_bias[None],
        norm_gain[None],
        norm_bias[None],
    )


def slot_rank(target):
    positions = jnp.arange(target.shape[0], dtype=jnp.int32)
    earlier = (target[:, None] == target[None, :]) & (positions[None, :] < positions[:, None])
    return jnp.sum(earlier.astype(jnp.int32), axis=1)


def place_ints(slot, values, slot_count):
    table = slot[None, :] == jnp.arange(slot_count, dtype=jnp.int32)[:, None]
    return jnp.sum(jnp.where(table, values[None, :] + 1, 0), axis=1) - 1


def pack_kernel(row_cap, own_slot, partner_slot, own_rows, partner_rows, *outs):
    slot_count = len(outs) * row_cap
    for source, (slot, rows) in enumerate(((own_slot, own_rows), (partner_slot, partner_rows))):
        spot = lax.broadcasted_iota(jnp.int32, (slot_count, rows.shape[0]), 0)
        table = jnp.where(slot[:, : rows.shape[0]] == spot, 1.0, 0.0).astype(jnp.bfloat16)
        packed = jnp.dot(table, rows[...], preferred_element_type=jnp.float32)
        packed = packed.astype(jnp.bfloat16)
        for step, out in enumerate(outs):
            out[source * row_cap : (source + 1) * row_cap, :] = packed[
                step * row_cap : (step + 1) * row_cap
            ]


def pack_rows(own_slot, partner_slot, own_rows, partner_rows, steps, row_cap):
    width = own_rows.shape[1]
    return pl.pallas_call(
        functools.partial(pack_kernel, row_cap),
        out_shape=[jax.ShapeDtypeStruct((2 * row_cap, width), jnp.bfloat16)] * steps,
        in_specs=[pl.BlockSpec(memory_space=pltpu.VMEM)] * 4,
        out_specs=[pl.BlockSpec(memory_space=pltpu.VMEM)] * steps,
        compiler_params=pltpu.CompilerParams(vmem_limit_bytes=32 * 1024 * 1024),
        cost_estimate=pl.CostEstimate(
            flops=4 * steps * row_cap * width * own_rows.shape[0],
            bytes_accessed=4 * width * (own_rows.shape[0] + steps * row_cap),
            transcendentals=0,
        ),
        name="pack",
    )(own_slot[None], partner_slot[None], own_rows, partner_rows)


def update_kernel(places, late, embeds, centroids, *rest):
    pieces, out, rows = rest[:-2], rest[-2], rest[-1]
    count = out.shape[0]
    step = pl.program_id(0)

    @pl.when(step == 0)
    def _():
        at = 0
        for piece in pieces:
            rows[at : at + piece.shape[0], :] = piece[...]
            at += piece.shape[0]

    def onehot(where_to):
        centre = lax.broadcasted_iota(jnp.int32, (count, where_to.shape[1]), 0) + step * count
        return jnp.where(centre == where_to[...], 1.0, 0.0)

    early_hot, late_hot = onehot(places), onehot(late)
    sums = jnp.dot(
        early_hot.astype(jnp.bfloat16), rows[...], preferred_element_type=jnp.float32
    ) + jnp.dot(late_hot.astype(jnp.bfloat16), embeds[...], preferred_element_type=jnp.float32)
    counts = jnp.sum(early_hot, axis=1, keepdims=True)
    out[...] = jnp.where(counts > 0, sums / jnp.maximum(counts, 1.0), centroids[...])


def update(places, late, embeds, centroids, pieces):
    centre_count, width = centroids.shape
    block = 128
    whole = lambda array: pl.BlockSpec(array.shape, lambda i: (0, 0))
    part = pl.BlockSpec((block, width), lambda i: (i, 0))
    row_total = sum(piece.shape[0] for piece in pieces)
    return pl.pallas_call(
        update_kernel,
        grid=(centre_count // block,),
        out_shape=jax.ShapeDtypeStruct(centroids.shape, jnp.float32),
        in_specs=[whole(places), whole(late), whole(embeds), part]
        + [whole(piece) for piece in pieces],
        out_specs=part,
        scratch_shapes=[pltpu.VMEM((row_total, width), jnp.bfloat16)],
        compiler_params=pltpu.CompilerParams(vmem_limit_bytes=32 * 1024 * 1024),
        cost_estimate=pl.CostEstimate(
            flops=2 * centre_count * width * row_total,
            bytes_accessed=8 * centre_count * width,
            transcendentals=0,
        ),
        name="update",
    )(places, late, embeds, centroids, *pieces)


def shards(
    token_ids,
    lengths,
    word_table,
    pos_table,
    emb_gain,
    emb_bias,
    w_qkv,
    w_out,
    out_bias,
    norm_gain,
    norm_bias,
    stored_rows,
    row_owner,
    row_slot,
    centroids,
):
    peer_count = lax.axis_size("dp")
    half = peer_count // 2
    me = lax.axis_index("dp")
    base = me // half * half
    peers = jnp.arange(peer_count, dtype=jnp.int32)
    width = word_table.shape[1]
    vocab_rows = word_table.shape[0]
    passes, seq_len = token_ids.shape
    token_list = token_ids.reshape(passes * seq_len)
    token_count = token_list.shape[0]
    row_count = row_slot.shape[0]
    store_count = stored_rows.shape[0]
    owners = row_owner[:, 0]
    token_cap = max(2, 3 * token_count // peer_count)
    row_cap = max(2, 3 * row_count // peer_count)

    across = [(i, (i + half) % peer_count) for i in range(peer_count)]
    partner_rows = lax.ppermute(stored_rows, "dp", across)
    row_rank = slot_rank(owners)

    def half_slot(holder):
        first = holder // half * half
        inside = (owners >= first) & (owners < first + half)
        return jnp.where(inside, (owners - holder + half) % half * row_cap + row_rank, -1)

    own_slot = half_slot(me)
    partner_slot = lax.ppermute(half_slot((me + half) % peer_count), "dp", across)

    target = token_list // vocab_rows
    token_slot = target * token_cap + slot_rank(target)
    requests = place_ints(token_slot, token_list - target * vocab_rows, peer_count * token_cap)
    places = place_ints(owners * row_cap + row_rank, row_slot, peer_count * row_cap)
    late = jnp.where(owners[None, store_count:] == peers[:, None], row_slot[None, store_count:], -1)
    plan = lax.all_to_all(
        jnp.concatenate(
            [requests.reshape(peer_count, token_cap), places.reshape(peer_count, row_cap), late],
            axis=1,
        ),
        "dp",
        split_axis=0,
        concat_axis=0,
        tiled=True,
    )
    plan, partner_rows = lax.optimization_barrier((plan, partner_rows))
    wanted = plan[:, :token_cap].reshape(peer_count * token_cap)
    chosen = wanted[:, None] == jnp.arange(vocab_rows, dtype=jnp.int32)[None, :]
    found = jnp.dot(
        chosen.astype(jnp.bfloat16), word_table, preferred_element_type=jnp.float32
    ).astype(jnp.bfloat16)
    fetched = lax.all_to_all(
        found.reshape(peer_count, token_cap, width), "dp", split_axis=0, concat_axis=0, tiled=True
    ).reshape(peer_count * token_cap, width)

    blocks = pack_rows(own_slot, partner_slot, stored_rows, partner_rows, half, row_cap)
    got_rows = [blocks[0]]
    for step in range(1, half):
        moves = [(i, i // half * half + (i + step) % half) for i in range(peer_count)]
        got_rows.append(lax.ppermute(blocks[step], "dp", moves))
    sources = base + (me - jnp.arange(half, dtype=jnp.int32)) % half
    sources = jnp.stack([sources, (sources + half) % peer_count], axis=1).reshape(peer_count)
    got_places = plan[:, token_cap : token_cap + row_cap][sources].reshape(1, peer_count * row_cap)
    late_places = plan[:, token_cap + row_cap :].reshape(1, -1)

    passage_embed = encode(
        token_slot,
        fetched,
        lengths,
        pos_table,
        emb_gain,
        emb_bias,
        w_qkv,
        w_out,
        out_bias,
        norm_gain,
        norm_bias,
    )
    all_embeds = lax.all_to_all(
        jnp.broadcast_to(passage_embed[None], (peer_count, passes, width)),
        "dp",
        split_axis=0,
        concat_axis=0,
        tiled=True,
    ).reshape(peer_count * passes, width)
    new_centroids = update(got_places, late_places, all_embeds, centroids, got_rows)
    return (passage_embed, new_centroids)


def solution(mesh):
    return jax.shard_map(
        shards,
        mesh=mesh,
        in_specs=(
            P(("groups", "dp"), None),
            P(("groups", "dp")),
            P("dp", None),
            P(),
            P(),
            P(),
            P(),
            P(),
            P(),
            P(),
            P(),
            P(("groups", "dp"), None),
            P(("groups", "dp"), None),
            P(("groups", "dp")),
            P(("groups", "dp"), None),
        ),
        out_specs=(P(("groups", "dp"), None), P(("groups", "dp"), None)),
        check_vma=False,
    )
```

```python
import functools

import jax
import jax.numpy as jnp
from jax import lax
from jax.experimental import pallas as pl
from jax.experimental.pallas import tpu as pltpu
from jax.sharding import PartitionSpec as P

HEADS = 8
HD = 64


def normed(values, gain, shift):
    center = values - jnp.mean(values, axis=-1, keepdims=True)
    spread = jnp.mean(center * center, axis=-1, keepdims=True)
    return center * lax.rsqrt(spread + 1e-12) * gain + shift


def head_sums(weights, seq):
    rows, columns = weights.shape
    lane = lax.broadcasted_iota(jnp.int32, (rows, 2 * seq), 1)
    sums = []
    for start in range(0, columns, 2 * seq):
        pair = weights[:, start : start + 2 * seq]
        first = jnp.sum(jnp.where(lane < seq, pair, 0.0), axis=1, keepdims=True)
        second = jnp.sum(jnp.where(lane < seq, 0.0, pair), axis=1, keepdims=True)
        sums.append(jnp.where(lane < seq, first, second))
    return jnp.concatenate(sums, axis=1)


def encode_kernel(
    lengths,
    slots,
    fetched,
    pos,
    emb_gain,
    emb_bias,
    w_qkv_far,
    w_out_far,
    out_bias,
    norm_gain,
    norm_bias,
    out,
    spread,
    w_qkv,
    w_out,
    arrived,
):
    qkv_copy = pltpu.make_async_copy(w_qkv_far, w_qkv, arrived.at[0])
    out_copy = pltpu.make_async_copy(w_out_far, w_out, arrived.at[1])
    qkv_copy.start()
    out_copy.start()
    tokens, slot_count = slots.shape[0], fetched.shape[0]
    passes = out.shape[0]
    seq = tokens // passes
    inner = HEADS * HD
    spot = lax.broadcasted_iota(jnp.int32, (tokens, slot_count), 1)
    picker = jnp.where(slots[...] == spot, 1.0, 0.0).astype(jnp.bfloat16)
    tok = jnp.dot(picker, fetched[...], preferred_element_type=jnp.float32)
    where_at = pos[...].astype(jnp.float32)
    summed = tok + jnp.concatenate([where_at] * passes, axis=0)
    embedded = normed(summed, emb_gain[...], emb_bias[...]).astype(jnp.bfloat16)
    qkv_copy.wait()
    projected = jnp.dot(embedded, w_qkv[...], preferred_element_type=jnp.float32)
    projected = projected.astype(jnp.bfloat16)

    block_row = lax.broadcasted_iota(jnp.int32, (HEADS * seq, inner), 0) // seq
    block_col = lax.broadcasted_iota(jnp.int32, (HEADS * seq, inner), 1) // HD
    same = block_row == block_col
    lane = lax.broadcasted_iota(jnp.int32, (seq, HEADS * seq), 1) % seq
    contexts = []
    for p in range(passes):
        part = projected[p * seq : (p + 1) * seq]
        query, keys, vals = part[:, :inner], part[:, inner : 2 * inner], part[:, 2 * inner :]
        zero = jnp.zeros((), jnp.bfloat16)
        keys = jnp.where(same, jnp.concatenate([keys] * HEADS, axis=0), zero)
        vals = jnp.where(same, jnp.concatenate([vals] * HEADS, axis=0), zero)
        scores = lax.dot_general(
            query, keys, (((1,), (1,)), ((), ())), preferred_element_type=jnp.float32
        ) * HD ** (-0.5)
        weights = jnp.where(lane < lengths[p], jnp.exp(scores), 0.0)
        probs = (weights / head_sums(weights, seq)).astype(jnp.bfloat16)
        contexts.append(jnp.dot(probs, vals, preferred_element_type=jnp.float32))
    context = jnp.concatenate(contexts, axis=0).astype(jnp.bfloat16)
    out_copy.wait()
    attended = jnp.dot(context, w_out[...], preferred_element_type=jnp.float32) + out_bias[...]
    hidden = normed(embedded.astype(jnp.float32) + attended, norm_gain[...], norm_bias[...])
    row = lax.broadcasted_iota(jnp.int32, (seq, 1), 0)
    for p in range(passes):
        kept = jnp.where(row < lengths[p], hidden[p * seq : (p + 1) * seq], 0.0)
        pooled = jnp.sum(kept, axis=0, keepdims=True) / lengths[p].astype(jnp.float32)
        scale = lax.rsqrt(jnp.mean(pooled * pooled, axis=-1, keepdims=True) + 1e-06)
        out[p : p + 1, :] = (pooled * scale).astype(jnp.bfloat16)
    spread[...] = jnp.broadcast_to(out[...][None], spread.shape)


def encode(
    peers, slots, fetched, lengths, pos_table, emb_gain, emb_bias, w_qkv, w_out, out_bias, norm_gain, norm_bias
):
    width = fetched.shape[1]
    tokens = slots.shape[0]
    passes = lengths.shape[0]
    macs = tokens * width * (fetched.shape[0] + 4 * HEADS * HD)
    return pl.pallas_call(
        encode_kernel,
        out_shape=[
            jax.ShapeDtypeStruct((passes, width), jnp.bfloat16),
            jax.ShapeDtypeStruct((peers, passes, width), jnp.bfloat16),
        ],
        in_specs=[pl.BlockSpec(memory_space=pltpu.SMEM)]
        + [pl.BlockSpec(memory_space=pltpu.VMEM)] * 5
        + [pl.BlockSpec(memory_space=pltpu.HBM)] * 2
        + [pl.BlockSpec(memory_space=pltpu.VMEM)] * 3,
        out_specs=[pl.BlockSpec(memory_space=pltpu.VMEM)] * 2,
        scratch_shapes=[
            pltpu.VMEM(w_qkv.shape, w_qkv.dtype),
            pltpu.VMEM(w_out.shape, w_out.dtype),
            pltpu.SemaphoreType.DMA((2,)),
        ],
        compiler_params=pltpu.CompilerParams(vmem_limit_bytes=32 * 1024 * 1024),
        cost_estimate=pl.CostEstimate(
            flops=2 * macs, bytes_accessed=6 * 1024 * 1024, transcendentals=0
        ),
        name="encode",
    )(
        lengths,
        slots,
        fetched,
        pos_table,
        emb_gain[None],
        emb_bias[None],
        w_qkv,
        w_out,
        out_bias[None],
        norm_gain[None],
        norm_bias[None],
    )


def route_kernel(
    sizes, token_ids, owners, row_slot, plan, token_slot, own_slot, partner_slot
):
    peers, vocab_rows, token_cap, row_cap, pooled = sizes
    half = peers // 2
    me = lax.axis_index("dp")
    ids = jnp.concatenate([token_ids[p : p + 1, :] for p in range(token_ids.shape[0])], axis=1)
    tokens, rows = ids.shape[1], owners.shape[1]
    count = tokens + rows
    edge = (lax.broadcasted_iota(jnp.int32, (peers, tokens), 0) + 1) * vocab_rows
    holder = jnp.sum(jnp.where(ids >= edge, 1, 0), axis=0, keepdims=True)
    values = jnp.concatenate([ids - holder * vocab_rows, row_slot[...]], axis=1)

    kind = jnp.concatenate([holder, owners[...] + peers], axis=1)
    at = lax.broadcasted_iota(jnp.int32, (count, count), 0)
    by = lax.broadcasted_iota(jnp.int32, (count, count), 1)
    across = jnp.broadcast_to(kind, (count, count))
    down = jnp.sum(jnp.where(at == by, across, 0), axis=1, keepdims=True)
    same = down == across
    rank_row = jnp.sum(jnp.where(same & (at < by), 1, 0), axis=0, keepdims=True)
    rank_col = jnp.sum(jnp.where(same & (by < at), 1, 0), axis=1, keepdims=True)

    goal = jnp.concatenate([holder, owners[...]], axis=1)
    peer = lax.broadcasted_iota(jnp.int32, (peers, count), 0)
    left = jnp.where(peer == goal, values + 1, 0).astype(jnp.float32)
    columns = plan.shape[1]
    column = lax.broadcasted_iota(jnp.int32, (count, columns), 1)
    entry = lax.broadcasted_iota(jnp.int32, (count, 1), 0)
    first = jnp.where(entry < tokens, rank_col, rank_col + token_cap)
    second = entry - (count - pooled) + token_cap + row_cap
    second = jnp.where(entry < count - pooled, -1, second)
    right = jnp.where((column == first) | (column == second), 1.0, 0.0)
    filled = jnp.dot(
        left, right, preferred_element_type=jnp.float32, precision=lax.Precision.HIGHEST
    )
    plan[...] = filled.astype(jnp.int32) - 1
    token_slot[...] = down[:tokens] * token_cap + rank_col[:tokens]

    def half_slot(device):
        first = jnp.where(device < half, 0, half)
        inside = (owners[...] >= first) & (owners[...] < first + half)
        step = owners[...] - device
        step = jnp.where(step < 0, step + half, step)
        return jnp.where(inside, step * row_cap + rank_row[:, tokens:], -1)

    own_slot[...] = half_slot(me)
    partner_slot[...] = half_slot(jnp.where(me < half, me + half, me - half))


def route(token_ids, owners, row_slot, sizes):
    peers, _, token_cap, row_cap, pooled = sizes
    passes, seq_len = token_ids.shape
    rows = owners.shape[1]
    ints = lambda *shape: jax.ShapeDtypeStruct(shape, jnp.int32)
    return pl.pallas_call(
        functools.partial(route_kernel, sizes),
        out_shape=[
            ints(peers, token_cap + row_cap + pooled),
            ints(passes * seq_len, 1),
            ints(1, rows),
            ints(1, rows),
        ],
        in_specs=[pl.BlockSpec(memory_space=pltpu.VMEM)] * 3,
        out_specs=[pl.BlockSpec(memory_space=pltpu.VMEM)] * 4,
        name="route",
    )(token_ids, owners, row_slot)


def pack_kernel(row_cap, own_slot, partner_slot, own_rows, partner_rows, *outs):
    slot_count = len(outs) * row_cap
    for source, (slot, rows) in enumerate(((own_slot, own_rows), (partner_slot, partner_rows))):
        spot = lax.broadcasted_iota(jnp.int32, (slot_count, rows.shape[0]), 0)
        table = jnp.where(slot[:, : rows.shape[0]] == spot, 1.0, 0.0).astype(jnp.bfloat16)
        packed = jnp.dot(table, rows[...], preferred_element_type=jnp.float32)
        packed = packed.astype(jnp.bfloat16)
        for step, out in enumerate(outs):
            out[source * row_cap : (source + 1) * row_cap, :] = packed[
                step * row_cap : (step + 1) * row_cap
            ]


def pack_rows(own_slot, partner_slot, own_rows, partner_rows, steps, row_cap):
    width = own_rows.shape[1]
    return pl.pallas_call(
        functools.partial(pack_kernel, row_cap),
        out_shape=[jax.ShapeDtypeStruct((2 * row_cap, width), jnp.bfloat16)] * steps,
        in_specs=[pl.BlockSpec(memory_space=pltpu.VMEM)] * 4,
        out_specs=[pl.BlockSpec(memory_space=pltpu.VMEM)] * steps,
        compiler_params=pltpu.CompilerParams(vmem_limit_bytes=32 * 1024 * 1024),
        cost_estimate=pl.CostEstimate(
            flops=4 * steps * row_cap * width * own_rows.shape[0],
            bytes_accessed=4 * width * (own_rows.shape[0] + steps * row_cap),
            transcendentals=0,
        ),
        name="pack",
    )(own_slot, partner_slot, own_rows, partner_rows)


def onehot(where_to, count):
    centre = lax.broadcasted_iota(jnp.int32, (count, where_to.shape[1]), 0)
    centre += pl.program_id(0) * count
    return jnp.where(centre == where_to[...], 1.0, 0.0)


def early_kernel(places, centroids, *rest):
    pieces, (out, share, rows) = rest[:-3], rest[-3:]
    count = out.shape[0]

    @pl.when(pl.program_id(0) == 0)
    def _():
        at = 0
        for piece in pieces:
            rows[at : at + piece.shape[0], :] = piece[...]
            at += piece.shape[0]

    hot = onehot(places, count)
    sums = jnp.dot(hot.astype(jnp.bfloat16), rows[...], preferred_element_type=jnp.float32)
    counts = jnp.sum(hot, axis=1, keepdims=True)
    scale = 1.0 / jnp.maximum(counts, 1.0)
    out[...] = jnp.where(counts > 0, sums * scale, centroids[...])
    share[...] = jnp.broadcast_to(scale, share.shape)


def late_kernel(late, embeds, early, share, out):
    hot = onehot(late, out.shape[0]).astype(jnp.bfloat16)
    sums = jnp.dot(hot, embeds[...], preferred_element_type=jnp.float32)
    out[...] = early[...] + sums * share[:, :1]


def update(places, late, embeds, centroids, pieces):
    centre_count, width = centroids.shape
    block = 128
    grid = (centre_count // block,)
    whole = lambda array: pl.BlockSpec(array.shape, lambda i: (0, 0))
    part = pl.BlockSpec((block, width), lambda i: (i, 0))
    thin = pl.BlockSpec((block, 128), lambda i: (i, 0))
    row_total = sum(piece.shape[0] for piece in pieces)
    full = jax.ShapeDtypeStruct(centroids.shape, jnp.float32)
    params = pltpu.CompilerParams(vmem_limit_bytes=32 * 1024 * 1024)
    early, share = pl.pallas_call(
        early_kernel,
        grid=grid,
        out_shape=[full, jax.ShapeDtypeStruct((centre_count, 128), jnp.float32)],
        in_specs=[whole(places), part] + [whole(piece) for piece in pieces],
        out_specs=[part, thin],
        scratch_shapes=[pltpu.VMEM((row_total, width), jnp.bfloat16)],
        compiler_params=params,
        cost_estimate=pl.CostEstimate(
            flops=2 * centre_count * width * row_total,
            bytes_accessed=8 * centre_count * width,
            transcendentals=0,
        ),
        name="early",
    )(places, centroids, *pieces)
    return pl.pallas_call(
        late_kernel,
        grid=grid,
        out_shape=full,
        in_specs=[whole(late), whole(embeds), part, thin],
        out_specs=part,
        compiler_params=params,
        cost_estimate=pl.CostEstimate(
            flops=2 * centre_count * width * late.shape[1],
            bytes_accessed=8 * centre_count * width,
            transcendentals=0,
        ),
        name="late",
    )(late, embeds, early, share)


def shards(
    token_ids,
    lengths,
    word_table,
    pos_table,
    emb_gain,
    emb_bias,
    w_qkv,
    w_out,
    out_bias,
    norm_gain,
    norm_bias,
    stored_rows,
    row_owner,
    row_slot,
    centroids,
):
    peer_count = lax.axis_size("dp")
    half = peer_count // 2
    me = lax.axis_index("dp")
    base = me // half * half
    width = word_table.shape[1]
    vocab_rows = word_table.shape[0]
    passes, seq_len = token_ids.shape
    token_count = passes * seq_len
    row_count = row_slot.shape[0]
    store_count = stored_rows.shape[0]
    token_cap = max(2, 3 * token_count // peer_count)
    row_cap = max(2, 3 * row_count // peer_count)

    across = [(i, (i + half) % peer_count) for i in range(peer_count)]
    partner_rows = lax.ppermute(stored_rows, "dp", across)
    sizes = (peer_count, vocab_rows, token_cap, row_cap, row_count - store_count)
    plan, token_slot, own_slot, partner_slot = route(
        token_ids, row_owner.reshape(1, row_count), row_slot[None], sizes
    )
    partner_slot = lax.ppermute(partner_slot, "dp", across)
    plan = lax.all_to_all(plan, "dp", split_axis=0, concat_axis=0, tiled=True)
    plan, partner_slot = lax.optimization_barrier((plan, partner_slot))
    wanted = plan[:, :token_cap].reshape(peer_count * token_cap)
    chosen = wanted[:, None] == jnp.arange(vocab_rows, dtype=jnp.int32)[None, :]
    found = jnp.dot(
        chosen.astype(jnp.bfloat16), word_table, preferred_element_type=jnp.float32
    ).astype(jnp.bfloat16)
    found, partner_rows = lax.optimization_barrier((found, partner_rows))
    fetched = lax.all_to_all(
        found.reshape(peer_count, token_cap, width), "dp", split_axis=0, concat_axis=0, tiled=True
    ).reshape(peer_count * token_cap, width)

    blocks = pack_rows(own_slot, partner_slot, stored_rows, partner_rows, half, row_cap)
    got_rows = [blocks[0]]
    for step in range(1, half):
        moves = [(i, i // half * half + (i + step) % half) for i in range(peer_count)]
        got_rows.append(lax.ppermute(blocks[step], "dp", moves))
    sources = base + (me - jnp.arange(half, dtype=jnp.int32)) % half
    sources = jnp.stack([sources, (sources + half) % peer_count], axis=1).reshape(peer_count)
    got_places = plan[:, token_cap : token_cap + row_cap][sources].reshape(1, peer_count * row_cap)
    late_places = plan[:, token_cap + row_cap :].reshape(1, -1)

    passage_embed, spread = encode(
        peer_count,
        token_slot,
        fetched,
        lengths,
        pos_table,
        emb_gain,
        emb_bias,
        w_qkv,
        w_out,
        out_bias,
        norm_gain,
        norm_bias,
    )
    all_embeds = lax.all_to_all(
        spread, "dp", split_axis=0, concat_axis=0, tiled=True
    ).reshape(peer_count * passes, width)
    new_centroids = update(got_places, late_places, all_embeds, centroids, got_rows)
    return (passage_embed, new_centroids)


def solution(mesh):
    return jax.shard_map(
        shards,
        mesh=mesh,
        in_specs=(
            P(("groups", "dp"), None),
            P(("groups", "dp")),
            P("dp", None),
            P(),
            P(),
            P(),
            P(),
            P(),
            P(),
            P(),
            P(),
            P(("groups", "dp"), None),
            P(("groups", "dp"), None),
            P(("groups", "dp")),
            P(("groups", "dp"), None),
        ),
        out_specs=(P(("groups", "dp"), None), P(("groups", "dp"), None)),
        check_vma=False,
    )
```

```python
import functools

import jax
import jax.numpy as jnp
from jax import lax
from jax.experimental import pallas as pl
from jax.experimental.pallas import tpu as pltpu
from jax.sharding import PartitionSpec as P

HEADS = 8
HD = 64


def normed(values, gain, shift):
    center = values - jnp.mean(values, axis=-1, keepdims=True)
    spread = jnp.mean(center * center, axis=-1, keepdims=True)
    return center * lax.rsqrt(spread + 1e-12) * gain + shift


def head_sums(weights, seq):
    rows, columns = weights.shape
    lane = lax.broadcasted_iota(jnp.int32, (rows, 2 * seq), 1)
    sums = []
    for start in range(0, columns, 2 * seq):
        pair = weights[:, start : start + 2 * seq]
        first = jnp.sum(jnp.where(lane < seq, pair, 0.0), axis=1, keepdims=True)
        second = jnp.sum(jnp.where(lane < seq, 0.0, pair), axis=1, keepdims=True)
        sums.append(jnp.where(lane < seq, first, second))
    return jnp.concatenate(sums, axis=1)


def encode_kernel(
    lengths,
    slots,
    fetched,
    pos,
    emb_gain,
    emb_bias,
    w_qkv_far,
    w_out_far,
    out_bias,
    norm_gain,
    norm_bias,
    out,
    spread,
    w_qkv,
    w_out,
    arrived,
):
    qkv_copy = pltpu.make_async_copy(w_qkv_far, w_qkv, arrived.at[0])
    out_copy = pltpu.make_async_copy(w_out_far, w_out, arrived.at[1])
    qkv_copy.start()
    out_copy.start()
    tokens, slot_count = slots.shape[0], fetched.shape[0]
    passes = out.shape[0]
    seq = tokens // passes
    inner = HEADS * HD
    spot = lax.broadcasted_iota(jnp.int32, (tokens, slot_count), 1)
    picker = jnp.where(slots[...] == spot, 1.0, 0.0).astype(jnp.bfloat16)
    tok = jnp.dot(picker, fetched[...], preferred_element_type=jnp.float32)
    where_at = pos[...].astype(jnp.float32)
    summed = tok + jnp.concatenate([where_at] * passes, axis=0)
    embedded = normed(summed, emb_gain[...], emb_bias[...]).astype(jnp.bfloat16)
    qkv_copy.wait()
    projected = jnp.dot(embedded, w_qkv[...], preferred_element_type=jnp.float32)
    projected = projected.astype(jnp.bfloat16)

    block_row = lax.broadcasted_iota(jnp.int32, (HEADS * seq, inner), 0) // seq
    block_col = lax.broadcasted_iota(jnp.int32, (HEADS * seq, inner), 1) // HD
    same = block_row == block_col
    lane = lax.broadcasted_iota(jnp.int32, (seq, HEADS * seq), 1) % seq
    contexts = []
    for p in range(passes):
        part = projected[p * seq : (p + 1) * seq]
        query, keys, vals = part[:, :inner], part[:, inner : 2 * inner], part[:, 2 * inner :]
        zero = jnp.zeros((), jnp.bfloat16)
        keys = jnp.where(same, jnp.concatenate([keys] * HEADS, axis=0), zero)
        vals = jnp.where(same, jnp.concatenate([vals] * HEADS, axis=0), zero)
        scores = lax.dot_general(
            query, keys, (((1,), (1,)), ((), ())), preferred_element_type=jnp.float32
        ) * HD ** (-0.5)
        weights = jnp.where(lane < lengths[p], jnp.exp(scores), 0.0)
        probs = (weights / head_sums(weights, seq)).astype(jnp.bfloat16)
        contexts.append(jnp.dot(probs, vals, preferred_element_type=jnp.float32))
    context = jnp.concatenate(contexts, axis=0).astype(jnp.bfloat16)
    out_copy.wait()
    attended = jnp.dot(context, w_out[...], preferred_element_type=jnp.float32) + out_bias[...]
    hidden = normed(embedded.astype(jnp.float32) + attended, norm_gain[...], norm_bias[...])
    row = lax.broadcasted_iota(jnp.int32, (seq, 1), 0)
    for p in range(passes):
        kept = jnp.where(row < lengths[p], hidden[p * seq : (p + 1) * seq], 0.0)
        pooled = jnp.sum(kept, axis=0, keepdims=True) / lengths[p].astype(jnp.float32)
        scale = lax.rsqrt(jnp.mean(pooled * pooled, axis=-1, keepdims=True) + 1e-06)
        out[p : p + 1, :] = (pooled * scale).astype(jnp.bfloat16)
    spread[...] = jnp.broadcast_to(out[...][None], spread.shape)


def encode(
    peers, slots, fetched, lengths, pos_table, emb_gain, emb_bias, w_qkv, w_out, out_bias, norm_gain, norm_bias
):
    width = fetched.shape[1]
    tokens = slots.shape[0]
    passes = lengths.shape[0]
    macs = tokens * width * (fetched.shape[0] + 4 * HEADS * HD)
    return pl.pallas_call(
        encode_kernel,
        out_shape=[
            jax.ShapeDtypeStruct((passes, width), jnp.bfloat16),
            jax.ShapeDtypeStruct((peers, passes, width), jnp.bfloat16),
        ],
        in_specs=[pl.BlockSpec(memory_space=pltpu.SMEM)]
        + [pl.BlockSpec(memory_space=pltpu.VMEM)] * 5
        + [pl.BlockSpec(memory_space=pltpu.HBM)] * 2
        + [pl.BlockSpec(memory_space=pltpu.VMEM)] * 3,
        out_specs=[pl.BlockSpec(memory_space=pltpu.VMEM)] * 2,
        scratch_shapes=[
            pltpu.VMEM(w_qkv.shape, w_qkv.dtype),
            pltpu.VMEM(w_out.shape, w_out.dtype),
            pltpu.SemaphoreType.DMA((2,)),
        ],
        compiler_params=pltpu.CompilerParams(vmem_limit_bytes=60 * 1024 * 1024),
        cost_estimate=pl.CostEstimate(
            flops=2 * macs, bytes_accessed=6 * 1024 * 1024, transcendentals=0
        ),
        name="encode",
    )(
        lengths,
        slots,
        fetched,
        pos_table,
        emb_gain[None],
        emb_bias[None],
        w_qkv,
        w_out,
        out_bias[None],
        norm_gain[None],
        norm_bias[None],
    )


def rank_bits(count):
    return max(1, (count - 1).bit_length())


def route_kernel(
    sizes, token_ids, owners, row_slot, plan, token_slot, code
):
    peers, vocab_rows, token_cap, row_cap, pooled = sizes
    ids = jnp.concatenate([token_ids[p : p + 1, :] for p in range(token_ids.shape[0])], axis=1)
    tokens, rows = ids.shape[1], owners.shape[1]
    count = tokens + rows
    edge = (lax.broadcasted_iota(jnp.int32, (peers, tokens), 0) + 1) * vocab_rows
    holder = jnp.sum(jnp.where(ids >= edge, 1, 0), axis=0, keepdims=True)
    values = jnp.concatenate([ids - holder * vocab_rows, row_slot[...]], axis=1)

    kind = jnp.concatenate([holder, owners[...] + peers], axis=1)
    at = lax.broadcasted_iota(jnp.int32, (count, count), 0)
    by = lax.broadcasted_iota(jnp.int32, (count, count), 1)
    across = jnp.broadcast_to(kind, (count, count))
    down = jnp.sum(jnp.where(at == by, across, 0), axis=1, keepdims=True)
    same = down == across
    rank_row = jnp.sum(jnp.where(same & (at < by), 1, 0), axis=0, keepdims=True)
    rank_col = jnp.sum(jnp.where(same & (by < at), 1, 0), axis=1, keepdims=True)

    code[...] = owners[...] * 2 ** rank_bits(rows) + rank_row[:, tokens:]
    goal = jnp.concatenate([holder, owners[...]], axis=1)
    peer = lax.broadcasted_iota(jnp.int32, (peers, count), 0)
    left = jnp.where(peer == goal, values + 1, 0).astype(jnp.float32)
    columns = token_cap + row_cap + pooled
    column = lax.broadcasted_iota(jnp.int32, (count, columns), 1)
    entry = lax.broadcasted_iota(jnp.int32, (count, 1), 0)
    first = jnp.where(entry < tokens, rank_col, rank_col + token_cap)
    second = entry - (count - pooled) + token_cap + row_cap
    second = jnp.where(entry < count - pooled, -1, second)
    right = jnp.where((column == first) | (column == second), 1.0, 0.0)
    filled = jnp.dot(
        left, right, preferred_element_type=jnp.float32, precision=lax.Precision.HIGHEST
    )
    plan[:, :rows] = jnp.broadcast_to(code[...], (peers, rows))
    plan[:, rows:] = filled.astype(jnp.int32) - 1
    token_slot[...] = down[:tokens] * token_cap + rank_col[:tokens]


def route(token_ids, owners, row_slot, sizes):
    peers, _, token_cap, row_cap, pooled = sizes
    passes, seq_len = token_ids.shape
    rows = owners.shape[1]
    ints = lambda *shape: jax.ShapeDtypeStruct(shape, jnp.int32)
    return pl.pallas_call(
        functools.partial(route_kernel, sizes),
        out_shape=[
            ints(peers, rows + token_cap + row_cap + pooled),
            ints(passes * seq_len, 1),
            ints(1, rows),
        ],
        in_specs=[pl.BlockSpec(memory_space=pltpu.VMEM)] * 3,
        out_specs=[pl.BlockSpec(memory_space=pltpu.VMEM)] * 3,
        name="route",
    )(token_ids, owners, row_slot)


def pack_kernel(half, row_cap, count, picks, codes_a, codes_b, rows_a, rows_b, *outs):
    me = lax.axis_index("dp")
    slot_count = len(outs) * row_cap
    for source, (codes, rows) in enumerate(((codes_a, rows_a), (codes_b, rows_b))):
        if picks is None:
            code = codes[...]
        else:
            code = codes[pl.ds(me ^ picks[source], 1), :count]
        bits = rank_bits(count)
        owner, rank = code >> bits, code & (2**bits - 1)
        fits = ((owner ^ me) & (1 | half)) == 0
        chip = ((owner ^ me) & (half - 1)) >> 1
        slot = jnp.where(fits, chip * row_cap + rank, -1)[:, : rows.shape[0]]
        spot = lax.broadcasted_iota(jnp.int32, (slot_count, rows.shape[0]), 0)
        table = jnp.where(slot == spot, 1.0, 0.0).astype(jnp.bfloat16)
        packed = jnp.dot(table, rows[...], preferred_element_type=jnp.float32)
        packed = packed.astype(jnp.bfloat16)
        for step, out in enumerate(outs):
            out[source * row_cap : (source + 1) * row_cap, :] = packed[
                step * row_cap : (step + 1) * row_cap
            ]


def pack_rows(codes_a, codes_b, rows_a, rows_b, half, row_cap, count, picks=None):
    width = rows_a.shape[1]
    steps = half // 2
    return pl.pallas_call(
        functools.partial(pack_kernel, half, row_cap, count, picks),
        out_shape=[jax.ShapeDtypeStruct((2 * row_cap, width), jnp.bfloat16)] * steps,
        in_specs=[pl.BlockSpec(memory_space=pltpu.VMEM)] * 4,
        out_specs=[pl.BlockSpec(memory_space=pltpu.VMEM)] * steps,
        compiler_params=pltpu.CompilerParams(vmem_limit_bytes=60 * 1024 * 1024),
        cost_estimate=pl.CostEstimate(
            flops=4 * steps * row_cap * width * rows_a.shape[0],
            bytes_accessed=4 * width * (rows_a.shape[0] + steps * row_cap),
            transcendentals=0,
        ),
        name="pack",
    )(codes_a, codes_b, rows_a, rows_b)


def onehot(where_to, count):
    centre = lax.broadcasted_iota(jnp.int32, (count, where_to.shape[1]), 0)
    centre += pl.program_id(0) * count
    return jnp.where(centre == where_to[...], 1.0, 0.0)


def early_kernel(places, centroids, *rest):
    pieces, (out, share, rows) = rest[:-3], rest[-3:]
    count = out.shape[0]

    @pl.when(pl.program_id(0) == 0)
    def _():
        at = 0
        for piece in pieces:
            rows[at : at + piece.shape[0], :] = piece[...]
            at += piece.shape[0]

    hot = onehot(places, count)
    sums = jnp.dot(hot.astype(jnp.bfloat16), rows[...], preferred_element_type=jnp.float32)
    counts = jnp.sum(hot, axis=1, keepdims=True)
    scale = 1.0 / jnp.maximum(counts, 1.0)
    out[...] = jnp.where(counts > 0, sums * scale, centroids[...])
    share[...] = jnp.broadcast_to(scale, share.shape)


def late_kernel(late, spread, early, share, out, embeds):
    passes = spread.shape[1]

    @pl.when(pl.program_id(0) == 0)
    def _():
        for peer in range(spread.shape[0]):
            embeds[peer * passes : (peer + 1) * passes, :] = spread[peer]

    hot = onehot(late, out.shape[0]).astype(jnp.bfloat16)
    sums = jnp.dot(hot, embeds[...], preferred_element_type=jnp.float32)
    out[...] = early[...] + sums * share[:, :1]


def update(places, late, embeds, centroids, pieces):
    centre_count, width = centroids.shape
    block = 128
    grid = (centre_count // block,)
    whole = lambda array: pl.BlockSpec(array.shape, lambda i: (0, 0))
    part = pl.BlockSpec((block, width), lambda i: (i, 0))
    thin = pl.BlockSpec((block, 128), lambda i: (i, 0))
    row_total = sum(piece.shape[0] for piece in pieces)
    full = jax.ShapeDtypeStruct(centroids.shape, jnp.float32)
    params = pltpu.CompilerParams(vmem_limit_bytes=60 * 1024 * 1024)
    early, share = pl.pallas_call(
        early_kernel,
        grid=grid,
        out_shape=[full, jax.ShapeDtypeStruct((centre_count, 128), jnp.float32)],
        in_specs=[whole(places), part] + [whole(piece) for piece in pieces],
        out_specs=[part, thin],
        scratch_shapes=[pltpu.VMEM((row_total, width), jnp.bfloat16)],
        compiler_params=params,
        cost_estimate=pl.CostEstimate(
            flops=2 * centre_count * width * row_total,
            bytes_accessed=8 * centre_count * width,
            transcendentals=0,
        ),
        name="early",
    )(places, centroids, *pieces)
    return pl.pallas_call(
        late_kernel,
        grid=grid,
        out_shape=full,
        in_specs=[whole(late), pl.BlockSpec(embeds.shape, lambda i: (0, 0, 0)), part, thin],
        out_specs=part,
        scratch_shapes=[pltpu.VMEM((late.shape[1], width), jnp.bfloat16)],
        compiler_params=params,
        cost_estimate=pl.CostEstimate(
            flops=2 * centre_count * width * late.shape[1],
            bytes_accessed=8 * centre_count * width,
            transcendentals=0,
        ),
        name="late",
    )(late, embeds, early, share)


def shards(
    token_ids,
    lengths,
    word_table,
    pos_table,
    emb_gain,
    emb_bias,
    w_qkv,
    w_out,
    out_bias,
    norm_gain,
    norm_bias,
    stored_rows,
    row_owner,
    row_slot,
    centroids,
):
    peer_count = lax.axis_size("dp")
    half = peer_count // 2
    width = word_table.shape[1]
    vocab_rows = word_table.shape[0]
    passes, seq_len = token_ids.shape
    token_count = passes * seq_len
    row_count = row_slot.shape[0]
    store_count = stored_rows.shape[0]
    token_cap = max(2, 3 * token_count // peer_count)
    row_cap = max(2, 3 * row_count // peer_count)

    across = [(i, i ^ half) for i in range(peer_count)]
    beside = [(i, i ^ 1) for i in range(peer_count)]

    def hand_on(blocks):
        got = [blocks[0]]
        for step in range(1, len(blocks)):
            moves = [(i, i ^ (2 * step)) for i in range(peer_count)]
            got.append(lax.ppermute(blocks[step], "dp", moves))
        return got

    partner_rows = lax.ppermute(stored_rows, "dp", across)
    sibling_rows = lax.ppermute(stored_rows, "dp", beside)
    sizes = (peer_count, vocab_rows, token_cap, row_cap, row_count - store_count)
    plan, token_slot, code = route(token_ids, row_owner.reshape(1, row_count), row_slot[None], sizes)
    sibling_code = lax.ppermute(code, "dp", beside)
    plan = lax.all_to_all(plan, "dp", split_axis=0, concat_axis=0, tiled=True)
    blocks = pack_rows(code, sibling_code, stored_rows, sibling_rows, half, row_cap, row_count)
    own_half = hand_on(blocks)
    codes, plan = plan[:, :row_count], plan[:, row_count:]
    wanted = plan[:, :token_cap].reshape(peer_count * token_cap)
    chosen = wanted[:, None] == jnp.arange(vocab_rows, dtype=jnp.int32)[None, :]
    found = jnp.dot(
        chosen.astype(jnp.bfloat16), word_table, preferred_element_type=jnp.float32
    ).astype(jnp.bfloat16)
    found, partner_rows, own_half = lax.optimization_barrier((found, partner_rows, own_half))
    fetched = lax.all_to_all(
        found.reshape(peer_count, token_cap, width), "dp", split_axis=0, concat_axis=0, tiled=True
    ).reshape(peer_count * token_cap, width)

    far_rows = lax.ppermute(partner_rows, "dp", beside)
    picks = (half, half ^ 1)
    blocks = pack_rows(codes, codes, partner_rows, far_rows, half, row_cap, row_count, picks)
    other_half = hand_on(blocks)
    sources = lax.axis_index("dp") ^ jnp.arange(peer_count, dtype=jnp.int32)
    got_places = plan[:, token_cap : token_cap + row_cap][sources].reshape(1, peer_count * row_cap)
    late_places = plan[:, token_cap + row_cap :].reshape(1, -1)

    passage_embed, spread = encode(
        peer_count,
        token_slot,
        fetched,
        lengths,
        pos_table,
        emb_gain,
        emb_bias,
        w_qkv,
        w_out,
        out_bias,
        norm_gain,
        norm_bias,
    )
    all_embeds = lax.all_to_all(
        spread, "dp", split_axis=0, concat_axis=0, tiled=True
    )
    new_centroids = update(
        got_places, late_places, all_embeds, centroids, own_half + other_half
    )
    return (passage_embed, new_centroids)


def solution(mesh):
    return jax.shard_map(
        shards,
        mesh=mesh,
        in_specs=(
            P(("groups", "dp"), None),
            P(("groups", "dp")),
            P("dp", None),
            P(),
            P(),
            P(),
            P(),
            P(),
            P(),
            P(),
            P(),
            P(("groups", "dp"), None),
            P(("groups", "dp"), None),
            P(("groups", "dp")),
            P(("groups", "dp"), None),
        ),
        out_specs=(P(("groups", "dp"), None), P(("groups", "dp"), None)),
        check_vma=False,
    )
```

```python
import functools

import jax
import jax.numpy as jnp
from jax import lax
from jax.experimental import pallas as pl
from jax.experimental.pallas import tpu as pltpu
from jax.sharding import PartitionSpec as P

HEADS = 8
HD = 64


def normed(values, gain, shift):
    center = values - jnp.mean(values, axis=-1, keepdims=True)
    spread = jnp.mean(center * center, axis=-1, keepdims=True)
    return center * lax.rsqrt(spread + 1e-12) * gain + shift


def head_sums(weights, seq):
    rows, columns = weights.shape
    lane = lax.broadcasted_iota(jnp.int32, (rows, 2 * seq), 1)
    sums = []
    for start in range(0, columns, 2 * seq):
        pair = weights[:, start : start + 2 * seq]
        first = jnp.sum(jnp.where(lane < seq, pair, 0.0), axis=1, keepdims=True)
        second = jnp.sum(jnp.where(lane < seq, 0.0, pair), axis=1, keepdims=True)
        sums.append(jnp.where(lane < seq, first, second))
    return jnp.concatenate(sums, axis=1)


def encode_kernel(
    lengths,
    slots,
    emb_gain,
    emb_bias,
    out_bias,
    norm_gain,
    norm_bias,
    fetched_far,
    pos_far,
    w_qkv_far,
    w_out_far,
    out,
    spread,
    fetched,
    pos,
    w_qkv,
    w_out,
    arrived,
):
    inner = HEADS * HD
    copies = [
        pltpu.make_async_copy(fetched_far, fetched, arrived.at[0]),
        pltpu.make_async_copy(pos_far, pos, arrived.at[1]),
        pltpu.make_async_copy(w_out_far, w_out, arrived.at[2]),
    ]
    for third in range(3):
        columns = pl.ds(third * inner, inner)
        copies.append(
            pltpu.make_async_copy(
                w_qkv_far.at[:, columns], w_qkv.at[:, columns], arrived.at[3 + third]
            )
        )
    for at in (0, 1, 3, 4, 5, 2):
        copies[at].start()
    tokens, slot_count = slots.shape[0], fetched.shape[0]
    passes = out.shape[0]
    seq = tokens // passes
    spot = lax.broadcasted_iota(jnp.int32, (tokens, slot_count), 1)
    picker = jnp.where(slots[...] == spot, 1.0, 0.0).astype(jnp.bfloat16)
    copies[0].wait()
    copies[1].wait()
    tok = jnp.dot(picker, fetched[...], preferred_element_type=jnp.float32)
    where_at = pos[...].astype(jnp.float32)
    summed = tok + jnp.concatenate([where_at] * passes, axis=0)
    embedded = normed(summed, emb_gain[...], emb_bias[...]).astype(jnp.bfloat16)
    parts = []
    for third in range(3):
        copies[3 + third].wait()
        weights = w_qkv[:, third * inner : (third + 1) * inner]
        part = jnp.dot(embedded, weights, preferred_element_type=jnp.float32)
        parts.append(part.astype(jnp.bfloat16))

    block_row = lax.broadcasted_iota(jnp.int32, (HEADS * seq, inner), 0) // seq
    block_col = lax.broadcasted_iota(jnp.int32, (HEADS * seq, inner), 1) // HD
    same = block_row == block_col
    lane = lax.broadcasted_iota(jnp.int32, (seq, HEADS * seq), 1) % seq
    contexts = []
    for p in range(passes):
        query, keys, vals = (part[p * seq : (p + 1) * seq] for part in parts)
        zero = jnp.zeros((), jnp.bfloat16)
        keys = jnp.where(same, jnp.concatenate([keys] * HEADS, axis=0), zero)
        vals = jnp.where(same, jnp.concatenate([vals] * HEADS, axis=0), zero)
        scores = lax.dot_general(
            query, keys, (((1,), (1,)), ((), ())), preferred_element_type=jnp.float32
        ) * HD ** (-0.5)
        weights = jnp.where(lane < lengths[p], jnp.exp(scores), 0.0)
        probs = (weights / head_sums(weights, seq)).astype(jnp.bfloat16)
        contexts.append(jnp.dot(probs, vals, preferred_element_type=jnp.float32))
    context = jnp.concatenate(contexts, axis=0).astype(jnp.bfloat16)
    copies[2].wait()
    attended = jnp.dot(context, w_out[...], preferred_element_type=jnp.float32) + out_bias[...]
    hidden = normed(embedded.astype(jnp.float32) + attended, norm_gain[...], norm_bias[...])
    row = lax.broadcasted_iota(jnp.int32, (seq, 1), 0)
    for p in range(passes):
        kept = jnp.where(row < lengths[p], hidden[p * seq : (p + 1) * seq], 0.0)
        pooled = jnp.sum(kept, axis=0, keepdims=True) / lengths[p].astype(jnp.float32)
        scale = lax.rsqrt(jnp.mean(pooled * pooled, axis=-1, keepdims=True) + 1e-06)
        out[p : p + 1, :] = (pooled * scale).astype(jnp.bfloat16)
    spread[...] = jnp.broadcast_to(out[...][None], spread.shape)


def encode(
    peers, slots, fetched, lengths, pos_table, emb_gain, emb_bias, w_qkv, w_out, out_bias, norm_gain, norm_bias
):
    width = fetched.shape[1]
    tokens = slots.shape[0]
    passes = lengths.shape[0]
    macs = tokens * width * (fetched.shape[0] + 4 * HEADS * HD)
    return pl.pallas_call(
        encode_kernel,
        out_shape=[
            jax.ShapeDtypeStruct((passes, width), jnp.bfloat16),
            jax.ShapeDtypeStruct((peers, passes, width), jnp.bfloat16),
        ],
        in_specs=[pl.BlockSpec(memory_space=pltpu.SMEM)]
        + [pl.BlockSpec(memory_space=pltpu.VMEM)] * 6
        + [pl.BlockSpec(memory_space=pltpu.HBM)] * 4,
        out_specs=[pl.BlockSpec(memory_space=pltpu.VMEM)] * 2,
        scratch_shapes=[
            pltpu.VMEM(fetched.shape, fetched.dtype),
            pltpu.VMEM(pos_table.shape, pos_table.dtype),
            pltpu.VMEM(w_qkv.shape, w_qkv.dtype),
            pltpu.VMEM(w_out.shape, w_out.dtype),
            pltpu.SemaphoreType.DMA((6,)),
        ],
        compiler_params=pltpu.CompilerParams(vmem_limit_bytes=60 * 1024 * 1024),
        cost_estimate=pl.CostEstimate(
            flops=2 * macs, bytes_accessed=6 * 1024 * 1024, transcendentals=0
        ),
        name="encode",
    )(
        lengths,
        slots,
        emb_gain[None],
        emb_bias[None],
        out_bias[None],
        norm_gain[None],
        norm_bias[None],
        fetched,
        pos_table,
        w_qkv,
        w_out,
    )


def padded(rows):
    return -(-rows // 16) * 16


def rank_bits(count):
    return max(1, (count - 1).bit_length())


def route_kernel(
    sizes, token_ids, owners, row_slot, plan, token_slot, code
):
    peers, vocab_rows, token_cap, row_cap, pooled = sizes
    ids = jnp.concatenate([token_ids[p : p + 1, :] for p in range(token_ids.shape[0])], axis=1)
    tokens, rows = ids.shape[1], owners.shape[1]
    count = tokens + rows
    edge = (lax.broadcasted_iota(jnp.int32, (peers, tokens), 0) + 1) * vocab_rows
    holder = jnp.sum(jnp.where(ids >= edge, 1, 0), axis=0, keepdims=True)
    values = jnp.concatenate([ids - holder * vocab_rows, row_slot[...]], axis=1)

    kind = jnp.concatenate([holder, owners[...] + peers], axis=1)
    at = lax.broadcasted_iota(jnp.int32, (count, count), 0)
    by = lax.broadcasted_iota(jnp.int32, (count, count), 1)
    across = jnp.broadcast_to(kind, (count, count))
    down = jnp.sum(jnp.where(at == by, across, 0), axis=1, keepdims=True)
    same = down == across
    rank_row = jnp.sum(jnp.where(same & (at < by), 1, 0), axis=0, keepdims=True)
    rank_col = jnp.sum(jnp.where(same & (by < at), 1, 0), axis=1, keepdims=True)

    code[...] = owners[...] * 2 ** rank_bits(rows) + rank_row[:, tokens:]
    goal = jnp.concatenate([holder, owners[...]], axis=1)
    peer = lax.broadcasted_iota(jnp.int32, (peers, count), 0)
    left = jnp.where(peer == goal, values + 1, 0).astype(jnp.float32)
    columns = token_cap + row_cap + pooled
    column = lax.broadcasted_iota(jnp.int32, (count, columns), 1)
    entry = lax.broadcasted_iota(jnp.int32, (count, 1), 0)
    first = jnp.where(entry < tokens, rank_col, rank_col + token_cap)
    second = entry - (count - pooled) + token_cap + row_cap
    second = jnp.where(entry < count - pooled, -1, second)
    right = jnp.where((column == first) | (column == second), 1.0, 0.0)
    filled = jnp.dot(
        left, right, preferred_element_type=jnp.float32, precision=lax.Precision.HIGHEST
    )
    filled = filled.astype(jnp.int32) - 1
    for p in range(peers):
        plan[p, :, :rows] = code[...]
        plan[p, :, rows:] = filled[p : p + 1]
    token_slot[...] = down[:tokens] * token_cap + rank_col[:tokens]


def route(token_ids, owners, row_slot, sizes):
    peers, _, token_cap, row_cap, pooled = sizes
    passes, seq_len = token_ids.shape
    rows = owners.shape[1]
    ints = lambda *shape: jax.ShapeDtypeStruct(shape, jnp.int32)
    return pl.pallas_call(
        functools.partial(route_kernel, sizes),
        out_shape=[
            ints(peers, 1, rows + token_cap + row_cap + pooled),
            ints(passes * seq_len, 1),
            ints(1, rows),
        ],
        in_specs=[pl.BlockSpec(memory_space=pltpu.VMEM)] * 3,
        out_specs=[pl.BlockSpec(memory_space=pltpu.VMEM)] * 3,
        name="route",
    )(token_ids, owners, row_slot)


def pack_kernel(half, row_cap, count, picks, codes_a, codes_b, rows_a, rows_b, *outs):
    me = lax.axis_index("dp")
    slot_count = len(outs) * row_cap
    for source, (codes, rows) in enumerate(((codes_a, rows_a), (codes_b, rows_b))):
        if picks is None:
            code = codes[...]
        else:
            code = codes[me ^ picks[source], :, :count]
        bits = rank_bits(count)
        owner, rank = code >> bits, code & (2**bits - 1)
        fits = ((owner ^ me) & (1 | half)) == 0
        chip = ((owner ^ me) & (half - 1)) >> 1
        slot = jnp.where(fits, chip * row_cap + rank, -1)[:, : rows.shape[0]]
        spot = lax.broadcasted_iota(jnp.int32, (slot_count, rows.shape[0]), 0)
        table = jnp.where(slot == spot, 1.0, 0.0).astype(jnp.bfloat16)
        packed = jnp.dot(table, rows[...], preferred_element_type=jnp.float32)
        packed = packed.astype(jnp.bfloat16)
        for step, out in enumerate(outs):
            if source == 0 and out.shape[0] > 2 * row_cap:
                out[...] = jnp.zeros(out.shape, out.dtype)
            out[source * row_cap : (source + 1) * row_cap, :] = packed[
                step * row_cap : (step + 1) * row_cap
            ]


def pack_rows(codes_a, codes_b, rows_a, rows_b, half, row_cap, count, picks=None):
    width = rows_a.shape[1]
    steps = half // 2
    return pl.pallas_call(
        functools.partial(pack_kernel, half, row_cap, count, picks),
        out_shape=[jax.ShapeDtypeStruct((padded(2 * row_cap), width), jnp.bfloat16)] * steps,
        in_specs=[pl.BlockSpec(memory_space=pltpu.VMEM)] * 4,
        out_specs=[pl.BlockSpec(memory_space=pltpu.VMEM)] * steps,
        compiler_params=pltpu.CompilerParams(vmem_limit_bytes=60 * 1024 * 1024),
        cost_estimate=pl.CostEstimate(
            flops=4 * steps * row_cap * width * rows_a.shape[0],
            bytes_accessed=4 * width * (rows_a.shape[0] + steps * row_cap),
            transcendentals=0,
        ),
        name="pack",
    )(codes_a, codes_b, rows_a, rows_b)


def onehot(where_to, first, count):
    centre = lax.broadcasted_iota(jnp.int32, (count, where_to.shape[1]), 0) + first
    return jnp.where(centre == where_to, 1.0, 0.0)


BLOCK = 128


def early_kernel(places, centroids_far, *rest):
    pieces, (out_far, share, rows, centroids, out, arrived, left) = rest[:-7], rest[-7:]
    size = pieces[0].shape[0]
    count = centroids.shape[0]
    copies = []
    for at, piece in enumerate(pieces):
        copies.append(
            pltpu.make_async_copy(piece, rows.at[pl.ds(at * size, size)], arrived.at[at])
        )
    copies.append(pltpu.make_async_copy(centroids_far, centroids, arrived.at[len(pieces)]))
    for copy in copies:
        copy.start()
    for copy in copies:
        copy.wait()
    sends = []
    for step in range(count // BLOCK):
        block = pl.ds(step * BLOCK, BLOCK)
        hot = onehot(places[...], step * BLOCK, BLOCK)
        counts = jnp.sum(hot, axis=1, keepdims=True)
        scale = jnp.where(counts > 0, 1.0 / jnp.maximum(counts, 1.0), 0.0)
        sums = jnp.dot(
            hot[:, : rows.shape[0]].astype(jnp.bfloat16),
            rows[...],
            preferred_element_type=jnp.float32,
        )
        out[block, :] = jnp.where(counts > 0, sums * scale, centroids[block, :])
        share[block, :] = jnp.broadcast_to(scale, (BLOCK, share.shape[1]))
        sends.append(pltpu.make_async_copy(out.at[block], out_far.at[block], left.at[step]))
        sends[-1].start()
    for send in sends:
        send.wait()


def late_kernel(places, late, spread, share, early_far, *rest):
    pieces, (out_far, rows, early, out, arrived, left) = rest[:-6], rest[-6:]
    size, passes = pieces[0].shape[0], spread.shape[1]
    count = early.shape[0]
    steps = count // BLOCK
    loads = []
    for at, piece in enumerate(pieces):
        loads.append(
            pltpu.make_async_copy(piece, rows.at[pl.ds(at * size, size)], arrived.at[at])
        )
    starts = []
    for step in range(steps):
        block = pl.ds(step * BLOCK, BLOCK)
        starts.append(
            pltpu.make_async_copy(
                early_far.at[block], early.at[block], arrived.at[len(pieces) + step]
            )
        )
    for copy in loads + starts:
        copy.start()
    top = len(pieces) * size
    for peer in range(spread.shape[0]):
        rows[top + peer * passes : top + (peer + 1) * passes, :] = spread[peer]
    for copy in loads:
        copy.wait()
    where_to = jnp.concatenate([places[...], late[...]], axis=1)
    sends = []
    for step in range(steps):
        block = pl.ds(step * BLOCK, BLOCK)
        hot = onehot(where_to, step * BLOCK, BLOCK).astype(jnp.bfloat16)
        sums = jnp.dot(hot, rows[...], preferred_element_type=jnp.float32)
        starts[step].wait()
        out[block, :] = early[block, :] + sums * share[block, :1]
        sends.append(pltpu.make_async_copy(out.at[block], out_far.at[block], left.at[step]))
        sends[-1].start()
    for send in sends:
        send.wait()


def early_update(places, centroids, pieces):
    centre_count, width = centroids.shape
    row_total = sum(piece.shape[0] for piece in pieces)
    wide = pltpu.VMEM(centroids.shape, jnp.float32)
    return pl.pallas_call(
        early_kernel,
        out_shape=[
            jax.ShapeDtypeStruct(centroids.shape, jnp.float32),
            jax.ShapeDtypeStruct((centre_count, 128), jnp.float32),
        ],
        in_specs=[pl.BlockSpec(memory_space=pltpu.VMEM)]
        + [pl.BlockSpec(memory_space=pltpu.HBM)] * (1 + len(pieces)),
        out_specs=[
            pl.BlockSpec(memory_space=pltpu.HBM),
            pl.BlockSpec(memory_space=pltpu.VMEM),
        ],
        scratch_shapes=[
            pltpu.VMEM((row_total, width), jnp.bfloat16),
            wide,
            wide,
            pltpu.SemaphoreType.DMA((len(pieces) + 1,)),
            pltpu.SemaphoreType.DMA((centre_count // BLOCK,)),
        ],
        compiler_params=pltpu.CompilerParams(vmem_limit_bytes=60 * 1024 * 1024),
        cost_estimate=pl.CostEstimate(
            flops=2 * centre_count * width * row_total,
            bytes_accessed=8 * centre_count * width,
            transcendentals=0,
        ),
        name="early",
    )(places, centroids, *pieces)


def late_update(places, late, spread, share, early, pieces):
    centre_count, width = early.shape
    row_total = places.shape[1] + late.shape[1]
    wide = pltpu.VMEM(early.shape, jnp.float32)
    steps = centre_count // BLOCK
    return pl.pallas_call(
        late_kernel,
        out_shape=jax.ShapeDtypeStruct(early.shape, jnp.float32),
        in_specs=[pl.BlockSpec(memory_space=pltpu.VMEM)] * 4
        + [pl.BlockSpec(memory_space=pltpu.HBM)] * (1 + len(pieces)),
        out_specs=pl.BlockSpec(memory_space=pltpu.HBM),
        scratch_shapes=[
            pltpu.VMEM((row_total, width), jnp.bfloat16),
            wide,
            wide,
            pltpu.SemaphoreType.DMA((len(pieces) + steps,)),
            pltpu.SemaphoreType.DMA((steps,)),
        ],
        compiler_params=pltpu.CompilerParams(vmem_limit_bytes=60 * 1024 * 1024),
        cost_estimate=pl.CostEstimate(
            flops=2 * centre_count * width * row_total,
            bytes_accessed=8 * centre_count * width,
            transcendentals=0,
        ),
        name="late",
    )(places, late, spread, share, early, *pieces)


def shards(
    token_ids,
    lengths,
    word_table,
    pos_table,
    emb_gain,
    emb_bias,
    w_qkv,
    w_out,
    out_bias,
    norm_gain,
    norm_bias,
    stored_rows,
    row_owner,
    row_slot,
    centroids,
):
    peer_count = lax.axis_size("dp")
    half = peer_count // 2
    width = word_table.shape[1]
    vocab_rows = word_table.shape[0]
    passes, seq_len = token_ids.shape
    token_count = passes * seq_len
    row_count = row_slot.shape[0]
    store_count = stored_rows.shape[0]
    token_cap = max(2, 3 * token_count // peer_count)
    row_cap = max(2, 3 * row_count // peer_count)

    across = [(i, i ^ half) for i in range(peer_count)]
    beside = [(i, i ^ 1) for i in range(peer_count)]

    def hand_on(blocks):
        got = [blocks[0]]
        for step in range(1, len(blocks)):
            moves = [(i, i ^ (2 * step)) for i in range(peer_count)]
            got.append(lax.ppermute(blocks[step], "dp", moves))
        return got

    partner_rows = lax.ppermute(stored_rows, "dp", across)
    sibling_rows = lax.ppermute(stored_rows, "dp", beside)
    sizes = (peer_count, vocab_rows, token_cap, row_cap, row_count - store_count)
    plan, token_slot, code = route(token_ids, row_owner.reshape(1, row_count), row_slot[None], sizes)
    sibling_code = lax.ppermute(code, "dp", beside)
    blocks = pack_rows(code, sibling_code, stored_rows, sibling_rows, half, row_cap, row_count)
    plan, *blocks = lax.optimization_barrier((plan, *blocks))
    own_half = hand_on(blocks)
    codes = lax.all_to_all(plan, "dp", split_axis=0, concat_axis=0, tiled=True)
    plan = codes[:, 0, row_count:]
    wanted = plan[:, :token_cap].reshape(peer_count * token_cap)
    chosen = wanted[:, None] == jnp.arange(vocab_rows, dtype=jnp.int32)[None, :]
    found = jnp.dot(
        chosen.astype(jnp.bfloat16), word_table, preferred_element_type=jnp.float32
    ).astype(jnp.bfloat16)
    found, partner_rows, own_half = lax.optimization_barrier((found, partner_rows, own_half))
    fetched = lax.all_to_all(
        found.reshape(peer_count, token_cap, width), "dp", split_axis=0, concat_axis=0, tiled=True
    ).reshape(peer_count * token_cap, width)

    far_rows = lax.ppermute(partner_rows, "dp", beside)
    picks = (half, half ^ 1)
    blocks = pack_rows(codes, codes, partner_rows, far_rows, half, row_cap, row_count, picks)
    other_half = hand_on(blocks)
    sources = lax.axis_index("dp") ^ jnp.arange(peer_count, dtype=jnp.int32)
    got_places = plan[:, token_cap : token_cap + row_cap][sources].reshape(half, 2 * row_cap)
    spare = padded(2 * row_cap) - 2 * row_cap
    got_places = jnp.pad(got_places, ((0, 0), (0, spare)), constant_values=-1).reshape(1, -1)
    means, share = early_update(got_places, centroids, own_half)
    fetched, means, share = lax.optimization_barrier((fetched, means, share))
    late_places = plan[:, token_cap + row_cap :].reshape(1, -1)

    passage_embed, spread = encode(
        peer_count,
        token_slot,
        fetched,
        lengths,
        pos_table,
        emb_gain,
        emb_bias,
        w_qkv,
        w_out,
        out_bias,
        norm_gain,
        norm_bias,
    )
    all_embeds = lax.all_to_all(
        spread, "dp", split_axis=0, concat_axis=0, tiled=True
    )
    other_places = got_places[:, got_places.shape[1] // 2 :]
    new_centroids = late_update(other_places, late_places, all_embeds, share, means, other_half)
    return (passage_embed, new_centroids)


def solution(mesh):
    return jax.shard_map(
        shards,
        mesh=mesh,
        in_specs=(
            P(("groups", "dp"), None),
            P(("groups", "dp")),
            P("dp", None),
            P(),
            P(),
            P(),
            P(),
            P(),
            P(),
            P(),
            P(),
            P(("groups", "dp"), None),
            P(("groups", "dp"), None),
            P(("groups", "dp")),
            P(("groups", "dp"), None),
        ),
        out_specs=(P(("groups", "dp"), None), P(("groups", "dp"), None)),
        check_vma=False,
    )
```

```python
import functools

import jax
import jax.numpy as jnp
from jax import lax
from jax.experimental import pallas as pl
from jax.experimental.pallas import tpu as pltpu
from jax.sharding import PartitionSpec as P

HEADS = 8
HD = 64


def normed(values, gain, shift):
    center = values - jnp.mean(values, axis=-1, keepdims=True)
    spread = jnp.mean(center * center, axis=-1, keepdims=True)
    return center * lax.rsqrt(spread + 1e-12) * gain + shift


def head_sums(weights, seq):
    rows, columns = weights.shape
    lane = lax.broadcasted_iota(jnp.int32, (rows, 2 * seq), 1)
    sums = []
    for start in range(0, columns, 2 * seq):
        pair = weights[:, start : start + 2 * seq]
        first = jnp.sum(jnp.where(lane < seq, pair, 0.0), axis=1, keepdims=True)
        second = jnp.sum(jnp.where(lane < seq, 0.0, pair), axis=1, keepdims=True)
        sums.append(jnp.where(lane < seq, first, second))
    return jnp.concatenate(sums, axis=1)


def encode_kernel(*refs):
    count = (len(refs) - 3) // 2
    far, (out, spread), near, arrived = refs[:count], refs[count : count + 2], refs[-count - 1 : -1], refs[-1]
    w_qkv_far, inner = far[-2], HEADS * HD
    copies = [
        pltpu.make_async_copy(source, target, arrived.at[at])
        for at, (source, target) in enumerate(zip(far, near))
        if source is not w_qkv_far
    ]
    lengths, slots, fetched, pos, emb_gain, emb_bias, out_bias, norm_gain, norm_bias, w_qkv, w_out = near
    out_copy = copies.pop()
    thirds = []
    for third in range(3):
        columns = pl.ds(third * inner, inner)
        thirds.append(
            pltpu.make_async_copy(
                w_qkv_far.at[:, columns], w_qkv.at[:, columns], arrived.at[count + third]
            )
        )
    for copy in copies + thirds + [out_copy]:
        copy.start()
    for copy in copies:
        copy.wait()
    passes = out.shape[0]
    size = [lengths[:, p : p + 1] for p in range(passes)]
    tokens, slot_count = slots.shape[0], fetched.shape[0]
    seq = tokens // passes
    spot = lax.broadcasted_iota(jnp.int32, (tokens, slot_count), 1)
    picker = jnp.where(slots[...] == spot, 1.0, 0.0).astype(jnp.bfloat16)
    tok = jnp.dot(picker, fetched[...], preferred_element_type=jnp.float32)
    where_at = pos[...].astype(jnp.float32)
    summed = tok + jnp.concatenate([where_at] * passes, axis=0)
    embedded = normed(summed, emb_gain[...], emb_bias[...]).astype(jnp.bfloat16)
    parts = []
    for third in range(3):
        thirds[third].wait()
        weights = w_qkv[:, third * inner : (third + 1) * inner]
        part = jnp.dot(embedded, weights, preferred_element_type=jnp.float32)
        parts.append(part.astype(jnp.bfloat16))

    block_row = lax.broadcasted_iota(jnp.int32, (HEADS * seq, inner), 0) // seq
    block_col = lax.broadcasted_iota(jnp.int32, (HEADS * seq, inner), 1) // HD
    same = block_row == block_col
    lane = lax.broadcasted_iota(jnp.int32, (seq, HEADS * seq), 1) % seq
    contexts = []
    for p in range(passes):
        query, keys, vals = (part[p * seq : (p + 1) * seq] for part in parts)
        zero = jnp.zeros((), jnp.bfloat16)
        keys = jnp.where(same, jnp.concatenate([keys] * HEADS, axis=0), zero)
        vals = jnp.where(same, jnp.concatenate([vals] * HEADS, axis=0), zero)
        scores = lax.dot_general(
            query, keys, (((1,), (1,)), ((), ())), preferred_element_type=jnp.float32
        ) * HD ** (-0.5)
        weights = jnp.where(lane < size[p], jnp.exp(scores), 0.0)
        probs = (weights / head_sums(weights, seq)).astype(jnp.bfloat16)
        contexts.append(jnp.dot(probs, vals, preferred_element_type=jnp.float32))
    context = jnp.concatenate(contexts, axis=0).astype(jnp.bfloat16)
    out_copy.wait()
    attended = jnp.dot(context, w_out[...], preferred_element_type=jnp.float32) + out_bias[...]
    hidden = normed(embedded.astype(jnp.float32) + attended, norm_gain[...], norm_bias[...])
    row = lax.broadcasted_iota(jnp.int32, (seq, 1), 0)
    for p in range(passes):
        kept = jnp.where(row < size[p], hidden[p * seq : (p + 1) * seq], 0.0)
        pooled = jnp.sum(kept, axis=0, keepdims=True) / size[p].astype(jnp.float32)
        scale = lax.rsqrt(jnp.mean(pooled * pooled, axis=-1, keepdims=True) + 1e-06)
        out[p : p + 1, :] = (pooled * scale).astype(jnp.bfloat16)
    spread[...] = jnp.broadcast_to(out[...][None], spread.shape)


def encode(
    peers, slots, fetched, lengths, pos_table, emb_gain, emb_bias, w_qkv, w_out, out_bias, norm_gain, norm_bias
):
    width = fetched.shape[1]
    tokens = slots.shape[0]
    passes = lengths.shape[0]
    macs = tokens * width * (fetched.shape[0] + 4 * HEADS * HD)
    operands = (
        lengths[None],
        slots,
        fetched,
        pos_table,
        emb_gain[None],
        emb_bias[None],
        out_bias[None],
        norm_gain[None],
        norm_bias[None],
        w_qkv,
        w_out,
    )
    return pl.pallas_call(
        encode_kernel,
        out_shape=[
            jax.ShapeDtypeStruct((passes, width), jnp.bfloat16),
            jax.ShapeDtypeStruct((peers, passes, width), jnp.bfloat16),
        ],
        in_specs=[pl.BlockSpec(memory_space=pltpu.HBM)] * len(operands),
        out_specs=[pl.BlockSpec(memory_space=pltpu.VMEM)] * 2,
        scratch_shapes=[pltpu.VMEM(operand.shape, operand.dtype) for operand in operands]
        + [pltpu.SemaphoreType.DMA((len(operands) + 3,))],
        compiler_params=pltpu.CompilerParams(vmem_limit_bytes=60 * 1024 * 1024),
        cost_estimate=pl.CostEstimate(
            flops=2 * macs, bytes_accessed=6 * 1024 * 1024, transcendentals=0
        ),
        name="encode",
    )(*operands)


def padded(rows):
    return -(-rows // 16) * 16


def rank_bits(count):
    return max(1, (count - 1).bit_length())


def route_kernel(
    sizes, token_ids_far, owners_far, row_slot_far, plan, token_slot_far, code, *near
):
    peers, vocab_rows, token_cap, row_cap, pooled = sizes
    token_ids, owners, row_slot, token_slot, arrived = near
    copies = [
        pltpu.make_async_copy(source, target, arrived.at[at])
        for at, (source, target) in enumerate(
            ((token_ids_far, token_ids), (owners_far, owners), (row_slot_far, row_slot))
        )
    ]
    for copy in copies:
        copy.start()
    for copy in copies:
        copy.wait()
    ids = jnp.concatenate([token_ids[p : p + 1, :] for p in range(token_ids.shape[0])], axis=1)
    tokens, rows = ids.shape[1], owners.shape[1]
    count = tokens + rows
    edge = (lax.broadcasted_iota(jnp.int32, (peers, tokens), 0) + 1) * vocab_rows
    holder = jnp.sum(jnp.where(ids >= edge, 1, 0), axis=0, keepdims=True)
    values = jnp.concatenate([ids - holder * vocab_rows, row_slot[...]], axis=1)

    kind = jnp.concatenate([holder, owners[...] + peers], axis=1)
    at = lax.broadcasted_iota(jnp.int32, (count, count), 0)
    by = lax.broadcasted_iota(jnp.int32, (count, count), 1)
    across = jnp.broadcast_to(kind, (count, count))
    down = jnp.sum(jnp.where(at == by, across, 0), axis=1, keepdims=True)
    same = down == across
    rank_row = jnp.sum(jnp.where(same & (at < by), 1, 0), axis=0, keepdims=True)
    rank_col = jnp.sum(jnp.where(same & (by < at), 1, 0), axis=1, keepdims=True)

    code[...] = owners[...] * 2 ** rank_bits(rows) + rank_row[:, tokens:]
    goal = jnp.concatenate([holder, owners[...]], axis=1)
    peer = lax.broadcasted_iota(jnp.int32, (peers, count), 0)
    left = jnp.where(peer == goal, values + 1, 0).astype(jnp.float32)
    columns = token_cap + row_cap + pooled
    column = lax.broadcasted_iota(jnp.int32, (count, columns), 1)
    entry = lax.broadcasted_iota(jnp.int32, (count, 1), 0)
    first = jnp.where(entry < tokens, rank_col, rank_col + token_cap)
    second = entry - (count - pooled) + token_cap + row_cap
    second = jnp.where(entry < count - pooled, -1, second)
    right = jnp.where((column == first) | (column == second), 1.0, 0.0)
    filled = jnp.dot(
        left, right, preferred_element_type=jnp.float32, precision=lax.Precision.HIGHEST
    )
    filled = filled.astype(jnp.int32) - 1
    for p in range(peers):
        plan[p, :, :rows] = code[...]
        plan[p, :, rows:] = filled[p : p + 1]
    token_slot[...] = down[:tokens] * token_cap + rank_col[:tokens]
    send = pltpu.make_async_copy(token_slot, token_slot_far, arrived.at[3])
    send.start()
    send.wait()


def route(token_ids, owners, row_slot, sizes):
    peers, _, token_cap, row_cap, pooled = sizes
    passes, seq_len = token_ids.shape
    rows = owners.shape[1]
    ints = lambda *shape: jax.ShapeDtypeStruct(shape, jnp.int32)
    return pl.pallas_call(
        functools.partial(route_kernel, sizes),
        out_shape=[
            ints(peers, 1, rows + token_cap + row_cap + pooled),
            ints(passes * seq_len, 1),
            ints(1, rows),
        ],
        in_specs=[pl.BlockSpec(memory_space=pltpu.HBM)] * 3,
        out_specs=[
            pl.BlockSpec(memory_space=pltpu.VMEM),
            pl.BlockSpec(memory_space=pltpu.HBM),
            pl.BlockSpec(memory_space=pltpu.VMEM),
        ],
        scratch_shapes=[
            pltpu.VMEM(token_ids.shape, jnp.int32),
            pltpu.VMEM(owners.shape, jnp.int32),
            pltpu.VMEM(row_slot.shape, jnp.int32),
            pltpu.VMEM((passes * seq_len, 1), jnp.int32),
            pltpu.SemaphoreType.DMA((4,)),
        ],
        name="route",
    )(token_ids, owners, row_slot)


def pack_kernel(half, row_cap, count, picks, pieces, *refs):
    me = lax.axis_index("dp")
    far, refs = refs[: 2 + 2 * pieces], refs[2 + 2 * pieces :]
    near, arrived = refs[-3 - 2 * pieces : -1], refs[-1]
    outs, codes_a, codes_b = refs[: -3 - 2 * pieces], near[0], near[1]
    slot_count = len(outs) * row_cap
    code_copies = [
        pltpu.make_async_copy(far[0], codes_a, arrived.at[0]),
        pltpu.make_async_copy(far[1], codes_b, arrived.at[1]),
    ]
    row_copies = [
        pltpu.make_async_copy(far[at], near[at], arrived.at[at]) for at in range(2, len(far))
    ]
    for copy in code_copies + row_copies:
        copy.start()
    for copy in code_copies:
        copy.wait()
    for source, codes in enumerate((codes_a, codes_b)):
        if picks is None:
            code = codes[...]
        else:
            code = codes[me ^ picks[source], :, :count]
        bits = rank_bits(count)
        owner, rank = code >> bits, code & (2**bits - 1)
        fits = ((owner ^ me) & (1 | half)) == 0
        chip = ((owner ^ me) & (half - 1)) >> 1
        slot = jnp.where(fits, chip * row_cap + rank, -1)
        packed, at = 0.0, 0
        for piece in range(source * pieces, (source + 1) * pieces):
            rows = near[2 + piece]
            spot = lax.broadcasted_iota(jnp.int32, (slot_count, rows.shape[0]), 0)
            table = jnp.where(slot[:, at : at + rows.shape[0]] == spot, 1.0, 0.0)
            row_copies[piece].wait()
            packed += jnp.dot(
                table.astype(jnp.bfloat16), rows[...], preferred_element_type=jnp.float32
            )
            at += rows.shape[0]
        packed = packed.astype(jnp.bfloat16)
        for step, out in enumerate(outs):
            if source == 0 and out.shape[0] > 2 * row_cap:
                out[...] = jnp.zeros(out.shape, out.dtype)
            out[source * row_cap : (source + 1) * row_cap, :] = packed[
                step * row_cap : (step + 1) * row_cap
            ]


def pack_rows(codes_a, codes_b, rows_a, rows_b, half, row_cap, count, picks=None):
    width = rows_a[0].shape[1]
    total = sum(piece.shape[0] for piece in rows_a)
    pieces = len(rows_a)
    steps = half // 2
    operands = (codes_a, codes_b, *rows_a, *rows_b)
    return pl.pallas_call(
        functools.partial(pack_kernel, half, row_cap, count, picks, pieces),
        out_shape=[jax.ShapeDtypeStruct((padded(2 * row_cap), width), jnp.bfloat16)] * steps,
        in_specs=[pl.BlockSpec(memory_space=pl.ANY)] * len(operands),
        out_specs=[pl.BlockSpec(memory_space=pltpu.VMEM)] * steps,
        scratch_shapes=[
            *(pltpu.VMEM(operand.shape, operand.dtype) for operand in operands),
            pltpu.SemaphoreType.DMA((len(operands),)),
        ],
        compiler_params=pltpu.CompilerParams(vmem_limit_bytes=20 * 1024 * 1024),
        cost_estimate=pl.CostEstimate(
            flops=4 * steps * row_cap * width * total,
            bytes_accessed=4 * width * (total + steps * row_cap),
            transcendentals=0,
        ),
        name="pack",
    )(*operands)


def onehot(where_to, first, count):
    centre = lax.broadcasted_iota(jnp.int32, (count, where_to.shape[1]), 0) + first
    return jnp.where(centre == where_to, 1.0, 0.0)


BLOCK = 128


def early_kernel(places_far, centroids_far, *rest):
    pieces, (out_far, share_far, places, rows, centroids, out, share, arrived, left) = rest[:-9], rest[-9:]
    size = pieces[0].shape[0]
    steps = centroids.shape[0] // BLOCK
    copies = [pltpu.make_async_copy(places_far, places, arrived.at[0])]
    for at, piece in enumerate(pieces):
        copies.append(
            pltpu.make_async_copy(piece, rows.at[pl.ds(at * size, size)], arrived.at[1 + at])
        )
    loads = []
    for step in range(steps):
        block = pl.ds(step * BLOCK, BLOCK)
        loads.append(
            pltpu.make_async_copy(
                centroids_far.at[block], centroids.at[block], arrived.at[1 + len(pieces) + step]
            )
        )
    for copy in copies + loads:
        copy.start()
    for copy in copies:
        copy.wait()
    sends = []
    for step in range(steps):
        block = pl.ds(step * BLOCK, BLOCK)
        hot = onehot(places[...], step * BLOCK, BLOCK)
        counts = jnp.sum(hot, axis=1, keepdims=True)
        scale = jnp.where(counts > 0, 1.0 / jnp.maximum(counts, 1.0), 0.0)
        sums = jnp.dot(
            hot[:, : rows.shape[0]].astype(jnp.bfloat16),
            rows[...],
            preferred_element_type=jnp.float32,
        )
        loads[step].wait()
        out[block, :] = jnp.where(counts > 0, sums * scale, centroids[block, :])
        share[block, :] = jnp.broadcast_to(scale, (BLOCK, share.shape[1]))
        sends.append(pltpu.make_async_copy(out.at[block], out_far.at[block], left.at[step]))
        sends[-1].start()
    sends.append(pltpu.make_async_copy(share, share_far, left.at[steps]))
    sends[-1].start()
    for send in sends:
        send.wait()


def late_kernel(places_far, late_far, spread_far, share_far, early_far, *rest):
    pieces, rest = rest[:-10], rest[-10:]
    out_far, places, late, spread, share, rows, early, out, arrived, left = rest
    size, passes = pieces[0].shape[0], spread.shape[1]
    steps = early.shape[0] // BLOCK
    loads = [
        pltpu.make_async_copy(source, target, arrived.at[at])
        for at, (source, target) in enumerate(
            ((places_far, places), (late_far, late), (spread_far, spread), (share_far, share))
        )
    ]
    for at, piece in enumerate(pieces):
        loads.append(
            pltpu.make_async_copy(piece, rows.at[pl.ds(at * size, size)], arrived.at[4 + at])
        )
    starts = []
    for step in range(steps):
        block = pl.ds(step * BLOCK, BLOCK)
        starts.append(
            pltpu.make_async_copy(
                early_far.at[block], early.at[block], arrived.at[len(loads) + step]
            )
        )
    for copy in loads + starts:
        copy.start()
    for copy in loads:
        copy.wait()
    top = len(pieces) * size
    for peer in range(spread.shape[0]):
        rows[top + peer * passes : top + (peer + 1) * passes, :] = spread[peer]
    where_to = jnp.concatenate([places[:, places.shape[1] - top :], late[...]], axis=1)
    sends = []
    for step in range(steps):
        block = pl.ds(step * BLOCK, BLOCK)
        hot = onehot(where_to, step * BLOCK, BLOCK).astype(jnp.bfloat16)
        sums = jnp.dot(hot, rows[...], preferred_element_type=jnp.float32)
        starts[step].wait()
        out[block, :] = early[block, :] + sums * share[block, :1]
        sends.append(pltpu.make_async_copy(out.at[block], out_far.at[block], left.at[step]))
        sends[-1].start()
    for send in sends:
        send.wait()


def early_update(places, centroids, pieces):
    centre_count, width = centroids.shape
    row_total = sum(piece.shape[0] for piece in pieces)
    wide = pltpu.VMEM(centroids.shape, jnp.float32)
    thin = (centre_count, 128)
    steps = centre_count // BLOCK
    return pl.pallas_call(
        early_kernel,
        out_shape=[
            jax.ShapeDtypeStruct(centroids.shape, jnp.float32),
            jax.ShapeDtypeStruct(thin, jnp.float32),
        ],
        in_specs=[pl.BlockSpec(memory_space=pl.ANY)] * (2 + len(pieces)),
        out_specs=[pl.BlockSpec(memory_space=pltpu.HBM)] * 2,
        scratch_shapes=[
            pltpu.VMEM(places.shape, jnp.int32),
            pltpu.VMEM((row_total, width), jnp.bfloat16),
            wide,
            wide,
            pltpu.VMEM(thin, jnp.float32),
            pltpu.SemaphoreType.DMA((1 + len(pieces) + steps,)),
            pltpu.SemaphoreType.DMA((steps + 1,)),
        ],
        compiler_params=pltpu.CompilerParams(vmem_limit_bytes=20 * 1024 * 1024),
        cost_estimate=pl.CostEstimate(
            flops=2 * centre_count * width * row_total,
            bytes_accessed=8 * centre_count * width,
            transcendentals=0,
        ),
        name="early",
    )(places, centroids, *pieces)


def late_update(places, late, spread, share, early, pieces):
    centre_count, width = early.shape
    row_total = places.shape[1] // 2 + late.shape[1]
    wide = pltpu.VMEM(early.shape, jnp.float32)
    steps = centre_count // BLOCK
    return pl.pallas_call(
        late_kernel,
        out_shape=jax.ShapeDtypeStruct(early.shape, jnp.float32),
        in_specs=[pl.BlockSpec(memory_space=pltpu.HBM)] * (5 + len(pieces)),
        out_specs=pl.BlockSpec(memory_space=pltpu.HBM),
        scratch_shapes=[
            pltpu.VMEM(places.shape, jnp.int32),
            pltpu.VMEM(late.shape, jnp.int32),
            pltpu.VMEM(spread.shape, jnp.bfloat16),
            pltpu.VMEM(share.shape, jnp.float32),
            pltpu.VMEM((row_total, width), jnp.bfloat16),
            wide,
            wide,
            pltpu.SemaphoreType.DMA((4 + len(pieces) + steps,)),
            pltpu.SemaphoreType.DMA((steps,)),
        ],
        compiler_params=pltpu.CompilerParams(vmem_limit_bytes=60 * 1024 * 1024),
        cost_estimate=pl.CostEstimate(
            flops=2 * centre_count * width * row_total,
            bytes_accessed=8 * centre_count * width,
            transcendentals=0,
        ),
        name="late",
    )(places, late, spread, share, early, *pieces)


def shards(
    token_ids,
    lengths,
    word_table,
    pos_table,
    emb_gain,
    emb_bias,
    w_qkv,
    w_out,
    out_bias,
    norm_gain,
    norm_bias,
    stored_rows,
    row_owner,
    row_slot,
    centroids,
):
    peer_count = lax.axis_size("dp")
    half = peer_count // 2
    width = word_table.shape[1]
    vocab_rows = word_table.shape[0]
    passes, seq_len = token_ids.shape
    token_count = passes * seq_len
    row_count = row_slot.shape[0]
    store_count = stored_rows.shape[0]
    token_cap = max(2, 3 * token_count // peer_count)
    row_cap = max(2, 3 * row_count // peer_count)

    across = [(i, i ^ half) for i in range(peer_count)]
    beside = [(i, i ^ 1) for i in range(peer_count)]

    def hand_on(blocks):
        got = [blocks[0]]
        for step in range(1, len(blocks)):
            moves = [(i, i ^ (2 * step)) for i in range(peer_count)]
            got.append(lax.ppermute(blocks[step], "dp", moves))
        return got

    ahead = store_count * 3 // 4 // 16 * 16
    first_rows = lax.ppermute(stored_rows[:ahead], "dp", across)
    sibling_rows = lax.ppermute(stored_rows, "dp", beside)
    sizes = (peer_count, vocab_rows, token_cap, row_cap, row_count - store_count)
    plan, token_slot, code = route(token_ids, row_owner.reshape(1, row_count), row_slot[None], sizes)
    sibling_code = lax.ppermute(code, "dp", beside)
    blocks = pack_rows(code, sibling_code, [stored_rows], [sibling_rows], half, row_cap, row_count)
    plan, *blocks = lax.optimization_barrier((plan, *blocks))
    own_half = hand_on(blocks)
    codes = lax.all_to_all(plan, "dp", split_axis=0, concat_axis=0, tiled=True)
    plan = codes[:, 0, row_count:]
    rest, plan = lax.optimization_barrier((stored_rows[ahead:], plan))
    last_rows = lax.ppermute(rest, "dp", across)
    wanted = plan[:, :token_cap].reshape(peer_count * token_cap)
    chosen = wanted[:, None] == jnp.arange(vocab_rows, dtype=jnp.int32)[None, :]
    found = jnp.dot(
        chosen.astype(jnp.bfloat16), word_table, preferred_element_type=jnp.float32
    ).astype(jnp.bfloat16)
    found, first_rows, own_half[:3] = lax.optimization_barrier(
        (found, first_rows, own_half[:3])
    )
    fetched = lax.all_to_all(
        found.reshape(peer_count, token_cap, width), "dp", split_axis=0, concat_axis=0, tiled=True
    ).reshape(peer_count * token_cap, width)

    partner_rows = [first_rows, last_rows]
    far_rows = [lax.ppermute(rows, "dp", beside) for rows in partner_rows]
    picks = (half, half ^ 1)
    blocks = pack_rows(codes, codes, partner_rows, far_rows, half, row_cap, row_count, picks)
    other_half = hand_on(blocks)
    sources = lax.axis_index("dp") ^ jnp.arange(peer_count, dtype=jnp.int32)
    got_places = plan[:, token_cap : token_cap + row_cap][sources].reshape(half, 2 * row_cap)
    spare = padded(2 * row_cap) - 2 * row_cap
    got_places = jnp.pad(got_places, ((0, 0), (0, spare)), constant_values=-1).reshape(1, -1)
    means, share = early_update(got_places, centroids, own_half)
    late_places = plan[:, token_cap + row_cap :].reshape(1, -1)
    fetched, means, share, got_places, late_places = lax.optimization_barrier(
        (fetched, means, share, got_places, late_places)
    )

    passage_embed, spread = encode(
        peer_count,
        token_slot,
        fetched,
        lengths,
        pos_table,
        emb_gain,
        emb_bias,
        w_qkv,
        w_out,
        out_bias,
        norm_gain,
        norm_bias,
    )
    all_embeds = lax.all_to_all(
        spread, "dp", split_axis=0, concat_axis=0, tiled=True
    )
    new_centroids = late_update(got_places, late_places, all_embeds, share, means, other_half)
    return (passage_embed, new_centroids)


def solution(mesh):
    return jax.shard_map(
        shards,
        mesh=mesh,
        in_specs=(
            P(("groups", "dp"), None),
            P(("groups", "dp")),
            P("dp", None),
            P(),
            P(),
            P(),
            P(),
            P(),
            P(),
            P(),
            P(),
            P(("groups", "dp"), None),
            P(("groups", "dp"), None),
            P(("groups", "dp")),
            P(("groups", "dp"), None),
        ),
        out_specs=(P(("groups", "dp"), None), P(("groups", "dp"), None)),
        check_vma=False,
    )
```

```python
import functools

import jax
import jax.numpy as jnp
from jax import lax
from jax.experimental import pallas as pl
from jax.experimental.pallas import tpu as pltpu
from jax.sharding import PartitionSpec as P

HEADS = 8
HD = 64


def normed(values, gain, shift):
    center = values - jnp.mean(values, axis=-1, keepdims=True)
    spread = jnp.mean(center * center, axis=-1, keepdims=True)
    return center * lax.rsqrt(spread + 1e-12) * gain + shift


def head_sums(weights, seq):
    rows, columns = weights.shape
    lane = lax.broadcasted_iota(jnp.int32, (rows, 2 * seq), 1)
    sums = []
    for start in range(0, columns, 2 * seq):
        pair = weights[:, start : start + 2 * seq]
        first = jnp.sum(jnp.where(lane < seq, pair, 0.0), axis=1, keepdims=True)
        second = jnp.sum(jnp.where(lane < seq, 0.0, pair), axis=1, keepdims=True)
        sums.append(jnp.where(lane < seq, first, second))
    return jnp.concatenate(sums, axis=1)


def encode_kernel(*refs):
    count = (len(refs) - 3) // 2
    far, (out, spread), near, arrived = refs[:count], refs[count : count + 2], refs[-count - 1 : -1], refs[-1]
    w_qkv_far, inner = far[-2], HEADS * HD
    copies = [
        pltpu.make_async_copy(source, target, arrived.at[at])
        for at, (source, target) in enumerate(zip(far, near))
        if source is not w_qkv_far
    ]
    lengths, slots, fetched, pos, emb_gain, emb_bias, out_bias, norm_gain, norm_bias, w_qkv, w_out = near
    out_copy = copies.pop()
    thirds = []
    for third in range(3):
        columns = pl.ds(third * inner, inner)
        thirds.append(
            pltpu.make_async_copy(
                w_qkv_far.at[:, columns], w_qkv.at[:, columns], arrived.at[count + third]
            )
        )
    for copy in copies + thirds + [out_copy]:
        copy.start()
    for copy in copies:
        copy.wait()
    passes = out.shape[0]
    size = [lengths[:, p : p + 1] for p in range(passes)]
    tokens, slot_count = slots.shape[0], fetched.shape[0]
    seq = tokens // passes
    spot = lax.broadcasted_iota(jnp.int32, (tokens, slot_count), 1)
    picker = jnp.where(slots[...] == spot, 1.0, 0.0).astype(jnp.bfloat16)
    tok = jnp.dot(picker, fetched[...], preferred_element_type=jnp.float32)
    where_at = pos[...].astype(jnp.float32)
    summed = tok + jnp.concatenate([where_at] * passes, axis=0)
    embedded = normed(summed, emb_gain[...], emb_bias[...]).astype(jnp.bfloat16)
    parts = []
    for third in range(3):
        thirds[third].wait()
        weights = w_qkv[:, third * inner : (third + 1) * inner]
        part = jnp.dot(embedded, weights, preferred_element_type=jnp.float32)
        parts.append(part.astype(jnp.bfloat16))

    block_row = lax.broadcasted_iota(jnp.int32, (HEADS * seq, inner), 0) // seq
    block_col = lax.broadcasted_iota(jnp.int32, (HEADS * seq, inner), 1) // HD
    same = block_row == block_col
    lane = lax.broadcasted_iota(jnp.int32, (seq, HEADS * seq), 1) % seq
    contexts = []
    for p in range(passes):
        query, keys, vals = (part[p * seq : (p + 1) * seq] for part in parts)
        zero = jnp.zeros((), jnp.bfloat16)
        keys = jnp.where(same, jnp.concatenate([keys] * HEADS, axis=0), zero)
        vals = jnp.where(same, jnp.concatenate([vals] * HEADS, axis=0), zero)
        scores = lax.dot_general(
            query, keys, (((1,), (1,)), ((), ())), preferred_element_type=jnp.float32
        ) * HD ** (-0.5)
        weights = jnp.where(lane < size[p], jnp.exp(scores), 0.0)
        probs = (weights / head_sums(weights, seq)).astype(jnp.bfloat16)
        contexts.append(jnp.dot(probs, vals, preferred_element_type=jnp.float32))
    context = jnp.concatenate(contexts, axis=0).astype(jnp.bfloat16)
    out_copy.wait()
    attended = jnp.dot(context, w_out[...], preferred_element_type=jnp.float32) + out_bias[...]
    hidden = normed(embedded.astype(jnp.float32) + attended, norm_gain[...], norm_bias[...])
    row = lax.broadcasted_iota(jnp.int32, (seq, 1), 0)
    for p in range(passes):
        kept = jnp.where(row < size[p], hidden[p * seq : (p + 1) * seq], 0.0)
        pooled = jnp.sum(kept, axis=0, keepdims=True) / size[p].astype(jnp.float32)
        scale = lax.rsqrt(jnp.mean(pooled * pooled, axis=-1, keepdims=True) + 1e-06)
        out[p : p + 1, :] = (pooled * scale).astype(jnp.bfloat16)
    spread[...] = jnp.broadcast_to(out[...][None], spread.shape)


def encode(
    peers, slots, fetched, lengths, pos_table, emb_gain, emb_bias, w_qkv, w_out, out_bias, norm_gain, norm_bias
):
    width = fetched.shape[1]
    tokens = slots.shape[0]
    passes = lengths.shape[0]
    macs = tokens * width * (fetched.shape[0] + 4 * HEADS * HD)
    operands = (
        lengths[None],
        slots,
        fetched,
        pos_table,
        emb_gain[None],
        emb_bias[None],
        out_bias[None],
        norm_gain[None],
        norm_bias[None],
        w_qkv,
        w_out,
    )
    return pl.pallas_call(
        encode_kernel,
        out_shape=[
            jax.ShapeDtypeStruct((passes, width), jnp.bfloat16),
            jax.ShapeDtypeStruct((peers, passes, width), jnp.bfloat16),
        ],
        in_specs=[pl.BlockSpec(memory_space=pltpu.HBM)] * len(operands),
        out_specs=[pl.BlockSpec(memory_space=pltpu.VMEM)] * 2,
        scratch_shapes=[pltpu.VMEM(operand.shape, operand.dtype) for operand in operands]
        + [pltpu.SemaphoreType.DMA((len(operands) + 3,))],
        compiler_params=pltpu.CompilerParams(vmem_limit_bytes=60 * 1024 * 1024),
        cost_estimate=pl.CostEstimate(
            flops=2 * macs, bytes_accessed=6 * 1024 * 1024, transcendentals=0
        ),
        name="encode",
    )(*operands)


def padded(rows):
    return -(-rows // 16) * 16


def rank_bits(count):
    return max(1, (count - 1).bit_length())


def route_kernel(
    sizes,
    token_ids_far,
    owners_far,
    row_slot_far,
    stored,
    plan,
    token_slot_far,
    code,
    first_rows,
    *near,
):
    peers, vocab_rows, token_cap, row_cap, pooled = sizes
    token_ids, owners, row_slot, token_slot, arrived = near
    copies = [
        pltpu.make_async_copy(source, target, arrived.at[at])
        for at, (source, target) in enumerate(
            ((token_ids_far, token_ids), (owners_far, owners), (row_slot_far, row_slot))
        )
    ]
    cut = pltpu.make_async_copy(
        stored.at[pl.ds(0, first_rows.shape[0])], first_rows, arrived.at[4]
    )
    for copy in copies + [cut]:
        copy.start()
    for copy in copies:
        copy.wait()
    ids = jnp.concatenate([token_ids[p : p + 1, :] for p in range(token_ids.shape[0])], axis=1)
    tokens, rows = ids.shape[1], owners.shape[1]
    count = tokens + rows
    edge = (lax.broadcasted_iota(jnp.int32, (peers, tokens), 0) + 1) * vocab_rows
    holder = jnp.sum(jnp.where(ids >= edge, 1, 0), axis=0, keepdims=True)
    values = jnp.concatenate([ids - holder * vocab_rows, row_slot[...]], axis=1)

    kind = jnp.concatenate([holder, owners[...] + peers], axis=1)
    at = lax.broadcasted_iota(jnp.int32, (count, count), 0)
    by = lax.broadcasted_iota(jnp.int32, (count, count), 1)
    across = jnp.broadcast_to(kind, (count, count))
    down = jnp.sum(jnp.where(at == by, across, 0), axis=1, keepdims=True)
    same = down == across
    rank_row = jnp.sum(jnp.where(same & (at < by), 1, 0), axis=0, keepdims=True)
    rank_col = jnp.sum(jnp.where(same & (by < at), 1, 0), axis=1, keepdims=True)

    code[...] = owners[...] * 2 ** rank_bits(rows) + rank_row[:, tokens:]
    goal = jnp.concatenate([holder, owners[...]], axis=1)
    peer = lax.broadcasted_iota(jnp.int32, (peers, count), 0)
    left = jnp.where(peer == goal, values + 1, 0).astype(jnp.float32)
    columns = token_cap + row_cap + pooled
    column = lax.broadcasted_iota(jnp.int32, (count, columns), 1)
    entry = lax.broadcasted_iota(jnp.int32, (count, 1), 0)
    first = jnp.where(entry < tokens, rank_col, rank_col + token_cap)
    second = entry - (count - pooled) + token_cap + row_cap
    second = jnp.where(entry < count - pooled, -1, second)
    right = jnp.where((column == first) | (column == second), 1.0, 0.0)
    filled = jnp.dot(
        left, right, preferred_element_type=jnp.float32, precision=lax.Precision.HIGHEST
    )
    filled = filled.astype(jnp.int32) - 1
    for p in range(peers):
        plan[p, :, :rows] = code[...]
        plan[p, :, rows:] = filled[p : p + 1]
    token_slot[...] = down[:tokens] * token_cap + rank_col[:tokens]
    send = pltpu.make_async_copy(token_slot, token_slot_far, arrived.at[3])
    send.start()
    cut.wait()
    send.wait()


def route(token_ids, owners, row_slot, stored_rows, ahead, sizes):
    peers, _, token_cap, row_cap, pooled = sizes
    passes, seq_len = token_ids.shape
    rows = owners.shape[1]
    ints = lambda *shape: jax.ShapeDtypeStruct(shape, jnp.int32)
    return pl.pallas_call(
        functools.partial(route_kernel, sizes),
        out_shape=[
            ints(peers, 1, rows + token_cap + row_cap + pooled),
            ints(passes * seq_len, 1),
            ints(1, rows),
            jax.ShapeDtypeStruct((ahead, stored_rows.shape[1]), stored_rows.dtype),
        ],
        in_specs=[pl.BlockSpec(memory_space=pltpu.HBM)] * 4,
        out_specs=[
            pl.BlockSpec(memory_space=pltpu.VMEM),
            pl.BlockSpec(memory_space=pltpu.HBM),
            pl.BlockSpec(memory_space=pltpu.VMEM),
            pl.BlockSpec(memory_space=pltpu.HBM),
        ],
        scratch_shapes=[
            pltpu.VMEM(token_ids.shape, jnp.int32),
            pltpu.VMEM(owners.shape, jnp.int32),
            pltpu.VMEM(row_slot.shape, jnp.int32),
            pltpu.VMEM((passes * seq_len, 1), jnp.int32),
            pltpu.SemaphoreType.DMA((5,)),
        ],
        compiler_params=pltpu.CompilerParams(vmem_limit_bytes=60 * 1024 * 1024),
        name="route",
    )(token_ids, owners, row_slot, stored_rows)


def pack_kernel(half, row_cap, count, picks, pieces, rest, *refs):
    me = lax.axis_index("dp")
    operands = 2 + 2 * pieces
    far, refs = refs[:operands], refs[operands:]
    steps = half // 2
    outs, refs = refs[: steps + bool(rest)], refs[steps + bool(rest) :]
    near, (blocks, tail, arrived, left) = refs[:operands], refs[operands:]
    size = blocks.shape[0] // steps
    copies = [
        pltpu.make_async_copy(far[at], near[at], arrived.at[at]) for at in range(operands)
    ]
    for copy in copies:
        copy.start()
    for copy in copies[:2]:
        copy.wait()
    if size > 2 * row_cap:
        blocks[...] = jnp.zeros(blocks.shape, blocks.dtype)
    for source in range(2):
        if picks is None:
            code = near[source][...]
        else:
            code = near[source][me ^ picks[source], :, :count]
        bits = rank_bits(count)
        owner, rank = code >> bits, code & (2**bits - 1)
        fits = ((owner ^ me) & (1 | half)) == 0
        chip = ((owner ^ me) & (half - 1)) >> 1
        slot = jnp.where(fits, chip * row_cap + rank, -1)
        packed, at = 0.0, 0
        for piece in range(2 + source * pieces, 2 + (source + 1) * pieces):
            rows = near[piece]
            spot = lax.broadcasted_iota(jnp.int32, (steps * row_cap, rows.shape[0]), 0)
            table = jnp.where(slot[:, at : at + rows.shape[0]] == spot, 1.0, 0.0)
            copies[piece].wait()
            packed += jnp.dot(
                table.astype(jnp.bfloat16), rows[...], preferred_element_type=jnp.float32
            )
            at += rows.shape[0]
        packed = packed.astype(jnp.bfloat16)
        for step in range(steps):
            first = step * size + source * row_cap
            blocks[first : first + row_cap, :] = packed[step * row_cap : (step + 1) * row_cap]
    sends = [
        pltpu.make_async_copy(
            blocks.at[pl.ds(step * size, size)], outs[step], left.at[step]
        )
        for step in range(steps)
    ]
    if rest:
        tail[...] = near[2][near[2].shape[0] - rest :, :]
        sends.append(pltpu.make_async_copy(tail, outs[steps], left.at[steps]))
    for send in sends:
        send.start()
    for send in sends:
        send.wait()


def pack_rows(codes_a, codes_b, rows_a, rows_b, half, row_cap, count, picks=None, rest=0):
    width = rows_a[0].shape[1]
    total = sum(piece.shape[0] for piece in rows_a)
    steps = half // 2
    size = padded(2 * row_cap)
    operands = (codes_a, codes_b, *rows_a, *rows_b)
    shapes = [(size, width)] * steps + [(rest, width)] * bool(rest)
    return pl.pallas_call(
        functools.partial(pack_kernel, half, row_cap, count, picks, len(rows_a), rest),
        out_shape=[jax.ShapeDtypeStruct(shape, jnp.bfloat16) for shape in shapes],
        in_specs=[pl.BlockSpec(memory_space=pltpu.HBM)] * len(operands),
        out_specs=[pl.BlockSpec(memory_space=pltpu.HBM)] * len(shapes),
        scratch_shapes=[
            *(pltpu.VMEM(operand.shape, operand.dtype) for operand in operands),
            pltpu.VMEM((steps * size, width), jnp.bfloat16),
            pltpu.VMEM((max(rest, 16), width), jnp.bfloat16),
            pltpu.SemaphoreType.DMA((len(operands),)),
            pltpu.SemaphoreType.DMA((len(shapes),)),
        ],
        compiler_params=pltpu.CompilerParams(vmem_limit_bytes=60 * 1024 * 1024),
        cost_estimate=pl.CostEstimate(
            flops=4 * steps * row_cap * width * total,
            bytes_accessed=4 * width * (total + steps * row_cap),
            transcendentals=0,
        ),
        name="pack",
    )(*operands)


def onehot(where_to, first, count):
    centre = lax.broadcasted_iota(jnp.int32, (count, where_to.shape[1]), 0) + first
    return jnp.where(centre == where_to, 1.0, 0.0)


BLOCK = 128


def early_kernel(places_far, centroids_far, *rest):
    pieces, (out_far, share_far, places, rows, centroids, out, share, arrived, left) = rest[:-9], rest[-9:]
    size = pieces[0].shape[0]
    steps = centroids.shape[0] // BLOCK
    copies = [pltpu.make_async_copy(places_far, places, arrived.at[0])]
    for at, piece in enumerate(pieces):
        copies.append(
            pltpu.make_async_copy(piece, rows.at[pl.ds(at * size, size)], arrived.at[1 + at])
        )
    loads = []
    for step in range(steps):
        block = pl.ds(step * BLOCK, BLOCK)
        loads.append(
            pltpu.make_async_copy(
                centroids_far.at[block], centroids.at[block], arrived.at[1 + len(pieces) + step]
            )
        )
    for copy in copies + loads:
        copy.start()
    for copy in copies:
        copy.wait()
    sends = []
    for step in range(steps):
        block = pl.ds(step * BLOCK, BLOCK)
        hot = onehot(places[...], step * BLOCK, BLOCK)
        counts = jnp.sum(hot, axis=1, keepdims=True)
        scale = jnp.where(counts > 0, 1.0 / jnp.maximum(counts, 1.0), 0.0)
        sums = jnp.dot(
            hot[:, : rows.shape[0]].astype(jnp.bfloat16),
            rows[...],
            preferred_element_type=jnp.float32,
        )
        loads[step].wait()
        out[block, :] = jnp.where(counts > 0, sums * scale, centroids[block, :])
        share[block, :] = jnp.broadcast_to(scale, (BLOCK, share.shape[1]))
        sends.append(pltpu.make_async_copy(out.at[block], out_far.at[block], left.at[step]))
        sends[-1].start()
    sends.append(pltpu.make_async_copy(share, share_far, left.at[steps]))
    sends[-1].start()
    for send in sends:
        send.wait()


def late_kernel(places_far, late_far, spread_far, share_far, early_far, *rest):
    pieces, rest = rest[:-10], rest[-10:]
    out_far, places, late, spread, share, rows, early, out, arrived, left = rest
    size, passes = pieces[0].shape[0], spread.shape[1]
    steps = early.shape[0] // BLOCK
    loads = [
        pltpu.make_async_copy(source, target, arrived.at[at])
        for at, (source, target) in enumerate(
            ((places_far, places), (late_far, late), (spread_far, spread), (share_far, share))
        )
    ]
    for at, piece in enumerate(pieces):
        loads.append(
            pltpu.make_async_copy(piece, rows.at[pl.ds(at * size, size)], arrived.at[4 + at])
        )
    starts = []
    for step in range(steps):
        block = pl.ds(step * BLOCK, BLOCK)
        starts.append(
            pltpu.make_async_copy(
                early_far.at[block], early.at[block], arrived.at[len(loads) + step]
            )
        )
    for copy in loads + starts:
        copy.start()
    for copy in loads:
        copy.wait()
    top = len(pieces) * size
    for peer in range(spread.shape[0]):
        rows[top + peer * passes : top + (peer + 1) * passes, :] = spread[peer]
    where_to = jnp.concatenate([places[:, places.shape[1] - top :], late[...]], axis=1)
    sends = []
    for step in range(steps):
        block = pl.ds(step * BLOCK, BLOCK)
        hot = onehot(where_to, step * BLOCK, BLOCK).astype(jnp.bfloat16)
        sums = jnp.dot(hot, rows[...], preferred_element_type=jnp.float32)
        starts[step].wait()
        out[block, :] = early[block, :] + sums * share[block, :1]
        sends.append(pltpu.make_async_copy(out.at[block], out_far.at[block], left.at[step]))
        sends[-1].start()
    for send in sends:
        send.wait()


def early_update(places, centroids, pieces):
    centre_count, width = centroids.shape
    row_total = sum(piece.shape[0] for piece in pieces)
    wide = pltpu.VMEM(centroids.shape, jnp.float32)
    thin = (centre_count, 128)
    steps = centre_count // BLOCK
    return pl.pallas_call(
        early_kernel,
        out_shape=[
            jax.ShapeDtypeStruct(centroids.shape, jnp.float32),
            jax.ShapeDtypeStruct(thin, jnp.float32),
        ],
        in_specs=[pl.BlockSpec(memory_space=pl.ANY)] * (2 + len(pieces)),
        out_specs=[pl.BlockSpec(memory_space=pltpu.HBM)] * 2,
        scratch_shapes=[
            pltpu.VMEM(places.shape, jnp.int32),
            pltpu.VMEM((row_total, width), jnp.bfloat16),
            wide,
            wide,
            pltpu.VMEM(thin, jnp.float32),
            pltpu.SemaphoreType.DMA((1 + len(pieces) + steps,)),
            pltpu.SemaphoreType.DMA((steps + 1,)),
        ],
        compiler_params=pltpu.CompilerParams(vmem_limit_bytes=60 * 1024 * 1024),
        cost_estimate=pl.CostEstimate(
            flops=100 * centre_count * width * row_total,
            bytes_accessed=200 * centre_count * width,
            transcendentals=0,
        ),
        name="early",
    )(places, centroids, *pieces)


def late_update(places, late, spread, share, early, pieces):
    centre_count, width = early.shape
    row_total = places.shape[1] // 2 + late.shape[1]
    wide = pltpu.VMEM(early.shape, jnp.float32)
    steps = centre_count // BLOCK
    return pl.pallas_call(
        late_kernel,
        out_shape=jax.ShapeDtypeStruct(early.shape, jnp.float32),
        in_specs=[pl.BlockSpec(memory_space=pltpu.HBM)] * (5 + len(pieces)),
        out_specs=pl.BlockSpec(memory_space=pltpu.HBM),
        scratch_shapes=[
            pltpu.VMEM(places.shape, jnp.int32),
            pltpu.VMEM(late.shape, jnp.int32),
            pltpu.VMEM(spread.shape, jnp.bfloat16),
            pltpu.VMEM(share.shape, jnp.float32),
            pltpu.VMEM((row_total, width), jnp.bfloat16),
            wide,
            wide,
            pltpu.SemaphoreType.DMA((4 + len(pieces) + steps,)),
            pltpu.SemaphoreType.DMA((steps,)),
        ],
        compiler_params=pltpu.CompilerParams(vmem_limit_bytes=60 * 1024 * 1024),
        cost_estimate=pl.CostEstimate(
            flops=2 * centre_count * width * row_total,
            bytes_accessed=8 * centre_count * width,
            transcendentals=0,
        ),
        name="late",
    )(places, late, spread, share, early, *pieces)


def shards(
    token_ids,
    lengths,
    word_table,
    pos_table,
    emb_gain,
    emb_bias,
    w_qkv,
    w_out,
    out_bias,
    norm_gain,
    norm_bias,
    stored_rows,
    row_owner,
    row_slot,
    centroids,
):
    peer_count = lax.axis_size("dp")
    half = peer_count // 2
    width = word_table.shape[1]
    vocab_rows = word_table.shape[0]
    passes, seq_len = token_ids.shape
    token_count = passes * seq_len
    row_count = row_slot.shape[0]
    store_count = stored_rows.shape[0]
    token_cap = max(2, 3 * token_count // peer_count)
    row_cap = max(2, 3 * row_count // peer_count)

    across = [(i, i ^ half) for i in range(peer_count)]
    beside = [(i, i ^ 1) for i in range(peer_count)]

    def hand_on(blocks):
        got = [blocks[0]]
        for step in range(1, len(blocks)):
            moves = [(i, i ^ (2 * step)) for i in range(peer_count)]
            got.append(lax.ppermute(blocks[step], "dp", moves))
        return got

    ahead = store_count * 7 // 16 // 16 * 16
    sibling_rows = lax.ppermute(stored_rows, "dp", beside)
    sizes = (peer_count, vocab_rows, token_cap, row_cap, row_count - store_count)
    plan, token_slot, code, first_rows = route(
        token_ids, row_owner.reshape(1, row_count), row_slot[None], stored_rows, ahead, sizes
    )
    first_rows = lax.ppermute(first_rows, "dp", across)
    sibling_code = lax.ppermute(code, "dp", beside)
    *blocks, last_rows = pack_rows(
        code,
        sibling_code,
        [stored_rows],
        [sibling_rows],
        half,
        row_cap,
        row_count,
        rest=store_count - ahead,
    )
    plan, last_rows, *blocks = lax.optimization_barrier((plan, last_rows, *blocks))
    codes = lax.all_to_all(plan, "dp", split_axis=0, concat_axis=0, tiled=True)
    last_rows = lax.ppermute(last_rows, "dp", across)
    own_half = hand_on(blocks)
    plan = codes[:, 0, row_count:]
    wanted = plan[:, :token_cap].reshape(peer_count * token_cap)
    chosen = wanted[:, None] == jnp.arange(vocab_rows, dtype=jnp.int32)[None, :]
    found = jnp.dot(
        chosen.astype(jnp.bfloat16), word_table, preferred_element_type=jnp.float32
    ).astype(jnp.bfloat16)
    found, first_rows, own_half[:3] = lax.optimization_barrier(
        (found, first_rows, own_half[:3])
    )
    fetched = lax.all_to_all(
        found.reshape(peer_count, token_cap, width), "dp", split_axis=0, concat_axis=0, tiled=True
    ).reshape(peer_count * token_cap, width)

    partner_rows = [first_rows, last_rows]
    far_rows = [lax.ppermute(rows, "dp", beside) for rows in partner_rows]
    picks = (half, half ^ 1)
    blocks = pack_rows(codes, codes, partner_rows, far_rows, half, row_cap, row_count, picks)
    other_half = hand_on(blocks)
    sources = lax.axis_index("dp") ^ jnp.arange(peer_count, dtype=jnp.int32)
    got_places = plan[:, token_cap : token_cap + row_cap][sources].reshape(half, 2 * row_cap)
    spare = padded(2 * row_cap) - 2 * row_cap
    got_places = jnp.pad(got_places, ((0, 0), (0, spare)), constant_values=-1).reshape(1, -1)
    means, share = early_update(got_places, centroids, own_half)
    late_places = plan[:, token_cap + row_cap :].reshape(1, -1)
    fetched, means, share, got_places, late_places = lax.optimization_barrier(
        (fetched, means, share, got_places, late_places)
    )

    passage_embed, spread = encode(
        peer_count,
        token_slot,
        fetched,
        lengths,
        pos_table,
        emb_gain,
        emb_bias,
        w_qkv,
        w_out,
        out_bias,
        norm_gain,
        norm_bias,
    )
    all_embeds = lax.all_to_all(
        spread, "dp", split_axis=0, concat_axis=0, tiled=True
    )
    new_centroids = late_update(got_places, late_places, all_embeds, share, means, other_half)
    return (passage_embed, new_centroids)


def solution(mesh):
    return jax.shard_map(
        shards,
        mesh=mesh,
        in_specs=(
            P(("groups", "dp"), None),
            P(("groups", "dp")),
            P("dp", None),
            P(),
            P(),
            P(),
            P(),
            P(),
            P(),
            P(),
            P(),
            P(("groups", "dp"), None),
            P(("groups", "dp"), None),
            P(("groups", "dp")),
            P(("groups", "dp"), None),
        ),
        out_specs=(P(("groups", "dp"), None), P(("groups", "dp"), None)),
        check_vma=False,
    )
```

```python
import functools

import jax
import jax.numpy as jnp
from jax import lax
from jax.experimental import pallas as pl
from jax.experimental.pallas import tpu as pltpu
from jax.sharding import PartitionSpec as P

HEADS = 8
HD = 64


def normed(values, gain, shift):
    center = values - jnp.mean(values, axis=-1, keepdims=True)
    spread = jnp.mean(center * center, axis=-1, keepdims=True)
    return center * lax.rsqrt(spread + 1e-12) * gain + shift


def head_sums(weights, seq):
    rows, columns = weights.shape
    lane = lax.broadcasted_iota(jnp.int32, (rows, 2 * seq), 1)
    sums = []
    for start in range(0, columns, 2 * seq):
        pair = weights[:, start : start + 2 * seq]
        first = jnp.sum(jnp.where(lane < seq, pair, 0.0), axis=1, keepdims=True)
        second = jnp.sum(jnp.where(lane < seq, 0.0, pair), axis=1, keepdims=True)
        sums.append(jnp.where(lane < seq, first, second))
    return jnp.concatenate(sums, axis=1)


def encode_kernel(*refs):
    count = (len(refs) - 3) // 2
    far, (out, spread), near, arrived = refs[:count], refs[count : count + 2], refs[-count - 1 : -1], refs[-1]
    w_qkv_far, inner = far[-2], HEADS * HD
    copies = [
        pltpu.make_async_copy(source, target, arrived.at[at])
        for at, (source, target) in enumerate(zip(far, near))
        if source is not w_qkv_far
    ]
    lengths, slots, fetched, pos, emb_gain, emb_bias, out_bias, norm_gain, norm_bias, w_qkv, w_out = near
    out_copy = copies.pop()
    thirds = []
    for third in range(3):
        columns = pl.ds(third * inner, inner)
        thirds.append(
            pltpu.make_async_copy(
                w_qkv_far.at[:, columns], w_qkv.at[:, columns], arrived.at[count + third]
            )
        )
    for copy in copies + thirds + [out_copy]:
        copy.start()
    for copy in copies:
        copy.wait()
    passes = out.shape[0]
    size = [lengths[:, p : p + 1] for p in range(passes)]
    tokens, slot_count = slots.shape[0], fetched.shape[0]
    seq = tokens // passes
    spot = lax.broadcasted_iota(jnp.int32, (tokens, slot_count), 1)
    picker = jnp.where(slots[...] == spot, 1.0, 0.0).astype(jnp.bfloat16)
    tok = jnp.dot(picker, fetched[...], preferred_element_type=jnp.float32)
    where_at = pos[...].astype(jnp.float32)
    summed = tok + jnp.concatenate([where_at] * passes, axis=0)
    embedded = normed(summed, emb_gain[...], emb_bias[...]).astype(jnp.bfloat16)
    parts = []
    for third in range(3):
        thirds[third].wait()
        weights = w_qkv[:, third * inner : (third + 1) * inner]
        part = jnp.dot(embedded, weights, preferred_element_type=jnp.float32)
        parts.append(part.astype(jnp.bfloat16))

    block_row = lax.broadcasted_iota(jnp.int32, (HEADS * seq, inner), 0) // seq
    block_col = lax.broadcasted_iota(jnp.int32, (HEADS * seq, inner), 1) // HD
    same = block_row == block_col
    lane = lax.broadcasted_iota(jnp.int32, (seq, HEADS * seq), 1) % seq
    contexts = []
    for p in range(passes):
        query, keys, vals = (part[p * seq : (p + 1) * seq] for part in parts)
        zero = jnp.zeros((), jnp.bfloat16)
        keys = jnp.where(same, jnp.concatenate([keys] * HEADS, axis=0), zero)
        vals = jnp.where(same, jnp.concatenate([vals] * HEADS, axis=0), zero)
        scores = lax.dot_general(
            query, keys, (((1,), (1,)), ((), ())), preferred_element_type=jnp.float32
        ) * HD ** (-0.5)
        weights = jnp.where(lane < size[p], jnp.exp(scores), 0.0)
        probs = (weights / head_sums(weights, seq)).astype(jnp.bfloat16)
        contexts.append(jnp.dot(probs, vals, preferred_element_type=jnp.float32))
    context = jnp.concatenate(contexts, axis=0).astype(jnp.bfloat16)
    out_copy.wait()
    attended = jnp.dot(context, w_out[...], preferred_element_type=jnp.float32) + out_bias[...]
    hidden = normed(embedded.astype(jnp.float32) + attended, norm_gain[...], norm_bias[...])
    row = lax.broadcasted_iota(jnp.int32, (seq, 1), 0)
    for p in range(passes):
        kept = jnp.where(row < size[p], hidden[p * seq : (p + 1) * seq], 0.0)
        pooled = jnp.sum(kept, axis=0, keepdims=True) / size[p].astype(jnp.float32)
        scale = lax.rsqrt(jnp.mean(pooled * pooled, axis=-1, keepdims=True) + 1e-06)
        out[p : p + 1, :] = (pooled * scale).astype(jnp.bfloat16)
    spread[...] = jnp.broadcast_to(out[...][None], spread.shape)


def encode(
    peers, slots, fetched, lengths, pos_table, emb_gain, emb_bias, w_qkv, w_out, out_bias, norm_gain, norm_bias
):
    width = fetched.shape[1]
    tokens = slots.shape[0]
    passes = lengths.shape[0]
    macs = tokens * width * (fetched.shape[0] + 4 * HEADS * HD)
    operands = (
        lengths[None],
        slots,
        fetched,
        pos_table,
        emb_gain[None],
        emb_bias[None],
        out_bias[None],
        norm_gain[None],
        norm_bias[None],
        w_qkv,
        w_out,
    )
    return pl.pallas_call(
        encode_kernel,
        out_shape=[
            jax.ShapeDtypeStruct((passes, width), jnp.bfloat16),
            jax.ShapeDtypeStruct((peers, passes, width), jnp.bfloat16),
        ],
        in_specs=[pl.BlockSpec(memory_space=pltpu.HBM)] * len(operands),
        out_specs=[pl.BlockSpec(memory_space=pltpu.VMEM)] * 2,
        scratch_shapes=[pltpu.VMEM(operand.shape, operand.dtype) for operand in operands]
        + [pltpu.SemaphoreType.DMA((len(operands) + 3,))],
        compiler_params=pltpu.CompilerParams(vmem_limit_bytes=60 * 1024 * 1024),
        cost_estimate=pl.CostEstimate(
            flops=2 * macs, bytes_accessed=6 * 1024 * 1024, transcendentals=0
        ),
        name="encode",
    )(*operands)


def padded(rows):
    return -(-rows // 16) * 16


def rank_bits(count):
    return max(1, (count - 1).bit_length())


def route_kernel(
    sizes,
    token_ids_far,
    owners_far,
    row_slot_far,
    plan,
    token_slot_far,
    code,
    *near,
):
    peers, vocab_rows, token_cap, row_cap, pooled = sizes
    token_ids, owners, row_slot, token_slot, arrived = near
    copies = [
        pltpu.make_async_copy(source, target, arrived.at[at])
        for at, (source, target) in enumerate(
            ((token_ids_far, token_ids), (owners_far, owners), (row_slot_far, row_slot))
        )
    ]
    for copy in copies:
        copy.start()
    for copy in copies:
        copy.wait()
    ids = jnp.concatenate([token_ids[p : p + 1, :] for p in range(token_ids.shape[0])], axis=1)
    tokens, rows = ids.shape[1], owners.shape[1]
    count = tokens + rows
    edge = (lax.broadcasted_iota(jnp.int32, (peers, tokens), 0) + 1) * vocab_rows
    holder = jnp.sum(jnp.where(ids >= edge, 1, 0), axis=0, keepdims=True)
    values = jnp.concatenate([ids - holder * vocab_rows, row_slot[...]], axis=1)

    kind = jnp.concatenate([holder, owners[...] + peers], axis=1)
    at = lax.broadcasted_iota(jnp.int32, (count, count), 0)
    by = lax.broadcasted_iota(jnp.int32, (count, count), 1)
    across = jnp.broadcast_to(kind, (count, count))
    down = jnp.sum(jnp.where(at == by, across, 0), axis=1, keepdims=True)
    same = down == across
    rank_row = jnp.sum(jnp.where(same & (at < by), 1, 0), axis=0, keepdims=True)
    rank_col = jnp.sum(jnp.where(same & (by < at), 1, 0), axis=1, keepdims=True)

    code[...] = owners[...] * 2 ** rank_bits(rows) + rank_row[:, tokens:]
    goal = jnp.concatenate([holder, owners[...]], axis=1)
    peer = lax.broadcasted_iota(jnp.int32, (peers, count), 0)
    left = jnp.where(peer == goal, values + 1, 0).astype(jnp.float32)
    columns = token_cap + row_cap + pooled
    column = lax.broadcasted_iota(jnp.int32, (count, columns), 1)
    entry = lax.broadcasted_iota(jnp.int32, (count, 1), 0)
    first = jnp.where(entry < tokens, rank_col, rank_col + token_cap)
    second = entry - (count - pooled) + token_cap + row_cap
    second = jnp.where(entry < count - pooled, -1, second)
    right = jnp.where((column == first) | (column == second), 1.0, 0.0)
    filled = jnp.dot(
        left, right, preferred_element_type=jnp.float32, precision=lax.Precision.HIGHEST
    )
    filled = filled.astype(jnp.int32) - 1
    for p in range(peers):
        plan[p, :, :rows] = code[...]
        plan[p, :, rows:] = filled[p : p + 1]
    token_slot[...] = down[:tokens] * token_cap + rank_col[:tokens]
    send = pltpu.make_async_copy(token_slot, token_slot_far, arrived.at[3])
    send.start()
    send.wait()


def cut_kernel(far, out_far, near, done):
    load = pltpu.make_async_copy(far.at[pl.ds(0, near.shape[0])], near, done.at[0])
    load.start()
    load.wait()
    send = pltpu.make_async_copy(near, out_far, done.at[1])
    send.start()
    send.wait()


def cut(rows, count):
    shape = (count, rows.shape[1])
    return pl.pallas_call(
        cut_kernel,
        out_shape=jax.ShapeDtypeStruct(shape, rows.dtype),
        in_specs=[pl.BlockSpec(memory_space=pltpu.HBM)],
        out_specs=pl.BlockSpec(memory_space=pltpu.HBM),
        scratch_shapes=[pltpu.VMEM(shape, rows.dtype), pltpu.SemaphoreType.DMA((2,))],
        compiler_params=pltpu.CompilerParams(vmem_limit_bytes=60 * 1024 * 1024),
        name="cut",
    )(rows)


def route(token_ids, owners, row_slot, sizes):
    peers, _, token_cap, row_cap, pooled = sizes
    passes, seq_len = token_ids.shape
    rows = owners.shape[1]
    ints = lambda *shape: jax.ShapeDtypeStruct(shape, jnp.int32)
    return pl.pallas_call(
        functools.partial(route_kernel, sizes),
        out_shape=[
            ints(peers, 1, rows + token_cap + row_cap + pooled),
            ints(passes * seq_len, 1),
            ints(1, rows),
        ],
        in_specs=[pl.BlockSpec(memory_space=pltpu.HBM)] * 3,
        out_specs=[
            pl.BlockSpec(memory_space=pltpu.VMEM),
            pl.BlockSpec(memory_space=pltpu.HBM),
            pl.BlockSpec(memory_space=pltpu.VMEM),
        ],
        scratch_shapes=[
            pltpu.VMEM(token_ids.shape, jnp.int32),
            pltpu.VMEM(owners.shape, jnp.int32),
            pltpu.VMEM(row_slot.shape, jnp.int32),
            pltpu.VMEM((passes * seq_len, 1), jnp.int32),
            pltpu.SemaphoreType.DMA((4,)),
        ],
        compiler_params=pltpu.CompilerParams(vmem_limit_bytes=60 * 1024 * 1024),
        name="route",
    )(token_ids, owners, row_slot)


def pack_kernel(half, row_cap, count, picks, pieces, rest, *refs):
    me = lax.axis_index("dp")
    operands = 2 + 2 * pieces
    far, refs = refs[:operands], refs[operands:]
    steps = half // 2
    outs, refs = refs[: steps + bool(rest)], refs[steps + bool(rest) :]
    near, (blocks, tail, arrived, left) = refs[:operands], refs[operands:]
    size = blocks.shape[0] // steps
    copies = [
        pltpu.make_async_copy(far[at], near[at], arrived.at[at]) for at in range(operands)
    ]
    for copy in copies:
        copy.start()
    for copy in copies[:2]:
        copy.wait()
    if size > 2 * row_cap:
        blocks[...] = jnp.zeros(blocks.shape, blocks.dtype)
    for source in range(2):
        if picks is None:
            code = near[source][...]
        else:
            code = near[source][me ^ picks[source], :, :count]
        bits = rank_bits(count)
        owner, rank = code >> bits, code & (2**bits - 1)
        fits = ((owner ^ me) & (1 | half)) == 0
        chip = ((owner ^ me) & (half - 1)) >> 1
        slot = jnp.where(fits, chip * row_cap + rank, -1)
        packed, at = 0.0, 0
        for piece in range(2 + source * pieces, 2 + (source + 1) * pieces):
            rows = near[piece]
            spot = lax.broadcasted_iota(jnp.int32, (steps * row_cap, rows.shape[0]), 0)
            table = jnp.where(slot[:, at : at + rows.shape[0]] == spot, 1.0, 0.0)
            copies[piece].wait()
            packed += jnp.dot(
                table.astype(jnp.bfloat16), rows[...], preferred_element_type=jnp.float32
            )
            at += rows.shape[0]
        packed = packed.astype(jnp.bfloat16)
        for step in range(steps):
            first = step * size + source * row_cap
            blocks[first : first + row_cap, :] = packed[step * row_cap : (step + 1) * row_cap]
    sends = [
        pltpu.make_async_copy(
            blocks.at[pl.ds(step * size, size)], outs[step], left.at[step]
        )
        for step in range(steps)
    ]
    if rest:
        tail[...] = near[2][near[2].shape[0] - rest :, :]
        sends.append(pltpu.make_async_copy(tail, outs[steps], left.at[steps]))
    for send in sends:
        send.start()
    for send in sends:
        send.wait()


def pack_rows(codes_a, codes_b, rows_a, rows_b, half, row_cap, count, picks=None, rest=0):
    width = rows_a[0].shape[1]
    total = sum(piece.shape[0] for piece in rows_a)
    steps = half // 2
    size = padded(2 * row_cap)
    operands = (codes_a, codes_b, *rows_a, *rows_b)
    shapes = [(size, width)] * steps + [(rest, width)] * bool(rest)
    return pl.pallas_call(
        functools.partial(pack_kernel, half, row_cap, count, picks, len(rows_a), rest),
        out_shape=[jax.ShapeDtypeStruct(shape, jnp.bfloat16) for shape in shapes],
        in_specs=[pl.BlockSpec(memory_space=pltpu.HBM)] * len(operands),
        out_specs=[pl.BlockSpec(memory_space=pltpu.HBM)] * len(shapes),
        scratch_shapes=[
            *(pltpu.VMEM(operand.shape, operand.dtype) for operand in operands),
            pltpu.VMEM((steps * size, width), jnp.bfloat16),
            pltpu.VMEM((max(rest, 16), width), jnp.bfloat16),
            pltpu.SemaphoreType.DMA((len(operands),)),
            pltpu.SemaphoreType.DMA((len(shapes),)),
        ],
        compiler_params=pltpu.CompilerParams(vmem_limit_bytes=60 * 1024 * 1024),
        cost_estimate=pl.CostEstimate(
            flops=4 * steps * row_cap * width * total,
            bytes_accessed=4 * width * (total + steps * row_cap),
            transcendentals=0,
        ),
        name="pack",
    )(*operands)


def onehot(where_to, first, count):
    centre = lax.broadcasted_iota(jnp.int32, (count, where_to.shape[1]), 0) + first
    return jnp.where(centre == where_to, 1.0, 0.0)


BLOCK = 128


def early_kernel(places_far, centroids_far, *rest):
    pieces, (out_far, share_far, places, rows, centroids, out, share, arrived, left) = rest[:-9], rest[-9:]
    size = pieces[0].shape[0]
    steps = centroids.shape[0] // BLOCK
    copies = [pltpu.make_async_copy(places_far, places, arrived.at[0])]
    for at, piece in enumerate(pieces):
        copies.append(
            pltpu.make_async_copy(piece, rows.at[pl.ds(at * size, size)], arrived.at[1 + at])
        )
    loads = []
    for step in range(steps):
        block = pl.ds(step * BLOCK, BLOCK)
        loads.append(
            pltpu.make_async_copy(
                centroids_far.at[block], centroids.at[block], arrived.at[1 + len(pieces) + step]
            )
        )
    for copy in copies + loads:
        copy.start()
    for copy in copies:
        copy.wait()
    sends = []
    for step in range(steps):
        block = pl.ds(step * BLOCK, BLOCK)
        hot = onehot(places[...], step * BLOCK, BLOCK)
        counts = jnp.sum(hot, axis=1, keepdims=True)
        scale = jnp.where(counts > 0, 1.0 / jnp.maximum(counts, 1.0), 0.0)
        sums = jnp.dot(
            hot[:, : rows.shape[0]].astype(jnp.bfloat16),
            rows[...],
            preferred_element_type=jnp.float32,
        )
        loads[step].wait()
        out[block, :] = jnp.where(counts > 0, sums * scale, centroids[block, :])
        share[block, :] = jnp.broadcast_to(scale, (BLOCK, share.shape[1]))
        sends.append(pltpu.make_async_copy(out.at[block], out_far.at[block], left.at[step]))
        sends[-1].start()
    sends.append(pltpu.make_async_copy(share, share_far, left.at[steps]))
    sends[-1].start()
    for send in sends:
        send.wait()


def late_kernel(places_far, late_far, spread_far, share_far, early_far, *rest):
    pieces, rest = rest[:-10], rest[-10:]
    out_far, places, late, spread, share, rows, early, out, arrived, left = rest
    size, passes = pieces[0].shape[0], spread.shape[1]
    steps = early.shape[0] // BLOCK
    loads = [
        pltpu.make_async_copy(source, target, arrived.at[at])
        for at, (source, target) in enumerate(
            ((places_far, places), (late_far, late), (spread_far, spread), (share_far, share))
        )
    ]
    for at, piece in enumerate(pieces):
        loads.append(
            pltpu.make_async_copy(piece, rows.at[pl.ds(at * size, size)], arrived.at[4 + at])
        )
    starts = []
    for step in range(steps):
        block = pl.ds(step * BLOCK, BLOCK)
        starts.append(
            pltpu.make_async_copy(
                early_far.at[block], early.at[block], arrived.at[len(loads) + step]
            )
        )
    for copy in loads + starts:
        copy.start()
    for copy in loads:
        copy.wait()
    top = len(pieces) * size
    for peer in range(spread.shape[0]):
        rows[top + peer * passes : top + (peer + 1) * passes, :] = spread[peer]
    where_to = jnp.concatenate([places[:, places.shape[1] - top :], late[...]], axis=1)
    sends = []
    for step in range(steps):
        block = pl.ds(step * BLOCK, BLOCK)
        hot = onehot(where_to, step * BLOCK, BLOCK).astype(jnp.bfloat16)
        sums = jnp.dot(hot, rows[...], preferred_element_type=jnp.float32)
        starts[step].wait()
        out[block, :] = early[block, :] + sums * share[block, :1]
        sends.append(pltpu.make_async_copy(out.at[block], out_far.at[block], left.at[step]))
        sends[-1].start()
    for send in sends:
        send.wait()


def early_update(places, centroids, pieces):
    centre_count, width = centroids.shape
    row_total = sum(piece.shape[0] for piece in pieces)
    wide = pltpu.VMEM(centroids.shape, jnp.float32)
    thin = (centre_count, 128)
    steps = centre_count // BLOCK
    return pl.pallas_call(
        early_kernel,
        out_shape=[
            jax.ShapeDtypeStruct(centroids.shape, jnp.float32),
            jax.ShapeDtypeStruct(thin, jnp.float32),
        ],
        in_specs=[pl.BlockSpec(memory_space=pl.ANY)] * (2 + len(pieces)),
        out_specs=[pl.BlockSpec(memory_space=pltpu.HBM)] * 2,
        scratch_shapes=[
            pltpu.VMEM(places.shape, jnp.int32),
            pltpu.VMEM((row_total, width), jnp.bfloat16),
            wide,
            wide,
            pltpu.VMEM(thin, jnp.float32),
            pltpu.SemaphoreType.DMA((1 + len(pieces) + steps,)),
            pltpu.SemaphoreType.DMA((steps + 1,)),
        ],
        compiler_params=pltpu.CompilerParams(vmem_limit_bytes=60 * 1024 * 1024),
        cost_estimate=pl.CostEstimate(
            flops=100 * centre_count * width * row_total,
            bytes_accessed=200 * centre_count * width,
            transcendentals=0,
        ),
        name="early",
    )(places, centroids, *pieces)


def late_update(places, late, spread, share, early, pieces):
    centre_count, width = early.shape
    row_total = places.shape[1] // 2 + late.shape[1]
    wide = pltpu.VMEM(early.shape, jnp.float32)
    steps = centre_count // BLOCK
    return pl.pallas_call(
        late_kernel,
        out_shape=jax.ShapeDtypeStruct(early.shape, jnp.float32),
        in_specs=[pl.BlockSpec(memory_space=pltpu.HBM)] * (5 + len(pieces)),
        out_specs=pl.BlockSpec(memory_space=pltpu.HBM),
        scratch_shapes=[
            pltpu.VMEM(places.shape, jnp.int32),
            pltpu.VMEM(late.shape, jnp.int32),
            pltpu.VMEM(spread.shape, jnp.bfloat16),
            pltpu.VMEM(share.shape, jnp.float32),
            pltpu.VMEM((row_total, width), jnp.bfloat16),
            wide,
            wide,
            pltpu.SemaphoreType.DMA((4 + len(pieces) + steps,)),
            pltpu.SemaphoreType.DMA((steps,)),
        ],
        compiler_params=pltpu.CompilerParams(vmem_limit_bytes=60 * 1024 * 1024),
        cost_estimate=pl.CostEstimate(
            flops=2 * centre_count * width * row_total,
            bytes_accessed=8 * centre_count * width,
            transcendentals=0,
        ),
        name="late",
    )(places, late, spread, share, early, *pieces)


def shards(
    token_ids,
    lengths,
    word_table,
    pos_table,
    emb_gain,
    emb_bias,
    w_qkv,
    w_out,
    out_bias,
    norm_gain,
    norm_bias,
    stored_rows,
    row_owner,
    row_slot,
    centroids,
):
    peer_count = lax.axis_size("dp")
    half = peer_count // 2
    width = word_table.shape[1]
    vocab_rows = word_table.shape[0]
    passes, seq_len = token_ids.shape
    token_count = passes * seq_len
    row_count = row_slot.shape[0]
    store_count = stored_rows.shape[0]
    token_cap = max(2, 3 * token_count // peer_count)
    row_cap = max(2, 3 * row_count // peer_count)

    across = [(i, i ^ half) for i in range(peer_count)]
    beside = [(i, i ^ 1) for i in range(peer_count)]

    def hand_on(blocks):
        got = [blocks[0]]
        for step in range(1, len(blocks)):
            moves = [(i, i ^ (2 * step)) for i in range(peer_count)]
            got.append(lax.ppermute(blocks[step], "dp", moves))
        return got

    ahead = store_count * 5 // 8 // 16 * 16
    sibling_rows = lax.ppermute(stored_rows, "dp", beside)
    first_rows = lax.ppermute(cut(stored_rows, ahead), "dp", across)
    sizes = (peer_count, vocab_rows, token_cap, row_cap, row_count - store_count)
    plan, token_slot, code = route(token_ids, row_owner.reshape(1, row_count), row_slot[None], sizes)
    sibling_code = lax.ppermute(code, "dp", beside)
    *blocks, last_rows = pack_rows(
        code,
        sibling_code,
        [stored_rows],
        [sibling_rows],
        half,
        row_cap,
        row_count,
        rest=store_count - ahead,
    )
    plan, *blocks = lax.optimization_barrier((plan, *blocks))
    codes = lax.all_to_all(plan, "dp", split_axis=0, concat_axis=0, tiled=True)
    own_half = hand_on(blocks)
    codes, last_rows = lax.optimization_barrier((codes, last_rows))
    last_rows = lax.ppermute(last_rows, "dp", across)
    plan = codes[:, 0, row_count:]
    wanted = plan[:, :token_cap].reshape(peer_count * token_cap)
    chosen = wanted[:, None] == jnp.arange(vocab_rows, dtype=jnp.int32)[None, :]
    found = jnp.dot(
        chosen.astype(jnp.bfloat16), word_table, preferred_element_type=jnp.float32
    ).astype(jnp.bfloat16)
    found, first_rows, own_half[:3] = lax.optimization_barrier(
        (found, first_rows, own_half[:3])
    )
    fetched = lax.all_to_all(
        found.reshape(peer_count, token_cap, width), "dp", split_axis=0, concat_axis=0, tiled=True
    ).reshape(peer_count * token_cap, width)

    partner_rows = [first_rows, last_rows]
    far_rows = [lax.ppermute(rows, "dp", beside) for rows in partner_rows]
    picks = (half, half ^ 1)
    blocks = pack_rows(codes, codes, partner_rows, far_rows, half, row_cap, row_count, picks)
    other_half = hand_on(blocks)
    sources = lax.axis_index("dp") ^ jnp.arange(peer_count, dtype=jnp.int32)
    got_places = plan[:, token_cap : token_cap + row_cap][sources].reshape(half, 2 * row_cap)
    spare = padded(2 * row_cap) - 2 * row_cap
    got_places = jnp.pad(got_places, ((0, 0), (0, spare)), constant_values=-1).reshape(1, -1)
    means, share = early_update(got_places, centroids, own_half)
    late_places = plan[:, token_cap + row_cap :].reshape(1, -1)
    fetched, means, share, got_places, late_places = lax.optimization_barrier(
        (fetched, means, share, got_places, late_places)
    )

    passage_embed, spread = encode(
        peer_count,
        token_slot,
        fetched,
        lengths,
        pos_table,
        emb_gain,
        emb_bias,
        w_qkv,
        w_out,
        out_bias,
        norm_gain,
        norm_bias,
    )
    all_embeds = lax.all_to_all(
        spread, "dp", split_axis=0, concat_axis=0, tiled=True
    )
    new_centroids = late_update(got_places, late_places, all_embeds, share, means, other_half)
    return (passage_embed, new_centroids)


def solution(mesh):
    return jax.shard_map(
        shards,
        mesh=mesh,
        in_specs=(
            P(("groups", "dp"), None),
            P(("groups", "dp")),
            P("dp", None),
            P(),
            P(),
            P(),
            P(),
            P(),
            P(),
            P(),
            P(),
            P(("groups", "dp"), None),
            P(("groups", "dp"), None),
            P(("groups", "dp")),
            P(("groups", "dp"), None),
        ),
        out_specs=(P(("groups", "dp"), None), P(("groups", "dp"), None)),
        check_vma=False,
    )
```

```python
import functools

import jax
import jax.numpy as jnp
from jax import lax
from jax.experimental import pallas as pl
from jax.experimental.pallas import tpu as pltpu
from jax.sharding import PartitionSpec as P

HEADS = 8
HD = 64


def normed(values, gain, shift):
    center = values - jnp.mean(values, axis=-1, keepdims=True)
    spread = jnp.mean(center * center, axis=-1, keepdims=True)
    return center * lax.rsqrt(spread + 1e-12) * gain + shift


def head_sums(weights, seq):
    rows, columns = weights.shape
    lane = lax.broadcasted_iota(jnp.int32, (rows, 2 * seq), 1)
    sums = []
    for start in range(0, columns, 2 * seq):
        pair = weights[:, start : start + 2 * seq]
        first = jnp.sum(jnp.where(lane < seq, pair, 0.0), axis=1, keepdims=True)
        second = jnp.sum(jnp.where(lane < seq, 0.0, pair), axis=1, keepdims=True)
        sums.append(jnp.where(lane < seq, first, second))
    return jnp.concatenate(sums, axis=1)


def encode_kernel(*refs):
    count = (len(refs) - 3) // 2
    far, (out, spread), near, arrived = refs[:count], refs[count : count + 2], refs[-count - 1 : -1], refs[-1]
    w_qkv_far, inner = far[-2], HEADS * HD
    copies = [
        pltpu.make_async_copy(source, target, arrived.at[at])
        for at, (source, target) in enumerate(zip(far, near))
        if source is not w_qkv_far
    ]
    lengths, slots, fetched, pos, emb_gain, emb_bias, out_bias, norm_gain, norm_bias, w_qkv, w_out = near
    out_copy = copies.pop()
    thirds = []
    for third in range(3):
        columns = pl.ds(third * inner, inner)
        thirds.append(
            pltpu.make_async_copy(
                w_qkv_far.at[:, columns], w_qkv.at[:, columns], arrived.at[count + third]
            )
        )
    for copy in copies + thirds + [out_copy]:
        copy.start()
    for copy in copies:
        copy.wait()
    passes = out.shape[0]
    size = [lengths[:, p : p + 1] for p in range(passes)]
    tokens, slot_count = slots.shape[0], fetched.shape[0]
    seq = tokens // passes
    spot = lax.broadcasted_iota(jnp.int32, (tokens, slot_count), 1)
    picker = jnp.where(slots[...] == spot, 1.0, 0.0).astype(jnp.bfloat16)
    tok = jnp.dot(picker, fetched[...], preferred_element_type=jnp.float32)
    where_at = pos[...].astype(jnp.float32)
    summed = tok + jnp.concatenate([where_at] * passes, axis=0)
    embedded = normed(summed, emb_gain[...], emb_bias[...]).astype(jnp.bfloat16)
    parts = []
    for third in range(3):
        thirds[third].wait()
        weights = w_qkv[:, third * inner : (third + 1) * inner]
        part = jnp.dot(embedded, weights, preferred_element_type=jnp.float32)
        parts.append(part.astype(jnp.bfloat16))

    block_row = lax.broadcasted_iota(jnp.int32, (HEADS * seq, inner), 0) // seq
    block_col = lax.broadcasted_iota(jnp.int32, (HEADS * seq, inner), 1) // HD
    same = block_row == block_col
    lane = lax.broadcasted_iota(jnp.int32, (seq, HEADS * seq), 1) % seq
    contexts = []
    for p in range(passes):
        query, keys, vals = (part[p * seq : (p + 1) * seq] for part in parts)
        zero = jnp.zeros((), jnp.bfloat16)
        keys = jnp.where(same, jnp.concatenate([keys] * HEADS, axis=0), zero)
        vals = jnp.where(same, jnp.concatenate([vals] * HEADS, axis=0), zero)
        scores = lax.dot_general(
            query, keys, (((1,), (1,)), ((), ())), preferred_element_type=jnp.float32
        ) * HD ** (-0.5)
        weights = jnp.where(lane < size[p], jnp.exp(scores), 0.0)
        probs = (weights / head_sums(weights, seq)).astype(jnp.bfloat16)
        contexts.append(jnp.dot(probs, vals, preferred_element_type=jnp.float32))
    context = jnp.concatenate(contexts, axis=0).astype(jnp.bfloat16)
    out_copy.wait()
    attended = jnp.dot(context, w_out[...], preferred_element_type=jnp.float32) + out_bias[...]
    hidden = normed(embedded.astype(jnp.float32) + attended, norm_gain[...], norm_bias[...])
    row = lax.broadcasted_iota(jnp.int32, (seq, 1), 0)
    for p in range(passes):
        kept = jnp.where(row < size[p], hidden[p * seq : (p + 1) * seq], 0.0)
        pooled = jnp.sum(kept, axis=0, keepdims=True) / size[p].astype(jnp.float32)
        scale = lax.rsqrt(jnp.mean(pooled * pooled, axis=-1, keepdims=True) + 1e-06)
        out[p : p + 1, :] = (pooled * scale).astype(jnp.bfloat16)
    spread[...] = jnp.broadcast_to(out[...][None], spread.shape)


def encode(
    peers, slots, fetched, lengths, pos_table, emb_gain, emb_bias, w_qkv, w_out, out_bias, norm_gain, norm_bias
):
    width = fetched.shape[1]
    tokens = slots.shape[0]
    passes = lengths.shape[0]
    macs = tokens * width * (fetched.shape[0] + 4 * HEADS * HD)
    operands = (
        lengths[None],
        slots,
        fetched,
        pos_table,
        emb_gain[None],
        emb_bias[None],
        out_bias[None],
        norm_gain[None],
        norm_bias[None],
        w_qkv,
        w_out,
    )
    return pl.pallas_call(
        encode_kernel,
        out_shape=[
            jax.ShapeDtypeStruct((passes, width), jnp.bfloat16),
            jax.ShapeDtypeStruct((peers, passes, width), jnp.bfloat16),
        ],
        in_specs=[pl.BlockSpec(memory_space=pltpu.HBM)] * len(operands),
        out_specs=[pl.BlockSpec(memory_space=pltpu.VMEM)] * 2,
        scratch_shapes=[pltpu.VMEM(operand.shape, operand.dtype) for operand in operands]
        + [pltpu.SemaphoreType.DMA((len(operands) + 3,))],
        compiler_params=pltpu.CompilerParams(vmem_limit_bytes=60 * 1024 * 1024),
        cost_estimate=pl.CostEstimate(
            flops=2 * macs, bytes_accessed=6 * 1024 * 1024, transcendentals=0
        ),
        name="encode",
    )(*operands)


def padded(rows):
    return -(-rows // 16) * 16


def rank_bits(count):
    return max(1, (count - 1).bit_length())


def route_kernel(
    sizes,
    token_ids_far,
    owners_far,
    row_slot_far,
    plan,
    token_slot_far,
    code,
    *near,
):
    peers, vocab_rows, token_cap, row_cap, pooled = sizes
    token_ids, owners, row_slot, token_slot, arrived = near
    copies = [
        pltpu.make_async_copy(source, target, arrived.at[at])
        for at, (source, target) in enumerate(
            ((token_ids_far, token_ids), (owners_far, owners), (row_slot_far, row_slot))
        )
    ]
    for copy in copies:
        copy.start()
    for copy in copies:
        copy.wait()
    ids = jnp.concatenate([token_ids[p : p + 1, :] for p in range(token_ids.shape[0])], axis=1)
    tokens, rows = ids.shape[1], owners.shape[1]
    count = tokens + rows
    edge = (lax.broadcasted_iota(jnp.int32, (peers, tokens), 0) + 1) * vocab_rows
    holder = jnp.sum(jnp.where(ids >= edge, 1, 0), axis=0, keepdims=True)
    values = jnp.concatenate([ids - holder * vocab_rows, row_slot[...]], axis=1)

    kind = jnp.concatenate([holder, owners[...] + peers], axis=1)
    at = lax.broadcasted_iota(jnp.int32, (count, count), 0)
    by = lax.broadcasted_iota(jnp.int32, (count, count), 1)
    across = jnp.broadcast_to(kind, (count, count))
    down = jnp.sum(jnp.where(at == by, across, 0), axis=1, keepdims=True)
    same = down == across
    rank_row = jnp.sum(jnp.where(same & (at < by), 1, 0), axis=0, keepdims=True)
    rank_col = jnp.sum(jnp.where(same & (by < at), 1, 0), axis=1, keepdims=True)

    code[...] = owners[...] * 2 ** rank_bits(rows) + rank_row[:, tokens:]
    goal = jnp.concatenate([holder, owners[...]], axis=1)
    peer = lax.broadcasted_iota(jnp.int32, (peers, count), 0)
    left = jnp.where(peer == goal, values + 1, 0).astype(jnp.float32)
    columns = token_cap + row_cap + pooled
    column = lax.broadcasted_iota(jnp.int32, (count, columns), 1)
    entry = lax.broadcasted_iota(jnp.int32, (count, 1), 0)
    first = jnp.where(entry < tokens, rank_col, rank_col + token_cap)
    second = entry - (count - pooled) + token_cap + row_cap
    second = jnp.where(entry < count - pooled, -1, second)
    right = jnp.where((column == first) | (column == second), 1.0, 0.0)
    filled = jnp.dot(
        left, right, preferred_element_type=jnp.float32, precision=lax.Precision.HIGHEST
    )
    filled = filled.astype(jnp.int32) - 1
    for p in range(peers):
        plan[p, :, :rows] = code[...]
        plan[p, :, rows:] = filled[p : p + 1]
    token_slot[...] = down[:tokens] * token_cap + rank_col[:tokens]
    send = pltpu.make_async_copy(token_slot, token_slot_far, arrived.at[3])
    send.start()
    send.wait()


def route(token_ids, owners, row_slot, sizes):
    peers, _, token_cap, row_cap, pooled = sizes
    passes, seq_len = token_ids.shape
    rows = owners.shape[1]
    ints = lambda *shape: jax.ShapeDtypeStruct(shape, jnp.int32)
    return pl.pallas_call(
        functools.partial(route_kernel, sizes),
        out_shape=[
            ints(peers, 1, rows + token_cap + row_cap + pooled),
            ints(passes * seq_len, 1),
            ints(1, rows),
        ],
        in_specs=[pl.BlockSpec(memory_space=pltpu.HBM)] * 3,
        out_specs=[
            pl.BlockSpec(memory_space=pltpu.VMEM),
            pl.BlockSpec(memory_space=pltpu.HBM),
            pl.BlockSpec(memory_space=pltpu.VMEM),
        ],
        scratch_shapes=[
            pltpu.VMEM(token_ids.shape, jnp.int32),
            pltpu.VMEM(owners.shape, jnp.int32),
            pltpu.VMEM(row_slot.shape, jnp.int32),
            pltpu.VMEM((passes * seq_len, 1), jnp.int32),
            pltpu.SemaphoreType.DMA((4,)),
        ],
        compiler_params=pltpu.CompilerParams(vmem_limit_bytes=60 * 1024 * 1024),
        name="route",
    )(token_ids, owners, row_slot)


def pack_kernel(half, row_cap, count, picks, *refs):
    me = lax.axis_index("dp")
    steps = half // 2
    far, outs, near, (blocks, arrived, left) = refs[:4], refs[4:-7], refs[-7:-3], refs[-3:]
    size = blocks.shape[0] // steps
    copies = [pltpu.make_async_copy(far[at], near[at], arrived.at[at]) for at in range(4)]
    for copy in copies:
        copy.start()
    for copy in copies[:2]:
        copy.wait()
    if size > 2 * row_cap:
        blocks[...] = jnp.zeros(blocks.shape, blocks.dtype)
    for source in range(2):
        codes, rows = near[source], near[2 + source]
        code = codes[...] if picks is None else codes[me ^ picks[source], :, :count]
        bits = rank_bits(count)
        owner, rank = code >> bits, code & (2**bits - 1)
        fits = ((owner ^ me) & (1 | half)) == 0
        chip = ((owner ^ me) & (half - 1)) >> 1
        slot = jnp.where(fits, chip * row_cap + rank, -1)[:, : rows.shape[0]]
        spot = lax.broadcasted_iota(jnp.int32, (steps * row_cap, rows.shape[0]), 0)
        table = jnp.where(slot == spot, 1.0, 0.0).astype(jnp.bfloat16)
        copies[2 + source].wait()
        packed = jnp.dot(table, rows[...], preferred_element_type=jnp.float32)
        packed = packed.astype(jnp.bfloat16)
        for step in range(steps):
            first = step * size + source * row_cap
            blocks[first : first + row_cap, :] = packed[step * row_cap : (step + 1) * row_cap]
    sends = [
        pltpu.make_async_copy(blocks.at[pl.ds(step * size, size)], outs[step], left.at[step])
        for step in range(steps)
    ]
    for send in sends:
        send.start()
    for send in sends:
        send.wait()


def pack_rows(codes_a, codes_b, rows_a, rows_b, half, row_cap, count, picks=None):
    total, width = rows_a.shape
    steps = half // 2
    size = padded(2 * row_cap)
    operands = (codes_a, codes_b, rows_a, rows_b)
    return pl.pallas_call(
        functools.partial(pack_kernel, half, row_cap, count, picks),
        out_shape=[jax.ShapeDtypeStruct((size, width), jnp.bfloat16)] * steps,
        in_specs=[pl.BlockSpec(memory_space=pltpu.HBM)] * 4,
        out_specs=[pl.BlockSpec(memory_space=pltpu.HBM)] * steps,
        scratch_shapes=[
            *(pltpu.VMEM(operand.shape, operand.dtype) for operand in operands),
            pltpu.VMEM((steps * size, width), jnp.bfloat16),
            pltpu.SemaphoreType.DMA((4,)),
            pltpu.SemaphoreType.DMA((steps,)),
        ],
        compiler_params=pltpu.CompilerParams(vmem_limit_bytes=60 * 1024 * 1024),
        cost_estimate=pl.CostEstimate(
            flops=4 * steps * row_cap * width * total,
            bytes_accessed=4 * width * (total + steps * row_cap),
            transcendentals=0,
        ),
        name="pack",
    )(*operands)


def onehot(where_to, first, count):
    centre = lax.broadcasted_iota(jnp.int32, (count, where_to.shape[1]), 0) + first
    return jnp.where(centre == where_to, 1.0, 0.0)


BLOCK = 128


def early_kernel(places_far, centroids_far, *rest):
    pieces, (out_far, share_far, places, rows, centroids, out, share, arrived, left) = rest[:-9], rest[-9:]
    size = pieces[0].shape[0]
    steps = centroids.shape[0] // BLOCK
    copies = [pltpu.make_async_copy(places_far, places, arrived.at[0])]
    for at, piece in enumerate(pieces):
        copies.append(
            pltpu.make_async_copy(piece, rows.at[pl.ds(at * size, size)], arrived.at[1 + at])
        )
    loads = []
    for step in range(steps):
        block = pl.ds(step * BLOCK, BLOCK)
        loads.append(
            pltpu.make_async_copy(
                centroids_far.at[block], centroids.at[block], arrived.at[1 + len(pieces) + step]
            )
        )
    for copy in copies + loads:
        copy.start()
    for copy in copies:
        copy.wait()
    sends = []
    for step in range(steps):
        block = pl.ds(step * BLOCK, BLOCK)
        hot = onehot(places[...], step * BLOCK, BLOCK)
        counts = jnp.sum(hot, axis=1, keepdims=True)
        scale = jnp.where(counts > 0, 1.0 / jnp.maximum(counts, 1.0), 0.0)
        sums = jnp.dot(
            hot[:, : rows.shape[0]].astype(jnp.bfloat16),
            rows[...],
            preferred_element_type=jnp.float32,
        )
        loads[step].wait()
        out[block, :] = jnp.where(counts > 0, sums * scale, centroids[block, :])
        share[block, :] = jnp.broadcast_to(scale, (BLOCK, share.shape[1]))
        sends.append(pltpu.make_async_copy(out.at[block], out_far.at[block], left.at[step]))
        sends[-1].start()
    sends.append(pltpu.make_async_copy(share, share_far, left.at[steps]))
    sends[-1].start()
    for send in sends:
        send.wait()


def late_kernel(places_far, late_far, spread_far, share_far, early_far, *rest):
    pieces, rest = rest[:-10], rest[-10:]
    out_far, places, late, spread, share, rows, early, out, arrived, left = rest
    size, passes = pieces[0].shape[0], spread.shape[1]
    steps = early.shape[0] // BLOCK
    loads = [
        pltpu.make_async_copy(source, target, arrived.at[at])
        for at, (source, target) in enumerate(
            ((places_far, places), (late_far, late), (spread_far, spread), (share_far, share))
        )
    ]
    for at, piece in enumerate(pieces):
        loads.append(
            pltpu.make_async_copy(piece, rows.at[pl.ds(at * size, size)], arrived.at[4 + at])
        )
    starts = []
    for step in range(steps):
        block = pl.ds(step * BLOCK, BLOCK)
        starts.append(
            pltpu.make_async_copy(
                early_far.at[block], early.at[block], arrived.at[len(loads) + step]
            )
        )
    for copy in loads + starts:
        copy.start()
    for copy in loads:
        copy.wait()
    top = len(pieces) * size
    for peer in range(spread.shape[0]):
        rows[top + peer * passes : top + (peer + 1) * passes, :] = spread[peer]
    where_to = jnp.concatenate([places[:, places.shape[1] - top :], late[...]], axis=1)
    sends = []
    for step in range(steps):
        block = pl.ds(step * BLOCK, BLOCK)
        hot = onehot(where_to, step * BLOCK, BLOCK).astype(jnp.bfloat16)
        sums = jnp.dot(hot, rows[...], preferred_element_type=jnp.float32)
        starts[step].wait()
        out[block, :] = early[block, :] + sums * share[block, :1]
        sends.append(pltpu.make_async_copy(out.at[block], out_far.at[block], left.at[step]))
        sends[-1].start()
    for send in sends:
        send.wait()


def early_update(places, centroids, pieces):
    centre_count, width = centroids.shape
    row_total = sum(piece.shape[0] for piece in pieces)
    wide = pltpu.VMEM(centroids.shape, jnp.float32)
    thin = (centre_count, 128)
    steps = centre_count // BLOCK
    return pl.pallas_call(
        early_kernel,
        out_shape=[
            jax.ShapeDtypeStruct(centroids.shape, jnp.float32),
            jax.ShapeDtypeStruct(thin, jnp.float32),
        ],
        in_specs=[pl.BlockSpec(memory_space=pl.ANY)] * (2 + len(pieces)),
        out_specs=[pl.BlockSpec(memory_space=pltpu.HBM)] * 2,
        scratch_shapes=[
            pltpu.VMEM(places.shape, jnp.int32),
            pltpu.VMEM((row_total, width), jnp.bfloat16),
            wide,
            wide,
            pltpu.VMEM(thin, jnp.float32),
            pltpu.SemaphoreType.DMA((1 + len(pieces) + steps,)),
            pltpu.SemaphoreType.DMA((steps + 1,)),
        ],
        compiler_params=pltpu.CompilerParams(vmem_limit_bytes=60 * 1024 * 1024),
        cost_estimate=pl.CostEstimate(
            flops=2 * centre_count * width * row_total,
            bytes_accessed=8 * centre_count * width,
            transcendentals=0,
        ),
        name="early",
    )(places, centroids, *pieces)


def late_update(places, late, spread, share, early, pieces):
    centre_count, width = early.shape
    row_total = places.shape[1] // 2 + late.shape[1]
    wide = pltpu.VMEM(early.shape, jnp.float32)
    steps = centre_count // BLOCK
    return pl.pallas_call(
        late_kernel,
        out_shape=jax.ShapeDtypeStruct(early.shape, jnp.float32),
        in_specs=[pl.BlockSpec(memory_space=pltpu.HBM)] * (5 + len(pieces)),
        out_specs=pl.BlockSpec(memory_space=pltpu.HBM),
        scratch_shapes=[
            pltpu.VMEM(places.shape, jnp.int32),
            pltpu.VMEM(late.shape, jnp.int32),
            pltpu.VMEM(spread.shape, jnp.bfloat16),
            pltpu.VMEM(share.shape, jnp.float32),
            pltpu.VMEM((row_total, width), jnp.bfloat16),
            wide,
            wide,
            pltpu.SemaphoreType.DMA((4 + len(pieces) + steps,)),
            pltpu.SemaphoreType.DMA((steps,)),
        ],
        compiler_params=pltpu.CompilerParams(vmem_limit_bytes=60 * 1024 * 1024),
        cost_estimate=pl.CostEstimate(
            flops=2 * centre_count * width * row_total,
            bytes_accessed=8 * centre_count * width,
            transcendentals=0,
        ),
        name="late",
    )(places, late, spread, share, early, *pieces)


def shards(
    token_ids,
    lengths,
    word_table,
    pos_table,
    emb_gain,
    emb_bias,
    w_qkv,
    w_out,
    out_bias,
    norm_gain,
    norm_bias,
    stored_rows,
    row_owner,
    row_slot,
    centroids,
):
    peer_count = lax.axis_size("dp")
    half = peer_count // 2
    width = word_table.shape[1]
    vocab_rows = word_table.shape[0]
    passes, seq_len = token_ids.shape
    token_count = passes * seq_len
    row_count = row_slot.shape[0]
    store_count = stored_rows.shape[0]
    token_cap = max(2, 3 * token_count // peer_count)
    row_cap = max(2, 3 * row_count // peer_count)

    across = [(i, i ^ half) for i in range(peer_count)]
    beside = [(i, i ^ 1) for i in range(peer_count)]

    def hand_on(blocks):
        got = [blocks[0]]
        for step in range(1, len(blocks)):
            moves = [(i, i ^ (2 * step)) for i in range(peer_count)]
            got.append(lax.ppermute(blocks[step], "dp", moves))
        return got

    partner_rows = lax.ppermute(stored_rows, "dp", across)
    sibling_rows = lax.ppermute(stored_rows, "dp", beside)
    sizes = (peer_count, vocab_rows, token_cap, row_cap, row_count - store_count)
    plan, token_slot, code = route(token_ids, row_owner.reshape(1, row_count), row_slot[None], sizes)
    sibling_code = lax.ppermute(code, "dp", beside)
    blocks = pack_rows(code, sibling_code, stored_rows, sibling_rows, half, row_cap, row_count)
    plan, *blocks = lax.optimization_barrier((plan, *blocks))
    codes = lax.all_to_all(plan, "dp", split_axis=0, concat_axis=0, tiled=True)
    own_half = hand_on(blocks)
    plan = codes[:, 0, row_count:]
    wanted = plan[:, :token_cap].reshape(peer_count * token_cap)
    chosen = wanted[:, None] == jnp.arange(vocab_rows, dtype=jnp.int32)[None, :]
    found = jnp.dot(
        chosen.astype(jnp.bfloat16), word_table, preferred_element_type=jnp.float32
    ).astype(jnp.bfloat16)
    found, partner_rows, own_half[:3] = lax.optimization_barrier(
        (found, partner_rows, own_half[:3])
    )
    fetched = lax.all_to_all(
        found.reshape(peer_count, token_cap, width), "dp", split_axis=0, concat_axis=0, tiled=True
    ).reshape(peer_count * token_cap, width)

    far_rows = lax.ppermute(partner_rows, "dp", beside)
    picks = (half, half ^ 1)
    blocks = pack_rows(codes, codes, partner_rows, far_rows, half, row_cap, row_count, picks)
    other_half = hand_on(blocks)
    sources = lax.axis_index("dp") ^ jnp.arange(peer_count, dtype=jnp.int32)
    got_places = plan[:, token_cap : token_cap + row_cap][sources].reshape(half, 2 * row_cap)
    spare = padded(2 * row_cap) - 2 * row_cap
    got_places = jnp.pad(got_places, ((0, 0), (0, spare)), constant_values=-1).reshape(1, -1)
    means, share = early_update(got_places, centroids, own_half)
    late_places = plan[:, token_cap + row_cap :].reshape(1, -1)
    fetched, means, share, got_places, late_places = lax.optimization_barrier(
        (fetched, means, share, got_places, late_places)
    )

    passage_embed, spread = encode(
        peer_count,
        token_slot,
        fetched,
        lengths,
        pos_table,
        emb_gain,
        emb_bias,
        w_qkv,
        w_out,
        out_bias,
        norm_gain,
        norm_bias,
    )
    all_embeds = lax.all_to_all(
        spread, "dp", split_axis=0, concat_axis=0, tiled=True
    )
    new_centroids = late_update(got_places, late_places, all_embeds, share, means, other_half)
    return (passage_embed, new_centroids)


def solution(mesh):
    return jax.shard_map(
        shards,
        mesh=mesh,
        in_specs=(
            P(("groups", "dp"), None),
            P(("groups", "dp")),
            P("dp", None),
            P(),
            P(),
            P(),
            P(),
            P(),
            P(),
            P(),
            P(),
            P(("groups", "dp"), None),
            P(("groups", "dp"), None),
            P(("groups", "dp")),
            P(("groups", "dp"), None),
        ),
        out_specs=(P(("groups", "dp"), None), P(("groups", "dp"), None)),
        check_vma=False,
    )
```

```python
import functools

import jax
import jax.numpy as jnp
from jax import lax
from jax.experimental import pallas as pl
from jax.experimental.pallas import tpu as pltpu
from jax.sharding import PartitionSpec as P

HEADS = 8
HD = 64


def normed(values, gain, shift):
    center = values - jnp.mean(values, axis=-1, keepdims=True)
    spread = jnp.mean(center * center, axis=-1, keepdims=True)
    return center * lax.rsqrt(spread + 1e-12) * gain + shift


def head_sums(weights, seq):
    rows, columns = weights.shape
    lane = lax.broadcasted_iota(jnp.int32, (rows, 2 * seq), 1)
    sums = []
    for start in range(0, columns, 2 * seq):
        pair = weights[:, start : start + 2 * seq]
        first = jnp.sum(jnp.where(lane < seq, pair, 0.0), axis=1, keepdims=True)
        second = jnp.sum(jnp.where(lane < seq, 0.0, pair), axis=1, keepdims=True)
        sums.append(jnp.where(lane < seq, first, second))
    return jnp.concatenate(sums, axis=1)


def encode_kernel(*refs):
    count = (len(refs) - 3) // 2
    far, (out, spread), near, arrived = refs[:count], refs[count : count + 2], refs[-count - 1 : -1], refs[-1]
    w_qkv_far, inner = far[-2], HEADS * HD
    copies = [
        pltpu.make_async_copy(source, target, arrived.at[at])
        for at, (source, target) in enumerate(zip(far, near))
        if source is not w_qkv_far
    ]
    lengths, slots, fetched, pos, emb_gain, emb_bias, out_bias, norm_gain, norm_bias, w_qkv, w_out = near
    out_copy = copies.pop()
    thirds = []
    for third in range(3):
        columns = pl.ds(third * inner, inner)
        thirds.append(
            pltpu.make_async_copy(
                w_qkv_far.at[:, columns], w_qkv.at[:, columns], arrived.at[count + third]
            )
        )
    for copy in copies + thirds + [out_copy]:
        copy.start()
    for copy in copies:
        copy.wait()
    passes = out.shape[0]
    size = [lengths[:, p : p + 1] for p in range(passes)]
    tokens, slot_count = slots.shape[0], fetched.shape[0]
    seq = tokens // passes
    spot = lax.broadcasted_iota(jnp.int32, (tokens, slot_count), 1)
    picker = jnp.where(slots[...] == spot, 1.0, 0.0).astype(jnp.bfloat16)
    tok = jnp.dot(picker, fetched[...], preferred_element_type=jnp.float32)
    where_at = pos[...].astype(jnp.float32)
    summed = tok + jnp.concatenate([where_at] * passes, axis=0)
    embedded = normed(summed, emb_gain[...], emb_bias[...]).astype(jnp.bfloat16)
    parts = []
    for third in range(3):
        thirds[third].wait()
        weights = w_qkv[:, third * inner : (third + 1) * inner]
        part = jnp.dot(embedded, weights, preferred_element_type=jnp.float32)
        parts.append(part.astype(jnp.bfloat16))

    block_row = lax.broadcasted_iota(jnp.int32, (HEADS * seq, inner), 0) // seq
    block_col = lax.broadcasted_iota(jnp.int32, (HEADS * seq, inner), 1) // HD
    same = block_row == block_col
    lane = lax.broadcasted_iota(jnp.int32, (seq, HEADS * seq), 1) % seq
    contexts = []
    for p in range(passes):
        query, keys, vals = (part[p * seq : (p + 1) * seq] for part in parts)
        zero = jnp.zeros((), jnp.bfloat16)
        keys = jnp.where(same, jnp.concatenate([keys] * HEADS, axis=0), zero)
        vals = jnp.where(same, jnp.concatenate([vals] * HEADS, axis=0), zero)
        scores = lax.dot_general(
            query, keys, (((1,), (1,)), ((), ())), preferred_element_type=jnp.float32
        ) * HD ** (-0.5)
        weights = jnp.where(lane < size[p], jnp.exp(scores), 0.0)
        probs = (weights / head_sums(weights, seq)).astype(jnp.bfloat16)
        contexts.append(jnp.dot(probs, vals, preferred_element_type=jnp.float32))
    context = jnp.concatenate(contexts, axis=0).astype(jnp.bfloat16)
    out_copy.wait()
    attended = jnp.dot(context, w_out[...], preferred_element_type=jnp.float32) + out_bias[...]
    hidden = normed(embedded.astype(jnp.float32) + attended, norm_gain[...], norm_bias[...])
    row = lax.broadcasted_iota(jnp.int32, (seq, 1), 0)
    for p in range(passes):
        kept = jnp.where(row < size[p], hidden[p * seq : (p + 1) * seq], 0.0)
        pooled = jnp.sum(kept, axis=0, keepdims=True) / size[p].astype(jnp.float32)
        scale = lax.rsqrt(jnp.mean(pooled * pooled, axis=-1, keepdims=True) + 1e-06)
        out[p : p + 1, :] = (pooled * scale).astype(jnp.bfloat16)
    spread[...] = jnp.broadcast_to(out[...][None], spread.shape)


def encode(
    peers, slots, fetched, lengths, pos_table, emb_gain, emb_bias, w_qkv, w_out, out_bias, norm_gain, norm_bias
):
    width = fetched.shape[1]
    tokens = slots.shape[0]
    passes = lengths.shape[0]
    macs = tokens * width * (fetched.shape[0] + 4 * HEADS * HD)
    operands = (
        lengths[None],
        slots,
        fetched,
        pos_table,
        emb_gain[None],
        emb_bias[None],
        out_bias[None],
        norm_gain[None],
        norm_bias[None],
        w_qkv,
        w_out,
    )
    return pl.pallas_call(
        encode_kernel,
        out_shape=[
            jax.ShapeDtypeStruct((passes, width), jnp.bfloat16),
            jax.ShapeDtypeStruct((peers, passes, width), jnp.bfloat16),
        ],
        in_specs=[pl.BlockSpec(memory_space=pltpu.HBM)] * len(operands),
        out_specs=[pl.BlockSpec(memory_space=pltpu.VMEM)] * 2,
        scratch_shapes=[pltpu.VMEM(operand.shape, operand.dtype) for operand in operands]
        + [pltpu.SemaphoreType.DMA((len(operands) + 3,))],
        compiler_params=pltpu.CompilerParams(vmem_limit_bytes=60 * 1024 * 1024),
        cost_estimate=pl.CostEstimate(
            flops=2 * macs, bytes_accessed=6 * 1024 * 1024, transcendentals=0
        ),
        name="encode",
    )(*operands)


def padded(rows):
    return -(-rows // 16) * 16


def rank_bits(count):
    return max(1, (count - 1).bit_length())


def route_kernel(
    sizes,
    token_ids_far,
    owners_far,
    row_slot_far,
    plan,
    token_slot_far,
    code,
    *near,
):
    peers, vocab_rows, token_cap, row_cap, pooled = sizes
    token_ids, owners, row_slot, token_slot, arrived = near
    copies = [
        pltpu.make_async_copy(source, target, arrived.at[at])
        for at, (source, target) in enumerate(
            ((token_ids_far, token_ids), (owners_far, owners), (row_slot_far, row_slot))
        )
    ]
    for copy in copies:
        copy.start()
    for copy in copies:
        copy.wait()
    ids = jnp.concatenate([token_ids[p : p + 1, :] for p in range(token_ids.shape[0])], axis=1)
    tokens, rows = ids.shape[1], owners.shape[1]
    count = tokens + rows
    edge = (lax.broadcasted_iota(jnp.int32, (peers, tokens), 0) + 1) * vocab_rows
    holder = jnp.sum(jnp.where(ids >= edge, 1, 0), axis=0, keepdims=True)
    values = jnp.concatenate([ids - holder * vocab_rows, row_slot[...]], axis=1)

    kind = jnp.concatenate([holder, owners[...] + peers], axis=1)
    at = lax.broadcasted_iota(jnp.int32, (count, count), 0)
    by = lax.broadcasted_iota(jnp.int32, (count, count), 1)
    across = jnp.broadcast_to(kind, (count, count))
    down = jnp.sum(jnp.where(at == by, across, 0), axis=1, keepdims=True)
    same = down == across
    rank_row = jnp.sum(jnp.where(same & (at < by), 1, 0), axis=0, keepdims=True)
    rank_col = jnp.sum(jnp.where(same & (by < at), 1, 0), axis=1, keepdims=True)

    code[...] = owners[...] * 2 ** rank_bits(rows) + rank_row[:, tokens:]
    goal = jnp.concatenate([holder, owners[...]], axis=1)
    peer = lax.broadcasted_iota(jnp.int32, (peers, count), 0)
    left = jnp.where(peer == goal, values + 1, 0).astype(jnp.float32)
    columns = token_cap + row_cap + pooled
    column = lax.broadcasted_iota(jnp.int32, (count, columns), 1)
    entry = lax.broadcasted_iota(jnp.int32, (count, 1), 0)
    first = jnp.where(entry < tokens, rank_col, rank_col + token_cap)
    second = entry - (count - pooled) + token_cap + row_cap
    second = jnp.where(entry < count - pooled, -1, second)
    right = jnp.where((column == first) | (column == second), 1.0, 0.0)
    filled = jnp.dot(
        left, right, preferred_element_type=jnp.float32, precision=lax.Precision.HIGHEST
    )
    filled = filled.astype(jnp.int32) - 1
    for p in range(peers):
        plan[p] = filled[p : p + 1]
    token_slot[...] = down[:tokens] * token_cap + rank_col[:tokens]
    send = pltpu.make_async_copy(token_slot, token_slot_far, arrived.at[3])
    send.start()
    send.wait()


def route(token_ids, owners, row_slot, sizes):
    peers, _, token_cap, row_cap, pooled = sizes
    passes, seq_len = token_ids.shape
    rows = owners.shape[1]
    ints = lambda *shape: jax.ShapeDtypeStruct(shape, jnp.int32)
    return pl.pallas_call(
        functools.partial(route_kernel, sizes),
        out_shape=[
            ints(peers, 1, token_cap + row_cap + pooled),
            ints(passes * seq_len, 1),
            ints(1, rows),
        ],
        in_specs=[pl.BlockSpec(memory_space=pltpu.HBM)] * 3,
        out_specs=[
            pl.BlockSpec(memory_space=pltpu.VMEM),
            pl.BlockSpec(memory_space=pltpu.HBM),
            pl.BlockSpec(memory_space=pltpu.VMEM),
        ],
        scratch_shapes=[
            pltpu.VMEM(token_ids.shape, jnp.int32),
            pltpu.VMEM(owners.shape, jnp.int32),
            pltpu.VMEM(row_slot.shape, jnp.int32),
            pltpu.VMEM((passes * seq_len, 1), jnp.int32),
            pltpu.SemaphoreType.DMA((4,)),
        ],
        compiler_params=pltpu.CompilerParams(vmem_limit_bytes=60 * 1024 * 1024),
        name="route",
    )(token_ids, owners, row_slot)


def pack_kernel(row_cap, *refs):
    me = lax.axis_index("dp")
    far, outs, near, (blocks, arrived, left) = refs[:4], refs[4:-7], refs[-7:-3], refs[-3:]
    chips = len(outs)
    size = blocks.shape[0] // chips
    copies = [pltpu.make_async_copy(far[at], near[at], arrived.at[at]) for at in range(4)]
    for copy in copies:
        copy.start()
    for copy in copies[:2]:
        copy.wait()
    if size > 2 * row_cap:
        blocks[...] = jnp.zeros(blocks.shape, blocks.dtype)
    for source in range(2):
        code, rows = near[source][...], near[2 + source]
        bits = rank_bits(code.shape[1])
        owner, rank = code >> bits, code & (2**bits - 1)
        fits = ((owner ^ me) & 1) == 0
        slot = jnp.where(fits, ((owner ^ me) >> 1) * row_cap + rank, -1)[:, : rows.shape[0]]
        spot = lax.broadcasted_iota(jnp.int32, (chips * row_cap, rows.shape[0]), 0)
        table = jnp.where(slot == spot, 1.0, 0.0).astype(jnp.bfloat16)
        copies[2 + source].wait()
        packed = jnp.dot(table, rows[...], preferred_element_type=jnp.float32)
        packed = packed.astype(jnp.bfloat16)
        for chip in range(chips):
            first = chip * size + source * row_cap
            blocks[first : first + row_cap, :] = packed[chip * row_cap : (chip + 1) * row_cap]
    sends = [
        pltpu.make_async_copy(blocks.at[pl.ds(chip * size, size)], outs[chip], left.at[chip])
        for chip in range(chips)
    ]
    for send in sends:
        send.start()
    for send in sends:
        send.wait()


def pack_rows(codes_a, codes_b, rows_a, rows_b, chips, row_cap):
    total, width = rows_a.shape
    size = padded(2 * row_cap)
    operands = (codes_a, codes_b, rows_a, rows_b)
    return pl.pallas_call(
        functools.partial(pack_kernel, row_cap),
        out_shape=[jax.ShapeDtypeStruct((size, width), jnp.bfloat16)] * chips,
        in_specs=[pl.BlockSpec(memory_space=pltpu.HBM)] * 4,
        out_specs=[pl.BlockSpec(memory_space=pltpu.HBM)] * chips,
        scratch_shapes=[
            *(pltpu.VMEM(operand.shape, operand.dtype) for operand in operands),
            pltpu.VMEM((chips * size, width), jnp.bfloat16),
            pltpu.SemaphoreType.DMA((4,)),
            pltpu.SemaphoreType.DMA((chips,)),
        ],
        compiler_params=pltpu.CompilerParams(vmem_limit_bytes=60 * 1024 * 1024),
        cost_estimate=pl.CostEstimate(
            flops=4 * chips * row_cap * width * total,
            bytes_accessed=4 * width * (total + chips * row_cap),
            transcendentals=0,
        ),
        name="pack",
    )(*operands)


def onehot(where_to, first, count):
    centre = lax.broadcasted_iota(jnp.int32, (count, where_to.shape[1]), 0) + first
    return jnp.where(centre == where_to, 1.0, 0.0)


BLOCK = 128


def early_kernel(places_far, centroids_far, *rest):
    pieces, (out_far, share_far, places, rows, centroids, out, share, arrived, left) = rest[:-9], rest[-9:]
    size = pieces[0].shape[0]
    steps = centroids.shape[0] // BLOCK
    copies = [pltpu.make_async_copy(places_far, places, arrived.at[0])]
    for at, piece in enumerate(pieces):
        copies.append(
            pltpu.make_async_copy(piece, rows.at[pl.ds(at * size, size)], arrived.at[1 + at])
        )
    loads = []
    for step in range(steps):
        block = pl.ds(step * BLOCK, BLOCK)
        loads.append(
            pltpu.make_async_copy(
                centroids_far.at[block], centroids.at[block], arrived.at[1 + len(pieces) + step]
            )
        )
    for copy in copies + loads:
        copy.start()
    for copy in copies:
        copy.wait()
    sends = []
    for step in range(steps):
        block = pl.ds(step * BLOCK, BLOCK)
        hot = onehot(places[...], step * BLOCK, BLOCK)
        counts = jnp.sum(hot, axis=1, keepdims=True)
        scale = jnp.where(counts > 0, 1.0 / jnp.maximum(counts, 1.0), 0.0)
        sums = jnp.dot(
            hot[:, : rows.shape[0]].astype(jnp.bfloat16),
            rows[...],
            preferred_element_type=jnp.float32,
        )
        loads[step].wait()
        out[block, :] = jnp.where(counts > 0, sums * scale, centroids[block, :])
        share[block, :] = jnp.broadcast_to(scale, (BLOCK, share.shape[1]))
        sends.append(pltpu.make_async_copy(out.at[block], out_far.at[block], left.at[step]))
        sends[-1].start()
    sends.append(pltpu.make_async_copy(share, share_far, left.at[steps]))
    sends[-1].start()
    for send in sends:
        send.wait()


def late_kernel(places_far, late_far, spread_far, share_far, early_far, *rest):
    pieces, rest = rest[:-10], rest[-10:]
    out_far, places, late, spread, share, rows, early, out, arrived, left = rest
    size, passes = pieces[0].shape[0], spread.shape[1]
    steps = early.shape[0] // BLOCK
    loads = [
        pltpu.make_async_copy(source, target, arrived.at[at])
        for at, (source, target) in enumerate(
            ((places_far, places), (late_far, late), (spread_far, spread), (share_far, share))
        )
    ]
    for at, piece in enumerate(pieces):
        loads.append(
            pltpu.make_async_copy(piece, rows.at[pl.ds(at * size, size)], arrived.at[4 + at])
        )
    starts = []
    for step in range(steps):
        block = pl.ds(step * BLOCK, BLOCK)
        starts.append(
            pltpu.make_async_copy(
                early_far.at[block], early.at[block], arrived.at[len(loads) + step]
            )
        )
    for copy in loads + starts:
        copy.start()
    for copy in loads:
        copy.wait()
    top = len(pieces) * size
    for peer in range(spread.shape[0]):
        rows[top + peer * passes : top + (peer + 1) * passes, :] = spread[peer]
    where_to = jnp.concatenate([places[:, places.shape[1] - top :], late[...]], axis=1)
    sends = []
    for step in range(steps):
        block = pl.ds(step * BLOCK, BLOCK)
        hot = onehot(where_to, step * BLOCK, BLOCK).astype(jnp.bfloat16)
        sums = jnp.dot(hot, rows[...], preferred_element_type=jnp.float32)
        starts[step].wait()
        out[block, :] = early[block, :] + sums * share[block, :1]
        sends.append(pltpu.make_async_copy(out.at[block], out_far.at[block], left.at[step]))
        sends[-1].start()
    for send in sends:
        send.wait()


def early_update(places, centroids, pieces):
    centre_count, width = centroids.shape
    row_total = sum(piece.shape[0] for piece in pieces)
    wide = pltpu.VMEM(centroids.shape, jnp.float32)
    thin = (centre_count, 128)
    steps = centre_count // BLOCK
    return pl.pallas_call(
        early_kernel,
        out_shape=[
            jax.ShapeDtypeStruct(centroids.shape, jnp.float32),
            jax.ShapeDtypeStruct(thin, jnp.float32),
        ],
        in_specs=[pl.BlockSpec(memory_space=pl.ANY)] * (2 + len(pieces)),
        out_specs=[pl.BlockSpec(memory_space=pltpu.HBM)] * 2,
        scratch_shapes=[
            pltpu.VMEM(places.shape, jnp.int32),
            pltpu.VMEM((row_total, width), jnp.bfloat16),
            wide,
            wide,
            pltpu.VMEM(thin, jnp.float32),
            pltpu.SemaphoreType.DMA((1 + len(pieces) + steps,)),
            pltpu.SemaphoreType.DMA((steps + 1,)),
        ],
        compiler_params=pltpu.CompilerParams(vmem_limit_bytes=60 * 1024 * 1024),
        cost_estimate=pl.CostEstimate(
            flops=2 * centre_count * width * row_total,
            bytes_accessed=8 * centre_count * width,
            transcendentals=0,
        ),
        name="early",
    )(places, centroids, *pieces)


def late_update(places, late, spread, share, early, pieces):
    centre_count, width = early.shape
    row_total = sum(piece.shape[0] for piece in pieces) + late.shape[1]
    wide = pltpu.VMEM(early.shape, jnp.float32)
    steps = centre_count // BLOCK
    return pl.pallas_call(
        late_kernel,
        out_shape=jax.ShapeDtypeStruct(early.shape, jnp.float32),
        in_specs=[pl.BlockSpec(memory_space=pltpu.HBM)] * (5 + len(pieces)),
        out_specs=pl.BlockSpec(memory_space=pltpu.HBM),
        scratch_shapes=[
            pltpu.VMEM(places.shape, jnp.int32),
            pltpu.VMEM(late.shape, jnp.int32),
            pltpu.VMEM(spread.shape, jnp.bfloat16),
            pltpu.VMEM(share.shape, jnp.float32),
            pltpu.VMEM((row_total, width), jnp.bfloat16),
            wide,
            wide,
            pltpu.SemaphoreType.DMA((4 + len(pieces) + steps,)),
            pltpu.SemaphoreType.DMA((steps,)),
        ],
        compiler_params=pltpu.CompilerParams(vmem_limit_bytes=60 * 1024 * 1024),
        cost_estimate=pl.CostEstimate(
            flops=2 * centre_count * width * row_total,
            bytes_accessed=8 * centre_count * width,
            transcendentals=0,
        ),
        name="late",
    )(places, late, spread, share, early, *pieces)


def shards(
    token_ids,
    lengths,
    word_table,
    pos_table,
    emb_gain,
    emb_bias,
    w_qkv,
    w_out,
    out_bias,
    norm_gain,
    norm_bias,
    stored_rows,
    row_owner,
    row_slot,
    centroids,
):
    peer_count = lax.axis_size("dp")
    width = word_table.shape[1]
    vocab_rows = word_table.shape[0]
    passes, seq_len = token_ids.shape
    token_count = passes * seq_len
    row_count = row_slot.shape[0]
    store_count = stored_rows.shape[0]
    token_cap = max(2, 3 * token_count // peer_count)
    row_cap = max(2, 3 * row_count // peer_count)

    beside = [(i, i ^ 1) for i in range(peer_count)]
    sibling_rows = lax.ppermute(stored_rows, "dp", beside)
    sizes = (peer_count, vocab_rows, token_cap, row_cap, row_count - store_count)
    plan, token_slot, code = route(token_ids, row_owner.reshape(1, row_count), row_slot[None], sizes)
    sibling_code = lax.ppermute(code, "dp", beside)
    plan, sibling_rows = lax.optimization_barrier((plan, sibling_rows))
    plan = lax.all_to_all(plan, "dp", split_axis=0, concat_axis=0, tiled=True)[:, 0]
    chips = peer_count // 2
    got_rows = [*pack_rows(code, sibling_code, stored_rows, sibling_rows, chips, row_cap)]
    for chip in range(1, chips):
        moves = [(i, i ^ (2 * chip)) for i in range(peer_count)]
        got_rows[chip] = lax.ppermute(got_rows[chip], "dp", moves)
    ahead = [0, 1, chips // 2]
    behind = [chip for chip in range(chips) if chip not in ahead]
    wanted = plan[:, :token_cap].reshape(peer_count * token_cap)
    chosen = wanted[:, None] == jnp.arange(vocab_rows, dtype=jnp.int32)[None, :]
    found = jnp.dot(
        chosen.astype(jnp.bfloat16), word_table, preferred_element_type=jnp.float32
    ).astype(jnp.bfloat16)
    first_rows = [got_rows[chip] for chip in ahead]
    found, first_rows = lax.optimization_barrier((found, first_rows))
    fetched = lax.all_to_all(
        found.reshape(peer_count, token_cap, width), "dp", split_axis=0, concat_axis=0, tiled=True
    ).reshape(peer_count * token_cap, width)

    sources = lax.axis_index("dp") ^ jnp.arange(peer_count, dtype=jnp.int32)
    got_places = plan[:, token_cap : token_cap + row_cap][sources].reshape(chips, 2 * row_cap)
    spare = padded(2 * row_cap) - 2 * row_cap
    got_places = jnp.pad(got_places, ((0, 0), (0, spare)), constant_values=-1)
    got_places = jnp.concatenate([got_places[chip] for chip in ahead + behind])[None]
    means, share = early_update(got_places, centroids, first_rows)
    late_places = plan[:, token_cap + row_cap :].reshape(1, -1)
    fetched, means, share, got_places, late_places = lax.optimization_barrier(
        (fetched, means, share, got_places, late_places)
    )

    passage_embed, spread = encode(
        peer_count,
        token_slot,
        fetched,
        lengths,
        pos_table,
        emb_gain,
        emb_bias,
        w_qkv,
        w_out,
        out_bias,
        norm_gain,
        norm_bias,
    )
    all_embeds = lax.all_to_all(
        spread, "dp", split_axis=0, concat_axis=0, tiled=True
    )
    last_rows = [got_rows[chip] for chip in behind]
    new_centroids = late_update(got_places, late_places, all_embeds, share, means, last_rows)
    return (passage_embed, new_centroids)


def solution(mesh):
    return jax.shard_map(
        shards,
        mesh=mesh,
        in_specs=(
            P(("groups", "dp"), None),
            P(("groups", "dp")),
            P("dp", None),
            P(),
            P(),
            P(),
            P(),
            P(),
            P(),
            P(),
            P(),
            P(("groups", "dp"), None),
            P(("groups", "dp"), None),
            P(("groups", "dp")),
            P(("groups", "dp"), None),
        ),
        out_specs=(P(("groups", "dp"), None), P(("groups", "dp"), None)),
        check_vma=False,
    )
```

```python
import functools

import jax
import jax.numpy as jnp
from jax import lax
from jax.experimental import pallas as pl
from jax.experimental.pallas import tpu as pltpu
from jax.sharding import PartitionSpec as P

HEADS = 8
HD = 64


def normed(values, gain, shift):
    center = values - jnp.mean(values, axis=-1, keepdims=True)
    spread = jnp.mean(center * center, axis=-1, keepdims=True)
    return center * lax.rsqrt(spread + 1e-12) * gain + shift


def head_sums(weights, seq):
    rows, columns = weights.shape
    lane = lax.broadcasted_iota(jnp.int32, (rows, 2 * seq), 1)
    sums = []
    for start in range(0, columns, 2 * seq):
        pair = weights[:, start : start + 2 * seq]
        first = jnp.sum(jnp.where(lane < seq, pair, 0.0), axis=1, keepdims=True)
        second = jnp.sum(jnp.where(lane < seq, 0.0, pair), axis=1, keepdims=True)
        sums.append(jnp.where(lane < seq, first, second))
    return jnp.concatenate(sums, axis=1)


def encode_kernel(*refs):
    count = (len(refs) - 3) // 2
    far, (out, spread), near, arrived = refs[:count], refs[count : count + 2], refs[-count - 1 : -1], refs[-1]
    w_qkv_far, inner = far[-2], HEADS * HD
    copies = [
        pltpu.make_async_copy(source, target, arrived.at[at])
        for at, (source, target) in enumerate(zip(far, near))
        if source is not w_qkv_far
    ]
    lengths, slots, fetched, pos, emb_gain, emb_bias, out_bias, norm_gain, norm_bias, w_qkv, w_out = near
    out_copy = copies.pop()
    thirds = []
    for third in range(3):
        columns = pl.ds(third * inner, inner)
        thirds.append(
            pltpu.make_async_copy(
                w_qkv_far.at[:, columns], w_qkv.at[:, columns], arrived.at[count + third]
            )
        )
    for copy in copies + thirds + [out_copy]:
        copy.start()
    for copy in copies:
        copy.wait()
    passes = out.shape[0]
    size = [lengths[:, p : p + 1] for p in range(passes)]
    tokens, slot_count = slots.shape[0], fetched.shape[0]
    seq = tokens // passes
    spot = lax.broadcasted_iota(jnp.int32, (tokens, slot_count), 1)
    picker = jnp.where(slots[...] == spot, 1.0, 0.0).astype(jnp.bfloat16)
    tok = jnp.dot(picker, fetched[...], preferred_element_type=jnp.float32)
    where_at = pos[...].astype(jnp.float32)
    summed = tok + jnp.concatenate([where_at] * passes, axis=0)
    embedded = normed(summed, emb_gain[...], emb_bias[...]).astype(jnp.bfloat16)
    parts = []
    for third in range(3):
        thirds[third].wait()
        weights = w_qkv[:, third * inner : (third + 1) * inner]
        part = jnp.dot(embedded, weights, preferred_element_type=jnp.float32)
        parts.append(part.astype(jnp.bfloat16))

    block_row = lax.broadcasted_iota(jnp.int32, (HEADS * seq, inner), 0) // seq
    block_col = lax.broadcasted_iota(jnp.int32, (HEADS * seq, inner), 1) // HD
    same = block_row == block_col
    lane = lax.broadcasted_iota(jnp.int32, (seq, HEADS * seq), 1) % seq
    contexts = []
    for p in range(passes):
        query, keys, vals = (part[p * seq : (p + 1) * seq] for part in parts)
        zero = jnp.zeros((), jnp.bfloat16)
        keys = jnp.where(same, jnp.concatenate([keys] * HEADS, axis=0), zero)
        vals = jnp.where(same, jnp.concatenate([vals] * HEADS, axis=0), zero)
        scores = lax.dot_general(
            query, keys, (((1,), (1,)), ((), ())), preferred_element_type=jnp.float32
        ) * HD ** (-0.5)
        weights = jnp.where(lane < size[p], jnp.exp(scores), 0.0)
        probs = (weights / head_sums(weights, seq)).astype(jnp.bfloat16)
        contexts.append(jnp.dot(probs, vals, preferred_element_type=jnp.float32))
    context = jnp.concatenate(contexts, axis=0).astype(jnp.bfloat16)
    out_copy.wait()
    attended = jnp.dot(context, w_out[...], preferred_element_type=jnp.float32) + out_bias[...]
    hidden = normed(embedded.astype(jnp.float32) + attended, norm_gain[...], norm_bias[...])
    row = lax.broadcasted_iota(jnp.int32, (seq, 1), 0)
    for p in range(passes):
        kept = jnp.where(row < size[p], hidden[p * seq : (p + 1) * seq], 0.0)
        pooled = jnp.sum(kept, axis=0, keepdims=True) / size[p].astype(jnp.float32)
        scale = lax.rsqrt(jnp.mean(pooled * pooled, axis=-1, keepdims=True) + 1e-06)
        out[p : p + 1, :] = (pooled * scale).astype(jnp.bfloat16)
    spread[...] = jnp.broadcast_to(out[...][None], spread.shape)


def encode(
    peers, slots, fetched, lengths, pos_table, emb_gain, emb_bias, w_qkv, w_out, out_bias, norm_gain, norm_bias
):
    width = fetched.shape[1]
    tokens = slots.shape[0]
    passes = lengths.shape[0]
    macs = tokens * width * (fetched.shape[0] + 4 * HEADS * HD)
    operands = (
        lengths[None],
        slots,
        fetched,
        pos_table,
        emb_gain[None],
        emb_bias[None],
        out_bias[None],
        norm_gain[None],
        norm_bias[None],
        w_qkv,
        w_out,
    )
    return pl.pallas_call(
        encode_kernel,
        out_shape=[
            jax.ShapeDtypeStruct((passes, width), jnp.bfloat16),
            jax.ShapeDtypeStruct((peers, passes, width), jnp.bfloat16),
        ],
        in_specs=[pl.BlockSpec(memory_space=pltpu.HBM)] * len(operands),
        out_specs=[pl.BlockSpec(memory_space=pltpu.VMEM)] * 2,
        scratch_shapes=[pltpu.VMEM(operand.shape, operand.dtype) for operand in operands]
        + [pltpu.SemaphoreType.DMA((len(operands) + 3,))],
        compiler_params=pltpu.CompilerParams(vmem_limit_bytes=60 * 1024 * 1024),
        cost_estimate=pl.CostEstimate(
            flops=2 * macs, bytes_accessed=6 * 1024 * 1024, transcendentals=0
        ),
        name="encode",
    )(*operands)


def padded(rows):
    return -(-rows // 16) * 16


def rank_bits(count):
    return max(1, (count - 1).bit_length())


def route_kernel(
    sizes,
    token_ids_far,
    owners_far,
    row_slot_far,
    plan,
    token_slot_far,
    code,
    *near,
):
    peers, vocab_rows, token_cap, row_cap, pooled = sizes
    token_ids, owners, row_slot, token_slot, arrived = near
    copies = [
        pltpu.make_async_copy(source, target, arrived.at[at])
        for at, (source, target) in enumerate(
            ((token_ids_far, token_ids), (owners_far, owners), (row_slot_far, row_slot))
        )
    ]
    for copy in copies:
        copy.start()
    for copy in copies:
        copy.wait()
    ids = jnp.concatenate([token_ids[p : p + 1, :] for p in range(token_ids.shape[0])], axis=1)
    tokens, rows = ids.shape[1], owners.shape[1]
    count = tokens + rows
    edge = (lax.broadcasted_iota(jnp.int32, (peers, tokens), 0) + 1) * vocab_rows
    holder = jnp.sum(jnp.where(ids >= edge, 1, 0), axis=0, keepdims=True)
    values = jnp.concatenate([ids - holder * vocab_rows, row_slot[...]], axis=1)

    kind = jnp.concatenate([holder, owners[...] + peers], axis=1)
    at = lax.broadcasted_iota(jnp.int32, (count, count), 0)
    by = lax.broadcasted_iota(jnp.int32, (count, count), 1)
    across = jnp.broadcast_to(kind, (count, count))
    down = jnp.sum(jnp.where(at == by, across, 0), axis=1, keepdims=True)
    same = down == across
    rank_row = jnp.sum(jnp.where(same & (at < by), 1, 0), axis=0, keepdims=True)
    rank_col = jnp.sum(jnp.where(same & (by < at), 1, 0), axis=1, keepdims=True)

    code[...] = owners[...] * 2 ** rank_bits(rows) + rank_row[:, tokens:]
    goal = jnp.concatenate([holder, owners[...]], axis=1)
    peer = lax.broadcasted_iota(jnp.int32, (peers, count), 0)
    left = jnp.where(peer == goal, values + 1, 0).astype(jnp.float32)
    columns = token_cap + row_cap + pooled
    column = lax.broadcasted_iota(jnp.int32, (count, columns), 1)
    entry = lax.broadcasted_iota(jnp.int32, (count, 1), 0)
    first = jnp.where(entry < tokens, rank_col, rank_col + token_cap)
    second = entry - (count - pooled) + token_cap + row_cap
    second = jnp.where(entry < count - pooled, -1, second)
    right = jnp.where((column == first) | (column == second), 1.0, 0.0)
    filled = jnp.dot(
        left, right, preferred_element_type=jnp.float32, precision=lax.Precision.HIGHEST
    )
    filled = filled.astype(jnp.int32) - 1
    for p in range(peers):
        plan[p, :, :rows] = code[...]
        plan[p, :, rows:] = filled[p : p + 1]
    token_slot[...] = down[:tokens] * token_cap + rank_col[:tokens]
    send = pltpu.make_async_copy(token_slot, token_slot_far, arrived.at[3])
    send.start()
    send.wait()


def route(token_ids, owners, row_slot, sizes):
    peers, _, token_cap, row_cap, pooled = sizes
    passes, seq_len = token_ids.shape
    rows = owners.shape[1]
    ints = lambda *shape: jax.ShapeDtypeStruct(shape, jnp.int32)
    return pl.pallas_call(
        functools.partial(route_kernel, sizes),
        out_shape=[
            ints(peers, 1, rows + token_cap + row_cap + pooled),
            ints(passes * seq_len, 1),
            ints(1, rows),
        ],
        in_specs=[pl.BlockSpec(memory_space=pltpu.HBM)] * 3,
        out_specs=[
            pl.BlockSpec(memory_space=pltpu.VMEM),
            pl.BlockSpec(memory_space=pltpu.HBM),
            pl.BlockSpec(memory_space=pltpu.VMEM),
        ],
        scratch_shapes=[
            pltpu.VMEM(token_ids.shape, jnp.int32),
            pltpu.VMEM(owners.shape, jnp.int32),
            pltpu.VMEM(row_slot.shape, jnp.int32),
            pltpu.VMEM((passes * seq_len, 1), jnp.int32),
            pltpu.SemaphoreType.DMA((4,)),
        ],
        compiler_params=pltpu.CompilerParams(vmem_limit_bytes=60 * 1024 * 1024),
        name="route",
    )(token_ids, owners, row_slot)


def pack_kernel(half, row_cap, count, picks, pieces, rest, *refs):
    me = lax.axis_index("dp")
    operands = 2 + 2 * pieces
    far, refs = refs[:operands], refs[operands:]
    steps = half // 2
    outs, refs = refs[: steps + bool(rest)], refs[steps + bool(rest) :]
    near, (blocks, tail, arrived, left) = refs[:operands], refs[operands:]
    size = blocks.shape[0] // steps
    copies = [
        pltpu.make_async_copy(far[at], near[at], arrived.at[at]) for at in range(operands)
    ]
    for copy in copies:
        copy.start()
    for copy in copies[:2]:
        copy.wait()
    if size > 2 * row_cap:
        blocks[...] = jnp.zeros(blocks.shape, blocks.dtype)
    for source in range(2):
        if picks is None:
            code = near[source][...]
        else:
            code = near[source][me ^ picks[source], :, :count]
        bits = rank_bits(count)
        owner, rank = code >> bits, code & (2**bits - 1)
        fits = ((owner ^ me) & (1 | half)) == 0
        chip = ((owner ^ me) & (half - 1)) >> 1
        slot = jnp.where(fits, chip * row_cap + rank, -1)
        packed, at = 0.0, 0
        for piece in range(2 + source * pieces, 2 + (source + 1) * pieces):
            rows = near[piece]
            spot = lax.broadcasted_iota(jnp.int32, (steps * row_cap, rows.shape[0]), 0)
            table = jnp.where(slot[:, at : at + rows.shape[0]] == spot, 1.0, 0.0)
            copies[piece].wait()
            packed += jnp.dot(
                table.astype(jnp.bfloat16), rows[...], preferred_element_type=jnp.float32
            )
            at += rows.shape[0]
        packed = packed.astype(jnp.bfloat16)
        for step in range(steps):
            first = step * size + source * row_cap
            blocks[first : first + row_cap, :] = packed[step * row_cap : (step + 1) * row_cap]
    sends = [
        pltpu.make_async_copy(
            blocks.at[pl.ds(step * size, size)], outs[step], left.at[step]
        )
        for step in range(steps)
    ]
    if rest:
        tail[...] = near[2][near[2].shape[0] - rest :, :]
        sends.append(pltpu.make_async_copy(tail, outs[steps], left.at[steps]))
    for send in sends:
        send.start()
    for send in sends:
        send.wait()


def pack_rows(codes_a, codes_b, rows_a, rows_b, half, row_cap, count, picks=None, rest=0):
    width = rows_a[0].shape[1]
    total = sum(piece.shape[0] for piece in rows_a)
    steps = half // 2
    size = padded(2 * row_cap)
    operands = (codes_a, codes_b, *rows_a, *rows_b)
    shapes = [(size, width)] * steps + [(rest, width)] * bool(rest)
    return pl.pallas_call(
        functools.partial(pack_kernel, half, row_cap, count, picks, len(rows_a), rest),
        out_shape=[jax.ShapeDtypeStruct(shape, jnp.bfloat16) for shape in shapes],
        in_specs=[pl.BlockSpec(memory_space=pltpu.HBM)] * len(operands),
        out_specs=[pl.BlockSpec(memory_space=pltpu.HBM)] * len(shapes),
        scratch_shapes=[
            *(pltpu.VMEM(operand.shape, operand.dtype) for operand in operands),
            pltpu.VMEM((steps * size, width), jnp.bfloat16),
            pltpu.VMEM((max(rest, 16), width), jnp.bfloat16),
            pltpu.SemaphoreType.DMA((len(operands),)),
            pltpu.SemaphoreType.DMA((len(shapes),)),
        ],
        compiler_params=pltpu.CompilerParams(vmem_limit_bytes=60 * 1024 * 1024),
        cost_estimate=pl.CostEstimate(
            flops=4 * steps * row_cap * width * total,
            bytes_accessed=4 * width * (total + steps * row_cap),
            transcendentals=0,
        ),
        name="pack",
    )(*operands)


def onehot(where_to, first, count):
    centre = lax.broadcasted_iota(jnp.int32, (count, where_to.shape[1]), 0) + first
    return jnp.where(centre == where_to, 1.0, 0.0)


BLOCK = 128


def early_kernel(places_far, centroids_far, *rest):
    pieces, (out_far, share_far, places, rows, centroids, out, share, arrived, left) = rest[:-9], rest[-9:]
    size = pieces[0].shape[0]
    steps = centroids.shape[0] // BLOCK
    copies = [pltpu.make_async_copy(places_far, places, arrived.at[0])]
    for at, piece in enumerate(pieces):
        copies.append(
            pltpu.make_async_copy(piece, rows.at[pl.ds(at * size, size)], arrived.at[1 + at])
        )
    loads = []
    for step in range(steps):
        block = pl.ds(step * BLOCK, BLOCK)
        loads.append(
            pltpu.make_async_copy(
                centroids_far.at[block], centroids.at[block], arrived.at[1 + len(pieces) + step]
            )
        )
    for copy in copies + loads:
        copy.start()
    for copy in copies:
        copy.wait()
    sends = []
    for step in range(steps):
        block = pl.ds(step * BLOCK, BLOCK)
        hot = onehot(places[...], step * BLOCK, BLOCK)
        counts = jnp.sum(hot, axis=1, keepdims=True)
        scale = jnp.where(counts > 0, 1.0 / jnp.maximum(counts, 1.0), 0.0)
        sums = jnp.dot(
            hot[:, : rows.shape[0]].astype(jnp.bfloat16),
            rows[...],
            preferred_element_type=jnp.float32,
        )
        loads[step].wait()
        out[block, :] = jnp.where(counts > 0, sums * scale, centroids[block, :])
        share[block, :] = jnp.broadcast_to(scale, (BLOCK, share.shape[1]))
        sends.append(pltpu.make_async_copy(out.at[block], out_far.at[block], left.at[step]))
        sends[-1].start()
    sends.append(pltpu.make_async_copy(share, share_far, left.at[steps]))
    sends[-1].start()
    for send in sends:
        send.wait()


def late_kernel(places_far, late_far, spread_far, share_far, early_far, *rest):
    pieces, rest = rest[:-10], rest[-10:]
    out_far, places, late, spread, share, rows, early, out, arrived, left = rest
    size, passes = pieces[0].shape[0], spread.shape[1]
    steps = early.shape[0] // BLOCK
    loads = [
        pltpu.make_async_copy(source, target, arrived.at[at])
        for at, (source, target) in enumerate(
            ((places_far, places), (late_far, late), (spread_far, spread), (share_far, share))
        )
    ]
    for at, piece in enumerate(pieces):
        loads.append(
            pltpu.make_async_copy(piece, rows.at[pl.ds(at * size, size)], arrived.at[4 + at])
        )
    starts = []
    for step in range(steps):
        block = pl.ds(step * BLOCK, BLOCK)
        starts.append(
            pltpu.make_async_copy(
                early_far.at[block], early.at[block], arrived.at[len(loads) + step]
            )
        )
    for copy in loads + starts:
        copy.start()
    for copy in loads:
        copy.wait()
    top = len(pieces) * size
    for peer in range(spread.shape[0]):
        rows[top + peer * passes : top + (peer + 1) * passes, :] = spread[peer]
    where_to = jnp.concatenate([places[:, places.shape[1] - top :], late[...]], axis=1)
    sends = []
    for step in range(steps):
        block = pl.ds(step * BLOCK, BLOCK)
        hot = onehot(where_to, step * BLOCK, BLOCK).astype(jnp.bfloat16)
        sums = jnp.dot(hot, rows[...], preferred_element_type=jnp.float32)
        starts[step].wait()
        out[block, :] = early[block, :] + sums * share[block, :1]
        sends.append(pltpu.make_async_copy(out.at[block], out_far.at[block], left.at[step]))
        sends[-1].start()
    for send in sends:
        send.wait()


def early_update(places, centroids, pieces):
    centre_count, width = centroids.shape
    row_total = sum(piece.shape[0] for piece in pieces)
    wide = pltpu.VMEM(centroids.shape, jnp.float32)
    thin = (centre_count, 128)
    steps = centre_count // BLOCK
    return pl.pallas_call(
        early_kernel,
        out_shape=[
            jax.ShapeDtypeStruct(centroids.shape, jnp.float32),
            jax.ShapeDtypeStruct(thin, jnp.float32),
        ],
        in_specs=[pl.BlockSpec(memory_space=pl.ANY)] * (2 + len(pieces)),
        out_specs=[pl.BlockSpec(memory_space=pltpu.HBM)] * 2,
        scratch_shapes=[
            pltpu.VMEM(places.shape, jnp.int32),
            pltpu.VMEM((row_total, width), jnp.bfloat16),
            wide,
            wide,
            pltpu.VMEM(thin, jnp.float32),
            pltpu.SemaphoreType.DMA((1 + len(pieces) + steps,)),
            pltpu.SemaphoreType.DMA((steps + 1,)),
        ],
        compiler_params=pltpu.CompilerParams(vmem_limit_bytes=60 * 1024 * 1024),
        cost_estimate=pl.CostEstimate(
            flops=2 * centre_count * width * row_total,
            bytes_accessed=8 * centre_count * width,
            transcendentals=0,
        ),
        name="early",
    )(places, centroids, *pieces)


def late_update(places, late, spread, share, early, pieces):
    centre_count, width = early.shape
    row_total = sum(piece.shape[0] for piece in pieces) + late.shape[1]
    wide = pltpu.VMEM(early.shape, jnp.float32)
    steps = centre_count // BLOCK
    return pl.pallas_call(
        late_kernel,
        out_shape=jax.ShapeDtypeStruct(early.shape, jnp.float32),
        in_specs=[pl.BlockSpec(memory_space=pltpu.HBM)] * (5 + len(pieces)),
        out_specs=pl.BlockSpec(memory_space=pltpu.HBM),
        scratch_shapes=[
            pltpu.VMEM(places.shape, jnp.int32),
            pltpu.VMEM(late.shape, jnp.int32),
            pltpu.VMEM(spread.shape, jnp.bfloat16),
            pltpu.VMEM(share.shape, jnp.float32),
            pltpu.VMEM((row_total, width), jnp.bfloat16),
            wide,
            wide,
            pltpu.SemaphoreType.DMA((4 + len(pieces) + steps,)),
            pltpu.SemaphoreType.DMA((steps,)),
        ],
        compiler_params=pltpu.CompilerParams(vmem_limit_bytes=60 * 1024 * 1024),
        cost_estimate=pl.CostEstimate(
            flops=2 * centre_count * width * row_total,
            bytes_accessed=8 * centre_count * width,
            transcendentals=0,
        ),
        name="late",
    )(places, late, spread, share, early, *pieces)


def shards(
    token_ids,
    lengths,
    word_table,
    pos_table,
    emb_gain,
    emb_bias,
    w_qkv,
    w_out,
    out_bias,
    norm_gain,
    norm_bias,
    stored_rows,
    row_owner,
    row_slot,
    centroids,
):
    peer_count = lax.axis_size("dp")
    half = peer_count // 2
    width = word_table.shape[1]
    vocab_rows = word_table.shape[0]
    passes, seq_len = token_ids.shape
    token_count = passes * seq_len
    row_count = row_slot.shape[0]
    store_count = stored_rows.shape[0]
    token_cap = max(2, 3 * token_count // peer_count)
    row_cap = max(2, 3 * row_count // peer_count)

    across = [(i, i ^ half) for i in range(peer_count)]
    beside = [(i, i ^ 1) for i in range(peer_count)]

    def hand_on(blocks):
        got = [blocks[0]]
        for step in range(1, len(blocks)):
            moves = [(i, i ^ (2 * step)) for i in range(peer_count)]
            got.append(lax.ppermute(blocks[step], "dp", moves))
        return got

    ahead = store_count * 3 // 4 // 16 * 16
    sibling_rows = lax.ppermute(stored_rows, "dp", beside)
    first_rows = lax.ppermute(stored_rows[:ahead], "dp", across)
    sizes = (peer_count, vocab_rows, token_cap, row_cap, row_count - store_count)
    plan, token_slot, code = route(token_ids, row_owner.reshape(1, row_count), row_slot[None], sizes)
    sibling_code = lax.ppermute(code, "dp", beside)
    plan, sibling_rows = lax.optimization_barrier((plan, sibling_rows))
    codes = lax.all_to_all(plan, "dp", split_axis=0, concat_axis=0, tiled=True)
    *blocks, last_rows = pack_rows(
        code,
        sibling_code,
        [stored_rows],
        [sibling_rows],
        half,
        row_cap,
        row_count,
        rest=store_count - ahead,
    )
    last_rows = lax.ppermute(last_rows, "dp", across)
    own_half = hand_on(blocks)
    plan = codes[:, 0, row_count:]
    wanted = plan[:, :token_cap].reshape(peer_count * token_cap)
    chosen = wanted[:, None] == jnp.arange(vocab_rows, dtype=jnp.int32)[None, :]
    found = jnp.dot(
        chosen.astype(jnp.bfloat16), word_table, preferred_element_type=jnp.float32
    ).astype(jnp.bfloat16)
    found, first_rows, last_rows, own_half[:3] = lax.optimization_barrier(
        (found, first_rows, last_rows, own_half[:3])
    )
    fetched = lax.all_to_all(
        found.reshape(peer_count, token_cap, width), "dp", split_axis=0, concat_axis=0, tiled=True
    ).reshape(peer_count * token_cap, width)

    partner_rows = [first_rows, last_rows]
    far_rows = [lax.ppermute(rows, "dp", beside) for rows in partner_rows]
    picks = (half, half ^ 1)
    blocks = pack_rows(codes, codes, partner_rows, far_rows, half, row_cap, row_count, picks)
    other_half = hand_on(blocks)
    sources = lax.axis_index("dp") ^ jnp.arange(peer_count, dtype=jnp.int32)
    got_places = plan[:, token_cap : token_cap + row_cap][sources].reshape(half, 2 * row_cap)
    spare = padded(2 * row_cap) - 2 * row_cap
    got_places = jnp.pad(got_places, ((0, 0), (0, spare)), constant_values=-1).reshape(1, -1)
    means, share = early_update(got_places, centroids, own_half[:3])
    late_places = plan[:, token_cap + row_cap :].reshape(1, -1)
    fetched, means, share, got_places, late_places = lax.optimization_barrier(
        (fetched, means, share, got_places, late_places)
    )

    passage_embed, spread = encode(
        peer_count,
        token_slot,
        fetched,
        lengths,
        pos_table,
        emb_gain,
        emb_bias,
        w_qkv,
        w_out,
        out_bias,
        norm_gain,
        norm_bias,
    )
    all_embeds = lax.all_to_all(
        spread, "dp", split_axis=0, concat_axis=0, tiled=True
    )
    pieces = own_half[3:] + other_half
    new_centroids = late_update(got_places, late_places, all_embeds, share, means, pieces)
    return (passage_embed, new_centroids)


def solution(mesh):
    return jax.shard_map(
        shards,
        mesh=mesh,
        in_specs=(
            P(("groups", "dp"), None),
            P(("groups", "dp")),
            P("dp", None),
            P(),
            P(),
            P(),
            P(),
            P(),
            P(),
            P(),
            P(),
            P(("groups", "dp"), None),
            P(("groups", "dp"), None),
            P(("groups", "dp")),
            P(("groups", "dp"), None),
        ),
        out_specs=(P(("groups", "dp"), None), P(("groups", "dp"), None)),
        check_vma=False,
    )
```

```python
import functools

import jax
import jax.numpy as jnp
from jax import lax
from jax.experimental import pallas as pl
from jax.experimental.pallas import tpu as pltpu
from jax.sharding import PartitionSpec as P

HEADS = 8
HD = 64


def normed(values, gain, shift):
    center = values - jnp.mean(values, axis=-1, keepdims=True)
    spread = jnp.mean(center * center, axis=-1, keepdims=True)
    return center * lax.rsqrt(spread + 1e-12) * gain + shift


def head_sums(weights, seq):
    rows, columns = weights.shape
    lane = lax.broadcasted_iota(jnp.int32, (rows, 2 * seq), 1)
    sums = []
    for start in range(0, columns, 2 * seq):
        pair = weights[:, start : start + 2 * seq]
        first = jnp.sum(jnp.where(lane < seq, pair, 0.0), axis=1, keepdims=True)
        second = jnp.sum(jnp.where(lane < seq, 0.0, pair), axis=1, keepdims=True)
        sums.append(jnp.where(lane < seq, first, second))
    return jnp.concatenate(sums, axis=1)


def encode_kernel(*refs):
    count = (len(refs) - 3) // 2
    far, (out, spread), near, arrived = refs[:count], refs[count : count + 2], refs[-count - 1 : -1], refs[-1]
    w_qkv_far, inner = far[-2], HEADS * HD
    copies = [
        pltpu.make_async_copy(source, target, arrived.at[at])
        for at, (source, target) in enumerate(zip(far, near))
        if source is not w_qkv_far
    ]
    lengths, slots, fetched, pos, emb_gain, emb_bias, out_bias, norm_gain, norm_bias, w_qkv, w_out = near
    out_copy = copies.pop()
    thirds = []
    for third in range(3):
        columns = pl.ds(third * inner, inner)
        thirds.append(
            pltpu.make_async_copy(
                w_qkv_far.at[:, columns], w_qkv.at[:, columns], arrived.at[count + third]
            )
        )
    for copy in copies + thirds + [out_copy]:
        copy.start()
    for copy in copies:
        copy.wait()
    passes = out.shape[0]
    size = [lengths[:, p : p + 1] for p in range(passes)]
    tokens, slot_count = slots.shape[0], fetched.shape[0]
    seq = tokens // passes
    spot = lax.broadcasted_iota(jnp.int32, (tokens, slot_count), 1)
    picker = jnp.where(slots[...] == spot, 1.0, 0.0).astype(jnp.bfloat16)
    tok = jnp.dot(picker, fetched[...], preferred_element_type=jnp.float32)
    where_at = pos[...].astype(jnp.float32)
    summed = tok + jnp.concatenate([where_at] * passes, axis=0)
    embedded = normed(summed, emb_gain[...], emb_bias[...]).astype(jnp.bfloat16)
    parts = []
    for third in range(3):
        thirds[third].wait()
        weights = w_qkv[:, third * inner : (third + 1) * inner]
        part = jnp.dot(embedded, weights, preferred_element_type=jnp.float32)
        parts.append(part.astype(jnp.bfloat16))

    block_row = lax.broadcasted_iota(jnp.int32, (HEADS * seq, inner), 0) // seq
    block_col = lax.broadcasted_iota(jnp.int32, (HEADS * seq, inner), 1) // HD
    same = block_row == block_col
    lane = lax.broadcasted_iota(jnp.int32, (seq, HEADS * seq), 1) % seq
    contexts = []
    for p in range(passes):
        query, keys, vals = (part[p * seq : (p + 1) * seq] for part in parts)
        zero = jnp.zeros((), jnp.bfloat16)
        keys = jnp.where(same, jnp.concatenate([keys] * HEADS, axis=0), zero)
        vals = jnp.where(same, jnp.concatenate([vals] * HEADS, axis=0), zero)
        scores = lax.dot_general(
            query, keys, (((1,), (1,)), ((), ())), preferred_element_type=jnp.float32
        ) * HD ** (-0.5)
        weights = jnp.where(lane < size[p], jnp.exp(scores), 0.0)
        probs = (weights / head_sums(weights, seq)).astype(jnp.bfloat16)
        contexts.append(jnp.dot(probs, vals, preferred_element_type=jnp.float32))
    context = jnp.concatenate(contexts, axis=0).astype(jnp.bfloat16)
    out_copy.wait()
    attended = jnp.dot(context, w_out[...], preferred_element_type=jnp.float32) + out_bias[...]
    hidden = normed(embedded.astype(jnp.float32) + attended, norm_gain[...], norm_bias[...])
    row = lax.broadcasted_iota(jnp.int32, (seq, 1), 0)
    for p in range(passes):
        kept = jnp.where(row < size[p], hidden[p * seq : (p + 1) * seq], 0.0)
        pooled = jnp.sum(kept, axis=0, keepdims=True) / size[p].astype(jnp.float32)
        scale = lax.rsqrt(jnp.mean(pooled * pooled, axis=-1, keepdims=True) + 1e-06)
        out[p : p + 1, :] = (pooled * scale).astype(jnp.bfloat16)
    spread[...] = jnp.broadcast_to(out[...][None], spread.shape)


def encode(
    peers, slots, fetched, lengths, pos_table, emb_gain, emb_bias, w_qkv, w_out, out_bias, norm_gain, norm_bias
):
    width = fetched.shape[1]
    tokens = slots.shape[0]
    passes = lengths.shape[0]
    macs = tokens * width * (fetched.shape[0] + 4 * HEADS * HD)
    operands = (
        lengths[None],
        slots,
        fetched,
        pos_table,
        emb_gain[None],
        emb_bias[None],
        out_bias[None],
        norm_gain[None],
        norm_bias[None],
        w_qkv,
        w_out,
    )
    return pl.pallas_call(
        encode_kernel,
        out_shape=[
            jax.ShapeDtypeStruct((passes, width), jnp.bfloat16),
            jax.ShapeDtypeStruct((peers, passes, width), jnp.bfloat16),
        ],
        in_specs=[pl.BlockSpec(memory_space=pltpu.HBM)] * len(operands),
        out_specs=[pl.BlockSpec(memory_space=pltpu.VMEM)] * 2,
        scratch_shapes=[pltpu.VMEM(operand.shape, operand.dtype) for operand in operands]
        + [pltpu.SemaphoreType.DMA((len(operands) + 3,))],
        compiler_params=pltpu.CompilerParams(vmem_limit_bytes=60 * 1024 * 1024),
        cost_estimate=pl.CostEstimate(
            flops=2 * macs, bytes_accessed=6 * 1024 * 1024, transcendentals=0
        ),
        name="encode",
    )(*operands)


def padded(rows):
    return -(-rows // 16) * 16


def rank_bits(count):
    return max(1, (count - 1).bit_length())


def route_kernel(
    sizes,
    token_ids_far,
    owners_far,
    row_slot_far,
    plan,
    token_slot_far,
    code,
    *near,
):
    peers, vocab_rows, token_cap, row_cap, pooled = sizes
    token_ids, owners, row_slot, token_slot, arrived = near
    copies = [
        pltpu.make_async_copy(source, target, arrived.at[at])
        for at, (source, target) in enumerate(
            ((token_ids_far, token_ids), (owners_far, owners), (row_slot_far, row_slot))
        )
    ]
    for copy in copies:
        copy.start()
    for copy in copies:
        copy.wait()
    ids = jnp.concatenate([token_ids[p : p + 1, :] for p in range(token_ids.shape[0])], axis=1)
    tokens, rows = ids.shape[1], owners.shape[1]
    count = tokens + rows
    edge = (lax.broadcasted_iota(jnp.int32, (peers, tokens), 0) + 1) * vocab_rows
    holder = jnp.sum(jnp.where(ids >= edge, 1, 0), axis=0, keepdims=True)
    values = jnp.concatenate([ids - holder * vocab_rows, row_slot[...]], axis=1)

    kind = jnp.concatenate([holder, owners[...] + peers], axis=1)
    at = lax.broadcasted_iota(jnp.int32, (count, count), 0)
    by = lax.broadcasted_iota(jnp.int32, (count, count), 1)
    across = jnp.broadcast_to(kind, (count, count))
    down = jnp.sum(jnp.where(at == by, across, 0), axis=1, keepdims=True)
    same = down == across
    rank_row = jnp.sum(jnp.where(same & (at < by), 1, 0), axis=0, keepdims=True)
    rank_col = jnp.sum(jnp.where(same & (by < at), 1, 0), axis=1, keepdims=True)

    code[...] = owners[...] * 2 ** rank_bits(rows) + rank_row[:, tokens:]
    goal = jnp.concatenate([holder, owners[...]], axis=1)
    peer = lax.broadcasted_iota(jnp.int32, (peers, count), 0)
    left = jnp.where(peer == goal, values + 1, 0).astype(jnp.float32)
    columns = token_cap + row_cap + pooled
    column = lax.broadcasted_iota(jnp.int32, (count, columns), 1)
    entry = lax.broadcasted_iota(jnp.int32, (count, 1), 0)
    first = jnp.where(entry < tokens, rank_col, rank_col + token_cap)
    second = entry - (count - pooled) + token_cap + row_cap
    second = jnp.where(entry < count - pooled, -1, second)
    right = jnp.where((column == first) | (column == second), 1.0, 0.0)
    filled = jnp.dot(
        left, right, preferred_element_type=jnp.float32, precision=lax.Precision.HIGHEST
    )
    filled = filled.astype(jnp.int32) - 1
    for p in range(peers):
        plan[p, :, :rows] = code[...]
        plan[p, :, rows:] = filled[p : p + 1]
    token_slot[...] = down[:tokens] * token_cap + rank_col[:tokens]
    send = pltpu.make_async_copy(token_slot, token_slot_far, arrived.at[3])
    send.start()
    send.wait()


def route(token_ids, owners, row_slot, sizes):
    peers, _, token_cap, row_cap, pooled = sizes
    passes, seq_len = token_ids.shape
    rows = owners.shape[1]
    ints = lambda *shape: jax.ShapeDtypeStruct(shape, jnp.int32)
    return pl.pallas_call(
        functools.partial(route_kernel, sizes),
        out_shape=[
            ints(peers, 1, rows + token_cap + row_cap + pooled),
            ints(passes * seq_len, 1),
            ints(1, rows),
        ],
        in_specs=[pl.BlockSpec(memory_space=pltpu.HBM)] * 3,
        out_specs=[
            pl.BlockSpec(memory_space=pltpu.VMEM),
            pl.BlockSpec(memory_space=pltpu.HBM),
            pl.BlockSpec(memory_space=pltpu.VMEM),
        ],
        scratch_shapes=[
            pltpu.VMEM(token_ids.shape, jnp.int32),
            pltpu.VMEM(owners.shape, jnp.int32),
            pltpu.VMEM(row_slot.shape, jnp.int32),
            pltpu.VMEM((passes * seq_len, 1), jnp.int32),
            pltpu.SemaphoreType.DMA((4,)),
        ],
        compiler_params=pltpu.CompilerParams(vmem_limit_bytes=60 * 1024 * 1024),
        name="route",
    )(token_ids, owners, row_slot)


def pack_kernel(half, row_cap, count, picks, pieces, rest, *refs):
    me = lax.axis_index("dp")
    operands = 2 + 2 * pieces
    far, refs = refs[:operands], refs[operands:]
    steps = half // 2
    outs, refs = refs[: steps + bool(rest)], refs[steps + bool(rest) :]
    near, (blocks, tail, arrived, left) = refs[:operands], refs[operands:]
    size = blocks.shape[0] // steps
    copies = [
        pltpu.make_async_copy(far[at], near[at], arrived.at[at]) for at in range(operands)
    ]
    for copy in copies:
        copy.start()
    for copy in copies[:2]:
        copy.wait()
    if size > 2 * row_cap:
        blocks[...] = jnp.zeros(blocks.shape, blocks.dtype)
    for source in range(2):
        if picks is None:
            code = near[source][...]
        else:
            code = near[source][me ^ picks[source], :, :count]
        bits = rank_bits(count)
        owner, rank = code >> bits, code & (2**bits - 1)
        fits = ((owner ^ me) & (1 | half)) == 0
        chip = ((owner ^ me) & (half - 1)) >> 1
        slot = jnp.where(fits, chip * row_cap + rank, -1)
        packed, at = 0.0, 0
        for piece in range(2 + source * pieces, 2 + (source + 1) * pieces):
            rows = near[piece]
            spot = lax.broadcasted_iota(jnp.int32, (steps * row_cap, rows.shape[0]), 0)
            table = jnp.where(slot[:, at : at + rows.shape[0]] == spot, 1.0, 0.0)
            copies[piece].wait()
            packed += jnp.dot(
                table.astype(jnp.bfloat16), rows[...], preferred_element_type=jnp.float32
            )
            at += rows.shape[0]
        packed = packed.astype(jnp.bfloat16)
        for step in range(steps):
            first = step * size + source * row_cap
            blocks[first : first + row_cap, :] = packed[step * row_cap : (step + 1) * row_cap]
    sends = [
        pltpu.make_async_copy(
            blocks.at[pl.ds(step * size, size)], outs[step], left.at[step]
        )
        for step in range(steps)
    ]
    if rest:
        tail[...] = near[2][near[2].shape[0] - rest :, :]
        sends.append(pltpu.make_async_copy(tail, outs[steps], left.at[steps]))
    for send in sends:
        send.start()
    for send in sends:
        send.wait()


def pack_rows(codes_a, codes_b, rows_a, rows_b, half, row_cap, count, picks=None, rest=0):
    width = rows_a[0].shape[1]
    total = sum(piece.shape[0] for piece in rows_a)
    steps = half // 2
    size = padded(2 * row_cap)
    operands = (codes_a, codes_b, *rows_a, *rows_b)
    shapes = [(size, width)] * steps + [(rest, width)] * bool(rest)
    return pl.pallas_call(
        functools.partial(pack_kernel, half, row_cap, count, picks, len(rows_a), rest),
        out_shape=[jax.ShapeDtypeStruct(shape, jnp.bfloat16) for shape in shapes],
        in_specs=[pl.BlockSpec(memory_space=pltpu.HBM)] * len(operands),
        out_specs=[pl.BlockSpec(memory_space=pltpu.HBM)] * len(shapes),
        scratch_shapes=[
            *(pltpu.VMEM(operand.shape, operand.dtype) for operand in operands),
            pltpu.VMEM((steps * size, width), jnp.bfloat16),
            pltpu.VMEM((max(rest, 16), width), jnp.bfloat16),
            pltpu.SemaphoreType.DMA((len(operands),)),
            pltpu.SemaphoreType.DMA((len(shapes),)),
        ],
        compiler_params=pltpu.CompilerParams(vmem_limit_bytes=60 * 1024 * 1024),
        cost_estimate=pl.CostEstimate(
            flops=4 * steps * row_cap * width * total,
            bytes_accessed=4 * width * (total + steps * row_cap),
            transcendentals=0,
        ),
        name="pack",
    )(*operands)


def onehot(where_to, first, count):
    centre = lax.broadcasted_iota(jnp.int32, (count, where_to.shape[1]), 0) + first
    return jnp.where(centre == where_to, 1.0, 0.0)


BLOCK = 128


def early_kernel(places_far, centroids_far, *rest):
    pieces, (out_far, share_far, places, rows, centroids, out, share, arrived, left) = rest[:-9], rest[-9:]
    size = pieces[0].shape[0]
    steps = centroids.shape[0] // BLOCK
    copies = [pltpu.make_async_copy(places_far, places, arrived.at[0])]
    for at, piece in enumerate(pieces):
        copies.append(
            pltpu.make_async_copy(piece, rows.at[pl.ds(at * size, size)], arrived.at[1 + at])
        )
    loads = []
    for step in range(steps):
        block = pl.ds(step * BLOCK, BLOCK)
        loads.append(
            pltpu.make_async_copy(
                centroids_far.at[block], centroids.at[block], arrived.at[1 + len(pieces) + step]
            )
        )
    for copy in copies + loads:
        copy.start()
    for copy in copies:
        copy.wait()
    sends = []
    for step in range(steps):
        block = pl.ds(step * BLOCK, BLOCK)
        hot = onehot(places[...], step * BLOCK, BLOCK)
        counts = jnp.sum(hot, axis=1, keepdims=True)
        scale = jnp.where(counts > 0, 1.0 / jnp.maximum(counts, 1.0), 0.0)
        sums = jnp.dot(
            hot[:, : rows.shape[0]].astype(jnp.bfloat16),
            rows[...],
            preferred_element_type=jnp.float32,
        )
        loads[step].wait()
        out[block, :] = jnp.where(counts > 0, sums * scale, centroids[block, :])
        share[block, :] = jnp.broadcast_to(scale, (BLOCK, share.shape[1]))
        sends.append(pltpu.make_async_copy(out.at[block], out_far.at[block], left.at[step]))
        sends[-1].start()
    sends.append(pltpu.make_async_copy(share, share_far, left.at[steps]))
    sends[-1].start()
    for send in sends:
        send.wait()


def late_kernel(places_far, late_far, spread_far, share_far, early_far, *rest):
    pieces, rest = rest[:-10], rest[-10:]
    out_far, places, late, spread, share, rows, early, out, arrived, left = rest
    size, passes = pieces[0].shape[0], spread.shape[1]
    steps = early.shape[0] // BLOCK
    loads = [
        pltpu.make_async_copy(source, target, arrived.at[at])
        for at, (source, target) in enumerate(
            ((places_far, places), (late_far, late), (spread_far, spread), (share_far, share))
        )
    ]
    for at, piece in enumerate(pieces):
        loads.append(
            pltpu.make_async_copy(piece, rows.at[pl.ds(at * size, size)], arrived.at[4 + at])
        )
    starts = []
    for step in range(steps):
        block = pl.ds(step * BLOCK, BLOCK)
        starts.append(
            pltpu.make_async_copy(
                early_far.at[block], early.at[block], arrived.at[len(loads) + step]
            )
        )
    for copy in loads + starts:
        copy.start()
    for copy in loads:
        copy.wait()
    top = len(pieces) * size
    for peer in range(spread.shape[0]):
        rows[top + peer * passes : top + (peer + 1) * passes, :] = spread[peer]
    where_to = jnp.concatenate([places[:, places.shape[1] - top :], late[...]], axis=1)
    sends = []
    for step in range(steps):
        block = pl.ds(step * BLOCK, BLOCK)
        hot = onehot(where_to, step * BLOCK, BLOCK).astype(jnp.bfloat16)
        sums = jnp.dot(hot, rows[...], preferred_element_type=jnp.float32)
        starts[step].wait()
        out[block, :] = early[block, :] + sums * share[block, :1]
        sends.append(pltpu.make_async_copy(out.at[block], out_far.at[block], left.at[step]))
        sends[-1].start()
    for send in sends:
        send.wait()


def early_update(places, centroids, pieces):
    centre_count, width = centroids.shape
    row_total = sum(piece.shape[0] for piece in pieces)
    wide = pltpu.VMEM(centroids.shape, jnp.float32)
    thin = (centre_count, 128)
    steps = centre_count // BLOCK
    return pl.pallas_call(
        early_kernel,
        out_shape=[
            jax.ShapeDtypeStruct(centroids.shape, jnp.float32),
            jax.ShapeDtypeStruct(thin, jnp.float32),
        ],
        in_specs=[pl.BlockSpec(memory_space=pl.ANY)] * (2 + len(pieces)),
        out_specs=[pl.BlockSpec(memory_space=pltpu.HBM)] * 2,
        scratch_shapes=[
            pltpu.VMEM(places.shape, jnp.int32),
            pltpu.VMEM((row_total, width), jnp.bfloat16),
            wide,
            wide,
            pltpu.VMEM(thin, jnp.float32),
            pltpu.SemaphoreType.DMA((1 + len(pieces) + steps,)),
            pltpu.SemaphoreType.DMA((steps + 1,)),
        ],
        compiler_params=pltpu.CompilerParams(vmem_limit_bytes=60 * 1024 * 1024),
        cost_estimate=pl.CostEstimate(
            flops=2 * centre_count * width * row_total,
            bytes_accessed=8 * centre_count * width,
            transcendentals=0,
        ),
        name="early",
    )(places, centroids, *pieces)


def late_update(places, late, spread, share, early, pieces):
    centre_count, width = early.shape
    row_total = sum(piece.shape[0] for piece in pieces) + late.shape[1]
    wide = pltpu.VMEM(early.shape, jnp.float32)
    steps = centre_count // BLOCK
    return pl.pallas_call(
        late_kernel,
        out_shape=jax.ShapeDtypeStruct(early.shape, jnp.float32),
        in_specs=[pl.BlockSpec(memory_space=pltpu.HBM)] * (5 + len(pieces)),
        out_specs=pl.BlockSpec(memory_space=pltpu.HBM),
        scratch_shapes=[
            pltpu.VMEM(places.shape, jnp.int32),
            pltpu.VMEM(late.shape, jnp.int32),
            pltpu.VMEM(spread.shape, jnp.bfloat16),
            pltpu.VMEM(share.shape, jnp.float32),
            pltpu.VMEM((row_total, width), jnp.bfloat16),
            wide,
            wide,
            pltpu.SemaphoreType.DMA((4 + len(pieces) + steps,)),
            pltpu.SemaphoreType.DMA((steps,)),
        ],
        compiler_params=pltpu.CompilerParams(vmem_limit_bytes=60 * 1024 * 1024),
        cost_estimate=pl.CostEstimate(
            flops=2 * centre_count * width * row_total,
            bytes_accessed=8 * centre_count * width,
            transcendentals=0,
        ),
        name="late",
    )(places, late, spread, share, early, *pieces)


def shards(
    token_ids,
    lengths,
    word_table,
    pos_table,
    emb_gain,
    emb_bias,
    w_qkv,
    w_out,
    out_bias,
    norm_gain,
    norm_bias,
    stored_rows,
    row_owner,
    row_slot,
    centroids,
):
    peer_count = lax.axis_size("dp")
    half = peer_count // 2
    width = word_table.shape[1]
    vocab_rows = word_table.shape[0]
    passes, seq_len = token_ids.shape
    token_count = passes * seq_len
    row_count = row_slot.shape[0]
    store_count = stored_rows.shape[0]
    token_cap = max(2, 3 * token_count // peer_count)
    row_cap = max(2, 3 * row_count // peer_count)

    across = [(i, i ^ half) for i in range(peer_count)]
    beside = [(i, i ^ 1) for i in range(peer_count)]

    def hand_on(blocks):
        got = [blocks[0]]
        for step in range(1, len(blocks)):
            moves = [(i, i ^ (2 * step)) for i in range(peer_count)]
            got.append(lax.ppermute(blocks[step], "dp", moves))
        return got

    ahead = store_count * 2 // 5 // 16 * 16
    sibling_rows = lax.ppermute(stored_rows, "dp", beside)
    first_rows = lax.ppermute(stored_rows[:ahead], "dp", across)
    sizes = (peer_count, vocab_rows, token_cap, row_cap, row_count - store_count)
    plan, token_slot, code = route(token_ids, row_owner.reshape(1, row_count), row_slot[None], sizes)
    sibling_code = lax.ppermute(code, "dp", beside)
    plan, sibling_rows, rest = lax.optimization_barrier((plan, sibling_rows, stored_rows))
    last_rows = lax.ppermute(rest[ahead:], "dp", across)
    codes = lax.all_to_all(plan, "dp", split_axis=0, concat_axis=0, tiled=True)
    blocks = pack_rows(code, sibling_code, [stored_rows], [sibling_rows], half, row_cap, row_count)
    own_half = hand_on(blocks)
    plan = codes[:, 0, row_count:]
    wanted = plan[:, :token_cap].reshape(peer_count * token_cap)
    chosen = wanted[:, None] == jnp.arange(vocab_rows, dtype=jnp.int32)[None, :]
    found = jnp.dot(
        chosen.astype(jnp.bfloat16), word_table, preferred_element_type=jnp.float32
    ).astype(jnp.bfloat16)
    found, first_rows, last_rows, own_half[:3] = lax.optimization_barrier(
        (found, first_rows, last_rows, own_half[:3])
    )
    fetched = lax.all_to_all(
        found.reshape(peer_count, token_cap, width), "dp", split_axis=0, concat_axis=0, tiled=True
    ).reshape(peer_count * token_cap, width)

    partner_rows = [first_rows, last_rows]
    far_rows = [lax.ppermute(rows, "dp", beside) for rows in partner_rows]
    picks = (half, half ^ 1)
    blocks = pack_rows(codes, codes, partner_rows, far_rows, half, row_cap, row_count, picks)
    other_half = hand_on(blocks)
    sources = lax.axis_index("dp") ^ jnp.arange(peer_count, dtype=jnp.int32)
    got_places = plan[:, token_cap : token_cap + row_cap][sources].reshape(half, 2 * row_cap)
    spare = padded(2 * row_cap) - 2 * row_cap
    got_places = jnp.pad(got_places, ((0, 0), (0, spare)), constant_values=-1).reshape(1, -1)
    means, share = early_update(got_places, centroids, own_half[:3])
    late_places = plan[:, token_cap + row_cap :].reshape(1, -1)
    fetched, means, share, got_places, late_places = lax.optimization_barrier(
        (fetched, means, share, got_places, late_places)
    )

    passage_embed, spread = encode(
        peer_count,
        token_slot,
        fetched,
        lengths,
        pos_table,
        emb_gain,
        emb_bias,
        w_qkv,
        w_out,
        out_bias,
        norm_gain,
        norm_bias,
    )
    all_embeds = lax.all_to_all(
        spread, "dp", split_axis=0, concat_axis=0, tiled=True
    )
    pieces = own_half[3:] + other_half
    new_centroids = late_update(got_places, late_places, all_embeds, share, means, pieces)
    return (passage_embed, new_centroids)


def solution(mesh):
    return jax.shard_map(
        shards,
        mesh=mesh,
        in_specs=(
            P(("groups", "dp"), None),
            P(("groups", "dp")),
            P("dp", None),
            P(),
            P(),
            P(),
            P(),
            P(),
            P(),
            P(),
            P(),
            P(("groups", "dp"), None),
            P(("groups", "dp"), None),
            P(("groups", "dp")),
            P(("groups", "dp"), None),
        ),
        out_specs=(P(("groups", "dp"), None), P(("groups", "dp"), None)),
        check_vma=False,
    )
```

```python
import functools

import jax
import jax.numpy as jnp
from jax import lax
from jax.experimental import pallas as pl
from jax.experimental.pallas import tpu as pltpu
from jax.sharding import PartitionSpec as P

HEADS = 8
HD = 64


def normed(values, gain, shift):
    center = values - jnp.mean(values, axis=-1, keepdims=True)
    spread = jnp.mean(center * center, axis=-1, keepdims=True)
    return center * lax.rsqrt(spread + 1e-12) * gain + shift


def head_sums(weights, seq):
    rows, columns = weights.shape
    lane = lax.broadcasted_iota(jnp.int32, (rows, 2 * seq), 1)
    sums = []
    for start in range(0, columns, 2 * seq):
        pair = weights[:, start : start + 2 * seq]
        first = jnp.sum(jnp.where(lane < seq, pair, 0.0), axis=1, keepdims=True)
        second = jnp.sum(jnp.where(lane < seq, 0.0, pair), axis=1, keepdims=True)
        sums.append(jnp.where(lane < seq, first, second))
    return jnp.concatenate(sums, axis=1)


def encode_kernel(*refs):
    count = (len(refs) - 3) // 2
    far, (out, spread), near, arrived = refs[:count], refs[count : count + 2], refs[-count - 1 : -1], refs[-1]
    w_qkv_far, inner = far[-2], HEADS * HD
    copies = [
        pltpu.make_async_copy(source, target, arrived.at[at])
        for at, (source, target) in enumerate(zip(far, near))
        if source is not w_qkv_far
    ]
    lengths, slots, fetched, pos, emb_gain, emb_bias, out_bias, norm_gain, norm_bias, w_qkv, w_out = near
    out_copy = copies.pop()
    thirds = []
    for third in range(3):
        columns = pl.ds(third * inner, inner)
        thirds.append(
            pltpu.make_async_copy(
                w_qkv_far.at[:, columns], w_qkv.at[:, columns], arrived.at[count + third]
            )
        )
    for copy in copies + thirds + [out_copy]:
        copy.start()
    for copy in copies:
        copy.wait()
    passes = out.shape[0]
    size = [lengths[:, p : p + 1] for p in range(passes)]
    tokens, slot_count = slots.shape[0], fetched.shape[0]
    seq = tokens // passes
    spot = lax.broadcasted_iota(jnp.int32, (tokens, slot_count), 1)
    picker = jnp.where(slots[...] == spot, 1.0, 0.0).astype(jnp.bfloat16)
    tok = jnp.dot(picker, fetched[...], preferred_element_type=jnp.float32)
    where_at = pos[...].astype(jnp.float32)
    summed = tok + jnp.concatenate([where_at] * passes, axis=0)
    embedded = normed(summed, emb_gain[...], emb_bias[...]).astype(jnp.bfloat16)
    parts = []
    for third in range(3):
        thirds[third].wait()
        weights = w_qkv[:, third * inner : (third + 1) * inner]
        part = jnp.dot(embedded, weights, preferred_element_type=jnp.float32)
        parts.append(part.astype(jnp.bfloat16))

    block_row = lax.broadcasted_iota(jnp.int32, (HEADS * seq, inner), 0) // seq
    block_col = lax.broadcasted_iota(jnp.int32, (HEADS * seq, inner), 1) // HD
    same = block_row == block_col
    lane = lax.broadcasted_iota(jnp.int32, (seq, HEADS * seq), 1) % seq
    contexts = []
    for p in range(passes):
        query, keys, vals = (part[p * seq : (p + 1) * seq] for part in parts)
        zero = jnp.zeros((), jnp.bfloat16)
        keys = jnp.where(same, jnp.concatenate([keys] * HEADS, axis=0), zero)
        vals = jnp.where(same, jnp.concatenate([vals] * HEADS, axis=0), zero)
        scores = lax.dot_general(
            query, keys, (((1,), (1,)), ((), ())), preferred_element_type=jnp.float32
        ) * HD ** (-0.5)
        weights = jnp.where(lane < size[p], jnp.exp(scores), 0.0)
        probs = (weights / head_sums(weights, seq)).astype(jnp.bfloat16)
        contexts.append(jnp.dot(probs, vals, preferred_element_type=jnp.float32))
    context = jnp.concatenate(contexts, axis=0).astype(jnp.bfloat16)
    out_copy.wait()
    attended = jnp.dot(context, w_out[...], preferred_element_type=jnp.float32) + out_bias[...]
    hidden = normed(embedded.astype(jnp.float32) + attended, norm_gain[...], norm_bias[...])
    row = lax.broadcasted_iota(jnp.int32, (seq, 1), 0)
    for p in range(passes):
        kept = jnp.where(row < size[p], hidden[p * seq : (p + 1) * seq], 0.0)
        pooled = jnp.sum(kept, axis=0, keepdims=True) / size[p].astype(jnp.float32)
        scale = lax.rsqrt(jnp.mean(pooled * pooled, axis=-1, keepdims=True) + 1e-06)
        out[p : p + 1, :] = (pooled * scale).astype(jnp.bfloat16)
    spread[...] = jnp.broadcast_to(out[...][None], spread.shape)


def encode(
    peers, slots, fetched, lengths, pos_table, emb_gain, emb_bias, w_qkv, w_out, out_bias, norm_gain, norm_bias
):
    width = fetched.shape[1]
    tokens = slots.shape[0]
    passes = lengths.shape[0]
    macs = tokens * width * (fetched.shape[0] + 4 * HEADS * HD)
    operands = (
        lengths[None],
        slots,
        fetched,
        pos_table,
        emb_gain[None],
        emb_bias[None],
        out_bias[None],
        norm_gain[None],
        norm_bias[None],
        w_qkv,
        w_out,
    )
    return pl.pallas_call(
        encode_kernel,
        out_shape=[
            jax.ShapeDtypeStruct((passes, width), jnp.bfloat16),
            jax.ShapeDtypeStruct((peers, passes, width), jnp.bfloat16),
        ],
        in_specs=[pl.BlockSpec(memory_space=pltpu.HBM)] * len(operands),
        out_specs=[pl.BlockSpec(memory_space=pltpu.VMEM)] * 2,
        scratch_shapes=[pltpu.VMEM(operand.shape, operand.dtype) for operand in operands]
        + [pltpu.SemaphoreType.DMA((len(operands) + 3,))],
        compiler_params=pltpu.CompilerParams(vmem_limit_bytes=60 * 1024 * 1024),
        cost_estimate=pl.CostEstimate(
            flops=2 * macs, bytes_accessed=6 * 1024 * 1024, transcendentals=0
        ),
        name="encode",
    )(*operands)


def padded(rows):
    return -(-rows // 16) * 16


def rank_bits(count):
    return max(1, (count - 1).bit_length())


def route_kernel(
    sizes,
    token_ids_far,
    owners_far,
    row_slot_far,
    plan,
    token_slot_far,
    code,
    *near,
):
    peers, vocab_rows, token_cap, row_cap, pooled = sizes
    token_ids, owners, row_slot, token_slot, arrived = near
    copies = [
        pltpu.make_async_copy(source, target, arrived.at[at])
        for at, (source, target) in enumerate(
            ((token_ids_far, token_ids), (owners_far, owners), (row_slot_far, row_slot))
        )
    ]
    for copy in copies:
        copy.start()
    for copy in copies:
        copy.wait()
    ids = jnp.concatenate([token_ids[p : p + 1, :] for p in range(token_ids.shape[0])], axis=1)
    tokens, rows = ids.shape[1], owners.shape[1]
    count = tokens + rows
    edge = (lax.broadcasted_iota(jnp.int32, (peers, tokens), 0) + 1) * vocab_rows
    holder = jnp.sum(jnp.where(ids >= edge, 1, 0), axis=0, keepdims=True)
    values = jnp.concatenate([ids - holder * vocab_rows, row_slot[...]], axis=1)

    kind = jnp.concatenate([holder, owners[...] + peers], axis=1)
    at = lax.broadcasted_iota(jnp.int32, (count, count), 0)
    by = lax.broadcasted_iota(jnp.int32, (count, count), 1)
    across = jnp.broadcast_to(kind, (count, count))
    down = jnp.sum(jnp.where(at == by, across, 0), axis=1, keepdims=True)
    same = down == across
    rank_row = jnp.sum(jnp.where(same & (at < by), 1, 0), axis=0, keepdims=True)
    rank_col = jnp.sum(jnp.where(same & (by < at), 1, 0), axis=1, keepdims=True)

    code[...] = owners[...] * 2 ** rank_bits(rows) + rank_row[:, tokens:]
    goal = jnp.concatenate([holder, owners[...]], axis=1)
    peer = lax.broadcasted_iota(jnp.int32, (peers, count), 0)
    left = jnp.where(peer == goal, values + 1, 0).astype(jnp.float32)
    columns = token_cap + row_cap + pooled
    column = lax.broadcasted_iota(jnp.int32, (count, columns), 1)
    entry = lax.broadcasted_iota(jnp.int32, (count, 1), 0)
    first = jnp.where(entry < tokens, rank_col, rank_col + token_cap)
    second = entry - (count - pooled) + token_cap + row_cap
    second = jnp.where(entry < count - pooled, -1, second)
    right = jnp.where((column == first) | (column == second), 1.0, 0.0)
    filled = jnp.dot(
        left, right, preferred_element_type=jnp.float32, precision=lax.Precision.HIGHEST
    )
    filled = filled.astype(jnp.int32) - 1
    for p in range(peers):
        plan[p, :, :rows] = code[...]
        plan[p, :, rows:] = filled[p : p + 1]
    token_slot[...] = down[:tokens] * token_cap + rank_col[:tokens]
    send = pltpu.make_async_copy(token_slot, token_slot_far, arrived.at[3])
    send.start()
    send.wait()


def route(token_ids, owners, row_slot, sizes):
    peers, _, token_cap, row_cap, pooled = sizes
    passes, seq_len = token_ids.shape
    rows = owners.shape[1]
    ints = lambda *shape: jax.ShapeDtypeStruct(shape, jnp.int32)
    return pl.pallas_call(
        functools.partial(route_kernel, sizes),
        out_shape=[
            ints(peers, 1, rows + token_cap + row_cap + pooled),
            ints(passes * seq_len, 1),
            ints(1, rows),
        ],
        in_specs=[pl.BlockSpec(memory_space=pltpu.HBM)] * 3,
        out_specs=[
            pl.BlockSpec(memory_space=pltpu.VMEM),
            pl.BlockSpec(memory_space=pltpu.HBM),
            pl.BlockSpec(memory_space=pltpu.VMEM),
        ],
        scratch_shapes=[
            pltpu.VMEM(token_ids.shape, jnp.int32),
            pltpu.VMEM(owners.shape, jnp.int32),
            pltpu.VMEM(row_slot.shape, jnp.int32),
            pltpu.VMEM((passes * seq_len, 1), jnp.int32),
            pltpu.SemaphoreType.DMA((4,)),
        ],
        compiler_params=pltpu.CompilerParams(vmem_limit_bytes=60 * 1024 * 1024),
        name="route",
    )(token_ids, owners, row_slot)


def pack_kernel(half, row_cap, count, picks, pieces, rest, *refs):
    me = lax.axis_index("dp")
    operands = 2 + 2 * pieces
    far, refs = refs[:operands], refs[operands:]
    steps = half // 2
    outs, refs = refs[: steps + bool(rest)], refs[steps + bool(rest) :]
    near, (blocks, tail, arrived, left) = refs[:operands], refs[operands:]
    size = blocks.shape[0] // steps
    copies = [
        pltpu.make_async_copy(far[at], near[at], arrived.at[at]) for at in range(operands)
    ]
    for copy in copies:
        copy.start()
    for copy in copies[:2]:
        copy.wait()
    if size > 2 * row_cap:
        blocks[...] = jnp.zeros(blocks.shape, blocks.dtype)
    for source in range(2):
        if picks is None:
            code = near[source][...]
        else:
            code = near[source][me ^ picks[source], :, :count]
        bits = rank_bits(count)
        owner, rank = code >> bits, code & (2**bits - 1)
        fits = ((owner ^ me) & (1 | half)) == 0
        chip = ((owner ^ me) & (half - 1)) >> 1
        slot = jnp.where(fits, chip * row_cap + rank, -1)
        packed, at = 0.0, 0
        for piece in range(2 + source * pieces, 2 + (source + 1) * pieces):
            rows = near[piece]
            spot = lax.broadcasted_iota(jnp.int32, (steps * row_cap, rows.shape[0]), 0)
            table = jnp.where(slot[:, at : at + rows.shape[0]] == spot, 1.0, 0.0)
            copies[piece].wait()
            packed += jnp.dot(
                table.astype(jnp.bfloat16), rows[...], preferred_element_type=jnp.float32
            )
            at += rows.shape[0]
        packed = packed.astype(jnp.bfloat16)
        for step in range(steps):
            first = step * size + source * row_cap
            blocks[first : first + row_cap, :] = packed[step * row_cap : (step + 1) * row_cap]
    sends = [
        pltpu.make_async_copy(
            blocks.at[pl.ds(step * size, size)], outs[step], left.at[step]
        )
        for step in range(steps)
    ]
    if rest:
        tail[...] = near[2][near[2].shape[0] - rest :, :]
        sends.append(pltpu.make_async_copy(tail, outs[steps], left.at[steps]))
    for send in sends:
        send.start()
    for send in sends:
        send.wait()


def pack_rows(codes_a, codes_b, rows_a, rows_b, half, row_cap, count, picks=None, rest=0):
    width = rows_a[0].shape[1]
    total = sum(piece.shape[0] for piece in rows_a)
    steps = half // 2
    size = padded(2 * row_cap)
    operands = (codes_a, codes_b, *rows_a, *rows_b)
    shapes = [(size, width)] * steps + [(rest, width)] * bool(rest)
    return pl.pallas_call(
        functools.partial(pack_kernel, half, row_cap, count, picks, len(rows_a), rest),
        out_shape=[jax.ShapeDtypeStruct(shape, jnp.bfloat16) for shape in shapes],
        in_specs=[pl.BlockSpec(memory_space=pltpu.HBM)] * len(operands),
        out_specs=[pl.BlockSpec(memory_space=pltpu.HBM)] * len(shapes),
        scratch_shapes=[
            *(pltpu.VMEM(operand.shape, operand.dtype) for operand in operands),
            pltpu.VMEM((steps * size, width), jnp.bfloat16),
            pltpu.VMEM((max(rest, 16), width), jnp.bfloat16),
            pltpu.SemaphoreType.DMA((len(operands),)),
            pltpu.SemaphoreType.DMA((len(shapes),)),
        ],
        compiler_params=pltpu.CompilerParams(vmem_limit_bytes=60 * 1024 * 1024),
        cost_estimate=pl.CostEstimate(
            flops=4 * steps * row_cap * width * total,
            bytes_accessed=4 * width * (total + steps * row_cap),
            transcendentals=0,
        ),
        name="pack",
    )(*operands)


def onehot(where_to, first, count):
    centre = lax.broadcasted_iota(jnp.int32, (count, where_to.shape[1]), 0) + first
    return jnp.where(centre == where_to, 1.0, 0.0)


BLOCK = 128


def early_kernel(places_far, centroids_far, *rest):
    pieces, (out_far, share_far, places, rows, centroids, out, share, arrived, left) = rest[:-9], rest[-9:]
    size = pieces[0].shape[0]
    steps = centroids.shape[0] // BLOCK
    copies = [pltpu.make_async_copy(places_far, places, arrived.at[0])]
    for at, piece in enumerate(pieces):
        copies.append(
            pltpu.make_async_copy(piece, rows.at[pl.ds(at * size, size)], arrived.at[1 + at])
        )
    loads = []
    for step in range(steps):
        block = pl.ds(step * BLOCK, BLOCK)
        loads.append(
            pltpu.make_async_copy(
                centroids_far.at[block], centroids.at[block], arrived.at[1 + len(pieces) + step]
            )
        )
    for copy in copies + loads:
        copy.start()
    for copy in copies:
        copy.wait()
    sends = []
    for step in range(steps):
        block = pl.ds(step * BLOCK, BLOCK)
        hot = onehot(places[...], step * BLOCK, BLOCK)
        counts = jnp.sum(hot, axis=1, keepdims=True)
        scale = jnp.where(counts > 0, 1.0 / jnp.maximum(counts, 1.0), 0.0)
        sums = jnp.dot(
            hot[:, : rows.shape[0]].astype(jnp.bfloat16),
            rows[...],
            preferred_element_type=jnp.float32,
        )
        loads[step].wait()
        out[block, :] = jnp.where(counts > 0, sums * scale, centroids[block, :])
        share[block, :] = jnp.broadcast_to(scale, (BLOCK, share.shape[1]))
        sends.append(pltpu.make_async_copy(out.at[block], out_far.at[block], left.at[step]))
        sends[-1].start()
    sends.append(pltpu.make_async_copy(share, share_far, left.at[steps]))
    sends[-1].start()
    for send in sends:
        send.wait()


def late_kernel(places_far, late_far, spread_far, share_far, early_far, *rest):
    pieces, rest = rest[:-10], rest[-10:]
    out_far, places, late, spread, share, rows, early, out, arrived, left = rest
    size, passes = pieces[0].shape[0], spread.shape[1]
    steps = early.shape[0] // BLOCK
    loads = [
        pltpu.make_async_copy(source, target, arrived.at[at])
        for at, (source, target) in enumerate(
            ((places_far, places), (late_far, late), (spread_far, spread), (share_far, share))
        )
    ]
    for at, piece in enumerate(pieces):
        loads.append(
            pltpu.make_async_copy(piece, rows.at[pl.ds(at * size, size)], arrived.at[4 + at])
        )
    starts = []
    for step in range(steps):
        block = pl.ds(step * BLOCK, BLOCK)
        starts.append(
            pltpu.make_async_copy(
                early_far.at[block], early.at[block], arrived.at[len(loads) + step]
            )
        )
    for copy in loads + starts:
        copy.start()
    for copy in loads:
        copy.wait()
    top = len(pieces) * size
    for peer in range(spread.shape[0]):
        rows[top + peer * passes : top + (peer + 1) * passes, :] = spread[peer]
    where_to = jnp.concatenate([places[:, places.shape[1] - top :], late[...]], axis=1)
    sends = []
    for step in range(steps):
        block = pl.ds(step * BLOCK, BLOCK)
        hot = onehot(where_to, step * BLOCK, BLOCK).astype(jnp.bfloat16)
        sums = jnp.dot(hot, rows[...], preferred_element_type=jnp.float32)
        starts[step].wait()
        out[block, :] = early[block, :] + sums * share[block, :1]
        sends.append(pltpu.make_async_copy(out.at[block], out_far.at[block], left.at[step]))
        sends[-1].start()
    for send in sends:
        send.wait()


def early_update(places, centroids, pieces):
    centre_count, width = centroids.shape
    row_total = sum(piece.shape[0] for piece in pieces)
    wide = pltpu.VMEM(centroids.shape, jnp.float32)
    thin = (centre_count, 128)
    steps = centre_count // BLOCK
    return pl.pallas_call(
        early_kernel,
        out_shape=[
            jax.ShapeDtypeStruct(centroids.shape, jnp.float32),
            jax.ShapeDtypeStruct(thin, jnp.float32),
        ],
        in_specs=[pl.BlockSpec(memory_space=pl.ANY)] * (2 + len(pieces)),
        out_specs=[pl.BlockSpec(memory_space=pltpu.HBM)] * 2,
        scratch_shapes=[
            pltpu.VMEM(places.shape, jnp.int32),
            pltpu.VMEM((row_total, width), jnp.bfloat16),
            wide,
            wide,
            pltpu.VMEM(thin, jnp.float32),
            pltpu.SemaphoreType.DMA((1 + len(pieces) + steps,)),
            pltpu.SemaphoreType.DMA((steps + 1,)),
        ],
        compiler_params=pltpu.CompilerParams(vmem_limit_bytes=60 * 1024 * 1024),
        cost_estimate=pl.CostEstimate(
            flops=2 * centre_count * width * row_total,
            bytes_accessed=8 * centre_count * width,
            transcendentals=0,
        ),
        name="early",
    )(places, centroids, *pieces)


def late_update(places, late, spread, share, early, pieces):
    centre_count, width = early.shape
    row_total = sum(piece.shape[0] for piece in pieces) + late.shape[1]
    wide = pltpu.VMEM(early.shape, jnp.float32)
    steps = centre_count // BLOCK
    return pl.pallas_call(
        late_kernel,
        out_shape=jax.ShapeDtypeStruct(early.shape, jnp.float32),
        in_specs=[pl.BlockSpec(memory_space=pltpu.HBM)] * (5 + len(pieces)),
        out_specs=pl.BlockSpec(memory_space=pltpu.HBM),
        scratch_shapes=[
            pltpu.VMEM(places.shape, jnp.int32),
            pltpu.VMEM(late.shape, jnp.int32),
            pltpu.VMEM(spread.shape, jnp.bfloat16),
            pltpu.VMEM(share.shape, jnp.float32),
            pltpu.VMEM((row_total, width), jnp.bfloat16),
            wide,
            wide,
            pltpu.SemaphoreType.DMA((4 + len(pieces) + steps,)),
            pltpu.SemaphoreType.DMA((steps,)),
        ],
        compiler_params=pltpu.CompilerParams(vmem_limit_bytes=60 * 1024 * 1024),
        cost_estimate=pl.CostEstimate(
            flops=2 * centre_count * width * row_total,
            bytes_accessed=8 * centre_count * width,
            transcendentals=0,
        ),
        name="late",
    )(places, late, spread, share, early, *pieces)


def shards(
    token_ids,
    lengths,
    word_table,
    pos_table,
    emb_gain,
    emb_bias,
    w_qkv,
    w_out,
    out_bias,
    norm_gain,
    norm_bias,
    stored_rows,
    row_owner,
    row_slot,
    centroids,
):
    peer_count = lax.axis_size("dp")
    half = peer_count // 2
    width = word_table.shape[1]
    vocab_rows = word_table.shape[0]
    passes, seq_len = token_ids.shape
    token_count = passes * seq_len
    row_count = row_slot.shape[0]
    store_count = stored_rows.shape[0]
    token_cap = max(2, 3 * token_count // peer_count)
    row_cap = max(2, 3 * row_count // peer_count)

    across = [(i, i ^ half) for i in range(peer_count)]
    beside = [(i, i ^ 1) for i in range(peer_count)]

    def hand_on(blocks):
        got = [blocks[0]]
        for step in range(1, len(blocks)):
            moves = [(i, i ^ (2 * step)) for i in range(peer_count)]
            got.append(lax.ppermute(blocks[step], "dp", moves))
        return got

    ahead = store_count * 5 // 8 // 16 * 16
    sibling_rows = lax.ppermute(stored_rows, "dp", beside)
    first_rows = lax.ppermute(stored_rows[:ahead], "dp", across)
    sizes = (peer_count, vocab_rows, token_cap, row_cap, row_count - store_count)
    plan, token_slot, code = route(token_ids, row_owner.reshape(1, row_count), row_slot[None], sizes)
    sibling_code = lax.ppermute(code, "dp", beside)
    plan, sibling_rows = lax.optimization_barrier((plan, sibling_rows))
    codes = lax.all_to_all(plan, "dp", split_axis=0, concat_axis=0, tiled=True)
    *blocks, last_rows = pack_rows(
        code,
        sibling_code,
        [stored_rows],
        [sibling_rows],
        half,
        row_cap,
        row_count,
        rest=store_count - ahead,
    )
    last_rows = lax.ppermute(last_rows, "dp", across)
    own_half = hand_on(blocks)
    plan = codes[:, 0, row_count:]
    wanted = plan[:, :token_cap].reshape(peer_count * token_cap)
    chosen = wanted[:, None] == jnp.arange(vocab_rows, dtype=jnp.int32)[None, :]
    found = jnp.dot(
        chosen.astype(jnp.bfloat16), word_table, preferred_element_type=jnp.float32
    ).astype(jnp.bfloat16)
    found, first_rows, last_rows, own_half[:3] = lax.optimization_barrier(
        (found, first_rows, last_rows, own_half[:3])
    )
    fetched = lax.all_to_all(
        found.reshape(peer_count, token_cap, width), "dp", split_axis=0, concat_axis=0, tiled=True
    ).reshape(peer_count * token_cap, width)

    partner_rows = [first_rows, last_rows]
    far_rows = [lax.ppermute(rows, "dp", beside) for rows in partner_rows]
    picks = (half, half ^ 1)
    blocks = pack_rows(codes, codes, partner_rows, far_rows, half, row_cap, row_count, picks)
    other_half = hand_on(blocks)
    sources = lax.axis_index("dp") ^ jnp.arange(peer_count, dtype=jnp.int32)
    got_places = plan[:, token_cap : token_cap + row_cap][sources].reshape(half, 2 * row_cap)
    spare = padded(2 * row_cap) - 2 * row_cap
    got_places = jnp.pad(got_places, ((0, 0), (0, spare)), constant_values=-1).reshape(1, -1)
    means, share = early_update(got_places, centroids, own_half[:3])
    late_places = plan[:, token_cap + row_cap :].reshape(1, -1)
    fetched, means, share, got_places, late_places = lax.optimization_barrier(
        (fetched, means, share, got_places, late_places)
    )

    passage_embed, spread = encode(
        peer_count,
        token_slot,
        fetched,
        lengths,
        pos_table,
        emb_gain,
        emb_bias,
        w_qkv,
        w_out,
        out_bias,
        norm_gain,
        norm_bias,
    )
    all_embeds = lax.all_to_all(
        spread, "dp", split_axis=0, concat_axis=0, tiled=True
    )
    pieces = own_half[3:] + other_half
    new_centroids = late_update(got_places, late_places, all_embeds, share, means, pieces)
    return (passage_embed, new_centroids)


def solution(mesh):
    return jax.shard_map(
        shards,
        mesh=mesh,
        in_specs=(
            P(("groups", "dp"), None),
            P(("groups", "dp")),
            P("dp", None),
            P(),
            P(),
            P(),
            P(),
            P(),
            P(),
            P(),
            P(),
            P(("groups", "dp"), None),
            P(("groups", "dp"), None),
            P(("groups", "dp")),
            P(("groups", "dp"), None),
        ),
        out_specs=(P(("groups", "dp"), None), P(("groups", "dp"), None)),
        check_vma=False,
    )
```

```python
import functools

import jax
import jax.numpy as jnp
from jax import lax
from jax.experimental import pallas as pl
from jax.experimental.pallas import tpu as pltpu
from jax.sharding import PartitionSpec as P

HEADS = 8
HD = 64


def normed(values, gain, shift):
    center = values - jnp.mean(values, axis=-1, keepdims=True)
    spread = jnp.mean(center * center, axis=-1, keepdims=True)
    return center * lax.rsqrt(spread + 1e-12) * gain + shift


def head_sums(weights, seq):
    rows, columns = weights.shape
    lane = lax.broadcasted_iota(jnp.int32, (rows, 2 * seq), 1)
    sums = []
    for start in range(0, columns, 2 * seq):
        pair = weights[:, start : start + 2 * seq]
        first = jnp.sum(jnp.where(lane < seq, pair, 0.0), axis=1, keepdims=True)
        second = jnp.sum(jnp.where(lane < seq, 0.0, pair), axis=1, keepdims=True)
        sums.append(jnp.where(lane < seq, first, second))
    return jnp.concatenate(sums, axis=1)


def encode_kernel(*refs):
    count = (len(refs) - 3) // 2
    far, (out, spread), near, arrived = refs[:count], refs[count : count + 2], refs[-count - 1 : -1], refs[-1]
    w_qkv_far, inner = far[-2], HEADS * HD
    copies = [
        pltpu.make_async_copy(source, target, arrived.at[at])
        for at, (source, target) in enumerate(zip(far, near))
        if source is not w_qkv_far
    ]
    lengths, slots, fetched, pos, emb_gain, emb_bias, out_bias, norm_gain, norm_bias, w_qkv, w_out = near
    out_copy = copies.pop()
    thirds = []
    for third in range(3):
        columns = pl.ds(third * inner, inner)
        thirds.append(
            pltpu.make_async_copy(
                w_qkv_far.at[:, columns], w_qkv.at[:, columns], arrived.at[count + third]
            )
        )
    for copy in copies + thirds + [out_copy]:
        copy.start()
    for copy in copies:
        copy.wait()
    passes = out.shape[0]
    size = [lengths[:, p : p + 1] for p in range(passes)]
    tokens, slot_count = slots.shape[0], fetched.shape[0]
    seq = tokens // passes
    spot = lax.broadcasted_iota(jnp.int32, (tokens, slot_count), 1)
    picker = jnp.where(slots[...] == spot, 1.0, 0.0).astype(jnp.bfloat16)
    tok = jnp.dot(picker, fetched[...], preferred_element_type=jnp.float32)
    where_at = pos[...].astype(jnp.float32)
    summed = tok + jnp.concatenate([where_at] * passes, axis=0)
    embedded = normed(summed, emb_gain[...], emb_bias[...]).astype(jnp.bfloat16)
    parts = []
    for third in range(3):
        thirds[third].wait()
        weights = w_qkv[:, third * inner : (third + 1) * inner]
        part = jnp.dot(embedded, weights, preferred_element_type=jnp.float32)
        parts.append(part.astype(jnp.bfloat16))

    block_row = lax.broadcasted_iota(jnp.int32, (HEADS * seq, inner), 0) // seq
    block_col = lax.broadcasted_iota(jnp.int32, (HEADS * seq, inner), 1) // HD
    same = block_row == block_col
    lane = lax.broadcasted_iota(jnp.int32, (seq, HEADS * seq), 1) % seq
    contexts = []
    for p in range(passes):
        query, keys, vals = (part[p * seq : (p + 1) * seq] for part in parts)
        zero = jnp.zeros((), jnp.bfloat16)
        keys = jnp.where(same, jnp.concatenate([keys] * HEADS, axis=0), zero)
        vals = jnp.where(same, jnp.concatenate([vals] * HEADS, axis=0), zero)
        scores = lax.dot_general(
            query, keys, (((1,), (1,)), ((), ())), preferred_element_type=jnp.float32
        ) * HD ** (-0.5)
        weights = jnp.where(lane < size[p], jnp.exp(scores), 0.0)
        probs = (weights / head_sums(weights, seq)).astype(jnp.bfloat16)
        contexts.append(jnp.dot(probs, vals, preferred_element_type=jnp.float32))
    context = jnp.concatenate(contexts, axis=0).astype(jnp.bfloat16)
    out_copy.wait()
    attended = jnp.dot(context, w_out[...], preferred_element_type=jnp.float32) + out_bias[...]
    hidden = normed(embedded.astype(jnp.float32) + attended, norm_gain[...], norm_bias[...])
    row = lax.broadcasted_iota(jnp.int32, (seq, 1), 0)
    for p in range(passes):
        kept = jnp.where(row < size[p], hidden[p * seq : (p + 1) * seq], 0.0)
        pooled = jnp.sum(kept, axis=0, keepdims=True) / size[p].astype(jnp.float32)
        scale = lax.rsqrt(jnp.mean(pooled * pooled, axis=-1, keepdims=True) + 1e-06)
        out[p : p + 1, :] = (pooled * scale).astype(jnp.bfloat16)
    spread[...] = jnp.broadcast_to(out[...][None], spread.shape)


def encode(
    peers, slots, fetched, lengths, pos_table, emb_gain, emb_bias, w_qkv, w_out, out_bias, norm_gain, norm_bias
):
    width = fetched.shape[1]
    tokens = slots.shape[0]
    passes = lengths.shape[0]
    macs = tokens * width * (fetched.shape[0] + 4 * HEADS * HD)
    operands = (
        lengths[None],
        slots,
        fetched,
        pos_table,
        emb_gain[None],
        emb_bias[None],
        out_bias[None],
        norm_gain[None],
        norm_bias[None],
        w_qkv,
        w_out,
    )
    return pl.pallas_call(
        encode_kernel,
        out_shape=[
            jax.ShapeDtypeStruct((passes, width), jnp.bfloat16),
            jax.ShapeDtypeStruct((peers, passes, width), jnp.bfloat16),
        ],
        in_specs=[pl.BlockSpec(memory_space=pltpu.HBM)] * len(operands),
        out_specs=[pl.BlockSpec(memory_space=pltpu.VMEM)] * 2,
        scratch_shapes=[pltpu.VMEM(operand.shape, operand.dtype) for operand in operands]
        + [pltpu.SemaphoreType.DMA((len(operands) + 3,))],
        compiler_params=pltpu.CompilerParams(vmem_limit_bytes=60 * 1024 * 1024),
        cost_estimate=pl.CostEstimate(
            flops=2 * macs, bytes_accessed=6 * 1024 * 1024, transcendentals=0
        ),
        name="encode",
    )(*operands)


def padded(rows):
    return -(-rows // 16) * 16


def rank_bits(count):
    return max(1, (count - 1).bit_length())


def ranks(kind):
    count = kind.shape[1]
    at = lax.broadcasted_iota(jnp.int32, (count, count), 0)
    by = lax.broadcasted_iota(jnp.int32, (count, count), 1)
    across = jnp.broadcast_to(kind, (count, count))
    down = jnp.sum(jnp.where(at == by, across, 0), axis=1, keepdims=True)
    same = down == across
    rank_row = jnp.sum(jnp.where(same & (at < by), 1, 0), axis=0, keepdims=True)
    rank_col = jnp.sum(jnp.where(same & (by < at), 1, 0), axis=1, keepdims=True)
    return down, rank_row, rank_col


def route_kernel(
    sizes,
    token_ids_far,
    owners_far,
    row_slot_far,
    sibling_far,
    plan,
    token_slot_far,
    code,
    sibling_code,
    *near,
):
    peers, vocab_rows, token_cap, row_cap, pooled = sizes
    token_ids, owners, row_slot, sibling, token_slot, arrived = near
    copies = [
        pltpu.make_async_copy(source, target, arrived.at[at])
        for at, (source, target) in enumerate(
            (
                (token_ids_far, token_ids),
                (owners_far, owners),
                (row_slot_far, row_slot),
                (sibling_far, sibling),
            )
        )
    ]
    for copy in copies:
        copy.start()
    for copy in copies:
        copy.wait()
    ids = jnp.concatenate([token_ids[p : p + 1, :] for p in range(token_ids.shape[0])], axis=1)
    tokens, rows = ids.shape[1], owners.shape[1]
    count = tokens + rows
    edge = (lax.broadcasted_iota(jnp.int32, (peers, tokens), 0) + 1) * vocab_rows
    holder = jnp.sum(jnp.where(ids >= edge, 1, 0), axis=0, keepdims=True)
    values = jnp.concatenate([ids - holder * vocab_rows, row_slot[...]], axis=1)

    kind = jnp.concatenate([holder, owners[...] + peers], axis=1)
    down, rank_row, rank_col = ranks(kind)

    code[...] = owners[...] * 2 ** rank_bits(rows) + rank_row[:, tokens:]
    sibling_code[...] = sibling[...] * 2 ** rank_bits(rows) + ranks(sibling[...])[1]
    goal = jnp.concatenate([holder, owners[...]], axis=1)
    peer = lax.broadcasted_iota(jnp.int32, (peers, count), 0)
    left = jnp.where(peer == goal, values + 1, 0).astype(jnp.float32)
    columns = token_cap + row_cap + pooled
    column = lax.broadcasted_iota(jnp.int32, (count, columns), 1)
    entry = lax.broadcasted_iota(jnp.int32, (count, 1), 0)
    first = jnp.where(entry < tokens, rank_col, rank_col + token_cap)
    second = entry - (count - pooled) + token_cap + row_cap
    second = jnp.where(entry < count - pooled, -1, second)
    right = jnp.where((column == first) | (column == second), 1.0, 0.0)
    filled = jnp.dot(
        left, right, preferred_element_type=jnp.float32, precision=lax.Precision.HIGHEST
    )
    filled = filled.astype(jnp.int32) - 1
    for p in range(peers):
        plan[p, :, :rows] = code[...]
        plan[p, :, rows:] = filled[p : p + 1]
    token_slot[...] = down[:tokens] * token_cap + rank_col[:tokens]
    send = pltpu.make_async_copy(token_slot, token_slot_far, arrived.at[4])
    send.start()
    send.wait()


def route(token_ids, owners, row_slot, sibling_owners, sizes):
    peers, _, token_cap, row_cap, pooled = sizes
    passes, seq_len = token_ids.shape
    rows = owners.shape[1]
    ints = lambda *shape: jax.ShapeDtypeStruct(shape, jnp.int32)
    return pl.pallas_call(
        functools.partial(route_kernel, sizes),
        out_shape=[
            ints(peers, 1, rows + token_cap + row_cap + pooled),
            ints(passes * seq_len, 1),
            ints(1, rows),
            ints(1, rows),
        ],
        in_specs=[pl.BlockSpec(memory_space=pltpu.HBM)] * 4,
        out_specs=[
            pl.BlockSpec(memory_space=pltpu.VMEM),
            pl.BlockSpec(memory_space=pltpu.HBM),
            pl.BlockSpec(memory_space=pltpu.VMEM),
            pl.BlockSpec(memory_space=pltpu.VMEM),
        ],
        scratch_shapes=[
            pltpu.VMEM(token_ids.shape, jnp.int32),
            pltpu.VMEM(owners.shape, jnp.int32),
            pltpu.VMEM(row_slot.shape, jnp.int32),
            pltpu.VMEM(owners.shape, jnp.int32),
            pltpu.VMEM((passes * seq_len, 1), jnp.int32),
            pltpu.SemaphoreType.DMA((5,)),
        ],
        compiler_params=pltpu.CompilerParams(vmem_limit_bytes=60 * 1024 * 1024),
        name="route",
    )(token_ids, owners, row_slot, sibling_owners)


def pack_kernel(half, row_cap, count, picks, pieces, rest, *refs):
    me = lax.axis_index("dp")
    operands = 2 + 2 * pieces
    far, refs = refs[:operands], refs[operands:]
    steps = half // 2
    outs, refs = refs[: steps + bool(rest)], refs[steps + bool(rest) :]
    near, (blocks, tail, arrived, left) = refs[:operands], refs[operands:]
    size = blocks.shape[0] // steps
    copies = [
        pltpu.make_async_copy(far[at], near[at], arrived.at[at]) for at in range(operands)
    ]
    for copy in copies:
        copy.start()
    for copy in copies[:2]:
        copy.wait()
    if size > 2 * row_cap:
        blocks[...] = jnp.zeros(blocks.shape, blocks.dtype)
    for source in range(2):
        if picks is None:
            code = near[source][...]
        else:
            code = near[source][me ^ picks[source], :, :count]
        bits = rank_bits(count)
        owner, rank = code >> bits, code & (2**bits - 1)
        fits = ((owner ^ me) & (1 | half)) == 0
        chip = ((owner ^ me) & (half - 1)) >> 1
        slot = jnp.where(fits, chip * row_cap + rank, -1)
        packed, at = 0.0, 0
        for piece in range(2 + source * pieces, 2 + (source + 1) * pieces):
            rows = near[piece]
            spot = lax.broadcasted_iota(jnp.int32, (steps * row_cap, rows.shape[0]), 0)
            table = jnp.where(slot[:, at : at + rows.shape[0]] == spot, 1.0, 0.0)
            copies[piece].wait()
            packed += jnp.dot(
                table.astype(jnp.bfloat16), rows[...], preferred_element_type=jnp.float32
            )
            at += rows.shape[0]
        packed = packed.astype(jnp.bfloat16)
        for step in range(steps):
            first = step * size + source * row_cap
            blocks[first : first + row_cap, :] = packed[step * row_cap : (step + 1) * row_cap]
    sends = [
        pltpu.make_async_copy(
            blocks.at[pl.ds(step * size, size)], outs[step], left.at[step]
        )
        for step in range(steps)
    ]
    if rest:
        tail[...] = near[2][near[2].shape[0] - rest :, :]
        sends.append(pltpu.make_async_copy(tail, outs[steps], left.at[steps]))
    for send in sends:
        send.start()
    for send in sends:
        send.wait()


def pack_rows(codes_a, codes_b, rows_a, rows_b, half, row_cap, count, picks=None, rest=0):
    width = rows_a[0].shape[1]
    total = sum(piece.shape[0] for piece in rows_a)
    steps = half // 2
    size = padded(2 * row_cap)
    operands = (codes_a, codes_b, *rows_a, *rows_b)
    shapes = [(size, width)] * steps + [(rest, width)] * bool(rest)
    return pl.pallas_call(
        functools.partial(pack_kernel, half, row_cap, count, picks, len(rows_a), rest),
        out_shape=[jax.ShapeDtypeStruct(shape, jnp.bfloat16) for shape in shapes],
        in_specs=[pl.BlockSpec(memory_space=pltpu.HBM)] * len(operands),
        out_specs=[pl.BlockSpec(memory_space=pltpu.HBM)] * len(shapes),
        scratch_shapes=[
            *(pltpu.VMEM(operand.shape, operand.dtype) for operand in operands),
            pltpu.VMEM((steps * size, width), jnp.bfloat16),
            pltpu.VMEM((max(rest, 16), width), jnp.bfloat16),
            pltpu.SemaphoreType.DMA((len(operands),)),
            pltpu.SemaphoreType.DMA((len(shapes),)),
        ],
        compiler_params=pltpu.CompilerParams(vmem_limit_bytes=60 * 1024 * 1024),
        cost_estimate=pl.CostEstimate(
            flops=4 * steps * row_cap * width * total,
            bytes_accessed=4 * width * (total + steps * row_cap),
            transcendentals=0,
        ),
        name="pack",
    )(*operands)


def onehot(where_to, first, count):
    centre = lax.broadcasted_iota(jnp.int32, (count, where_to.shape[1]), 0) + first
    return jnp.where(centre == where_to, 1.0, 0.0)


BLOCK = 128


def early_kernel(places_far, centroids_far, *rest):
    pieces, (out_far, share_far, places, rows, centroids, out, share, arrived, left) = rest[:-9], rest[-9:]
    size = pieces[0].shape[0]
    steps = centroids.shape[0] // BLOCK
    copies = [pltpu.make_async_copy(places_far, places, arrived.at[0])]
    for at, piece in enumerate(pieces):
        copies.append(
            pltpu.make_async_copy(piece, rows.at[pl.ds(at * size, size)], arrived.at[1 + at])
        )
    loads = []
    for step in range(steps):
        block = pl.ds(step * BLOCK, BLOCK)
        loads.append(
            pltpu.make_async_copy(
                centroids_far.at[block], centroids.at[block], arrived.at[1 + len(pieces) + step]
            )
        )
    for copy in copies + loads:
        copy.start()
    for copy in copies:
        copy.wait()
    sends = []
    for step in range(steps):
        block = pl.ds(step * BLOCK, BLOCK)
        hot = onehot(places[...], step * BLOCK, BLOCK)
        counts = jnp.sum(hot, axis=1, keepdims=True)
        scale = jnp.where(counts > 0, 1.0 / jnp.maximum(counts, 1.0), 0.0)
        sums = jnp.dot(
            hot[:, : rows.shape[0]].astype(jnp.bfloat16),
            rows[...],
            preferred_element_type=jnp.float32,
        )
        loads[step].wait()
        out[block, :] = jnp.where(counts > 0, sums * scale, centroids[block, :])
        share[block, :] = jnp.broadcast_to(scale, (BLOCK, share.shape[1]))
        sends.append(pltpu.make_async_copy(out.at[block], out_far.at[block], left.at[step]))
        sends[-1].start()
    sends.append(pltpu.make_async_copy(share, share_far, left.at[steps]))
    sends[-1].start()
    for send in sends:
        send.wait()


def late_kernel(places_far, late_far, spread_far, share_far, early_far, *rest):
    pieces, rest = rest[:-10], rest[-10:]
    out_far, places, late, spread, share, rows, early, out, arrived, left = rest
    size, passes = pieces[0].shape[0], spread.shape[1]
    steps = early.shape[0] // BLOCK
    loads = [
        pltpu.make_async_copy(source, target, arrived.at[at])
        for at, (source, target) in enumerate(
            ((places_far, places), (late_far, late), (spread_far, spread), (share_far, share))
        )
    ]
    for at, piece in enumerate(pieces):
        loads.append(
            pltpu.make_async_copy(piece, rows.at[pl.ds(at * size, size)], arrived.at[4 + at])
        )
    starts = []
    for step in range(steps):
        block = pl.ds(step * BLOCK, BLOCK)
        starts.append(
            pltpu.make_async_copy(
                early_far.at[block], early.at[block], arrived.at[len(loads) + step]
            )
        )
    for copy in loads + starts:
        copy.start()
    for copy in loads:
        copy.wait()
    top = len(pieces) * size
    for peer in range(spread.shape[0]):
        rows[top + peer * passes : top + (peer + 1) * passes, :] = spread[peer]
    where_to = jnp.concatenate([places[:, places.shape[1] - top :], late[...]], axis=1)
    sends = []
    for step in range(steps):
        block = pl.ds(step * BLOCK, BLOCK)
        hot = onehot(where_to, step * BLOCK, BLOCK).astype(jnp.bfloat16)
        sums = jnp.dot(hot, rows[...], preferred_element_type=jnp.float32)
        starts[step].wait()
        out[block, :] = early[block, :] + sums * share[block, :1]
        sends.append(pltpu.make_async_copy(out.at[block], out_far.at[block], left.at[step]))
        sends[-1].start()
    for send in sends:
        send.wait()


def early_update(places, centroids, pieces):
    centre_count, width = centroids.shape
    row_total = sum(piece.shape[0] for piece in pieces)
    wide = pltpu.VMEM(centroids.shape, jnp.float32)
    thin = (centre_count, 128)
    steps = centre_count // BLOCK
    return pl.pallas_call(
        early_kernel,
        out_shape=[
            jax.ShapeDtypeStruct(centroids.shape, jnp.float32),
            jax.ShapeDtypeStruct(thin, jnp.float32),
        ],
        in_specs=[pl.BlockSpec(memory_space=pl.ANY)] * (2 + len(pieces)),
        out_specs=[pl.BlockSpec(memory_space=pltpu.HBM)] * 2,
        scratch_shapes=[
            pltpu.VMEM(places.shape, jnp.int32),
            pltpu.VMEM((row_total, width), jnp.bfloat16),
            wide,
            wide,
            pltpu.VMEM(thin, jnp.float32),
            pltpu.SemaphoreType.DMA((1 + len(pieces) + steps,)),
            pltpu.SemaphoreType.DMA((steps + 1,)),
        ],
        compiler_params=pltpu.CompilerParams(vmem_limit_bytes=60 * 1024 * 1024),
        cost_estimate=pl.CostEstimate(
            flops=2 * centre_count * width * row_total,
            bytes_accessed=8 * centre_count * width,
            transcendentals=0,
        ),
        name="early",
    )(places, centroids, *pieces)


def late_update(places, late, spread, share, early, pieces):
    centre_count, width = early.shape
    row_total = sum(piece.shape[0] for piece in pieces) + late.shape[1]
    wide = pltpu.VMEM(early.shape, jnp.float32)
    steps = centre_count // BLOCK
    return pl.pallas_call(
        late_kernel,
        out_shape=jax.ShapeDtypeStruct(early.shape, jnp.float32),
        in_specs=[pl.BlockSpec(memory_space=pltpu.HBM)] * (5 + len(pieces)),
        out_specs=pl.BlockSpec(memory_space=pltpu.HBM),
        scratch_shapes=[
            pltpu.VMEM(places.shape, jnp.int32),
            pltpu.VMEM(late.shape, jnp.int32),
            pltpu.VMEM(spread.shape, jnp.bfloat16),
            pltpu.VMEM(share.shape, jnp.float32),
            pltpu.VMEM((row_total, width), jnp.bfloat16),
            wide,
            wide,
            pltpu.SemaphoreType.DMA((4 + len(pieces) + steps,)),
            pltpu.SemaphoreType.DMA((steps,)),
        ],
        compiler_params=pltpu.CompilerParams(vmem_limit_bytes=60 * 1024 * 1024),
        cost_estimate=pl.CostEstimate(
            flops=2 * centre_count * width * row_total,
            bytes_accessed=8 * centre_count * width,
            transcendentals=0,
        ),
        name="late",
    )(places, late, spread, share, early, *pieces)


def shards(
    token_ids,
    lengths,
    word_table,
    pos_table,
    emb_gain,
    emb_bias,
    w_qkv,
    w_out,
    out_bias,
    norm_gain,
    norm_bias,
    stored_rows,
    row_owner,
    row_slot,
    centroids,
):
    peer_count = lax.axis_size("dp")
    half = peer_count // 2
    width = word_table.shape[1]
    vocab_rows = word_table.shape[0]
    passes, seq_len = token_ids.shape
    token_count = passes * seq_len
    row_count = row_slot.shape[0]
    store_count = stored_rows.shape[0]
    token_cap = max(2, 3 * token_count // peer_count)
    row_cap = max(2, 3 * row_count // peer_count)

    across = [(i, i ^ half) for i in range(peer_count)]
    beside = [(i, i ^ 1) for i in range(peer_count)]

    def hand_on(blocks):
        got = [blocks[0]]
        for step in range(1, len(blocks)):
            moves = [(i, i ^ (2 * step)) for i in range(peer_count)]
            got.append(lax.ppermute(blocks[step], "dp", moves))
        return got

    ahead = store_count * 2 // 3 // 16 * 16
    sibling_rows = lax.ppermute(stored_rows, "dp", beside)
    first_rows = lax.ppermute(stored_rows[:ahead], "dp", across)
    sizes = (peer_count, vocab_rows, token_cap, row_cap, row_count - store_count)
    owners = row_owner.reshape(1, row_count)
    sibling_owners = lax.ppermute(owners, "dp", beside)
    plan, token_slot, code, sibling_code = route(
        token_ids, owners, row_slot[None], sibling_owners, sizes
    )
    plan, sibling_rows = lax.optimization_barrier((plan, sibling_rows))
    codes = lax.all_to_all(plan, "dp", split_axis=0, concat_axis=0, tiled=True)
    *blocks, last_rows = pack_rows(
        code,
        sibling_code,
        [stored_rows],
        [sibling_rows],
        half,
        row_cap,
        row_count,
        rest=store_count - ahead,
    )
    last_rows = lax.ppermute(last_rows, "dp", across)
    own_half = hand_on(blocks)
    plan = codes[:, 0, row_count:]
    wanted = plan[:, :token_cap].reshape(peer_count * token_cap)
    chosen = wanted[:, None] == jnp.arange(vocab_rows, dtype=jnp.int32)[None, :]
    found = jnp.dot(
        chosen.astype(jnp.bfloat16), word_table, preferred_element_type=jnp.float32
    ).astype(jnp.bfloat16)
    found, first_rows, last_rows, own_half[:2] = lax.optimization_barrier(
        (found, first_rows, last_rows, own_half[:2])
    )
    fetched = lax.all_to_all(
        found.reshape(peer_count, token_cap, width), "dp", split_axis=0, concat_axis=0, tiled=True
    ).reshape(peer_count * token_cap, width)

    partner_rows = [first_rows, last_rows]
    far_rows = [lax.ppermute(rows, "dp", beside) for rows in partner_rows]
    picks = (half, half ^ 1)
    blocks = pack_rows(codes, codes, partner_rows, far_rows, half, row_cap, row_count, picks)
    other_half = hand_on(blocks)
    sources = lax.axis_index("dp") ^ jnp.arange(peer_count, dtype=jnp.int32)
    got_places = plan[:, token_cap : token_cap + row_cap][sources].reshape(half, 2 * row_cap)
    spare = padded(2 * row_cap) - 2 * row_cap
    got_places = jnp.pad(got_places, ((0, 0), (0, spare)), constant_values=-1).reshape(1, -1)
    means, share = early_update(got_places, centroids, own_half[:2])
    late_places = plan[:, token_cap + row_cap :].reshape(1, -1)
    fetched, means, share, got_places, late_places = lax.optimization_barrier(
        (fetched, means, share, got_places, late_places)
    )

    passage_embed, spread = encode(
        peer_count,
        token_slot,
        fetched,
        lengths,
        pos_table,
        emb_gain,
        emb_bias,
        w_qkv,
        w_out,
        out_bias,
        norm_gain,
        norm_bias,
    )
    all_embeds = lax.all_to_all(
        spread, "dp", split_axis=0, concat_axis=0, tiled=True
    )
    pieces = own_half[2:] + other_half
    new_centroids = late_update(got_places, late_places, all_embeds, share, means, pieces)
    return (passage_embed, new_centroids)


def solution(mesh):
    return jax.shard_map(
        shards,
        mesh=mesh,
        in_specs=(
            P(("groups", "dp"), None),
            P(("groups", "dp")),
            P("dp", None),
            P(),
            P(),
            P(),
            P(),
            P(),
            P(),
            P(),
            P(),
            P(("groups", "dp"), None),
            P(("groups", "dp"), None),
            P(("groups", "dp")),
            P(("groups", "dp"), None),
        ),
        out_specs=(P(("groups", "dp"), None), P(("groups", "dp"), None)),
        check_vma=False,
    )
```

```python
import functools

import jax
import jax.numpy as jnp
from jax import lax
from jax.experimental import pallas as pl
from jax.experimental.pallas import tpu as pltpu
from jax.sharding import PartitionSpec as P

HEADS = 8
HD = 64


def normed(values, gain, shift):
    center = values - jnp.mean(values, axis=-1, keepdims=True)
    spread = jnp.mean(center * center, axis=-1, keepdims=True)
    return center * lax.rsqrt(spread + 1e-12) * gain + shift


def head_sums(weights, seq):
    rows, columns = weights.shape
    lane = lax.broadcasted_iota(jnp.int32, (rows, 2 * seq), 1)
    sums = []
    for start in range(0, columns, 2 * seq):
        pair = weights[:, start : start + 2 * seq]
        first = jnp.sum(jnp.where(lane < seq, pair, 0.0), axis=1, keepdims=True)
        second = jnp.sum(jnp.where(lane < seq, 0.0, pair), axis=1, keepdims=True)
        sums.append(jnp.where(lane < seq, first, second))
    return jnp.concatenate(sums, axis=1)


def encode_kernel(*refs):
    count = (len(refs) - 3) // 2
    far, (out, spread), near, arrived = refs[:count], refs[count : count + 2], refs[-count - 1 : -1], refs[-1]
    w_qkv_far, inner = far[-2], HEADS * HD
    copies = [
        pltpu.make_async_copy(source, target, arrived.at[at])
        for at, (source, target) in enumerate(zip(far, near))
        if source is not w_qkv_far
    ]
    lengths, slots, fetched, pos, emb_gain, emb_bias, out_bias, norm_gain, norm_bias, w_qkv, w_out = near
    out_copy = copies.pop()
    thirds = []
    for third in range(3):
        columns = pl.ds(third * inner, inner)
        thirds.append(
            pltpu.make_async_copy(
                w_qkv_far.at[:, columns], w_qkv.at[:, columns], arrived.at[count + third]
            )
        )
    for copy in copies + thirds + [out_copy]:
        copy.start()
    for copy in copies:
        copy.wait()
    passes = out.shape[0]
    size = [lengths[:, p : p + 1] for p in range(passes)]
    tokens, slot_count = slots.shape[0], fetched.shape[0]
    seq = tokens // passes
    spot = lax.broadcasted_iota(jnp.int32, (tokens, slot_count), 1)
    picker = jnp.where(slots[...] == spot, 1.0, 0.0).astype(jnp.bfloat16)
    tok = jnp.dot(picker, fetched[...], preferred_element_type=jnp.float32)
    where_at = pos[...].astype(jnp.float32)
    summed = tok + jnp.concatenate([where_at] * passes, axis=0)
    embedded = normed(summed, emb_gain[...], emb_bias[...]).astype(jnp.bfloat16)
    parts = []
    for third in range(3):
        thirds[third].wait()
        weights = w_qkv[:, third * inner : (third + 1) * inner]
        part = jnp.dot(embedded, weights, preferred_element_type=jnp.float32)
        parts.append(part.astype(jnp.bfloat16))

    block_row = lax.broadcasted_iota(jnp.int32, (HEADS * seq, inner), 0) // seq
    block_col = lax.broadcasted_iota(jnp.int32, (HEADS * seq, inner), 1) // HD
    same = block_row == block_col
    lane = lax.broadcasted_iota(jnp.int32, (seq, HEADS * seq), 1) % seq
    contexts = []
    for p in range(passes):
        query, keys, vals = (part[p * seq : (p + 1) * seq] for part in parts)
        zero = jnp.zeros((), jnp.bfloat16)
        keys = jnp.where(same, jnp.concatenate([keys] * HEADS, axis=0), zero)
        vals = jnp.where(same, jnp.concatenate([vals] * HEADS, axis=0), zero)
        scores = lax.dot_general(
            query, keys, (((1,), (1,)), ((), ())), preferred_element_type=jnp.float32
        ) * HD ** (-0.5)
        weights = jnp.where(lane < size[p], jnp.exp(scores), 0.0)
        probs = (weights / head_sums(weights, seq)).astype(jnp.bfloat16)
        contexts.append(jnp.dot(probs, vals, preferred_element_type=jnp.float32))
    context = jnp.concatenate(contexts, axis=0).astype(jnp.bfloat16)
    out_copy.wait()
    attended = jnp.dot(context, w_out[...], preferred_element_type=jnp.float32) + out_bias[...]
    hidden = normed(embedded.astype(jnp.float32) + attended, norm_gain[...], norm_bias[...])
    row = lax.broadcasted_iota(jnp.int32, (seq, 1), 0)
    for p in range(passes):
        kept = jnp.where(row < size[p], hidden[p * seq : (p + 1) * seq], 0.0)
        pooled = jnp.sum(kept, axis=0, keepdims=True) / size[p].astype(jnp.float32)
        scale = lax.rsqrt(jnp.mean(pooled * pooled, axis=-1, keepdims=True) + 1e-06)
        out[p : p + 1, :] = (pooled * scale).astype(jnp.bfloat16)
    spread[...] = jnp.broadcast_to(out[...][None], spread.shape)


def encode(
    peers, slots, fetched, lengths, pos_table, emb_gain, emb_bias, w_qkv, w_out, out_bias, norm_gain, norm_bias
):
    width = fetched.shape[1]
    tokens = slots.shape[0]
    passes = lengths.shape[0]
    macs = tokens * width * (fetched.shape[0] + 4 * HEADS * HD)
    operands = (
        lengths[None],
        slots,
        fetched,
        pos_table,
        emb_gain[None],
        emb_bias[None],
        out_bias[None],
        norm_gain[None],
        norm_bias[None],
        w_qkv,
        w_out,
    )
    return pl.pallas_call(
        encode_kernel,
        out_shape=[
            jax.ShapeDtypeStruct((passes, width), jnp.bfloat16),
            jax.ShapeDtypeStruct((peers, passes, width), jnp.bfloat16),
        ],
        in_specs=[pl.BlockSpec(memory_space=pltpu.HBM)] * len(operands),
        out_specs=[pl.BlockSpec(memory_space=pltpu.VMEM)] * 2,
        scratch_shapes=[pltpu.VMEM(operand.shape, operand.dtype) for operand in operands]
        + [pltpu.SemaphoreType.DMA((len(operands) + 3,))],
        compiler_params=pltpu.CompilerParams(vmem_limit_bytes=60 * 1024 * 1024),
        cost_estimate=pl.CostEstimate(
            flops=2 * macs, bytes_accessed=6 * 1024 * 1024, transcendentals=0
        ),
        name="encode",
    )(*operands)


def padded(rows):
    return -(-rows // 16) * 16


def rank_bits(count):
    return max(1, (count - 1).bit_length())


def ranks(kind):
    count = kind.shape[1]
    at = lax.broadcasted_iota(jnp.int32, (count, count), 0)
    by = lax.broadcasted_iota(jnp.int32, (count, count), 1)
    across = jnp.broadcast_to(kind, (count, count))
    down = jnp.sum(jnp.where(at == by, across, 0), axis=1, keepdims=True)
    same = down == across
    rank_row = jnp.sum(jnp.where(same & (at < by), 1, 0), axis=0, keepdims=True)
    rank_col = jnp.sum(jnp.where(same & (by < at), 1, 0), axis=1, keepdims=True)
    return down, rank_row, rank_col


def route_kernel(
    sizes,
    token_ids_far,
    owners_far,
    row_slot_far,
    sibling_far,
    plan,
    token_slot_far,
    code,
    sibling_code,
    *near,
):
    peers, vocab_rows, token_cap, row_cap, pooled = sizes
    token_ids, owners, row_slot, sibling, token_slot, arrived = near
    copies = [
        pltpu.make_async_copy(source, target, arrived.at[at])
        for at, (source, target) in enumerate(
            (
                (token_ids_far, token_ids),
                (owners_far, owners),
                (row_slot_far, row_slot),
                (sibling_far, sibling),
            )
        )
    ]
    for copy in copies:
        copy.start()
    for copy in copies:
        copy.wait()
    ids = jnp.concatenate([token_ids[p : p + 1, :] for p in range(token_ids.shape[0])], axis=1)
    tokens, rows = ids.shape[1], owners.shape[1]
    count = tokens + rows
    edge = (lax.broadcasted_iota(jnp.int32, (peers, tokens), 0) + 1) * vocab_rows
    holder = jnp.sum(jnp.where(ids >= edge, 1, 0), axis=0, keepdims=True)
    values = jnp.concatenate([ids - holder * vocab_rows, row_slot[...]], axis=1)

    kind = jnp.concatenate([holder, owners[...] + peers], axis=1)
    down, rank_row, rank_col = ranks(kind)

    code[...] = owners[...] * 2 ** rank_bits(rows) + rank_row[:, tokens:]
    sibling_code[...] = sibling[...] * 2 ** rank_bits(rows) + ranks(sibling[...])[1]
    goal = jnp.concatenate([holder, owners[...]], axis=1)
    peer = lax.broadcasted_iota(jnp.int32, (peers, count), 0)
    left = jnp.where(peer == goal, values + 1, 0).astype(jnp.float32)
    columns = token_cap + row_cap + pooled
    column = lax.broadcasted_iota(jnp.int32, (count, columns), 1)
    entry = lax.broadcasted_iota(jnp.int32, (count, 1), 0)
    first = jnp.where(entry < tokens, rank_col, rank_col + token_cap)
    second = entry - (count - pooled) + token_cap + row_cap
    second = jnp.where(entry < count - pooled, -1, second)
    right = jnp.where((column == first) | (column == second), 1.0, 0.0)
    filled = jnp.dot(
        left, right, preferred_element_type=jnp.float32, precision=lax.Precision.HIGHEST
    )
    filled = filled.astype(jnp.int32) - 1
    for p in range(peers):
        plan[p, :, :rows] = code[...]
        plan[p, :, rows:] = filled[p : p + 1]
    token_slot[...] = down[:tokens] * token_cap + rank_col[:tokens]
    send = pltpu.make_async_copy(token_slot, token_slot_far, arrived.at[4])
    send.start()
    send.wait()


def route(token_ids, owners, row_slot, sibling_owners, sizes):
    peers, _, token_cap, row_cap, pooled = sizes
    passes, seq_len = token_ids.shape
    rows = owners.shape[1]
    ints = lambda *shape: jax.ShapeDtypeStruct(shape, jnp.int32)
    return pl.pallas_call(
        functools.partial(route_kernel, sizes),
        out_shape=[
            ints(peers, 1, rows + token_cap + row_cap + pooled),
            ints(passes * seq_len, 1),
            ints(1, rows),
            ints(1, rows),
        ],
        in_specs=[pl.BlockSpec(memory_space=pltpu.HBM)] * 4,
        out_specs=[
            pl.BlockSpec(memory_space=pltpu.VMEM),
            pl.BlockSpec(memory_space=pltpu.HBM),
            pl.BlockSpec(memory_space=pltpu.VMEM),
            pl.BlockSpec(memory_space=pltpu.VMEM),
        ],
        scratch_shapes=[
            pltpu.VMEM(token_ids.shape, jnp.int32),
            pltpu.VMEM(owners.shape, jnp.int32),
            pltpu.VMEM(row_slot.shape, jnp.int32),
            pltpu.VMEM(owners.shape, jnp.int32),
            pltpu.VMEM((passes * seq_len, 1), jnp.int32),
            pltpu.SemaphoreType.DMA((5,)),
        ],
        compiler_params=pltpu.CompilerParams(vmem_limit_bytes=60 * 1024 * 1024),
        name="route",
    )(token_ids, owners, row_slot, sibling_owners)


def pack_kernel(half, row_cap, count, picks, pieces, rest, *refs):
    me = lax.axis_index("dp")
    operands = 2 + 2 * pieces
    far, refs = refs[:operands], refs[operands:]
    steps = half // 2
    outs, refs = refs[: steps + bool(rest)], refs[steps + bool(rest) :]
    near, (blocks, tail, arrived, left) = refs[:operands], refs[operands:]
    size = blocks.shape[0] // steps
    copies = [
        pltpu.make_async_copy(far[at], near[at], arrived.at[at]) for at in range(operands)
    ]
    for copy in copies:
        copy.start()
    for copy in copies[:2]:
        copy.wait()
    if size > 2 * row_cap:
        blocks[...] = jnp.zeros(blocks.shape, blocks.dtype)
    for source in range(2):
        if picks is None:
            code = near[source][...]
        else:
            code = near[source][me ^ picks[source], :, :count]
        bits = rank_bits(count)
        owner, rank = code >> bits, code & (2**bits - 1)
        fits = ((owner ^ me) & (1 | half)) == 0
        chip = ((owner ^ me) & (half - 1)) >> 1
        slot = jnp.where(fits, chip * row_cap + rank, -1)
        packed, at = 0.0, 0
        for piece in range(2 + source * pieces, 2 + (source + 1) * pieces):
            rows = near[piece]
            spot = lax.broadcasted_iota(jnp.int32, (steps * row_cap, rows.shape[0]), 0)
            table = jnp.where(slot[:, at : at + rows.shape[0]] == spot, 1.0, 0.0)
            copies[piece].wait()
            packed += jnp.dot(
                table.astype(jnp.bfloat16), rows[...], preferred_element_type=jnp.float32
            )
            at += rows.shape[0]
        packed = packed.astype(jnp.bfloat16)
        for step in range(steps):
            first = step * size + source * row_cap
            blocks[first : first + row_cap, :] = packed[step * row_cap : (step + 1) * row_cap]
    sends = [
        pltpu.make_async_copy(
            blocks.at[pl.ds(step * size, size)], outs[step], left.at[step]
        )
        for step in range(steps)
    ]
    if rest:
        tail[...] = near[2][near[2].shape[0] - rest :, :]
        sends.append(pltpu.make_async_copy(tail, outs[steps], left.at[steps]))
    for send in sends:
        send.start()
    for send in sends:
        send.wait()


def pack_rows(codes_a, codes_b, rows_a, rows_b, half, row_cap, count, picks=None, rest=0):
    width = rows_a[0].shape[1]
    total = sum(piece.shape[0] for piece in rows_a)
    steps = half // 2
    size = padded(2 * row_cap)
    operands = (codes_a, codes_b, *rows_a, *rows_b)
    shapes = [(size, width)] * steps + [(rest, width)] * bool(rest)
    return pl.pallas_call(
        functools.partial(pack_kernel, half, row_cap, count, picks, len(rows_a), rest),
        out_shape=[jax.ShapeDtypeStruct(shape, jnp.bfloat16) for shape in shapes],
        in_specs=[pl.BlockSpec(memory_space=pltpu.HBM)] * len(operands),
        out_specs=[pl.BlockSpec(memory_space=pltpu.HBM)] * len(shapes),
        scratch_shapes=[
            *(pltpu.VMEM(operand.shape, operand.dtype) for operand in operands),
            pltpu.VMEM((steps * size, width), jnp.bfloat16),
            pltpu.VMEM((max(rest, 16), width), jnp.bfloat16),
            pltpu.SemaphoreType.DMA((len(operands),)),
            pltpu.SemaphoreType.DMA((len(shapes),)),
        ],
        compiler_params=pltpu.CompilerParams(vmem_limit_bytes=60 * 1024 * 1024),
        cost_estimate=pl.CostEstimate(
            flops=4 * steps * row_cap * width * total,
            bytes_accessed=4 * width * (total + steps * row_cap),
            transcendentals=0,
        ),
        name="pack",
    )(*operands)


def onehot(where_to, first, count):
    centre = lax.broadcasted_iota(jnp.int32, (count, where_to.shape[1]), 0) + first
    return jnp.where(centre == where_to, 1.0, 0.0)


BLOCK = 128


def early_kernel(places_far, centroids_far, *rest):
    pieces, (out_far, share_far, places, rows, centroids, out, share, arrived, left) = rest[:-9], rest[-9:]
    size = pieces[0].shape[0]
    steps = centroids.shape[0] // BLOCK
    copies = [pltpu.make_async_copy(places_far, places, arrived.at[0])]
    for at, piece in enumerate(pieces):
        copies.append(
            pltpu.make_async_copy(piece, rows.at[pl.ds(at * size, size)], arrived.at[1 + at])
        )
    loads = []
    for step in range(steps):
        block = pl.ds(step * BLOCK, BLOCK)
        loads.append(
            pltpu.make_async_copy(
                centroids_far.at[block], centroids.at[block], arrived.at[1 + len(pieces) + step]
            )
        )
    for copy in copies + loads:
        copy.start()
    for copy in copies:
        copy.wait()
    sends = []
    for step in range(steps):
        block = pl.ds(step * BLOCK, BLOCK)
        hot = onehot(places[...], step * BLOCK, BLOCK)
        counts = jnp.sum(hot, axis=1, keepdims=True)
        scale = jnp.where(counts > 0, 1.0 / jnp.maximum(counts, 1.0), 0.0)
        sums = jnp.dot(
            hot[:, : rows.shape[0]].astype(jnp.bfloat16),
            rows[...],
            preferred_element_type=jnp.float32,
        )
        loads[step].wait()
        out[block, :] = jnp.where(counts > 0, sums * scale, centroids[block, :])
        share[block, :] = jnp.broadcast_to(scale, (BLOCK, share.shape[1]))
        sends.append(pltpu.make_async_copy(out.at[block], out_far.at[block], left.at[step]))
        sends[-1].start()
    sends.append(pltpu.make_async_copy(share, share_far, left.at[steps]))
    sends[-1].start()
    for send in sends:
        send.wait()


def late_kernel(places_far, late_far, spread_far, share_far, early_far, *rest):
    pieces, rest = rest[:-10], rest[-10:]
    out_far, places, late, spread, share, rows, early, out, arrived, left = rest
    size, passes = pieces[0].shape[0], spread.shape[1]
    steps = early.shape[0] // BLOCK
    loads = [
        pltpu.make_async_copy(source, target, arrived.at[at])
        for at, (source, target) in enumerate(
            ((places_far, places), (late_far, late), (spread_far, spread), (share_far, share))
        )
    ]
    for at, piece in enumerate(pieces):
        loads.append(
            pltpu.make_async_copy(piece, rows.at[pl.ds(at * size, size)], arrived.at[4 + at])
        )
    starts = []
    for step in range(steps):
        block = pl.ds(step * BLOCK, BLOCK)
        starts.append(
            pltpu.make_async_copy(
                early_far.at[block], early.at[block], arrived.at[len(loads) + step]
            )
        )
    for copy in loads + starts:
        copy.start()
    for copy in loads:
        copy.wait()
    top = len(pieces) * size
    for peer in range(spread.shape[0]):
        rows[top + peer * passes : top + (peer + 1) * passes, :] = spread[peer]
    where_to = jnp.concatenate([places[:, places.shape[1] - top :], late[...]], axis=1)
    sends = []
    for step in range(steps):
        block = pl.ds(step * BLOCK, BLOCK)
        hot = onehot(where_to, step * BLOCK, BLOCK).astype(jnp.bfloat16)
        sums = jnp.dot(hot, rows[...], preferred_element_type=jnp.float32)
        starts[step].wait()
        out[block, :] = early[block, :] + sums * share[block, :1]
        sends.append(pltpu.make_async_copy(out.at[block], out_far.at[block], left.at[step]))
        sends[-1].start()
    for send in sends:
        send.wait()


def early_update(places, centroids, pieces):
    centre_count, width = centroids.shape
    row_total = sum(piece.shape[0] for piece in pieces)
    wide = pltpu.VMEM(centroids.shape, jnp.float32)
    thin = (centre_count, 128)
    steps = centre_count // BLOCK
    return pl.pallas_call(
        early_kernel,
        out_shape=[
            jax.ShapeDtypeStruct(centroids.shape, jnp.float32),
            jax.ShapeDtypeStruct(thin, jnp.float32),
        ],
        in_specs=[pl.BlockSpec(memory_space=pl.ANY)] * (2 + len(pieces)),
        out_specs=[pl.BlockSpec(memory_space=pltpu.HBM)] * 2,
        scratch_shapes=[
            pltpu.VMEM(places.shape, jnp.int32),
            pltpu.VMEM((row_total, width), jnp.bfloat16),
            wide,
            wide,
            pltpu.VMEM(thin, jnp.float32),
            pltpu.SemaphoreType.DMA((1 + len(pieces) + steps,)),
            pltpu.SemaphoreType.DMA((steps + 1,)),
        ],
        compiler_params=pltpu.CompilerParams(vmem_limit_bytes=60 * 1024 * 1024),
        cost_estimate=pl.CostEstimate(
            flops=2 * centre_count * width * row_total,
            bytes_accessed=18 * centre_count * width,
            transcendentals=0,
        ),
        name="early",
    )(places, centroids, *pieces)


def late_update(places, late, spread, share, early, pieces):
    centre_count, width = early.shape
    row_total = sum(piece.shape[0] for piece in pieces) + late.shape[1]
    wide = pltpu.VMEM(early.shape, jnp.float32)
    steps = centre_count // BLOCK
    return pl.pallas_call(
        late_kernel,
        out_shape=jax.ShapeDtypeStruct(early.shape, jnp.float32),
        in_specs=[pl.BlockSpec(memory_space=pltpu.HBM)] * (5 + len(pieces)),
        out_specs=pl.BlockSpec(memory_space=pltpu.HBM),
        scratch_shapes=[
            pltpu.VMEM(places.shape, jnp.int32),
            pltpu.VMEM(late.shape, jnp.int32),
            pltpu.VMEM(spread.shape, jnp.bfloat16),
            pltpu.VMEM(share.shape, jnp.float32),
            pltpu.VMEM((row_total, width), jnp.bfloat16),
            wide,
            wide,
            pltpu.SemaphoreType.DMA((4 + len(pieces) + steps,)),
            pltpu.SemaphoreType.DMA((steps,)),
        ],
        compiler_params=pltpu.CompilerParams(vmem_limit_bytes=60 * 1024 * 1024),
        cost_estimate=pl.CostEstimate(
            flops=2 * centre_count * width * row_total,
            bytes_accessed=8 * centre_count * width,
            transcendentals=0,
        ),
        name="late",
    )(places, late, spread, share, early, *pieces)


def shards(
    token_ids,
    lengths,
    word_table,
    pos_table,
    emb_gain,
    emb_bias,
    w_qkv,
    w_out,
    out_bias,
    norm_gain,
    norm_bias,
    stored_rows,
    row_owner,
    row_slot,
    centroids,
):
    peer_count = lax.axis_size("dp")
    half = peer_count // 2
    width = word_table.shape[1]
    vocab_rows = word_table.shape[0]
    passes, seq_len = token_ids.shape
    token_count = passes * seq_len
    row_count = row_slot.shape[0]
    store_count = stored_rows.shape[0]
    token_cap = max(2, 3 * token_count // peer_count)
    row_cap = max(2, 3 * row_count // peer_count)

    across = [(i, i ^ half) for i in range(peer_count)]
    beside = [(i, i ^ 1) for i in range(peer_count)]

    def hand_on(blocks):
        got = [blocks[0]]
        for step in range(1, len(blocks)):
            moves = [(i, i ^ (2 * step)) for i in range(peer_count)]
            got.append(lax.ppermute(blocks[step], "dp", moves))
        return got

    ahead = store_count * 2 // 3 // 16 * 16
    sibling_rows = lax.ppermute(stored_rows, "dp", beside)
    first_rows = lax.ppermute(stored_rows[:ahead], "dp", across)
    sizes = (peer_count, vocab_rows, token_cap, row_cap, row_count - store_count)
    owners = row_owner.reshape(1, row_count)
    sibling_owners = lax.ppermute(owners, "dp", beside)
    plan, token_slot, code, sibling_code = route(
        token_ids, owners, row_slot[None], sibling_owners, sizes
    )
    plan, sibling_rows = lax.optimization_barrier((plan, sibling_rows))
    codes = lax.all_to_all(plan, "dp", split_axis=0, concat_axis=0, tiled=True)
    *blocks, last_rows = pack_rows(
        code,
        sibling_code,
        [stored_rows],
        [sibling_rows],
        half,
        row_cap,
        row_count,
        rest=store_count - ahead,
    )
    last_rows = lax.ppermute(last_rows, "dp", across)
    own_half = hand_on(blocks)
    plan = codes[:, 0, row_count:]
    wanted = plan[:, :token_cap].reshape(peer_count * token_cap)
    chosen = wanted[:, None] == jnp.arange(vocab_rows, dtype=jnp.int32)[None, :]
    found = jnp.dot(
        chosen.astype(jnp.bfloat16), word_table, preferred_element_type=jnp.float32
    ).astype(jnp.bfloat16)
    found, first_rows, own_half[:2] = lax.optimization_barrier(
        (found, first_rows, own_half[:2])
    )
    fetched = lax.all_to_all(
        found.reshape(peer_count, token_cap, width), "dp", split_axis=0, concat_axis=0, tiled=True
    ).reshape(peer_count * token_cap, width)

    partner_rows = [first_rows, last_rows]
    far_rows = [lax.ppermute(rows, "dp", beside) for rows in partner_rows]
    picks = (half, half ^ 1)
    blocks = pack_rows(codes, codes, partner_rows, far_rows, half, row_cap, row_count, picks)
    other_half = hand_on(blocks)
    sources = lax.axis_index("dp") ^ jnp.arange(peer_count, dtype=jnp.int32)
    got_places = plan[:, token_cap : token_cap + row_cap][sources].reshape(half, 2 * row_cap)
    spare = padded(2 * row_cap) - 2 * row_cap
    got_places = jnp.pad(got_places, ((0, 0), (0, spare)), constant_values=-1).reshape(1, -1)
    means, share = early_update(got_places, centroids, own_half[:2])
    late_places = plan[:, token_cap + row_cap :].reshape(1, -1)
    fetched, means, share, got_places, late_places = lax.optimization_barrier(
        (fetched, means, share, got_places, late_places)
    )

    passage_embed, spread = encode(
        peer_count,
        token_slot,
        fetched,
        lengths,
        pos_table,
        emb_gain,
        emb_bias,
        w_qkv,
        w_out,
        out_bias,
        norm_gain,
        norm_bias,
    )
    all_embeds = lax.all_to_all(
        spread, "dp", split_axis=0, concat_axis=0, tiled=True
    )
    pieces = own_half[2:] + other_half
    new_centroids = late_update(got_places, late_places, all_embeds, share, means, pieces)
    return (passage_embed, new_centroids)


def solution(mesh):
    return jax.shard_map(
        shards,
        mesh=mesh,
        in_specs=(
            P(("groups", "dp"), None),
            P(("groups", "dp")),
            P("dp", None),
            P(),
            P(),
            P(),
            P(),
            P(),
            P(),
            P(),
            P(),
            P(("groups", "dp"), None),
            P(("groups", "dp"), None),
            P(("groups", "dp")),
            P(("groups", "dp"), None),
        ),
        out_specs=(P(("groups", "dp"), None), P(("groups", "dp"), None)),
        check_vma=False,
    )
```

```python
import functools

import jax
import jax.numpy as jnp
from jax import lax
from jax.experimental import pallas as pl
from jax.experimental.pallas import tpu as pltpu
from jax.sharding import PartitionSpec as P

HEADS = 8
HD = 64


def normed(values, gain, shift):
    center = values - jnp.mean(values, axis=-1, keepdims=True)
    spread = jnp.mean(center * center, axis=-1, keepdims=True)
    return center * lax.rsqrt(spread + 1e-12) * gain + shift


def head_sums(weights, seq):
    rows, columns = weights.shape
    lane = lax.broadcasted_iota(jnp.int32, (rows, 2 * seq), 1)
    sums = []
    for start in range(0, columns, 2 * seq):
        pair = weights[:, start : start + 2 * seq]
        first = jnp.sum(jnp.where(lane < seq, pair, 0.0), axis=1, keepdims=True)
        second = jnp.sum(jnp.where(lane < seq, 0.0, pair), axis=1, keepdims=True)
        sums.append(jnp.where(lane < seq, first, second))
    return jnp.concatenate(sums, axis=1)


def encode_kernel(*refs):
    count = (len(refs) - 3) // 2
    far, (out, spread), near, arrived = refs[:count], refs[count : count + 2], refs[-count - 1 : -1], refs[-1]
    w_qkv_far, inner = far[-2], HEADS * HD
    copies = [
        pltpu.make_async_copy(source, target, arrived.at[at])
        for at, (source, target) in enumerate(zip(far, near))
        if source is not w_qkv_far
    ]
    lengths, slots, fetched, pos, emb_gain, emb_bias, out_bias, norm_gain, norm_bias, w_qkv, w_out = near
    out_copy = copies.pop()
    thirds = []
    for third in range(3):
        columns = pl.ds(third * inner, inner)
        thirds.append(
            pltpu.make_async_copy(
                w_qkv_far.at[:, columns], w_qkv.at[:, columns], arrived.at[count + third]
            )
        )
    for copy in copies + thirds + [out_copy]:
        copy.start()
    for copy in copies:
        copy.wait()
    passes = out.shape[0]
    size = [lengths[:, p : p + 1] for p in range(passes)]
    tokens, slot_count = slots.shape[0], fetched.shape[0]
    seq = tokens // passes
    spot = lax.broadcasted_iota(jnp.int32, (tokens, slot_count), 1)
    picker = jnp.where(slots[...] == spot, 1.0, 0.0).astype(jnp.bfloat16)
    tok = jnp.dot(picker, fetched[...], preferred_element_type=jnp.float32)
    where_at = pos[...].astype(jnp.float32)
    summed = tok + jnp.concatenate([where_at] * passes, axis=0)
    embedded = normed(summed, emb_gain[...], emb_bias[...]).astype(jnp.bfloat16)
    parts = []
    for third in range(3):
        thirds[third].wait()
        weights = w_qkv[:, third * inner : (third + 1) * inner]
        part = jnp.dot(embedded, weights, preferred_element_type=jnp.float32)
        parts.append(part.astype(jnp.bfloat16))

    block_row = lax.broadcasted_iota(jnp.int32, (HEADS * seq, inner), 0) // seq
    block_col = lax.broadcasted_iota(jnp.int32, (HEADS * seq, inner), 1) // HD
    same = block_row == block_col
    lane = lax.broadcasted_iota(jnp.int32, (seq, HEADS * seq), 1) % seq
    contexts = []
    for p in range(passes):
        query, keys, vals = (part[p * seq : (p + 1) * seq] for part in parts)
        zero = jnp.zeros((), jnp.bfloat16)
        keys = jnp.where(same, jnp.concatenate([keys] * HEADS, axis=0), zero)
        vals = jnp.where(same, jnp.concatenate([vals] * HEADS, axis=0), zero)
        scores = lax.dot_general(
            query, keys, (((1,), (1,)), ((), ())), preferred_element_type=jnp.float32
        ) * HD ** (-0.5)
        weights = jnp.where(lane < size[p], jnp.exp(scores), 0.0)
        probs = (weights / head_sums(weights, seq)).astype(jnp.bfloat16)
        contexts.append(jnp.dot(probs, vals, preferred_element_type=jnp.float32))
    context = jnp.concatenate(contexts, axis=0).astype(jnp.bfloat16)
    out_copy.wait()
    attended = jnp.dot(context, w_out[...], preferred_element_type=jnp.float32) + out_bias[...]
    hidden = normed(embedded.astype(jnp.float32) + attended, norm_gain[...], norm_bias[...])
    row = lax.broadcasted_iota(jnp.int32, (seq, 1), 0)
    for p in range(passes):
        kept = jnp.where(row < size[p], hidden[p * seq : (p + 1) * seq], 0.0)
        pooled = jnp.sum(kept, axis=0, keepdims=True) / size[p].astype(jnp.float32)
        scale = lax.rsqrt(jnp.mean(pooled * pooled, axis=-1, keepdims=True) + 1e-06)
        out[p : p + 1, :] = (pooled * scale).astype(jnp.bfloat16)
    spread[...] = jnp.broadcast_to(out[...][None], spread.shape)


def encode(
    peers, slots, fetched, lengths, pos_table, emb_gain, emb_bias, w_qkv, w_out, out_bias, norm_gain, norm_bias
):
    width = fetched.shape[1]
    tokens = slots.shape[0]
    passes = lengths.shape[0]
    macs = tokens * width * (fetched.shape[0] + 4 * HEADS * HD)
    operands = (
        lengths[None],
        slots,
        fetched,
        pos_table,
        emb_gain[None],
        emb_bias[None],
        out_bias[None],
        norm_gain[None],
        norm_bias[None],
        w_qkv,
        w_out,
    )
    return pl.pallas_call(
        encode_kernel,
        out_shape=[
            jax.ShapeDtypeStruct((passes, width), jnp.bfloat16),
            jax.ShapeDtypeStruct((peers, passes, width), jnp.bfloat16),
        ],
        in_specs=[pl.BlockSpec(memory_space=pltpu.HBM)] * len(operands),
        out_specs=[pl.BlockSpec(memory_space=pltpu.VMEM)] * 2,
        scratch_shapes=[pltpu.VMEM(operand.shape, operand.dtype) for operand in operands]
        + [pltpu.SemaphoreType.DMA((len(operands) + 3,))],
        compiler_params=pltpu.CompilerParams(vmem_limit_bytes=60 * 1024 * 1024),
        cost_estimate=pl.CostEstimate(
            flops=2 * macs, bytes_accessed=6 * 1024 * 1024, transcendentals=0
        ),
        name="encode",
    )(*operands)


def padded(rows):
    return -(-rows // 16) * 16


def rank_bits(count):
    return max(1, (count - 1).bit_length())


def ranks(kind):
    count = kind.shape[1]
    at = lax.broadcasted_iota(jnp.int32, (count, count), 0)
    by = lax.broadcasted_iota(jnp.int32, (count, count), 1)
    across = jnp.broadcast_to(kind, (count, count))
    down = jnp.sum(jnp.where(at == by, across, 0), axis=1, keepdims=True)
    same = down == across
    rank_row = jnp.sum(jnp.where(same & (at < by), 1, 0), axis=0, keepdims=True)
    rank_col = jnp.sum(jnp.where(same & (by < at), 1, 0), axis=1, keepdims=True)
    return down, rank_row, rank_col


def route_kernel(
    sizes,
    token_ids_far,
    owners_far,
    row_slot_far,
    sibling_far,
    plan,
    token_slot_far,
    code,
    sibling_code,
    *near,
):
    peers, vocab_rows, token_cap, row_cap, pooled = sizes
    token_ids, owners, row_slot, sibling, token_slot, arrived = near
    copies = [
        pltpu.make_async_copy(source, target, arrived.at[at])
        for at, (source, target) in enumerate(
            (
                (token_ids_far, token_ids),
                (owners_far, owners),
                (row_slot_far, row_slot),
                (sibling_far, sibling),
            )
        )
    ]
    for copy in copies:
        copy.start()
    for copy in copies:
        copy.wait()
    ids = jnp.concatenate([token_ids[p : p + 1, :] for p in range(token_ids.shape[0])], axis=1)
    tokens, rows = ids.shape[1], owners.shape[1]
    count = tokens + rows
    edge = (lax.broadcasted_iota(jnp.int32, (peers, tokens), 0) + 1) * vocab_rows
    holder = jnp.sum(jnp.where(ids >= edge, 1, 0), axis=0, keepdims=True)
    values = jnp.concatenate([ids - holder * vocab_rows, row_slot[...]], axis=1)

    kind = jnp.concatenate([holder, owners[...] + peers], axis=1)
    down, rank_row, rank_col = ranks(kind)

    code[...] = owners[...] * 2 ** rank_bits(rows) + rank_row[:, tokens:]
    sibling_code[...] = sibling[...] * 2 ** rank_bits(rows) + ranks(sibling[...])[1]
    goal = jnp.concatenate([holder, owners[...]], axis=1)
    peer = lax.broadcasted_iota(jnp.int32, (peers, count), 0)
    left = jnp.where(peer == goal, values + 1, 0).astype(jnp.float32)
    columns = token_cap + row_cap + pooled
    column = lax.broadcasted_iota(jnp.int32, (count, columns), 1)
    entry = lax.broadcasted_iota(jnp.int32, (count, 1), 0)
    first = jnp.where(entry < tokens, rank_col, rank_col + token_cap)
    second = entry - (count - pooled) + token_cap + row_cap
    second = jnp.where(entry < count - pooled, -1, second)
    right = jnp.where((column == first) | (column == second), 1.0, 0.0)
    filled = jnp.dot(
        left, right, preferred_element_type=jnp.float32, precision=lax.Precision.HIGHEST
    )
    filled = filled.astype(jnp.int32) - 1
    for p in range(peers):
        plan[p, :, :rows] = code[...]
        plan[p, :, rows:] = filled[p : p + 1]
    token_slot[...] = down[:tokens] * token_cap + rank_col[:tokens]
    send = pltpu.make_async_copy(token_slot, token_slot_far, arrived.at[4])
    send.start()
    send.wait()


def route(token_ids, owners, row_slot, sibling_owners, sizes):
    peers, _, token_cap, row_cap, pooled = sizes
    passes, seq_len = token_ids.shape
    rows = owners.shape[1]
    ints = lambda *shape: jax.ShapeDtypeStruct(shape, jnp.int32)
    return pl.pallas_call(
        functools.partial(route_kernel, sizes),
        out_shape=[
            ints(peers, 1, rows + token_cap + row_cap + pooled),
            ints(passes * seq_len, 1),
            ints(1, rows),
            ints(1, rows),
        ],
        in_specs=[pl.BlockSpec(memory_space=pltpu.HBM)] * 4,
        out_specs=[
            pl.BlockSpec(memory_space=pltpu.VMEM),
            pl.BlockSpec(memory_space=pltpu.HBM),
            pl.BlockSpec(memory_space=pltpu.VMEM),
            pl.BlockSpec(memory_space=pltpu.VMEM),
        ],
        scratch_shapes=[
            pltpu.VMEM(token_ids.shape, jnp.int32),
            pltpu.VMEM(owners.shape, jnp.int32),
            pltpu.VMEM(row_slot.shape, jnp.int32),
            pltpu.VMEM(owners.shape, jnp.int32),
            pltpu.VMEM((passes * seq_len, 1), jnp.int32),
            pltpu.SemaphoreType.DMA((5,)),
        ],
        compiler_params=pltpu.CompilerParams(vmem_limit_bytes=60 * 1024 * 1024),
        name="route",
    )(token_ids, owners, row_slot, sibling_owners)


def pack_kernel(half, row_cap, count, picks, pieces, rest, *refs):
    me = lax.axis_index("dp")
    operands = 2 + 2 * pieces
    far, refs = refs[:operands], refs[operands:]
    steps = half // 2
    outs, refs = refs[: steps + bool(rest)], refs[steps + bool(rest) :]
    near, (blocks, tail, arrived, left) = refs[:operands], refs[operands:]
    size = blocks.shape[0] // steps
    copies = [
        pltpu.make_async_copy(far[at], near[at], arrived.at[at]) for at in range(operands)
    ]
    for copy in copies:
        copy.start()
    for copy in copies[:2]:
        copy.wait()
    if size > 2 * row_cap:
        blocks[...] = jnp.zeros(blocks.shape, blocks.dtype)
    for source in range(2):
        if picks is None:
            code = near[source][...]
        else:
            code = near[source][me ^ picks[source], :, :count]
        bits = rank_bits(count)
        owner, rank = code >> bits, code & (2**bits - 1)
        fits = ((owner ^ me) & (1 | half)) == 0
        chip = ((owner ^ me) & (half - 1)) >> 1
        slot = jnp.where(fits, chip * row_cap + rank, -1)
        packed, at = 0.0, 0
        for piece in range(2 + source * pieces, 2 + (source + 1) * pieces):
            rows = near[piece]
            spot = lax.broadcasted_iota(jnp.int32, (steps * row_cap, rows.shape[0]), 0)
            table = jnp.where(slot[:, at : at + rows.shape[0]] == spot, 1.0, 0.0)
            copies[piece].wait()
            packed += jnp.dot(
                table.astype(jnp.bfloat16), rows[...], preferred_element_type=jnp.float32
            )
            at += rows.shape[0]
        packed = packed.astype(jnp.bfloat16)
        for step in range(steps):
            first = step * size + source * row_cap
            blocks[first : first + row_cap, :] = packed[step * row_cap : (step + 1) * row_cap]
    sends = [
        pltpu.make_async_copy(
            blocks.at[pl.ds(step * size, size)], outs[step], left.at[step]
        )
        for step in range(steps)
    ]
    if rest:
        tail[...] = near[2][near[2].shape[0] - rest :, :]
        sends.append(pltpu.make_async_copy(tail, outs[steps], left.at[steps]))
    for send in sends:
        send.start()
    for send in sends:
        send.wait()


def pack_rows(codes_a, codes_b, rows_a, rows_b, half, row_cap, count, picks=None, rest=0):
    width = rows_a[0].shape[1]
    total = sum(piece.shape[0] for piece in rows_a)
    steps = half // 2
    size = padded(2 * row_cap)
    operands = (codes_a, codes_b, *rows_a, *rows_b)
    shapes = [(size, width)] * steps + [(rest, width)] * bool(rest)
    return pl.pallas_call(
        functools.partial(pack_kernel, half, row_cap, count, picks, len(rows_a), rest),
        out_shape=[jax.ShapeDtypeStruct(shape, jnp.bfloat16) for shape in shapes],
        in_specs=[pl.BlockSpec(memory_space=pltpu.HBM)] * len(operands),
        out_specs=[pl.BlockSpec(memory_space=pltpu.HBM)] * len(shapes),
        scratch_shapes=[
            *(pltpu.VMEM(operand.shape, operand.dtype) for operand in operands),
            pltpu.VMEM((steps * size, width), jnp.bfloat16),
            pltpu.VMEM((max(rest, 16), width), jnp.bfloat16),
            pltpu.SemaphoreType.DMA((len(operands),)),
            pltpu.SemaphoreType.DMA((len(shapes),)),
        ],
        compiler_params=pltpu.CompilerParams(vmem_limit_bytes=60 * 1024 * 1024),
        cost_estimate=pl.CostEstimate(
            flops=4 * steps * row_cap * width * total,
            bytes_accessed=4 * width * (total + steps * row_cap),
            transcendentals=0,
        ),
        name="pack",
    )(*operands)


def onehot(where_to, first, count):
    centre = lax.broadcasted_iota(jnp.int32, (count, where_to.shape[1]), 0) + first
    return jnp.where(centre == where_to, 1.0, 0.0)


BLOCK = 128


def early_kernel(places_far, centroids_far, *rest):
    pieces, (out_far, share_far, places, rows, centroids, out, share, arrived, left) = rest[:-9], rest[-9:]
    size = pieces[0].shape[0]
    steps = centroids.shape[0] // BLOCK
    copies = [pltpu.make_async_copy(places_far, places, arrived.at[0])]
    for at, piece in enumerate(pieces):
        copies.append(
            pltpu.make_async_copy(piece, rows.at[pl.ds(at * size, size)], arrived.at[1 + at])
        )
    loads = []
    for step in range(steps):
        block = pl.ds(step * BLOCK, BLOCK)
        loads.append(
            pltpu.make_async_copy(
                centroids_far.at[block], centroids.at[block], arrived.at[1 + len(pieces) + step]
            )
        )
    for copy in copies + loads:
        copy.start()
    for copy in copies:
        copy.wait()
    sends = []
    for step in range(steps):
        block = pl.ds(step * BLOCK, BLOCK)
        hot = onehot(places[...], step * BLOCK, BLOCK)
        counts = jnp.sum(hot, axis=1, keepdims=True)
        scale = jnp.where(counts > 0, 1.0 / jnp.maximum(counts, 1.0), 0.0)
        sums = jnp.dot(
            hot[:, : rows.shape[0]].astype(jnp.bfloat16),
            rows[...],
            preferred_element_type=jnp.float32,
        )
        loads[step].wait()
        out[block, :] = jnp.where(counts > 0, sums * scale, centroids[block, :])
        share[block, :] = jnp.broadcast_to(scale, (BLOCK, share.shape[1]))
        sends.append(pltpu.make_async_copy(out.at[block], out_far.at[block], left.at[step]))
        sends[-1].start()
    sends.append(pltpu.make_async_copy(share, share_far, left.at[steps]))
    sends[-1].start()
    for send in sends:
        send.wait()


def late_kernel(places_far, late_far, spread_far, share_far, early_far, *rest):
    pieces, rest = rest[:-10], rest[-10:]
    out_far, places, late, spread, share, rows, early, out, arrived, left = rest
    size, passes = pieces[0].shape[0], spread.shape[1]
    steps = early.shape[0] // BLOCK
    loads = [
        pltpu.make_async_copy(source, target, arrived.at[at])
        for at, (source, target) in enumerate(
            ((places_far, places), (late_far, late), (spread_far, spread), (share_far, share))
        )
    ]
    for at, piece in enumerate(pieces):
        loads.append(
            pltpu.make_async_copy(piece, rows.at[pl.ds(at * size, size)], arrived.at[4 + at])
        )
    starts = []
    for step in range(steps):
        block = pl.ds(step * BLOCK, BLOCK)
        starts.append(
            pltpu.make_async_copy(
                early_far.at[block], early.at[block], arrived.at[len(loads) + step]
            )
        )
    for copy in loads + starts:
        copy.start()
    for copy in loads:
        copy.wait()
    top = len(pieces) * size
    for peer in range(spread.shape[0]):
        rows[top + peer * passes : top + (peer + 1) * passes, :] = spread[peer]
    where_to = jnp.concatenate([places[:, places.shape[1] - top :], late[...]], axis=1)
    sends = []
    for step in range(steps):
        block = pl.ds(step * BLOCK, BLOCK)
        hot = onehot(where_to, step * BLOCK, BLOCK).astype(jnp.bfloat16)
        sums = jnp.dot(hot, rows[...], preferred_element_type=jnp.float32)
        starts[step].wait()
        out[block, :] = early[block, :] + sums * share[block, :1]
        sends.append(pltpu.make_async_copy(out.at[block], out_far.at[block], left.at[step]))
        sends[-1].start()
    for send in sends:
        send.wait()


def early_update(places, centroids, pieces):
    centre_count, width = centroids.shape
    row_total = sum(piece.shape[0] for piece in pieces)
    wide = pltpu.VMEM(centroids.shape, jnp.float32)
    thin = (centre_count, 128)
    steps = centre_count // BLOCK
    return pl.pallas_call(
        early_kernel,
        out_shape=[
            jax.ShapeDtypeStruct(centroids.shape, jnp.float32),
            jax.ShapeDtypeStruct(thin, jnp.float32),
        ],
        in_specs=[pl.BlockSpec(memory_space=pl.ANY)] * (2 + len(pieces)),
        out_specs=[pl.BlockSpec(memory_space=pltpu.HBM)] * 2,
        scratch_shapes=[
            pltpu.VMEM(places.shape, jnp.int32),
            pltpu.VMEM((row_total, width), jnp.bfloat16),
            wide,
            wide,
            pltpu.VMEM(thin, jnp.float32),
            pltpu.SemaphoreType.DMA((1 + len(pieces) + steps,)),
            pltpu.SemaphoreType.DMA((steps + 1,)),
        ],
        compiler_params=pltpu.CompilerParams(vmem_limit_bytes=60 * 1024 * 1024),
        cost_estimate=pl.CostEstimate(
            flops=2 * centre_count * width * row_total,
            bytes_accessed=60 * centre_count * width,
            transcendentals=0,
        ),
        name="early",
    )(places, centroids, *pieces)


def late_update(places, late, spread, share, early, pieces):
    centre_count, width = early.shape
    row_total = sum(piece.shape[0] for piece in pieces) + late.shape[1]
    wide = pltpu.VMEM(early.shape, jnp.float32)
    steps = centre_count // BLOCK
    return pl.pallas_call(
        late_kernel,
        out_shape=jax.ShapeDtypeStruct(early.shape, jnp.float32),
        in_specs=[pl.BlockSpec(memory_space=pltpu.HBM)] * (5 + len(pieces)),
        out_specs=pl.BlockSpec(memory_space=pltpu.HBM),
        scratch_shapes=[
            pltpu.VMEM(places.shape, jnp.int32),
            pltpu.VMEM(late.shape, jnp.int32),
            pltpu.VMEM(spread.shape, jnp.bfloat16),
            pltpu.VMEM(share.shape, jnp.float32),
            pltpu.VMEM((row_total, width), jnp.bfloat16),
            wide,
            wide,
            pltpu.SemaphoreType.DMA((4 + len(pieces) + steps,)),
            pltpu.SemaphoreType.DMA((steps,)),
        ],
        compiler_params=pltpu.CompilerParams(vmem_limit_bytes=60 * 1024 * 1024),
        cost_estimate=pl.CostEstimate(
            flops=2 * centre_count * width * row_total,
            bytes_accessed=8 * centre_count * width,
            transcendentals=0,
        ),
        name="late",
    )(places, late, spread, share, early, *pieces)


def shards(
    token_ids,
    lengths,
    word_table,
    pos_table,
    emb_gain,
    emb_bias,
    w_qkv,
    w_out,
    out_bias,
    norm_gain,
    norm_bias,
    stored_rows,
    row_owner,
    row_slot,
    centroids,
):
    peer_count = lax.axis_size("dp")
    half = peer_count // 2
    width = word_table.shape[1]
    vocab_rows = word_table.shape[0]
    passes, seq_len = token_ids.shape
    token_count = passes * seq_len
    row_count = row_slot.shape[0]
    store_count = stored_rows.shape[0]
    token_cap = max(2, 3 * token_count // peer_count)
    row_cap = max(2, 3 * row_count // peer_count)

    across = [(i, i ^ half) for i in range(peer_count)]
    beside = [(i, i ^ 1) for i in range(peer_count)]

    def hand_on(blocks):
        got = [blocks[0]]
        for step in range(1, len(blocks)):
            moves = [(i, i ^ (2 * step)) for i in range(peer_count)]
            got.append(lax.ppermute(blocks[step], "dp", moves))
        return got

    ahead = store_count * 2 // 3 // 16 * 16
    sibling_rows = lax.ppermute(stored_rows, "dp", beside)
    first_rows = lax.ppermute(stored_rows[:ahead], "dp", across)
    sizes = (peer_count, vocab_rows, token_cap, row_cap, row_count - store_count)
    owners = row_owner.reshape(1, row_count)
    sibling_owners = lax.ppermute(owners, "dp", beside)
    plan, token_slot, code, sibling_code = route(
        token_ids, owners, row_slot[None], sibling_owners, sizes
    )
    plan, sibling_rows = lax.optimization_barrier((plan, sibling_rows))
    codes = lax.all_to_all(plan, "dp", split_axis=0, concat_axis=0, tiled=True)
    *blocks, last_rows = pack_rows(
        code,
        sibling_code,
        [stored_rows],
        [sibling_rows],
        half,
        row_cap,
        row_count,
        rest=store_count - ahead,
    )
    last_rows = lax.ppermute(last_rows, "dp", across)
    own_half = hand_on(blocks)
    plan = codes[:, 0, row_count:]
    wanted = plan[:, :token_cap].reshape(peer_count * token_cap)
    chosen = wanted[:, None] == jnp.arange(vocab_rows, dtype=jnp.int32)[None, :]
    found = jnp.dot(
        chosen.astype(jnp.bfloat16), word_table, preferred_element_type=jnp.float32
    ).astype(jnp.bfloat16)
    found, first_rows, own_half[:2] = lax.optimization_barrier(
        (found, first_rows, own_half[:2])
    )
    fetched = lax.all_to_all(
        found.reshape(peer_count, token_cap, width), "dp", split_axis=0, concat_axis=0, tiled=True
    ).reshape(peer_count * token_cap, width)

    partner_rows = [first_rows, last_rows]
    far_rows = [lax.ppermute(rows, "dp", beside) for rows in partner_rows]
    picks = (half, half ^ 1)
    blocks = pack_rows(codes, codes, partner_rows, far_rows, half, row_cap, row_count, picks)
    other_half = hand_on(blocks)
    sources = lax.axis_index("dp") ^ jnp.arange(peer_count, dtype=jnp.int32)
    got_places = plan[:, token_cap : token_cap + row_cap][sources].reshape(half, 2 * row_cap)
    spare = padded(2 * row_cap) - 2 * row_cap
    got_places = jnp.pad(got_places, ((0, 0), (0, spare)), constant_values=-1).reshape(1, -1)
    means, share = early_update(got_places, centroids, own_half[:2])
    late_places = plan[:, token_cap + row_cap :].reshape(1, -1)
    fetched, means, share, got_places, late_places = lax.optimization_barrier(
        (fetched, means, share, got_places, late_places)
    )

    passage_embed, spread = encode(
        peer_count,
        token_slot,
        fetched,
        lengths,
        pos_table,
        emb_gain,
        emb_bias,
        w_qkv,
        w_out,
        out_bias,
        norm_gain,
        norm_bias,
    )
    all_embeds = lax.all_to_all(
        spread, "dp", split_axis=0, concat_axis=0, tiled=True
    )
    pieces = own_half[2:] + other_half
    new_centroids = late_update(got_places, late_places, all_embeds, share, means, pieces)
    return (passage_embed, new_centroids)


def solution(mesh):
    return jax.shard_map(
        shards,
        mesh=mesh,
        in_specs=(
            P(("groups", "dp"), None),
            P(("groups", "dp")),
            P("dp", None),
            P(),
            P(),
            P(),
            P(),
            P(),
            P(),
            P(),
            P(),
            P(("groups", "dp"), None),
            P(("groups", "dp"), None),
            P(("groups", "dp")),
            P(("groups", "dp"), None),
        ),
        out_specs=(P(("groups", "dp"), None), P(("groups", "dp"), None)),
        check_vma=False,
    )
```

```python
import functools

import jax
import jax.numpy as jnp
from jax import lax
from jax.experimental import pallas as pl
from jax.experimental.pallas import tpu as pltpu
from jax.sharding import PartitionSpec as P

HEADS = 8
HD = 64


def normed(values, gain, shift):
    center = values - jnp.mean(values, axis=-1, keepdims=True)
    spread = jnp.mean(center * center, axis=-1, keepdims=True)
    return center * lax.rsqrt(spread + 1e-12) * gain + shift


def head_sums(weights, seq):
    rows, columns = weights.shape
    lane = lax.broadcasted_iota(jnp.int32, (rows, 2 * seq), 1)
    sums = []
    for start in range(0, columns, 2 * seq):
        pair = weights[:, start : start + 2 * seq]
        first = jnp.sum(jnp.where(lane < seq, pair, 0.0), axis=1, keepdims=True)
        second = jnp.sum(jnp.where(lane < seq, 0.0, pair), axis=1, keepdims=True)
        sums.append(jnp.where(lane < seq, first, second))
    return jnp.concatenate(sums, axis=1)


def encode_kernel(*refs):
    count = (len(refs) - 3) // 2
    far, (out, spread), near, arrived = refs[:count], refs[count : count + 2], refs[-count - 1 : -1], refs[-1]
    w_qkv_far, inner = far[-2], HEADS * HD
    copies = [
        pltpu.make_async_copy(source, target, arrived.at[at])
        for at, (source, target) in enumerate(zip(far, near))
        if source is not w_qkv_far
    ]
    lengths, slots, fetched, pos, emb_gain, emb_bias, out_bias, norm_gain, norm_bias, w_qkv, w_out = near
    out_copy = copies.pop()
    thirds = []
    for third in range(3):
        columns = pl.ds(third * inner, inner)
        thirds.append(
            pltpu.make_async_copy(
                w_qkv_far.at[:, columns], w_qkv.at[:, columns], arrived.at[count + third]
            )
        )
    for copy in copies + thirds + [out_copy]:
        copy.start()
    for copy in copies:
        copy.wait()
    passes = out.shape[0]
    size = [lengths[:, p : p + 1] for p in range(passes)]
    tokens, slot_count = slots.shape[0], fetched.shape[0]
    seq = tokens // passes
    spot = lax.broadcasted_iota(jnp.int32, (tokens, slot_count), 1)
    picker = jnp.where(slots[...] == spot, 1.0, 0.0).astype(jnp.bfloat16)
    tok = jnp.dot(picker, fetched[...], preferred_element_type=jnp.float32)
    where_at = pos[...].astype(jnp.float32)
    summed = tok + jnp.concatenate([where_at] * passes, axis=0)
    embedded = normed(summed, emb_gain[...], emb_bias[...]).astype(jnp.bfloat16)
    parts = []
    for third in range(3):
        thirds[third].wait()
        weights = w_qkv[:, third * inner : (third + 1) * inner]
        part = jnp.dot(embedded, weights, preferred_element_type=jnp.float32)
        parts.append(part.astype(jnp.bfloat16))

    block_row = lax.broadcasted_iota(jnp.int32, (HEADS * seq, inner), 0) // seq
    block_col = lax.broadcasted_iota(jnp.int32, (HEADS * seq, inner), 1) // HD
    same = block_row == block_col
    lane = lax.broadcasted_iota(jnp.int32, (seq, HEADS * seq), 1) % seq
    contexts = []
    for p in range(passes):
        query, keys, vals = (part[p * seq : (p + 1) * seq] for part in parts)
        zero = jnp.zeros((), jnp.bfloat16)
        keys = jnp.where(same, jnp.concatenate([keys] * HEADS, axis=0), zero)
        vals = jnp.where(same, jnp.concatenate([vals] * HEADS, axis=0), zero)
        scores = lax.dot_general(
            query, keys, (((1,), (1,)), ((), ())), preferred_element_type=jnp.float32
        ) * HD ** (-0.5)
        weights = jnp.where(lane < size[p], jnp.exp(scores), 0.0)
        probs = (weights / head_sums(weights, seq)).astype(jnp.bfloat16)
        contexts.append(jnp.dot(probs, vals, preferred_element_type=jnp.float32))
    context = jnp.concatenate(contexts, axis=0).astype(jnp.bfloat16)
    out_copy.wait()
    attended = jnp.dot(context, w_out[...], preferred_element_type=jnp.float32) + out_bias[...]
    hidden = normed(embedded.astype(jnp.float32) + attended, norm_gain[...], norm_bias[...])
    row = lax.broadcasted_iota(jnp.int32, (seq, 1), 0)
    for p in range(passes):
        kept = jnp.where(row < size[p], hidden[p * seq : (p + 1) * seq], 0.0)
        pooled = jnp.sum(kept, axis=0, keepdims=True) / size[p].astype(jnp.float32)
        scale = lax.rsqrt(jnp.mean(pooled * pooled, axis=-1, keepdims=True) + 1e-06)
        out[p : p + 1, :] = (pooled * scale).astype(jnp.bfloat16)
    spread[...] = jnp.broadcast_to(out[...][None], spread.shape)


def encode(
    peers, slots, fetched, lengths, pos_table, emb_gain, emb_bias, w_qkv, w_out, out_bias, norm_gain, norm_bias
):
    width = fetched.shape[1]
    tokens = slots.shape[0]
    passes = lengths.shape[0]
    macs = tokens * width * (fetched.shape[0] + 4 * HEADS * HD)
    operands = (
        lengths[None],
        slots,
        fetched,
        pos_table,
        emb_gain[None],
        emb_bias[None],
        out_bias[None],
        norm_gain[None],
        norm_bias[None],
        w_qkv,
        w_out,
    )
    return pl.pallas_call(
        encode_kernel,
        out_shape=[
            jax.ShapeDtypeStruct((passes, width), jnp.bfloat16),
            jax.ShapeDtypeStruct((peers, passes, width), jnp.bfloat16),
        ],
        in_specs=[pl.BlockSpec(memory_space=pltpu.HBM)] * len(operands),
        out_specs=[pl.BlockSpec(memory_space=pltpu.VMEM)] * 2,
        scratch_shapes=[pltpu.VMEM(operand.shape, operand.dtype) for operand in operands]
        + [pltpu.SemaphoreType.DMA((len(operands) + 3,))],
        compiler_params=pltpu.CompilerParams(vmem_limit_bytes=60 * 1024 * 1024),
        cost_estimate=pl.CostEstimate(
            flops=2 * macs, bytes_accessed=6 * 1024 * 1024, transcendentals=0
        ),
        name="encode",
    )(*operands)


def padded(rows):
    return -(-rows // 16) * 16


def rank_bits(count):
    return max(1, (count - 1).bit_length())


def ranks(kind):
    count = kind.shape[1]
    at = lax.broadcasted_iota(jnp.int32, (count, count), 0)
    by = lax.broadcasted_iota(jnp.int32, (count, count), 1)
    across = jnp.broadcast_to(kind, (count, count))
    down = jnp.sum(jnp.where(at == by, across, 0), axis=1, keepdims=True)
    same = down == across
    rank_row = jnp.sum(jnp.where(same & (at < by), 1, 0), axis=0, keepdims=True)
    rank_col = jnp.sum(jnp.where(same & (by < at), 1, 0), axis=1, keepdims=True)
    return down, rank_row, rank_col


def route_kernel(
    sizes,
    token_ids_far,
    owners_far,
    row_slot_far,
    sibling_far,
    plan,
    token_slot_far,
    code,
    sibling_code,
    *near,
):
    peers, vocab_rows, token_cap, row_cap, pooled = sizes
    token_ids, owners, row_slot, sibling, token_slot, arrived = near
    copies = [
        pltpu.make_async_copy(source, target, arrived.at[at])
        for at, (source, target) in enumerate(
            (
                (token_ids_far, token_ids),
                (owners_far, owners),
                (row_slot_far, row_slot),
                (sibling_far, sibling),
            )
        )
    ]
    for copy in copies:
        copy.start()
    for copy in copies:
        copy.wait()
    ids = jnp.concatenate([token_ids[p : p + 1, :] for p in range(token_ids.shape[0])], axis=1)
    tokens, rows = ids.shape[1], owners.shape[1]
    count = tokens + rows
    edge = (lax.broadcasted_iota(jnp.int32, (peers, tokens), 0) + 1) * vocab_rows
    holder = jnp.sum(jnp.where(ids >= edge, 1, 0), axis=0, keepdims=True)
    values = jnp.concatenate([ids - holder * vocab_rows, row_slot[...]], axis=1)

    kind = jnp.concatenate([holder, owners[...] + peers], axis=1)
    down, rank_row, rank_col = ranks(kind)

    code[...] = owners[...] * 2 ** rank_bits(rows) + rank_row[:, tokens:]
    sibling_code[...] = sibling[...] * 2 ** rank_bits(rows) + ranks(sibling[...])[1]
    goal = jnp.concatenate([holder, owners[...]], axis=1)
    peer = lax.broadcasted_iota(jnp.int32, (peers, count), 0)
    left = jnp.where(peer == goal, values + 1, 0).astype(jnp.float32)
    columns = token_cap + row_cap + pooled
    column = lax.broadcasted_iota(jnp.int32, (count, columns), 1)
    entry = lax.broadcasted_iota(jnp.int32, (count, 1), 0)
    first = jnp.where(entry < tokens, rank_col, rank_col + token_cap)
    second = entry - (count - pooled) + token_cap + row_cap
    second = jnp.where(entry < count - pooled, -1, second)
    right = jnp.where((column == first) | (column == second), 1.0, 0.0)
    filled = jnp.dot(
        left, right, preferred_element_type=jnp.float32, precision=lax.Precision.HIGHEST
    )
    filled = filled.astype(jnp.int32) - 1
    for p in range(peers):
        plan[p, :, :rows] = code[...]
        plan[p, :, rows:] = filled[p : p + 1]
    token_slot[...] = down[:tokens] * token_cap + rank_col[:tokens]
    send = pltpu.make_async_copy(token_slot, token_slot_far, arrived.at[4])
    send.start()
    send.wait()


def route(token_ids, owners, row_slot, sibling_owners, sizes):
    peers, _, token_cap, row_cap, pooled = sizes
    passes, seq_len = token_ids.shape
    rows = owners.shape[1]
    ints = lambda *shape: jax.ShapeDtypeStruct(shape, jnp.int32)
    return pl.pallas_call(
        functools.partial(route_kernel, sizes),
        out_shape=[
            ints(peers, 1, rows + token_cap + row_cap + pooled),
            ints(passes * seq_len, 1),
            ints(1, rows),
            ints(1, rows),
        ],
        in_specs=[pl.BlockSpec(memory_space=pltpu.HBM)] * 4,
        out_specs=[
            pl.BlockSpec(memory_space=pltpu.VMEM),
            pl.BlockSpec(memory_space=pltpu.HBM),
            pl.BlockSpec(memory_space=pltpu.VMEM),
            pl.BlockSpec(memory_space=pltpu.VMEM),
        ],
        scratch_shapes=[
            pltpu.VMEM(token_ids.shape, jnp.int32),
            pltpu.VMEM(owners.shape, jnp.int32),
            pltpu.VMEM(row_slot.shape, jnp.int32),
            pltpu.VMEM(owners.shape, jnp.int32),
            pltpu.VMEM((passes * seq_len, 1), jnp.int32),
            pltpu.SemaphoreType.DMA((5,)),
        ],
        compiler_params=pltpu.CompilerParams(vmem_limit_bytes=60 * 1024 * 1024),
        name="route",
    )(token_ids, owners, row_slot, sibling_owners)


def pack_kernel(half, row_cap, count, picks, pieces, rest, *refs):
    me = lax.axis_index("dp")
    operands = 2 + 2 * pieces
    far, refs = refs[:operands], refs[operands:]
    steps = half // 2
    outs, refs = refs[: steps + bool(rest)], refs[steps + bool(rest) :]
    near, (blocks, tail, arrived, left) = refs[:operands], refs[operands:]
    size = blocks.shape[0] // steps
    copies = [
        pltpu.make_async_copy(far[at], near[at], arrived.at[at]) for at in range(operands)
    ]
    for copy in copies:
        copy.start()
    for copy in copies[:2]:
        copy.wait()
    if size > 2 * row_cap:
        blocks[...] = jnp.zeros(blocks.shape, blocks.dtype)
    for source in range(2):
        if picks is None:
            code = near[source][...]
        else:
            code = near[source][me ^ picks[source], :, :count]
        bits = rank_bits(count)
        owner, rank = code >> bits, code & (2**bits - 1)
        fits = ((owner ^ me) & (1 | half)) == 0
        chip = ((owner ^ me) & (half - 1)) >> 1
        slot = jnp.where(fits, chip * row_cap + rank, -1)
        packed, at = 0.0, 0
        for piece in range(2 + source * pieces, 2 + (source + 1) * pieces):
            rows = near[piece]
            spot = lax.broadcasted_iota(jnp.int32, (steps * row_cap, rows.shape[0]), 0)
            table = jnp.where(slot[:, at : at + rows.shape[0]] == spot, 1.0, 0.0)
            copies[piece].wait()
            packed += jnp.dot(
                table.astype(jnp.bfloat16), rows[...], preferred_element_type=jnp.float32
            )
            at += rows.shape[0]
        packed = packed.astype(jnp.bfloat16)
        for step in range(steps):
            first = step * size + source * row_cap
            blocks[first : first + row_cap, :] = packed[step * row_cap : (step + 1) * row_cap]
    sends = [
        pltpu.make_async_copy(
            blocks.at[pl.ds(step * size, size)], outs[step], left.at[step]
        )
        for step in range(steps)
    ]
    if rest:
        tail[...] = near[2][near[2].shape[0] - rest :, :]
        sends.append(pltpu.make_async_copy(tail, outs[steps], left.at[steps]))
    for send in sends:
        send.start()
    for send in sends:
        send.wait()


def pack_rows(codes_a, codes_b, rows_a, rows_b, half, row_cap, count, picks=None, rest=0):
    width = rows_a[0].shape[1]
    total = sum(piece.shape[0] for piece in rows_a)
    steps = half // 2
    size = padded(2 * row_cap)
    operands = (codes_a, codes_b, *rows_a, *rows_b)
    shapes = [(size, width)] * steps + [(rest, width)] * bool(rest)
    return pl.pallas_call(
        functools.partial(pack_kernel, half, row_cap, count, picks, len(rows_a), rest),
        out_shape=[jax.ShapeDtypeStruct(shape, jnp.bfloat16) for shape in shapes],
        in_specs=[pl.BlockSpec(memory_space=pltpu.HBM)] * len(operands),
        out_specs=[pl.BlockSpec(memory_space=pltpu.HBM)] * len(shapes),
        scratch_shapes=[
            *(pltpu.VMEM(operand.shape, operand.dtype) for operand in operands),
            pltpu.VMEM((steps * size, width), jnp.bfloat16),
            pltpu.VMEM((max(rest, 16), width), jnp.bfloat16),
            pltpu.SemaphoreType.DMA((len(operands),)),
            pltpu.SemaphoreType.DMA((len(shapes),)),
        ],
        compiler_params=pltpu.CompilerParams(vmem_limit_bytes=60 * 1024 * 1024),
        cost_estimate=pl.CostEstimate(
            flops=4 * steps * row_cap * width * total,
            bytes_accessed=4 * width * (total + steps * row_cap),
            transcendentals=0,
        ),
        name="pack",
    )(*operands)


def onehot(where_to, first, count):
    centre = lax.broadcasted_iota(jnp.int32, (count, where_to.shape[1]), 0) + first
    return jnp.where(centre == where_to, 1.0, 0.0)


BLOCK = 128


def early_kernel(places_far, centroids_far, *rest):
    pieces, (out_far, share_far, places, rows, centroids, out, share, arrived, left) = rest[:-9], rest[-9:]
    size = pieces[0].shape[0]
    steps = centroids.shape[0] // BLOCK
    copies = [pltpu.make_async_copy(places_far, places, arrived.at[0])]
    for at, piece in enumerate(pieces):
        copies.append(
            pltpu.make_async_copy(piece, rows.at[pl.ds(at * size, size)], arrived.at[1 + at])
        )
    loads = []
    for step in range(steps):
        block = pl.ds(step * BLOCK, BLOCK)
        loads.append(
            pltpu.make_async_copy(
                centroids_far.at[block], centroids.at[block], arrived.at[1 + len(pieces) + step]
            )
        )
    for copy in copies + loads:
        copy.start()
    for copy in copies:
        copy.wait()
    sends = []
    for step in range(steps):
        block = pl.ds(step * BLOCK, BLOCK)
        hot = onehot(places[...], step * BLOCK, BLOCK)
        counts = jnp.sum(hot, axis=1, keepdims=True)
        scale = jnp.where(counts > 0, 1.0 / jnp.maximum(counts, 1.0), 0.0)
        sums = jnp.dot(
            hot[:, : rows.shape[0]].astype(jnp.bfloat16),
            rows[...],
            preferred_element_type=jnp.float32,
        )
        loads[step].wait()
        out[block, :] = jnp.where(counts > 0, sums * scale, centroids[block, :])
        share[block, :] = jnp.broadcast_to(scale, (BLOCK, share.shape[1]))
        sends.append(pltpu.make_async_copy(out.at[block], out_far.at[block], left.at[step]))
        sends[-1].start()
    sends.append(pltpu.make_async_copy(share, share_far, left.at[steps]))
    sends[-1].start()
    for send in sends:
        send.wait()


def late_kernel(places_far, late_far, spread_far, share_far, early_far, *rest):
    pieces, rest = rest[:-10], rest[-10:]
    out_far, places, late, spread, share, rows, early, out, arrived, left = rest
    size, passes = pieces[0].shape[0], spread.shape[1]
    steps = early.shape[0] // BLOCK
    loads = [
        pltpu.make_async_copy(source, target, arrived.at[at])
        for at, (source, target) in enumerate(
            ((places_far, places), (late_far, late), (spread_far, spread), (share_far, share))
        )
    ]
    for at, piece in enumerate(pieces):
        loads.append(
            pltpu.make_async_copy(piece, rows.at[pl.ds(at * size, size)], arrived.at[4 + at])
        )
    starts = []
    for step in range(steps):
        block = pl.ds(step * BLOCK, BLOCK)
        starts.append(
            pltpu.make_async_copy(
                early_far.at[block], early.at[block], arrived.at[len(loads) + step]
            )
        )
    for copy in loads + starts:
        copy.start()
    for copy in loads:
        copy.wait()
    top = len(pieces) * size
    for peer in range(spread.shape[0]):
        rows[top + peer * passes : top + (peer + 1) * passes, :] = spread[peer]
    where_to = jnp.concatenate([places[:, places.shape[1] - top :], late[...]], axis=1)
    sends = []
    for step in range(steps):
        block = pl.ds(step * BLOCK, BLOCK)
        hot = onehot(where_to, step * BLOCK, BLOCK).astype(jnp.bfloat16)
        sums = jnp.dot(hot, rows[...], preferred_element_type=jnp.float32)
        starts[step].wait()
        out[block, :] = early[block, :] + sums * share[block, :1]
        sends.append(pltpu.make_async_copy(out.at[block], out_far.at[block], left.at[step]))
        sends[-1].start()
    for send in sends:
        send.wait()


def early_update(places, centroids, pieces):
    centre_count, width = centroids.shape
    row_total = sum(piece.shape[0] for piece in pieces)
    wide = pltpu.VMEM(centroids.shape, jnp.float32)
    thin = (centre_count, 128)
    steps = centre_count // BLOCK
    return pl.pallas_call(
        early_kernel,
        out_shape=[
            jax.ShapeDtypeStruct(centroids.shape, jnp.float32),
            jax.ShapeDtypeStruct(thin, jnp.float32),
        ],
        in_specs=[pl.BlockSpec(memory_space=pl.ANY)] * (2 + len(pieces)),
        out_specs=[pl.BlockSpec(memory_space=pltpu.HBM)] * 2,
        scratch_shapes=[
            pltpu.VMEM(places.shape, jnp.int32),
            pltpu.VMEM((row_total, width), jnp.bfloat16),
            wide,
            wide,
            pltpu.VMEM(thin, jnp.float32),
            pltpu.SemaphoreType.DMA((1 + len(pieces) + steps,)),
            pltpu.SemaphoreType.DMA((steps + 1,)),
        ],
        compiler_params=pltpu.CompilerParams(vmem_limit_bytes=60 * 1024 * 1024),
        cost_estimate=pl.CostEstimate(
            flops=2 * centre_count * width * row_total,
            bytes_accessed=200 * centre_count * width,
            transcendentals=0,
        ),
        name="early",
    )(places, centroids, *pieces)


def late_update(places, late, spread, share, early, pieces):
    centre_count, width = early.shape
    row_total = sum(piece.shape[0] for piece in pieces) + late.shape[1]
    wide = pltpu.VMEM(early.shape, jnp.float32)
    steps = centre_count // BLOCK
    return pl.pallas_call(
        late_kernel,
        out_shape=jax.ShapeDtypeStruct(early.shape, jnp.float32),
        in_specs=[pl.BlockSpec(memory_space=pltpu.HBM)] * (5 + len(pieces)),
        out_specs=pl.BlockSpec(memory_space=pltpu.HBM),
        scratch_shapes=[
            pltpu.VMEM(places.shape, jnp.int32),
            pltpu.VMEM(late.shape, jnp.int32),
            pltpu.VMEM(spread.shape, jnp.bfloat16),
            pltpu.VMEM(share.shape, jnp.float32),
            pltpu.VMEM((row_total, width), jnp.bfloat16),
            wide,
            wide,
            pltpu.SemaphoreType.DMA((4 + len(pieces) + steps,)),
            pltpu.SemaphoreType.DMA((steps,)),
        ],
        compiler_params=pltpu.CompilerParams(vmem_limit_bytes=60 * 1024 * 1024),
        cost_estimate=pl.CostEstimate(
            flops=2 * centre_count * width * row_total,
            bytes_accessed=8 * centre_count * width,
            transcendentals=0,
        ),
        name="late",
    )(places, late, spread, share, early, *pieces)


def shards(
    token_ids,
    lengths,
    word_table,
    pos_table,
    emb_gain,
    emb_bias,
    w_qkv,
    w_out,
    out_bias,
    norm_gain,
    norm_bias,
    stored_rows,
    row_owner,
    row_slot,
    centroids,
):
    peer_count = lax.axis_size("dp")
    half = peer_count // 2
    width = word_table.shape[1]
    vocab_rows = word_table.shape[0]
    passes, seq_len = token_ids.shape
    token_count = passes * seq_len
    row_count = row_slot.shape[0]
    store_count = stored_rows.shape[0]
    token_cap = max(2, 3 * token_count // peer_count)
    row_cap = max(2, 3 * row_count // peer_count)

    across = [(i, i ^ half) for i in range(peer_count)]
    beside = [(i, i ^ 1) for i in range(peer_count)]

    def hand_on(blocks):
        got = [blocks[0]]
        for step in range(1, len(blocks)):
            moves = [(i, i ^ (2 * step)) for i in range(peer_count)]
            got.append(lax.ppermute(blocks[step], "dp", moves))
        return got

    ahead = store_count * 2 // 3 // 16 * 16
    sibling_rows = lax.ppermute(stored_rows, "dp", beside)
    first_rows = lax.ppermute(stored_rows[:ahead], "dp", across)
    sizes = (peer_count, vocab_rows, token_cap, row_cap, row_count - store_count)
    owners = row_owner.reshape(1, row_count)
    sibling_owners = lax.ppermute(owners, "dp", beside)
    plan, token_slot, code, sibling_code = route(
        token_ids, owners, row_slot[None], sibling_owners, sizes
    )
    plan, sibling_rows = lax.optimization_barrier((plan, sibling_rows))
    codes = lax.all_to_all(plan, "dp", split_axis=0, concat_axis=0, tiled=True)
    *blocks, last_rows = pack_rows(
        code,
        sibling_code,
        [stored_rows],
        [sibling_rows],
        half,
        row_cap,
        row_count,
        rest=store_count - ahead,
    )
    last_rows = lax.ppermute(last_rows, "dp", across)
    own_half = hand_on(blocks)
    plan = codes[:, 0, row_count:]
    wanted = plan[:, :token_cap].reshape(peer_count * token_cap)
    chosen = wanted[:, None] == jnp.arange(vocab_rows, dtype=jnp.int32)[None, :]
    found = jnp.dot(
        chosen.astype(jnp.bfloat16), word_table, preferred_element_type=jnp.float32
    ).astype(jnp.bfloat16)
    found, first_rows, own_half[:2] = lax.optimization_barrier(
        (found, first_rows, own_half[:2])
    )
    fetched = lax.all_to_all(
        found.reshape(peer_count, token_cap, width), "dp", split_axis=0, concat_axis=0, tiled=True
    ).reshape(peer_count * token_cap, width)

    sources = lax.axis_index("dp") ^ jnp.arange(peer_count, dtype=jnp.int32)
    got_places = plan[:, token_cap : token_cap + row_cap][sources].reshape(half, 2 * row_cap)
    spare = padded(2 * row_cap) - 2 * row_cap
    got_places = jnp.pad(got_places, ((0, 0), (0, spare)), constant_values=-1).reshape(1, -1)
    near_rows, last_rows = lax.optimization_barrier((own_half[:2], last_rows))
    means, share = early_update(got_places, centroids, near_rows)
    first_rows, last_rows, means = lax.optimization_barrier((first_rows, last_rows, means))
    partner_rows = [first_rows, last_rows]
    far_rows = [lax.ppermute(rows, "dp", beside) for rows in partner_rows]
    picks = (half, half ^ 1)
    blocks = pack_rows(codes, codes, partner_rows, far_rows, half, row_cap, row_count, picks)
    other_half = hand_on(blocks)
    late_places = plan[:, token_cap + row_cap :].reshape(1, -1)
    fetched, means, share, got_places, late_places = lax.optimization_barrier(
        (fetched, means, share, got_places, late_places)
    )

    passage_embed, spread = encode(
        peer_count,
        token_slot,
        fetched,
        lengths,
        pos_table,
        emb_gain,
        emb_bias,
        w_qkv,
        w_out,
        out_bias,
        norm_gain,
        norm_bias,
    )
    all_embeds = lax.all_to_all(
        spread, "dp", split_axis=0, concat_axis=0, tiled=True
    )
    pieces = own_half[2:] + other_half
    new_centroids = late_update(got_places, late_places, all_embeds, share, means, pieces)
    return (passage_embed, new_centroids)


def solution(mesh):
    return jax.shard_map(
        shards,
        mesh=mesh,
        in_specs=(
            P(("groups", "dp"), None),
            P(("groups", "dp")),
            P("dp", None),
            P(),
            P(),
            P(),
            P(),
            P(),
            P(),
            P(),
            P(),
            P(("groups", "dp"), None),
            P(("groups", "dp"), None),
            P(("groups", "dp")),
            P(("groups", "dp"), None),
        ),
        out_specs=(P(("groups", "dp"), None), P(("groups", "dp"), None)),
        check_vma=False,
    )
```

```python
import functools

import jax
import jax.numpy as jnp
from jax import lax
from jax.experimental import pallas as pl
from jax.experimental.pallas import tpu as pltpu
from jax.sharding import PartitionSpec as P

HEADS = 8
HD = 64


def normed(values, gain, shift):
    center = values - jnp.mean(values, axis=-1, keepdims=True)
    spread = jnp.mean(center * center, axis=-1, keepdims=True)
    return center * lax.rsqrt(spread + 1e-12) * gain + shift


def head_sums(weights, seq):
    rows, columns = weights.shape
    lane = lax.broadcasted_iota(jnp.int32, (rows, 2 * seq), 1)
    sums = []
    for start in range(0, columns, 2 * seq):
        pair = weights[:, start : start + 2 * seq]
        first = jnp.sum(jnp.where(lane < seq, pair, 0.0), axis=1, keepdims=True)
        second = jnp.sum(jnp.where(lane < seq, 0.0, pair), axis=1, keepdims=True)
        sums.append(jnp.where(lane < seq, first, second))
    return jnp.concatenate(sums, axis=1)


def encode_kernel(*refs):
    count = (len(refs) - 3) // 2
    far, (out, spread), near, arrived = refs[:count], refs[count : count + 2], refs[-count - 1 : -1], refs[-1]
    w_qkv_far, inner = far[-2], HEADS * HD
    copies = [
        pltpu.make_async_copy(source, target, arrived.at[at])
        for at, (source, target) in enumerate(zip(far, near))
        if source is not w_qkv_far
    ]
    lengths, slots, fetched, pos, emb_gain, emb_bias, out_bias, norm_gain, norm_bias, w_qkv, w_out = near
    out_copy = copies.pop()
    thirds = []
    for third in range(3):
        columns = pl.ds(third * inner, inner)
        thirds.append(
            pltpu.make_async_copy(
                w_qkv_far.at[:, columns], w_qkv.at[:, columns], arrived.at[count + third]
            )
        )
    for copy in copies + thirds + [out_copy]:
        copy.start()
    for copy in copies:
        copy.wait()
    passes = out.shape[0]
    size = [lengths[:, p : p + 1] for p in range(passes)]
    tokens, slot_count = slots.shape[0], fetched.shape[0]
    seq = tokens // passes
    spot = lax.broadcasted_iota(jnp.int32, (tokens, slot_count), 1)
    picker = jnp.where(slots[...] == spot, 1.0, 0.0).astype(jnp.bfloat16)
    tok = jnp.dot(picker, fetched[...], preferred_element_type=jnp.float32)
    where_at = pos[...].astype(jnp.float32)
    summed = tok + jnp.concatenate([where_at] * passes, axis=0)
    embedded = normed(summed, emb_gain[...], emb_bias[...]).astype(jnp.bfloat16)
    parts = []
    for third in range(3):
        thirds[third].wait()
        weights = w_qkv[:, third * inner : (third + 1) * inner]
        part = jnp.dot(embedded, weights, preferred_element_type=jnp.float32)
        parts.append(part.astype(jnp.bfloat16))

    block_row = lax.broadcasted_iota(jnp.int32, (HEADS * seq, inner), 0) // seq
    block_col = lax.broadcasted_iota(jnp.int32, (HEADS * seq, inner), 1) // HD
    same = block_row == block_col
    lane = lax.broadcasted_iota(jnp.int32, (seq, HEADS * seq), 1) % seq
    contexts = []
    for p in range(passes):
        query, keys, vals = (part[p * seq : (p + 1) * seq] for part in parts)
        zero = jnp.zeros((), jnp.bfloat16)
        keys = jnp.where(same, jnp.concatenate([keys] * HEADS, axis=0), zero)
        vals = jnp.where(same, jnp.concatenate([vals] * HEADS, axis=0), zero)
        scores = lax.dot_general(
            query, keys, (((1,), (1,)), ((), ())), preferred_element_type=jnp.float32
        ) * HD ** (-0.5)
        weights = jnp.where(lane < size[p], jnp.exp(scores), 0.0)
        probs = (weights / head_sums(weights, seq)).astype(jnp.bfloat16)
        contexts.append(jnp.dot(probs, vals, preferred_element_type=jnp.float32))
    context = jnp.concatenate(contexts, axis=0).astype(jnp.bfloat16)
    out_copy.wait()
    attended = jnp.dot(context, w_out[...], preferred_element_type=jnp.float32) + out_bias[...]
    hidden = normed(embedded.astype(jnp.float32) + attended, norm_gain[...], norm_bias[...])
    row = lax.broadcasted_iota(jnp.int32, (seq, 1), 0)
    for p in range(passes):
        kept = jnp.where(row < size[p], hidden[p * seq : (p + 1) * seq], 0.0)
        pooled = jnp.sum(kept, axis=0, keepdims=True) / size[p].astype(jnp.float32)
        scale = lax.rsqrt(jnp.mean(pooled * pooled, axis=-1, keepdims=True) + 1e-06)
        out[p : p + 1, :] = (pooled * scale).astype(jnp.bfloat16)
    spread[...] = jnp.broadcast_to(out[...][None], spread.shape)


def encode(
    peers, slots, fetched, lengths, pos_table, emb_gain, emb_bias, w_qkv, w_out, out_bias, norm_gain, norm_bias
):
    width = fetched.shape[1]
    tokens = slots.shape[0]
    passes = lengths.shape[0]
    macs = tokens * width * (fetched.shape[0] + 4 * HEADS * HD)
    operands = (
        lengths[None],
        slots,
        fetched,
        pos_table,
        emb_gain[None],
        emb_bias[None],
        out_bias[None],
        norm_gain[None],
        norm_bias[None],
        w_qkv,
        w_out,
    )
    return pl.pallas_call(
        encode_kernel,
        out_shape=[
            jax.ShapeDtypeStruct((passes, width), jnp.bfloat16),
            jax.ShapeDtypeStruct((peers, passes, width), jnp.bfloat16),
        ],
        in_specs=[pl.BlockSpec(memory_space=pltpu.HBM)] * len(operands),
        out_specs=[pl.BlockSpec(memory_space=pltpu.VMEM)] * 2,
        scratch_shapes=[pltpu.VMEM(operand.shape, operand.dtype) for operand in operands]
        + [pltpu.SemaphoreType.DMA((len(operands) + 3,))],
        compiler_params=pltpu.CompilerParams(vmem_limit_bytes=60 * 1024 * 1024),
        cost_estimate=pl.CostEstimate(
            flops=2 * macs, bytes_accessed=6 * 1024 * 1024, transcendentals=0
        ),
        name="encode",
    )(*operands)


def padded(rows):
    return -(-rows // 16) * 16


def rank_bits(count):
    return max(1, (count - 1).bit_length())


def ranks(kind):
    count = kind.shape[1]
    at = lax.broadcasted_iota(jnp.int32, (count, count), 0)
    by = lax.broadcasted_iota(jnp.int32, (count, count), 1)
    across = jnp.broadcast_to(kind, (count, count))
    down = jnp.sum(jnp.where(at == by, across, 0), axis=1, keepdims=True)
    same = down == across
    rank_row = jnp.sum(jnp.where(same & (at < by), 1, 0), axis=0, keepdims=True)
    rank_col = jnp.sum(jnp.where(same & (by < at), 1, 0), axis=1, keepdims=True)
    return down, rank_row, rank_col


def route_kernel(
    sizes,
    token_ids_far,
    owners_far,
    row_slot_far,
    sibling_far,
    plan,
    token_slot_far,
    code,
    sibling_code,
    *near,
):
    peers, vocab_rows, token_cap, row_cap, pooled = sizes
    token_ids, owners, row_slot, sibling, token_slot, arrived = near
    copies = [
        pltpu.make_async_copy(source, target, arrived.at[at])
        for at, (source, target) in enumerate(
            (
                (token_ids_far, token_ids),
                (owners_far, owners),
                (row_slot_far, row_slot),
                (sibling_far, sibling),
            )
        )
    ]
    for copy in copies:
        copy.start()
    for copy in copies:
        copy.wait()
    ids = jnp.concatenate([token_ids[p : p + 1, :] for p in range(token_ids.shape[0])], axis=1)
    tokens, rows = ids.shape[1], owners.shape[1]
    count = tokens + rows
    edge = (lax.broadcasted_iota(jnp.int32, (peers, tokens), 0) + 1) * vocab_rows
    holder = jnp.sum(jnp.where(ids >= edge, 1, 0), axis=0, keepdims=True)
    values = jnp.concatenate([ids - holder * vocab_rows, row_slot[...]], axis=1)

    kind = jnp.concatenate([holder, owners[...] + peers], axis=1)
    down, rank_row, rank_col = ranks(kind)

    code[...] = owners[...] * 2 ** rank_bits(rows) + rank_row[:, tokens:]
    sibling_code[...] = sibling[...] * 2 ** rank_bits(rows) + ranks(sibling[...])[1]
    goal = jnp.concatenate([holder, owners[...]], axis=1)
    peer = lax.broadcasted_iota(jnp.int32, (peers, count), 0)
    left = jnp.where(peer == goal, values + 1, 0).astype(jnp.float32)
    columns = token_cap + row_cap + pooled
    column = lax.broadcasted_iota(jnp.int32, (count, columns), 1)
    entry = lax.broadcasted_iota(jnp.int32, (count, 1), 0)
    first = jnp.where(entry < tokens, rank_col, rank_col + token_cap)
    second = entry - (count - pooled) + token_cap + row_cap
    second = jnp.where(entry < count - pooled, -1, second)
    right = jnp.where((column == first) | (column == second), 1.0, 0.0)
    filled = jnp.dot(
        left, right, preferred_element_type=jnp.float32, precision=lax.Precision.HIGHEST
    )
    filled = filled.astype(jnp.int32) - 1
    for p in range(peers):
        plan[p, :, :rows] = code[...]
        plan[p, :, rows:] = filled[p : p + 1]
    token_slot[...] = down[:tokens] * token_cap + rank_col[:tokens]
    send = pltpu.make_async_copy(token_slot, token_slot_far, arrived.at[4])
    send.start()
    send.wait()


def route(token_ids, owners, row_slot, sibling_owners, sizes):
    peers, _, token_cap, row_cap, pooled = sizes
    passes, seq_len = token_ids.shape
    rows = owners.shape[1]
    ints = lambda *shape: jax.ShapeDtypeStruct(shape, jnp.int32)
    return pl.pallas_call(
        functools.partial(route_kernel, sizes),
        out_shape=[
            ints(peers, 1, rows + token_cap + row_cap + pooled),
            ints(passes * seq_len, 1),
            ints(1, rows),
            ints(1, rows),
        ],
        in_specs=[pl.BlockSpec(memory_space=pltpu.HBM)] * 4,
        out_specs=[
            pl.BlockSpec(memory_space=pltpu.VMEM),
            pl.BlockSpec(memory_space=pltpu.HBM),
            pl.BlockSpec(memory_space=pltpu.VMEM),
            pl.BlockSpec(memory_space=pltpu.VMEM),
        ],
        scratch_shapes=[
            pltpu.VMEM(token_ids.shape, jnp.int32),
            pltpu.VMEM(owners.shape, jnp.int32),
            pltpu.VMEM(row_slot.shape, jnp.int32),
            pltpu.VMEM(owners.shape, jnp.int32),
            pltpu.VMEM((passes * seq_len, 1), jnp.int32),
            pltpu.SemaphoreType.DMA((5,)),
        ],
        compiler_params=pltpu.CompilerParams(vmem_limit_bytes=60 * 1024 * 1024),
        name="route",
    )(token_ids, owners, row_slot, sibling_owners)


def pack_kernel(half, row_cap, count, picks, pieces, rest, *refs):
    me = lax.axis_index("dp")
    operands = 2 + 2 * pieces
    far, refs = refs[:operands], refs[operands:]
    steps = half // 2
    outs, refs = refs[: steps + bool(rest)], refs[steps + bool(rest) :]
    near, (blocks, tail, arrived, left) = refs[:operands], refs[operands:]
    size = blocks.shape[0] // steps
    copies = [
        pltpu.make_async_copy(far[at], near[at], arrived.at[at]) for at in range(operands)
    ]
    for copy in copies:
        copy.start()
    for copy in copies[:2]:
        copy.wait()
    if size > 2 * row_cap:
        blocks[...] = jnp.zeros(blocks.shape, blocks.dtype)
    for source in range(2):
        if picks is None:
            code = near[source][...]
        else:
            code = near[source][me ^ picks[source], :, :count]
        bits = rank_bits(count)
        owner, rank = code >> bits, code & (2**bits - 1)
        fits = ((owner ^ me) & (1 | half)) == 0
        chip = ((owner ^ me) & (half - 1)) >> 1
        slot = jnp.where(fits, chip * row_cap + rank, -1)
        packed, at = 0.0, 0
        for piece in range(2 + source * pieces, 2 + (source + 1) * pieces):
            rows = near[piece]
            spot = lax.broadcasted_iota(jnp.int32, (steps * row_cap, rows.shape[0]), 0)
            table = jnp.where(slot[:, at : at + rows.shape[0]] == spot, 1.0, 0.0)
            copies[piece].wait()
            packed += jnp.dot(
                table.astype(jnp.bfloat16), rows[...], preferred_element_type=jnp.float32
            )
            at += rows.shape[0]
        packed = packed.astype(jnp.bfloat16)
        for step in range(steps):
            first = step * size + source * row_cap
            blocks[first : first + row_cap, :] = packed[step * row_cap : (step + 1) * row_cap]
    sends = [
        pltpu.make_async_copy(
            blocks.at[pl.ds(step * size, size)], outs[step], left.at[step]
        )
        for step in range(steps)
    ]
    if rest:
        tail[...] = near[2][near[2].shape[0] - rest :, :]
        sends.append(pltpu.make_async_copy(tail, outs[steps], left.at[steps]))
    for send in sends:
        send.start()
    for send in sends:
        send.wait()


def pack_rows(codes_a, codes_b, rows_a, rows_b, half, row_cap, count, picks=None, rest=0):
    width = rows_a[0].shape[1]
    total = sum(piece.shape[0] for piece in rows_a)
    steps = half // 2
    size = padded(2 * row_cap)
    operands = (codes_a, codes_b, *rows_a, *rows_b)
    shapes = [(size, width)] * steps + [(rest, width)] * bool(rest)
    return pl.pallas_call(
        functools.partial(pack_kernel, half, row_cap, count, picks, len(rows_a), rest),
        out_shape=[jax.ShapeDtypeStruct(shape, jnp.bfloat16) for shape in shapes],
        in_specs=[pl.BlockSpec(memory_space=pltpu.HBM)] * len(operands),
        out_specs=[pl.BlockSpec(memory_space=pltpu.HBM)] * len(shapes),
        scratch_shapes=[
            *(pltpu.VMEM(operand.shape, operand.dtype) for operand in operands),
            pltpu.VMEM((steps * size, width), jnp.bfloat16),
            pltpu.VMEM((max(rest, 16), width), jnp.bfloat16),
            pltpu.SemaphoreType.DMA((len(operands),)),
            pltpu.SemaphoreType.DMA((len(shapes),)),
        ],
        compiler_params=pltpu.CompilerParams(vmem_limit_bytes=60 * 1024 * 1024),
        cost_estimate=pl.CostEstimate(
            flops=4 * steps * row_cap * width * total,
            bytes_accessed=4 * width * (total + steps * row_cap),
            transcendentals=0,
        ),
        name="pack",
    )(*operands)


def onehot(where_to, first, count):
    centre = lax.broadcasted_iota(jnp.int32, (count, where_to.shape[1]), 0) + first
    return jnp.where(centre == where_to, 1.0, 0.0)


BLOCK = 128


def early_kernel(places_far, centroids_far, *rest):
    pieces, (out_far, share_far, places, rows, centroids, out, share, arrived, left) = rest[:-9], rest[-9:]
    size = pieces[0].shape[0]
    steps = centroids.shape[0] // BLOCK
    copies = [pltpu.make_async_copy(places_far, places, arrived.at[0])]
    for at, piece in enumerate(pieces):
        copies.append(
            pltpu.make_async_copy(piece, rows.at[pl.ds(at * size, size)], arrived.at[1 + at])
        )
    loads = []
    for step in range(steps):
        block = pl.ds(step * BLOCK, BLOCK)
        loads.append(
            pltpu.make_async_copy(
                centroids_far.at[block], centroids.at[block], arrived.at[1 + len(pieces) + step]
            )
        )
    for copy in copies + loads:
        copy.start()
    for copy in copies:
        copy.wait()
    sends = []
    for step in range(steps):
        block = pl.ds(step * BLOCK, BLOCK)
        hot = onehot(places[...], step * BLOCK, BLOCK)
        counts = jnp.sum(hot, axis=1, keepdims=True)
        scale = jnp.where(counts > 0, 1.0 / jnp.maximum(counts, 1.0), 0.0)
        sums = jnp.dot(
            hot[:, : rows.shape[0]].astype(jnp.bfloat16),
            rows[...],
            preferred_element_type=jnp.float32,
        )
        loads[step].wait()
        out[block, :] = jnp.where(counts > 0, sums * scale, centroids[block, :])
        share[block, :] = jnp.broadcast_to(scale, (BLOCK, share.shape[1]))
        sends.append(pltpu.make_async_copy(out.at[block], out_far.at[block], left.at[step]))
        sends[-1].start()
    sends.append(pltpu.make_async_copy(share, share_far, left.at[steps]))
    sends[-1].start()
    for send in sends:
        send.wait()


def late_kernel(places_far, late_far, spread_far, share_far, early_far, *rest):
    pieces, rest = rest[:-10], rest[-10:]
    out_far, places, late, spread, share, rows, early, out, arrived, left = rest
    size, passes = pieces[0].shape[0], spread.shape[1]
    steps = early.shape[0] // BLOCK
    loads = [
        pltpu.make_async_copy(source, target, arrived.at[at])
        for at, (source, target) in enumerate(
            ((places_far, places), (late_far, late), (spread_far, spread), (share_far, share))
        )
    ]
    for at, piece in enumerate(pieces):
        loads.append(
            pltpu.make_async_copy(piece, rows.at[pl.ds(at * size, size)], arrived.at[4 + at])
        )
    starts = []
    for step in range(steps):
        block = pl.ds(step * BLOCK, BLOCK)
        starts.append(
            pltpu.make_async_copy(
                early_far.at[block], early.at[block], arrived.at[len(loads) + step]
            )
        )
    for copy in loads + starts:
        copy.start()
    for copy in loads:
        copy.wait()
    top = len(pieces) * size
    for peer in range(spread.shape[0]):
        rows[top + peer * passes : top + (peer + 1) * passes, :] = spread[peer]
    where_to = jnp.concatenate([places[:, places.shape[1] - top :], late[...]], axis=1)
    sends = []
    for step in range(steps):
        block = pl.ds(step * BLOCK, BLOCK)
        hot = onehot(where_to, step * BLOCK, BLOCK).astype(jnp.bfloat16)
        sums = jnp.dot(hot, rows[...], preferred_element_type=jnp.float32)
        starts[step].wait()
        out[block, :] = early[block, :] + sums * share[block, :1]
        sends.append(pltpu.make_async_copy(out.at[block], out_far.at[block], left.at[step]))
        sends[-1].start()
    for send in sends:
        send.wait()


def early_update(places, centroids, pieces):
    centre_count, width = centroids.shape
    row_total = sum(piece.shape[0] for piece in pieces)
    wide = pltpu.VMEM(centroids.shape, jnp.float32)
    thin = (centre_count, 128)
    steps = centre_count // BLOCK
    return pl.pallas_call(
        early_kernel,
        out_shape=[
            jax.ShapeDtypeStruct(centroids.shape, jnp.float32),
            jax.ShapeDtypeStruct(thin, jnp.float32),
        ],
        in_specs=[pl.BlockSpec(memory_space=pl.ANY)] * (2 + len(pieces)),
        out_specs=[pl.BlockSpec(memory_space=pltpu.HBM)] * 2,
        scratch_shapes=[
            pltpu.VMEM(places.shape, jnp.int32),
            pltpu.VMEM((row_total, width), jnp.bfloat16),
            wide,
            wide,
            pltpu.VMEM(thin, jnp.float32),
            pltpu.SemaphoreType.DMA((1 + len(pieces) + steps,)),
            pltpu.SemaphoreType.DMA((steps + 1,)),
        ],
        compiler_params=pltpu.CompilerParams(vmem_limit_bytes=60 * 1024 * 1024),
        cost_estimate=pl.CostEstimate(
            flops=100 * centre_count * width * row_total,
            bytes_accessed=200 * centre_count * width,
            transcendentals=0,
        ),
        name="early",
    )(places, centroids, *pieces)


def late_update(places, late, spread, share, early, pieces):
    centre_count, width = early.shape
    row_total = sum(piece.shape[0] for piece in pieces) + late.shape[1]
    wide = pltpu.VMEM(early.shape, jnp.float32)
    steps = centre_count // BLOCK
    return pl.pallas_call(
        late_kernel,
        out_shape=jax.ShapeDtypeStruct(early.shape, jnp.float32),
        in_specs=[pl.BlockSpec(memory_space=pltpu.HBM)] * (5 + len(pieces)),
        out_specs=pl.BlockSpec(memory_space=pltpu.HBM),
        scratch_shapes=[
            pltpu.VMEM(places.shape, jnp.int32),
            pltpu.VMEM(late.shape, jnp.int32),
            pltpu.VMEM(spread.shape, jnp.bfloat16),
            pltpu.VMEM(share.shape, jnp.float32),
            pltpu.VMEM((row_total, width), jnp.bfloat16),
            wide,
            wide,
            pltpu.SemaphoreType.DMA((4 + len(pieces) + steps,)),
            pltpu.SemaphoreType.DMA((steps,)),
        ],
        compiler_params=pltpu.CompilerParams(vmem_limit_bytes=60 * 1024 * 1024),
        cost_estimate=pl.CostEstimate(
            flops=2 * centre_count * width * row_total,
            bytes_accessed=8 * centre_count * width,
            transcendentals=0,
        ),
        name="late",
    )(places, late, spread, share, early, *pieces)


def shards(
    token_ids,
    lengths,
    word_table,
    pos_table,
    emb_gain,
    emb_bias,
    w_qkv,
    w_out,
    out_bias,
    norm_gain,
    norm_bias,
    stored_rows,
    row_owner,
    row_slot,
    centroids,
):
    peer_count = lax.axis_size("dp")
    half = peer_count // 2
    width = word_table.shape[1]
    vocab_rows = word_table.shape[0]
    passes, seq_len = token_ids.shape
    token_count = passes * seq_len
    row_count = row_slot.shape[0]
    store_count = stored_rows.shape[0]
    token_cap = max(2, 3 * token_count // peer_count)
    row_cap = max(2, 3 * row_count // peer_count)

    across = [(i, i ^ half) for i in range(peer_count)]
    beside = [(i, i ^ 1) for i in range(peer_count)]

    def hand_on(blocks):
        got = [blocks[0]]
        for step in range(1, len(blocks)):
            moves = [(i, i ^ (2 * step)) for i in range(peer_count)]
            got.append(lax.ppermute(blocks[step], "dp", moves))
        return got

    ahead = store_count * 2 // 3 // 16 * 16
    sibling_rows = lax.ppermute(stored_rows, "dp", beside)
    first_rows = lax.ppermute(stored_rows[:ahead], "dp", across)
    sizes = (peer_count, vocab_rows, token_cap, row_cap, row_count - store_count)
    owners = row_owner.reshape(1, row_count)
    sibling_owners = lax.ppermute(owners, "dp", beside)
    plan, token_slot, code, sibling_code = route(
        token_ids, owners, row_slot[None], sibling_owners, sizes
    )
    plan, sibling_rows = lax.optimization_barrier((plan, sibling_rows))
    codes = lax.all_to_all(plan, "dp", split_axis=0, concat_axis=0, tiled=True)
    *blocks, last_rows = pack_rows(
        code,
        sibling_code,
        [stored_rows],
        [sibling_rows],
        half,
        row_cap,
        row_count,
        rest=store_count - ahead,
    )
    last_rows = lax.ppermute(last_rows, "dp", across)
    own_half = hand_on(blocks)
    plan = codes[:, 0, row_count:]
    wanted = plan[:, :token_cap].reshape(peer_count * token_cap)
    chosen = wanted[:, None] == jnp.arange(vocab_rows, dtype=jnp.int32)[None, :]
    found = jnp.dot(
        chosen.astype(jnp.bfloat16), word_table, preferred_element_type=jnp.float32
    ).astype(jnp.bfloat16)
    found, first_rows, own_half[:2] = lax.optimization_barrier(
        (found, first_rows, own_half[:2])
    )
    fetched = lax.all_to_all(
        found.reshape(peer_count, token_cap, width), "dp", split_axis=0, concat_axis=0, tiled=True
    ).reshape(peer_count * token_cap, width)

    sources = lax.axis_index("dp") ^ jnp.arange(peer_count, dtype=jnp.int32)
    got_places = plan[:, token_cap : token_cap + row_cap][sources].reshape(half, 2 * row_cap)
    spare = padded(2 * row_cap) - 2 * row_cap
    got_places = jnp.pad(got_places, ((0, 0), (0, spare)), constant_values=-1).reshape(1, -1)
    near_rows, last_rows = lax.optimization_barrier((own_half[:2], last_rows))
    means, share = early_update(got_places, centroids, near_rows)
    first_rows, last_rows, means = lax.optimization_barrier((first_rows, last_rows, means))
    partner_rows = [first_rows, last_rows]
    far_rows = [lax.ppermute(rows, "dp", beside) for rows in partner_rows]
    picks = (half, half ^ 1)
    blocks = pack_rows(codes, codes, partner_rows, far_rows, half, row_cap, row_count, picks)
    other_half = hand_on(blocks)
    late_places = plan[:, token_cap + row_cap :].reshape(1, -1)
    fetched, means, share, got_places, late_places = lax.optimization_barrier(
        (fetched, means, share, got_places, late_places)
    )

    passage_embed, spread = encode(
        peer_count,
        token_slot,
        fetched,
        lengths,
        pos_table,
        emb_gain,
        emb_bias,
        w_qkv,
        w_out,
        out_bias,
        norm_gain,
        norm_bias,
    )
    all_embeds = lax.all_to_all(
        spread, "dp", split_axis=0, concat_axis=0, tiled=True
    )
    pieces = own_half[2:] + other_half
    new_centroids = late_update(got_places, late_places, all_embeds, share, means, pieces)
    return (passage_embed, new_centroids)


def solution(mesh):
    return jax.shard_map(
        shards,
        mesh=mesh,
        in_specs=(
            P(("groups", "dp"), None),
            P(("groups", "dp")),
            P("dp", None),
            P(),
            P(),
            P(),
            P(),
            P(),
            P(),
            P(),
            P(),
            P(("groups", "dp"), None),
            P(("groups", "dp"), None),
            P(("groups", "dp")),
            P(("groups", "dp"), None),
        ),
        out_specs=(P(("groups", "dp"), None), P(("groups", "dp"), None)),
        check_vma=False,
    )
```

```python
import functools

import jax
import jax.numpy as jnp
from jax import lax
from jax.experimental import pallas as pl
from jax.experimental.pallas import tpu as pltpu
from jax.sharding import PartitionSpec as P

HEADS = 8
HD = 64


def normed(values, gain, shift):
    center = values - jnp.mean(values, axis=-1, keepdims=True)
    spread = jnp.mean(center * center, axis=-1, keepdims=True)
    return center * lax.rsqrt(spread + 1e-12) * gain + shift


def head_sums(weights, seq):
    rows, columns = weights.shape
    lane = lax.broadcasted_iota(jnp.int32, (rows, 2 * seq), 1)
    sums = []
    for start in range(0, columns, 2 * seq):
        pair = weights[:, start : start + 2 * seq]
        first = jnp.sum(jnp.where(lane < seq, pair, 0.0), axis=1, keepdims=True)
        second = jnp.sum(jnp.where(lane < seq, 0.0, pair), axis=1, keepdims=True)
        sums.append(jnp.where(lane < seq, first, second))
    return jnp.concatenate(sums, axis=1)


def encode_kernel(*refs):
    count = (len(refs) - 3) // 2
    far, (out, spread), near, arrived = refs[:count], refs[count : count + 2], refs[-count - 1 : -1], refs[-1]
    w_qkv_far, inner = far[-2], HEADS * HD
    copies = [
        pltpu.make_async_copy(source, target, arrived.at[at])
        for at, (source, target) in enumerate(zip(far, near))
        if source is not w_qkv_far
    ]
    lengths, slots, fetched, pos, emb_gain, emb_bias, out_bias, norm_gain, norm_bias, w_qkv, w_out = near
    out_copy = copies.pop()
    thirds = []
    for third in range(3):
        columns = pl.ds(third * inner, inner)
        thirds.append(
            pltpu.make_async_copy(
                w_qkv_far.at[:, columns], w_qkv.at[:, columns], arrived.at[count + third]
            )
        )
    for copy in copies + thirds + [out_copy]:
        copy.start()
    for copy in copies:
        copy.wait()
    passes = out.shape[0]
    size = [lengths[:, p : p + 1] for p in range(passes)]
    tokens, slot_count = slots.shape[0], fetched.shape[0]
    seq = tokens // passes
    spot = lax.broadcasted_iota(jnp.int32, (tokens, slot_count), 1)
    picker = jnp.where(slots[...] == spot, 1.0, 0.0).astype(jnp.bfloat16)
    tok = jnp.dot(picker, fetched[...], preferred_element_type=jnp.float32)
    where_at = pos[...].astype(jnp.float32)
    summed = tok + jnp.concatenate([where_at] * passes, axis=0)
    embedded = normed(summed, emb_gain[...], emb_bias[...]).astype(jnp.bfloat16)
    parts = []
    for third in range(3):
        thirds[third].wait()
        weights = w_qkv[:, third * inner : (third + 1) * inner]
        part = jnp.dot(embedded, weights, preferred_element_type=jnp.float32)
        parts.append(part.astype(jnp.bfloat16))

    block_row = lax.broadcasted_iota(jnp.int32, (HEADS * seq, inner), 0) // seq
    block_col = lax.broadcasted_iota(jnp.int32, (HEADS * seq, inner), 1) // HD
    same = block_row == block_col
    lane = lax.broadcasted_iota(jnp.int32, (seq, HEADS * seq), 1) % seq
    contexts = []
    for p in range(passes):
        query, keys, vals = (part[p * seq : (p + 1) * seq] for part in parts)
        zero = jnp.zeros((), jnp.bfloat16)
        keys = jnp.where(same, jnp.concatenate([keys] * HEADS, axis=0), zero)
        vals = jnp.where(same, jnp.concatenate([vals] * HEADS, axis=0), zero)
        scores = lax.dot_general(
            query, keys, (((1,), (1,)), ((), ())), preferred_element_type=jnp.float32
        ) * HD ** (-0.5)
        weights = jnp.where(lane < size[p], jnp.exp(scores), 0.0)
        probs = (weights / head_sums(weights, seq)).astype(jnp.bfloat16)
        contexts.append(jnp.dot(probs, vals, preferred_element_type=jnp.float32))
    context = jnp.concatenate(contexts, axis=0).astype(jnp.bfloat16)
    out_copy.wait()
    attended = jnp.dot(context, w_out[...], preferred_element_type=jnp.float32) + out_bias[...]
    hidden = normed(embedded.astype(jnp.float32) + attended, norm_gain[...], norm_bias[...])
    row = lax.broadcasted_iota(jnp.int32, (seq, 1), 0)
    for p in range(passes):
        kept = jnp.where(row < size[p], hidden[p * seq : (p + 1) * seq], 0.0)
        pooled = jnp.sum(kept, axis=0, keepdims=True) / size[p].astype(jnp.float32)
        scale = lax.rsqrt(jnp.mean(pooled * pooled, axis=-1, keepdims=True) + 1e-06)
        out[p : p + 1, :] = (pooled * scale).astype(jnp.bfloat16)
    spread[...] = jnp.broadcast_to(out[...][None], spread.shape)


def encode(
    peers, slots, fetched, lengths, pos_table, emb_gain, emb_bias, w_qkv, w_out, out_bias, norm_gain, norm_bias
):
    width = fetched.shape[1]
    tokens = slots.shape[0]
    passes = lengths.shape[0]
    macs = tokens * width * (fetched.shape[0] + 4 * HEADS * HD)
    operands = (
        lengths[None],
        slots,
        fetched,
        pos_table,
        emb_gain[None],
        emb_bias[None],
        out_bias[None],
        norm_gain[None],
        norm_bias[None],
        w_qkv,
        w_out,
    )
    return pl.pallas_call(
        encode_kernel,
        out_shape=[
            jax.ShapeDtypeStruct((passes, width), jnp.bfloat16),
            jax.ShapeDtypeStruct((peers, passes, width), jnp.bfloat16),
        ],
        in_specs=[pl.BlockSpec(memory_space=pltpu.HBM)] * len(operands),
        out_specs=[pl.BlockSpec(memory_space=pltpu.VMEM)] * 2,
        scratch_shapes=[pltpu.VMEM(operand.shape, operand.dtype) for operand in operands]
        + [pltpu.SemaphoreType.DMA((len(operands) + 3,))],
        compiler_params=pltpu.CompilerParams(vmem_limit_bytes=60 * 1024 * 1024),
        cost_estimate=pl.CostEstimate(
            flops=2 * macs, bytes_accessed=6 * 1024 * 1024, transcendentals=0
        ),
        name="encode",
    )(*operands)


def padded(rows):
    return -(-rows // 16) * 16


def rank_bits(count):
    return max(1, (count - 1).bit_length())


def ranks(kind):
    count = kind.shape[1]
    at = lax.broadcasted_iota(jnp.int32, (count, count), 0)
    by = lax.broadcasted_iota(jnp.int32, (count, count), 1)
    across = jnp.broadcast_to(kind, (count, count))
    down = jnp.sum(jnp.where(at == by, across, 0), axis=1, keepdims=True)
    same = down == across
    rank_row = jnp.sum(jnp.where(same & (at < by), 1, 0), axis=0, keepdims=True)
    rank_col = jnp.sum(jnp.where(same & (by < at), 1, 0), axis=1, keepdims=True)
    return down, rank_row, rank_col


def route_kernel(
    sizes,
    token_ids_far,
    owners_far,
    row_slot_far,
    sibling_far,
    plan,
    token_slot_far,
    code,
    sibling_code,
    *near,
):
    peers, vocab_rows, token_cap, row_cap, pooled = sizes
    token_ids, owners, row_slot, sibling, token_slot, arrived = near
    copies = [
        pltpu.make_async_copy(source, target, arrived.at[at])
        for at, (source, target) in enumerate(
            (
                (token_ids_far, token_ids),
                (owners_far, owners),
                (row_slot_far, row_slot),
                (sibling_far, sibling),
            )
        )
    ]
    for copy in copies:
        copy.start()
    for copy in copies:
        copy.wait()
    ids = jnp.concatenate([token_ids[p : p + 1, :] for p in range(token_ids.shape[0])], axis=1)
    tokens, rows = ids.shape[1], owners.shape[1]
    count = tokens + rows
    edge = (lax.broadcasted_iota(jnp.int32, (peers, tokens), 0) + 1) * vocab_rows
    holder = jnp.sum(jnp.where(ids >= edge, 1, 0), axis=0, keepdims=True)
    values = jnp.concatenate([ids - holder * vocab_rows, row_slot[...]], axis=1)

    kind = jnp.concatenate([holder, owners[...] + peers], axis=1)
    down, rank_row, rank_col = ranks(kind)

    code[...] = owners[...] * 2 ** rank_bits(rows) + rank_row[:, tokens:]
    sibling_code[...] = sibling[...] * 2 ** rank_bits(rows) + ranks(sibling[...])[1]
    goal = jnp.concatenate([holder, owners[...]], axis=1)
    peer = lax.broadcasted_iota(jnp.int32, (peers, count), 0)
    left = jnp.where(peer == goal, values + 1, 0).astype(jnp.float32)
    columns = token_cap + row_cap + pooled
    column = lax.broadcasted_iota(jnp.int32, (count, columns), 1)
    entry = lax.broadcasted_iota(jnp.int32, (count, 1), 0)
    first = jnp.where(entry < tokens, rank_col, rank_col + token_cap)
    second = entry - (count - pooled) + token_cap + row_cap
    second = jnp.where(entry < count - pooled, -1, second)
    right = jnp.where((column == first) | (column == second), 1.0, 0.0)
    filled = jnp.dot(
        left, right, preferred_element_type=jnp.float32, precision=lax.Precision.HIGHEST
    )
    filled = filled.astype(jnp.int32) - 1
    for p in range(peers):
        plan[p, :, :rows] = code[...]
        plan[p, :, rows:] = filled[p : p + 1]
    token_slot[...] = down[:tokens] * token_cap + rank_col[:tokens]
    send = pltpu.make_async_copy(token_slot, token_slot_far, arrived.at[4])
    send.start()
    send.wait()


def route(token_ids, owners, row_slot, sibling_owners, sizes):
    peers, _, token_cap, row_cap, pooled = sizes
    passes, seq_len = token_ids.shape
    rows = owners.shape[1]
    ints = lambda *shape: jax.ShapeDtypeStruct(shape, jnp.int32)
    return pl.pallas_call(
        functools.partial(route_kernel, sizes),
        out_shape=[
            ints(peers, 1, rows + token_cap + row_cap + pooled),
            ints(passes * seq_len, 1),
            ints(1, rows),
            ints(1, rows),
        ],
        in_specs=[pl.BlockSpec(memory_space=pltpu.HBM)] * 4,
        out_specs=[
            pl.BlockSpec(memory_space=pltpu.VMEM),
            pl.BlockSpec(memory_space=pltpu.HBM),
            pl.BlockSpec(memory_space=pltpu.VMEM),
            pl.BlockSpec(memory_space=pltpu.VMEM),
        ],
        scratch_shapes=[
            pltpu.VMEM(token_ids.shape, jnp.int32),
            pltpu.VMEM(owners.shape, jnp.int32),
            pltpu.VMEM(row_slot.shape, jnp.int32),
            pltpu.VMEM(owners.shape, jnp.int32),
            pltpu.VMEM((passes * seq_len, 1), jnp.int32),
            pltpu.SemaphoreType.DMA((5,)),
        ],
        compiler_params=pltpu.CompilerParams(vmem_limit_bytes=60 * 1024 * 1024),
        name="route",
    )(token_ids, owners, row_slot, sibling_owners)


def pack_kernel(half, row_cap, count, picks, pieces, rest, *refs):
    me = lax.axis_index("dp")
    operands = 2 + 2 * pieces
    far, refs = refs[:operands], refs[operands:]
    steps = half // 2
    outs, refs = refs[: steps + bool(rest)], refs[steps + bool(rest) :]
    near, (blocks, tail, arrived, left) = refs[:operands], refs[operands:]
    size = blocks.shape[0] // steps
    copies = [
        pltpu.make_async_copy(far[at], near[at], arrived.at[at]) for at in range(operands)
    ]
    for copy in copies:
        copy.start()
    for copy in copies[:2]:
        copy.wait()
    if size > 2 * row_cap:
        blocks[...] = jnp.zeros(blocks.shape, blocks.dtype)
    for source in range(2):
        if picks is None:
            code = near[source][...]
        else:
            code = near[source][me ^ picks[source], :, :count]
        bits = rank_bits(count)
        owner, rank = code >> bits, code & (2**bits - 1)
        fits = ((owner ^ me) & (1 | half)) == 0
        chip = ((owner ^ me) & (half - 1)) >> 1
        slot = jnp.where(fits, chip * row_cap + rank, -1)
        packed, at = 0.0, 0
        for piece in range(2 + source * pieces, 2 + (source + 1) * pieces):
            rows = near[piece]
            spot = lax.broadcasted_iota(jnp.int32, (steps * row_cap, rows.shape[0]), 0)
            table = jnp.where(slot[:, at : at + rows.shape[0]] == spot, 1.0, 0.0)
            copies[piece].wait()
            packed += jnp.dot(
                table.astype(jnp.bfloat16), rows[...], preferred_element_type=jnp.float32
            )
            at += rows.shape[0]
        packed = packed.astype(jnp.bfloat16)
        for step in range(steps):
            first = step * size + source * row_cap
            blocks[first : first + row_cap, :] = packed[step * row_cap : (step + 1) * row_cap]
    sends = [
        pltpu.make_async_copy(
            blocks.at[pl.ds(step * size, size)], outs[step], left.at[step]
        )
        for step in range(steps)
    ]
    if rest:
        tail[...] = near[2][near[2].shape[0] - rest :, :]
        sends.append(pltpu.make_async_copy(tail, outs[steps], left.at[steps]))
    for send in sends:
        send.start()
    for send in sends:
        send.wait()


def pack_rows(codes_a, codes_b, rows_a, rows_b, half, row_cap, count, picks=None, rest=0):
    width = rows_a[0].shape[1]
    total = sum(piece.shape[0] for piece in rows_a)
    steps = half // 2
    size = padded(2 * row_cap)
    operands = (codes_a, codes_b, *rows_a, *rows_b)
    shapes = [(size, width)] * steps + [(rest, width)] * bool(rest)
    return pl.pallas_call(
        functools.partial(pack_kernel, half, row_cap, count, picks, len(rows_a), rest),
        out_shape=[jax.ShapeDtypeStruct(shape, jnp.bfloat16) for shape in shapes],
        in_specs=[pl.BlockSpec(memory_space=pltpu.HBM)] * len(operands),
        out_specs=[pl.BlockSpec(memory_space=pltpu.HBM)] * len(shapes),
        scratch_shapes=[
            *(pltpu.VMEM(operand.shape, operand.dtype) for operand in operands),
            pltpu.VMEM((steps * size, width), jnp.bfloat16),
            pltpu.VMEM((max(rest, 16), width), jnp.bfloat16),
            pltpu.SemaphoreType.DMA((len(operands),)),
            pltpu.SemaphoreType.DMA((len(shapes),)),
        ],
        compiler_params=pltpu.CompilerParams(vmem_limit_bytes=60 * 1024 * 1024),
        cost_estimate=pl.CostEstimate(
            flops=4 * steps * row_cap * width * total,
            bytes_accessed=4 * width * (total + steps * row_cap),
            transcendentals=0,
        ),
        name="pack",
    )(*operands)


def onehot(where_to, first, count):
    centre = lax.broadcasted_iota(jnp.int32, (count, where_to.shape[1]), 0) + first
    return jnp.where(centre == where_to, 1.0, 0.0)


BLOCK = 128


def early_kernel(places_far, centroids_far, *rest):
    pieces, (out_far, share_far, places, rows, centroids, out, share, arrived, left) = rest[:-9], rest[-9:]
    size = pieces[0].shape[0]
    steps = centroids.shape[0] // BLOCK
    copies = [pltpu.make_async_copy(places_far, places, arrived.at[0])]
    for at, piece in enumerate(pieces):
        copies.append(
            pltpu.make_async_copy(piece, rows.at[pl.ds(at * size, size)], arrived.at[1 + at])
        )
    loads = []
    for step in range(steps):
        block = pl.ds(step * BLOCK, BLOCK)
        loads.append(
            pltpu.make_async_copy(
                centroids_far.at[block], centroids.at[block], arrived.at[1 + len(pieces) + step]
            )
        )
    for copy in copies + loads:
        copy.start()
    for copy in copies:
        copy.wait()
    sends = []
    for step in range(steps):
        block = pl.ds(step * BLOCK, BLOCK)
        hot = onehot(places[...], step * BLOCK, BLOCK)
        counts = jnp.sum(hot, axis=1, keepdims=True)
        scale = jnp.where(counts > 0, 1.0 / jnp.maximum(counts, 1.0), 0.0)
        sums = jnp.dot(
            hot[:, : rows.shape[0]].astype(jnp.bfloat16),
            rows[...],
            preferred_element_type=jnp.float32,
        )
        loads[step].wait()
        out[block, :] = jnp.where(counts > 0, sums * scale, centroids[block, :])
        share[block, :] = jnp.broadcast_to(scale, (BLOCK, share.shape[1]))
        sends.append(pltpu.make_async_copy(out.at[block], out_far.at[block], left.at[step]))
        sends[-1].start()
    sends.append(pltpu.make_async_copy(share, share_far, left.at[steps]))
    sends[-1].start()
    for send in sends:
        send.wait()


def late_kernel(places_far, late_far, spread_far, share_far, early_far, *rest):
    pieces, rest = rest[:-10], rest[-10:]
    out_far, places, late, spread, share, rows, early, out, arrived, left = rest
    size, passes = pieces[0].shape[0], spread.shape[1]
    steps = early.shape[0] // BLOCK
    loads = [
        pltpu.make_async_copy(source, target, arrived.at[at])
        for at, (source, target) in enumerate(
            ((places_far, places), (late_far, late), (spread_far, spread), (share_far, share))
        )
    ]
    for at, piece in enumerate(pieces):
        loads.append(
            pltpu.make_async_copy(piece, rows.at[pl.ds(at * size, size)], arrived.at[4 + at])
        )
    starts = []
    for step in range(steps):
        block = pl.ds(step * BLOCK, BLOCK)
        starts.append(
            pltpu.make_async_copy(
                early_far.at[block], early.at[block], arrived.at[len(loads) + step]
            )
        )
    for copy in loads + starts:
        copy.start()
    for copy in loads:
        copy.wait()
    top = len(pieces) * size
    for peer in range(spread.shape[0]):
        rows[top + peer * passes : top + (peer + 1) * passes, :] = spread[peer]
    where_to = jnp.concatenate([places[:, places.shape[1] - top :], late[...]], axis=1)
    sends = []
    for step in range(steps):
        block = pl.ds(step * BLOCK, BLOCK)
        hot = onehot(where_to, step * BLOCK, BLOCK).astype(jnp.bfloat16)
        sums = jnp.dot(hot, rows[...], preferred_element_type=jnp.float32)
        starts[step].wait()
        out[block, :] = early[block, :] + sums * share[block, :1]
        sends.append(pltpu.make_async_copy(out.at[block], out_far.at[block], left.at[step]))
        sends[-1].start()
    for send in sends:
        send.wait()


def early_update(places, centroids, pieces):
    centre_count, width = centroids.shape
    row_total = sum(piece.shape[0] for piece in pieces)
    wide = pltpu.VMEM(centroids.shape, jnp.float32)
    thin = (centre_count, 128)
    steps = centre_count // BLOCK
    return pl.pallas_call(
        early_kernel,
        out_shape=[
            jax.ShapeDtypeStruct(centroids.shape, jnp.float32),
            jax.ShapeDtypeStruct(thin, jnp.float32),
        ],
        in_specs=[pl.BlockSpec(memory_space=pl.ANY)] * (2 + len(pieces)),
        out_specs=[pl.BlockSpec(memory_space=pltpu.HBM)] * 2,
        scratch_shapes=[
            pltpu.VMEM(places.shape, jnp.int32),
            pltpu.VMEM((row_total, width), jnp.bfloat16),
            wide,
            wide,
            pltpu.VMEM(thin, jnp.float32),
            pltpu.SemaphoreType.DMA((1 + len(pieces) + steps,)),
            pltpu.SemaphoreType.DMA((steps + 1,)),
        ],
        compiler_params=pltpu.CompilerParams(vmem_limit_bytes=60 * 1024 * 1024),
        cost_estimate=pl.CostEstimate(
            flops=100 * centre_count * width * row_total,
            bytes_accessed=200 * centre_count * width,
            transcendentals=0,
        ),
        name="early",
    )(places, centroids, *pieces)


def late_update(places, late, spread, share, early, pieces):
    centre_count, width = early.shape
    row_total = sum(piece.shape[0] for piece in pieces) + late.shape[1]
    wide = pltpu.VMEM(early.shape, jnp.float32)
    steps = centre_count // BLOCK
    return pl.pallas_call(
        late_kernel,
        out_shape=jax.ShapeDtypeStruct(early.shape, jnp.float32),
        in_specs=[pl.BlockSpec(memory_space=pltpu.HBM)] * (5 + len(pieces)),
        out_specs=pl.BlockSpec(memory_space=pltpu.HBM),
        scratch_shapes=[
            pltpu.VMEM(places.shape, jnp.int32),
            pltpu.VMEM(late.shape, jnp.int32),
            pltpu.VMEM(spread.shape, jnp.bfloat16),
            pltpu.VMEM(share.shape, jnp.float32),
            pltpu.VMEM((row_total, width), jnp.bfloat16),
            wide,
            wide,
            pltpu.SemaphoreType.DMA((4 + len(pieces) + steps,)),
            pltpu.SemaphoreType.DMA((steps,)),
        ],
        compiler_params=pltpu.CompilerParams(vmem_limit_bytes=60 * 1024 * 1024),
        cost_estimate=pl.CostEstimate(
            flops=2 * centre_count * width * row_total,
            bytes_accessed=8 * centre_count * width,
            transcendentals=0,
        ),
        name="late",
    )(places, late, spread, share, early, *pieces)


def shards(
    token_ids,
    lengths,
    word_table,
    pos_table,
    emb_gain,
    emb_bias,
    w_qkv,
    w_out,
    out_bias,
    norm_gain,
    norm_bias,
    stored_rows,
    row_owner,
    row_slot,
    centroids,
):
    peer_count = lax.axis_size("dp")
    half = peer_count // 2
    width = word_table.shape[1]
    vocab_rows = word_table.shape[0]
    passes, seq_len = token_ids.shape
    token_count = passes * seq_len
    row_count = row_slot.shape[0]
    store_count = stored_rows.shape[0]
    token_cap = max(2, 3 * token_count // peer_count)
    row_cap = max(2, 3 * row_count // peer_count)

    across = [(i, i ^ half) for i in range(peer_count)]
    beside = [(i, i ^ 1) for i in range(peer_count)]

    def hand_on(blocks):
        got = [blocks[0]]
        for step in range(1, len(blocks)):
            moves = [(i, i ^ (2 * step)) for i in range(peer_count)]
            got.append(lax.ppermute(blocks[step], "dp", moves))
        return got

    ahead = store_count * 2 // 3 // 16 * 16
    sibling_rows = lax.ppermute(stored_rows, "dp", beside)
    first_rows = lax.ppermute(stored_rows[:ahead], "dp", across)
    sizes = (peer_count, vocab_rows, token_cap, row_cap, row_count - store_count)
    owners = row_owner.reshape(1, row_count)
    sibling_owners = lax.ppermute(owners, "dp", beside)
    plan, token_slot, code, sibling_code = route(
        token_ids, owners, row_slot[None], sibling_owners, sizes
    )
    plan, sibling_rows = lax.optimization_barrier((plan, sibling_rows))
    codes = lax.all_to_all(plan, "dp", split_axis=0, concat_axis=0, tiled=True)
    *blocks, last_rows = pack_rows(
        code,
        sibling_code,
        [stored_rows],
        [sibling_rows],
        half,
        row_cap,
        row_count,
        rest=store_count - ahead,
    )
    codes, last_rows = lax.optimization_barrier((codes, last_rows))
    last_rows = lax.ppermute(last_rows, "dp", across)
    own_half = hand_on(blocks)
    plan = codes[:, 0, row_count:]
    wanted = plan[:, :token_cap].reshape(peer_count * token_cap)
    chosen = wanted[:, None] == jnp.arange(vocab_rows, dtype=jnp.int32)[None, :]
    found = jnp.dot(
        chosen.astype(jnp.bfloat16), word_table, preferred_element_type=jnp.float32
    ).astype(jnp.bfloat16)
    found, first_rows, own_half[:2] = lax.optimization_barrier(
        (found, first_rows, own_half[:2])
    )
    fetched = lax.all_to_all(
        found.reshape(peer_count, token_cap, width), "dp", split_axis=0, concat_axis=0, tiled=True
    ).reshape(peer_count * token_cap, width)

    sources = lax.axis_index("dp") ^ jnp.arange(peer_count, dtype=jnp.int32)
    got_places = plan[:, token_cap : token_cap + row_cap][sources].reshape(half, 2 * row_cap)
    spare = padded(2 * row_cap) - 2 * row_cap
    got_places = jnp.pad(got_places, ((0, 0), (0, spare)), constant_values=-1).reshape(1, -1)
    near_rows, last_rows = lax.optimization_barrier((own_half[:2], last_rows))
    means, share = early_update(got_places, centroids, near_rows)
    first_rows, last_rows, means = lax.optimization_barrier((first_rows, last_rows, means))
    partner_rows = [first_rows, last_rows]
    far_rows = [lax.ppermute(rows, "dp", beside) for rows in partner_rows]
    picks = (half, half ^ 1)
    blocks = pack_rows(codes, codes, partner_rows, far_rows, half, row_cap, row_count, picks)
    other_half = hand_on(blocks)
    late_places = plan[:, token_cap + row_cap :].reshape(1, -1)
    fetched, means, share, got_places, late_places = lax.optimization_barrier(
        (fetched, means, share, got_places, late_places)
    )

    passage_embed, spread = encode(
        peer_count,
        token_slot,
        fetched,
        lengths,
        pos_table,
        emb_gain,
        emb_bias,
        w_qkv,
        w_out,
        out_bias,
        norm_gain,
        norm_bias,
    )
    all_embeds = lax.all_to_all(
        spread, "dp", split_axis=0, concat_axis=0, tiled=True
    )
    pieces = own_half[2:] + other_half
    new_centroids = late_update(got_places, late_places, all_embeds, share, means, pieces)
    return (passage_embed, new_centroids)


def solution(mesh):
    return jax.shard_map(
        shards,
        mesh=mesh,
        in_specs=(
            P(("groups", "dp"), None),
            P(("groups", "dp")),
            P("dp", None),
            P(),
            P(),
            P(),
            P(),
            P(),
            P(),
            P(),
            P(),
            P(("groups", "dp"), None),
            P(("groups", "dp"), None),
            P(("groups", "dp")),
            P(("groups", "dp"), None),
        ),
        out_specs=(P(("groups", "dp"), None), P(("groups", "dp"), None)),
        check_vma=False,
    )
```

```python
import functools

import jax
import jax.numpy as jnp
from jax import lax
from jax.experimental import pallas as pl
from jax.experimental.pallas import tpu as pltpu
from jax.sharding import PartitionSpec as P

HEADS = 8
HD = 64


def normed(values, gain, shift):
    center = values - jnp.mean(values, axis=-1, keepdims=True)
    spread = jnp.mean(center * center, axis=-1, keepdims=True)
    return center * lax.rsqrt(spread + 1e-12) * gain + shift


def head_sums(weights, seq):
    rows, columns = weights.shape
    lane = lax.broadcasted_iota(jnp.int32, (rows, 2 * seq), 1)
    sums = []
    for start in range(0, columns, 2 * seq):
        pair = weights[:, start : start + 2 * seq]
        first = jnp.sum(jnp.where(lane < seq, pair, 0.0), axis=1, keepdims=True)
        second = jnp.sum(jnp.where(lane < seq, 0.0, pair), axis=1, keepdims=True)
        sums.append(jnp.where(lane < seq, first, second))
    return jnp.concatenate(sums, axis=1)


def encode_kernel(*refs):
    count = (len(refs) - 3) // 2
    far, (out, spread), near, arrived = refs[:count], refs[count : count + 2], refs[-count - 1 : -1], refs[-1]
    w_qkv_far, inner = far[-2], HEADS * HD
    copies = [
        pltpu.make_async_copy(source, target, arrived.at[at])
        for at, (source, target) in enumerate(zip(far, near))
        if source is not w_qkv_far
    ]
    lengths, slots, fetched, pos, emb_gain, emb_bias, out_bias, norm_gain, norm_bias, w_qkv, w_out = near
    out_copy = copies.pop()
    thirds = []
    for third in range(3):
        columns = pl.ds(third * inner, inner)
        thirds.append(
            pltpu.make_async_copy(
                w_qkv_far.at[:, columns], w_qkv.at[:, columns], arrived.at[count + third]
            )
        )
    for copy in copies + thirds + [out_copy]:
        copy.start()
    for copy in copies:
        copy.wait()
    passes = out.shape[0]
    size = [lengths[:, p : p + 1] for p in range(passes)]
    tokens, slot_count = slots.shape[0], fetched.shape[0]
    seq = tokens // passes
    spot = lax.broadcasted_iota(jnp.int32, (tokens, slot_count), 1)
    picker = jnp.where(slots[...] == spot, 1.0, 0.0).astype(jnp.bfloat16)
    tok = jnp.dot(picker, fetched[...], preferred_element_type=jnp.float32)
    where_at = pos[...].astype(jnp.float32)
    summed = tok + jnp.concatenate([where_at] * passes, axis=0)
    embedded = normed(summed, emb_gain[...], emb_bias[...]).astype(jnp.bfloat16)
    parts = []
    for third in range(3):
        thirds[third].wait()
        weights = w_qkv[:, third * inner : (third + 1) * inner]
        part = jnp.dot(embedded, weights, preferred_element_type=jnp.float32)
        parts.append(part.astype(jnp.bfloat16))

    block_row = lax.broadcasted_iota(jnp.int32, (HEADS * seq, inner), 0) // seq
    block_col = lax.broadcasted_iota(jnp.int32, (HEADS * seq, inner), 1) // HD
    same = block_row == block_col
    lane = lax.broadcasted_iota(jnp.int32, (seq, HEADS * seq), 1) % seq
    contexts = []
    for p in range(passes):
        query, keys, vals = (part[p * seq : (p + 1) * seq] for part in parts)
        zero = jnp.zeros((), jnp.bfloat16)
        keys = jnp.where(same, jnp.concatenate([keys] * HEADS, axis=0), zero)
        vals = jnp.where(same, jnp.concatenate([vals] * HEADS, axis=0), zero)
        scores = lax.dot_general(
            query, keys, (((1,), (1,)), ((), ())), preferred_element_type=jnp.float32
        ) * HD ** (-0.5)
        weights = jnp.where(lane < size[p], jnp.exp(scores), 0.0)
        probs = (weights / head_sums(weights, seq)).astype(jnp.bfloat16)
        contexts.append(jnp.dot(probs, vals, preferred_element_type=jnp.float32))
    context = jnp.concatenate(contexts, axis=0).astype(jnp.bfloat16)
    out_copy.wait()
    attended = jnp.dot(context, w_out[...], preferred_element_type=jnp.float32) + out_bias[...]
    hidden = normed(embedded.astype(jnp.float32) + attended, norm_gain[...], norm_bias[...])
    row = lax.broadcasted_iota(jnp.int32, (seq, 1), 0)
    for p in range(passes):
        kept = jnp.where(row < size[p], hidden[p * seq : (p + 1) * seq], 0.0)
        pooled = jnp.sum(kept, axis=0, keepdims=True) / size[p].astype(jnp.float32)
        scale = lax.rsqrt(jnp.mean(pooled * pooled, axis=-1, keepdims=True) + 1e-06)
        out[p : p + 1, :] = (pooled * scale).astype(jnp.bfloat16)
    spread[...] = jnp.broadcast_to(out[...][None], spread.shape)


def encode(
    peers, slots, fetched, lengths, pos_table, emb_gain, emb_bias, w_qkv, w_out, out_bias, norm_gain, norm_bias
):
    width = fetched.shape[1]
    tokens = slots.shape[0]
    passes = lengths.shape[0]
    macs = tokens * width * (fetched.shape[0] + 4 * HEADS * HD)
    operands = (
        lengths[None],
        slots,
        fetched,
        pos_table,
        emb_gain[None],
        emb_bias[None],
        out_bias[None],
        norm_gain[None],
        norm_bias[None],
        w_qkv,
        w_out,
    )
    return pl.pallas_call(
        encode_kernel,
        out_shape=[
            jax.ShapeDtypeStruct((passes, width), jnp.bfloat16),
            jax.ShapeDtypeStruct((peers, passes, width), jnp.bfloat16),
        ],
        in_specs=[pl.BlockSpec(memory_space=pltpu.HBM)] * len(operands),
        out_specs=[pl.BlockSpec(memory_space=pltpu.VMEM)] * 2,
        scratch_shapes=[pltpu.VMEM(operand.shape, operand.dtype) for operand in operands]
        + [pltpu.SemaphoreType.DMA((len(operands) + 3,))],
        compiler_params=pltpu.CompilerParams(vmem_limit_bytes=60 * 1024 * 1024),
        cost_estimate=pl.CostEstimate(
            flops=2 * macs, bytes_accessed=6 * 1024 * 1024, transcendentals=0
        ),
        name="encode",
    )(*operands)


def padded(rows):
    return -(-rows // 16) * 16


def rank_bits(count):
    return max(1, (count - 1).bit_length())


def ranks(kind):
    count = kind.shape[1]
    at = lax.broadcasted_iota(jnp.int32, (count, count), 0)
    by = lax.broadcasted_iota(jnp.int32, (count, count), 1)
    across = jnp.broadcast_to(kind, (count, count))
    down = jnp.sum(jnp.where(at == by, across, 0), axis=1, keepdims=True)
    same = down == across
    rank_row = jnp.sum(jnp.where(same & (at < by), 1, 0), axis=0, keepdims=True)
    rank_col = jnp.sum(jnp.where(same & (by < at), 1, 0), axis=1, keepdims=True)
    return down, rank_row, rank_col


def route_kernel(
    sizes,
    token_ids_far,
    owners_far,
    row_slot_far,
    sibling_far,
    plan,
    token_slot_far,
    code,
    sibling_code,
    *near,
):
    peers, vocab_rows, token_cap, row_cap, pooled = sizes
    token_ids, owners, row_slot, sibling, token_slot, arrived = near
    copies = [
        pltpu.make_async_copy(source, target, arrived.at[at])
        for at, (source, target) in enumerate(
            (
                (token_ids_far, token_ids),
                (owners_far, owners),
                (row_slot_far, row_slot),
                (sibling_far, sibling),
            )
        )
    ]
    for copy in copies:
        copy.start()
    for copy in copies:
        copy.wait()
    ids = jnp.concatenate([token_ids[p : p + 1, :] for p in range(token_ids.shape[0])], axis=1)
    tokens, rows = ids.shape[1], owners.shape[1]
    count = tokens + rows
    edge = (lax.broadcasted_iota(jnp.int32, (peers, tokens), 0) + 1) * vocab_rows
    holder = jnp.sum(jnp.where(ids >= edge, 1, 0), axis=0, keepdims=True)
    values = jnp.concatenate([ids - holder * vocab_rows, row_slot[...]], axis=1)

    kind = jnp.concatenate([holder, owners[...] + peers], axis=1)
    down, rank_row, rank_col = ranks(kind)

    code[...] = owners[...] * 2 ** rank_bits(rows) + rank_row[:, tokens:]
    sibling_code[...] = sibling[...] * 2 ** rank_bits(rows) + ranks(sibling[...])[1]
    goal = jnp.concatenate([holder, owners[...]], axis=1)
    peer = lax.broadcasted_iota(jnp.int32, (peers, count), 0)
    left = jnp.where(peer == goal, values + 1, 0).astype(jnp.float32)
    columns = token_cap + row_cap + pooled
    column = lax.broadcasted_iota(jnp.int32, (count, columns), 1)
    entry = lax.broadcasted_iota(jnp.int32, (count, 1), 0)
    first = jnp.where(entry < tokens, rank_col, rank_col + token_cap)
    second = entry - (count - pooled) + token_cap + row_cap
    second = jnp.where(entry < count - pooled, -1, second)
    right = jnp.where((column == first) | (column == second), 1.0, 0.0)
    filled = jnp.dot(
        left, right, preferred_element_type=jnp.float32, precision=lax.Precision.HIGHEST
    )
    filled = filled.astype(jnp.int32) - 1
    for p in range(peers):
        plan[p, :, :rows] = code[...]
        plan[p, :, rows:] = filled[p : p + 1]
    token_slot[...] = down[:tokens] * token_cap + rank_col[:tokens]
    send = pltpu.make_async_copy(token_slot, token_slot_far, arrived.at[4])
    send.start()
    send.wait()


def route(token_ids, owners, row_slot, sibling_owners, sizes):
    peers, _, token_cap, row_cap, pooled = sizes
    passes, seq_len = token_ids.shape
    rows = owners.shape[1]
    ints = lambda *shape: jax.ShapeDtypeStruct(shape, jnp.int32)
    return pl.pallas_call(
        functools.partial(route_kernel, sizes),
        out_shape=[
            ints(peers, 1, rows + token_cap + row_cap + pooled),
            ints(passes * seq_len, 1),
            ints(1, rows),
            ints(1, rows),
        ],
        in_specs=[pl.BlockSpec(memory_space=pltpu.HBM)] * 4,
        out_specs=[
            pl.BlockSpec(memory_space=pltpu.VMEM),
            pl.BlockSpec(memory_space=pltpu.HBM),
            pl.BlockSpec(memory_space=pltpu.VMEM),
            pl.BlockSpec(memory_space=pltpu.VMEM),
        ],
        scratch_shapes=[
            pltpu.VMEM(token_ids.shape, jnp.int32),
            pltpu.VMEM(owners.shape, jnp.int32),
            pltpu.VMEM(row_slot.shape, jnp.int32),
            pltpu.VMEM(owners.shape, jnp.int32),
            pltpu.VMEM((passes * seq_len, 1), jnp.int32),
            pltpu.SemaphoreType.DMA((5,)),
        ],
        compiler_params=pltpu.CompilerParams(vmem_limit_bytes=60 * 1024 * 1024),
        name="route",
    )(token_ids, owners, row_slot, sibling_owners)


def pack_kernel(half, row_cap, count, picks, pieces, rest, *refs):
    me = lax.axis_index("dp")
    operands = 2 + 2 * pieces
    far, refs = refs[:operands], refs[operands:]
    steps = half // 2
    outs, refs = refs[: steps + bool(rest)], refs[steps + bool(rest) :]
    near, (blocks, tail, arrived, left) = refs[:operands], refs[operands:]
    size = blocks.shape[0] // steps
    copies = [
        pltpu.make_async_copy(far[at], near[at], arrived.at[at]) for at in range(operands)
    ]
    for copy in copies:
        copy.start()
    for copy in copies[:2]:
        copy.wait()
    if size > 2 * row_cap:
        blocks[...] = jnp.zeros(blocks.shape, blocks.dtype)
    for source in range(2):
        if picks is None:
            code = near[source][...]
        else:
            code = near[source][me ^ picks[source], :, :count]
        bits = rank_bits(count)
        owner, rank = code >> bits, code & (2**bits - 1)
        fits = ((owner ^ me) & (1 | half)) == 0
        chip = ((owner ^ me) & (half - 1)) >> 1
        slot = jnp.where(fits, chip * row_cap + rank, -1)
        packed, at = 0.0, 0
        for piece in range(2 + source * pieces, 2 + (source + 1) * pieces):
            rows = near[piece]
            spot = lax.broadcasted_iota(jnp.int32, (steps * row_cap, rows.shape[0]), 0)
            table = jnp.where(slot[:, at : at + rows.shape[0]] == spot, 1.0, 0.0)
            copies[piece].wait()
            packed += jnp.dot(
                table.astype(jnp.bfloat16), rows[...], preferred_element_type=jnp.float32
            )
            at += rows.shape[0]
        packed = packed.astype(jnp.bfloat16)
        for step in range(steps):
            first = step * size + source * row_cap
            blocks[first : first + row_cap, :] = packed[step * row_cap : (step + 1) * row_cap]
    sends = [
        pltpu.make_async_copy(
            blocks.at[pl.ds(step * size, size)], outs[step], left.at[step]
        )
        for step in range(steps)
    ]
    if rest:
        tail[...] = near[2][near[2].shape[0] - rest :, :]
        sends.append(pltpu.make_async_copy(tail, outs[steps], left.at[steps]))
    for send in sends:
        send.start()
    for send in sends:
        send.wait()


def pack_rows(codes_a, codes_b, rows_a, rows_b, half, row_cap, count, picks=None, rest=0):
    width = rows_a[0].shape[1]
    total = sum(piece.shape[0] for piece in rows_a)
    steps = half // 2
    size = padded(2 * row_cap)
    operands = (codes_a, codes_b, *rows_a, *rows_b)
    shapes = [(size, width)] * steps + [(rest, width)] * bool(rest)
    return pl.pallas_call(
        functools.partial(pack_kernel, half, row_cap, count, picks, len(rows_a), rest),
        out_shape=[jax.ShapeDtypeStruct(shape, jnp.bfloat16) for shape in shapes],
        in_specs=[pl.BlockSpec(memory_space=pltpu.HBM)] * len(operands),
        out_specs=[pl.BlockSpec(memory_space=pltpu.HBM)] * len(shapes),
        scratch_shapes=[
            *(pltpu.VMEM(operand.shape, operand.dtype) for operand in operands),
            pltpu.VMEM((steps * size, width), jnp.bfloat16),
            pltpu.VMEM((max(rest, 16), width), jnp.bfloat16),
            pltpu.SemaphoreType.DMA((len(operands),)),
            pltpu.SemaphoreType.DMA((len(shapes),)),
        ],
        compiler_params=pltpu.CompilerParams(vmem_limit_bytes=60 * 1024 * 1024),
        cost_estimate=pl.CostEstimate(
            flops=4 * steps * row_cap * width * total,
            bytes_accessed=4 * width * (total + steps * row_cap),
            transcendentals=0,
        ),
        name="pack",
    )(*operands)


def onehot(where_to, first, count):
    centre = lax.broadcasted_iota(jnp.int32, (count, where_to.shape[1]), 0) + first
    return jnp.where(centre == where_to, 1.0, 0.0)


BLOCK = 128


def early_kernel(places_far, centroids_far, *rest):
    pieces, (out_far, share_far, places, rows, centroids, out, share, arrived, left) = rest[:-9], rest[-9:]
    size = pieces[0].shape[0]
    steps = centroids.shape[0] // BLOCK
    copies = [pltpu.make_async_copy(places_far, places, arrived.at[0])]
    for at, piece in enumerate(pieces):
        copies.append(
            pltpu.make_async_copy(piece, rows.at[pl.ds(at * size, size)], arrived.at[1 + at])
        )
    loads = []
    for step in range(steps):
        block = pl.ds(step * BLOCK, BLOCK)
        loads.append(
            pltpu.make_async_copy(
                centroids_far.at[block], centroids.at[block], arrived.at[1 + len(pieces) + step]
            )
        )
    for copy in copies + loads:
        copy.start()
    for copy in copies:
        copy.wait()
    sends = []
    for step in range(steps):
        block = pl.ds(step * BLOCK, BLOCK)
        hot = onehot(places[...], step * BLOCK, BLOCK)
        counts = jnp.sum(hot, axis=1, keepdims=True)
        scale = jnp.where(counts > 0, 1.0 / jnp.maximum(counts, 1.0), 0.0)
        sums = jnp.dot(
            hot[:, : rows.shape[0]].astype(jnp.bfloat16),
            rows[...],
            preferred_element_type=jnp.float32,
        )
        loads[step].wait()
        out[block, :] = jnp.where(counts > 0, sums * scale, centroids[block, :])
        share[block, :] = jnp.broadcast_to(scale, (BLOCK, share.shape[1]))
        sends.append(pltpu.make_async_copy(out.at[block], out_far.at[block], left.at[step]))
        sends[-1].start()
    sends.append(pltpu.make_async_copy(share, share_far, left.at[steps]))
    sends[-1].start()
    for send in sends:
        send.wait()


def late_kernel(places_far, late_far, spread_far, share_far, early_far, *rest):
    pieces, rest = rest[:-10], rest[-10:]
    out_far, places, late, spread, share, rows, early, out, arrived, left = rest
    size, passes = pieces[0].shape[0], spread.shape[1]
    steps = early.shape[0] // BLOCK
    loads = [
        pltpu.make_async_copy(source, target, arrived.at[at])
        for at, (source, target) in enumerate(
            ((places_far, places), (late_far, late), (spread_far, spread), (share_far, share))
        )
    ]
    for at, piece in enumerate(pieces):
        loads.append(
            pltpu.make_async_copy(piece, rows.at[pl.ds(at * size, size)], arrived.at[4 + at])
        )
    starts = []
    for step in range(steps):
        block = pl.ds(step * BLOCK, BLOCK)
        starts.append(
            pltpu.make_async_copy(
                early_far.at[block], early.at[block], arrived.at[len(loads) + step]
            )
        )
    for copy in loads + starts:
        copy.start()
    for copy in loads:
        copy.wait()
    top = len(pieces) * size
    for peer in range(spread.shape[0]):
        rows[top + peer * passes : top + (peer + 1) * passes, :] = spread[peer]
    where_to = jnp.concatenate([places[:, places.shape[1] - top :], late[...]], axis=1)
    sends = []
    for step in range(steps):
        block = pl.ds(step * BLOCK, BLOCK)
        hot = onehot(where_to, step * BLOCK, BLOCK).astype(jnp.bfloat16)
        sums = jnp.dot(hot, rows[...], preferred_element_type=jnp.float32)
        starts[step].wait()
        out[block, :] = early[block, :] + sums * share[block, :1]
        sends.append(pltpu.make_async_copy(out.at[block], out_far.at[block], left.at[step]))
        sends[-1].start()
    for send in sends:
        send.wait()


def early_update(places, centroids, pieces):
    centre_count, width = centroids.shape
    row_total = sum(piece.shape[0] for piece in pieces)
    wide = pltpu.VMEM(centroids.shape, jnp.float32)
    thin = (centre_count, 128)
    steps = centre_count // BLOCK
    return pl.pallas_call(
        early_kernel,
        out_shape=[
            jax.ShapeDtypeStruct(centroids.shape, jnp.float32),
            jax.ShapeDtypeStruct(thin, jnp.float32),
        ],
        in_specs=[pl.BlockSpec(memory_space=pl.ANY)] * (2 + len(pieces)),
        out_specs=[pl.BlockSpec(memory_space=pltpu.HBM)] * 2,
        scratch_shapes=[
            pltpu.VMEM(places.shape, jnp.int32),
            pltpu.VMEM((row_total, width), jnp.bfloat16),
            wide,
            wide,
            pltpu.VMEM(thin, jnp.float32),
            pltpu.SemaphoreType.DMA((1 + len(pieces) + steps,)),
            pltpu.SemaphoreType.DMA((steps + 1,)),
        ],
        compiler_params=pltpu.CompilerParams(vmem_limit_bytes=60 * 1024 * 1024),
        cost_estimate=pl.CostEstimate(
            flops=100 * centre_count * width * row_total,
            bytes_accessed=200 * centre_count * width,
            transcendentals=0,
        ),
        name="early",
    )(places, centroids, *pieces)


def late_update(places, late, spread, share, early, pieces):
    centre_count, width = early.shape
    row_total = sum(piece.shape[0] for piece in pieces) + late.shape[1]
    wide = pltpu.VMEM(early.shape, jnp.float32)
    steps = centre_count // BLOCK
    return pl.pallas_call(
        late_kernel,
        out_shape=jax.ShapeDtypeStruct(early.shape, jnp.float32),
        in_specs=[pl.BlockSpec(memory_space=pltpu.HBM)] * (5 + len(pieces)),
        out_specs=pl.BlockSpec(memory_space=pltpu.HBM),
        scratch_shapes=[
            pltpu.VMEM(places.shape, jnp.int32),
            pltpu.VMEM(late.shape, jnp.int32),
            pltpu.VMEM(spread.shape, jnp.bfloat16),
            pltpu.VMEM(share.shape, jnp.float32),
            pltpu.VMEM((row_total, width), jnp.bfloat16),
            wide,
            wide,
            pltpu.SemaphoreType.DMA((4 + len(pieces) + steps,)),
            pltpu.SemaphoreType.DMA((steps,)),
        ],
        compiler_params=pltpu.CompilerParams(vmem_limit_bytes=60 * 1024 * 1024),
        cost_estimate=pl.CostEstimate(
            flops=2 * centre_count * width * row_total,
            bytes_accessed=8 * centre_count * width,
            transcendentals=0,
        ),
        name="late",
    )(places, late, spread, share, early, *pieces)


def shards(
    token_ids,
    lengths,
    word_table,
    pos_table,
    emb_gain,
    emb_bias,
    w_qkv,
    w_out,
    out_bias,
    norm_gain,
    norm_bias,
    stored_rows,
    row_owner,
    row_slot,
    centroids,
):
    peer_count = lax.axis_size("dp")
    half = peer_count // 2
    width = word_table.shape[1]
    vocab_rows = word_table.shape[0]
    passes, seq_len = token_ids.shape
    token_count = passes * seq_len
    row_count = row_slot.shape[0]
    store_count = stored_rows.shape[0]
    token_cap = max(2, 3 * token_count // peer_count)
    row_cap = max(2, 3 * row_count // peer_count)

    across = [(i, i ^ half) for i in range(peer_count)]
    beside = [(i, i ^ 1) for i in range(peer_count)]

    def hand_on(blocks):
        got = [blocks[0]]
        for step in range(1, len(blocks)):
            moves = [(i, i ^ (2 * step)) for i in range(peer_count)]
            got.append(lax.ppermute(blocks[step], "dp", moves))
        return got

    ahead = store_count * 3 // 4 // 16 * 16
    sibling_rows = lax.ppermute(stored_rows, "dp", beside)
    first_rows = lax.ppermute(stored_rows[:ahead], "dp", across)
    sizes = (peer_count, vocab_rows, token_cap, row_cap, row_count - store_count)
    owners = row_owner.reshape(1, row_count)
    sibling_owners = lax.ppermute(owners, "dp", beside)
    plan, token_slot, code, sibling_code = route(
        token_ids, owners, row_slot[None], sibling_owners, sizes
    )
    plan, sibling_rows = lax.optimization_barrier((plan, sibling_rows))
    codes = lax.all_to_all(plan, "dp", split_axis=0, concat_axis=0, tiled=True)
    *blocks, last_rows = pack_rows(
        code,
        sibling_code,
        [stored_rows],
        [sibling_rows],
        half,
        row_cap,
        row_count,
        rest=store_count - ahead,
    )
    codes, last_rows = lax.optimization_barrier((codes, last_rows))
    last_rows = lax.ppermute(last_rows, "dp", across)
    own_half = hand_on(blocks)
    plan = codes[:, 0, row_count:]
    wanted = plan[:, :token_cap].reshape(peer_count * token_cap)
    chosen = wanted[:, None] == jnp.arange(vocab_rows, dtype=jnp.int32)[None, :]
    found = jnp.dot(
        chosen.astype(jnp.bfloat16), word_table, preferred_element_type=jnp.float32
    ).astype(jnp.bfloat16)
    found, first_rows, own_half[:2] = lax.optimization_barrier(
        (found, first_rows, own_half[:2])
    )
    fetched = lax.all_to_all(
        found.reshape(peer_count, token_cap, width), "dp", split_axis=0, concat_axis=0, tiled=True
    ).reshape(peer_count * token_cap, width)

    sources = lax.axis_index("dp") ^ jnp.arange(peer_count, dtype=jnp.int32)
    got_places = plan[:, token_cap : token_cap + row_cap][sources].reshape(half, 2 * row_cap)
    spare = padded(2 * row_cap) - 2 * row_cap
    got_places = jnp.pad(got_places, ((0, 0), (0, spare)), constant_values=-1).reshape(1, -1)
    near_rows, last_rows = lax.optimization_barrier((own_half[:2], last_rows))
    means, share = early_update(got_places, centroids, near_rows)
    first_rows, last_rows, means = lax.optimization_barrier((first_rows, last_rows, means))
    partner_rows = [first_rows, last_rows]
    far_rows = [lax.ppermute(rows, "dp", beside) for rows in partner_rows]
    picks = (half, half ^ 1)
    blocks = pack_rows(codes, codes, partner_rows, far_rows, half, row_cap, row_count, picks)
    other_half = hand_on(blocks)
    late_places = plan[:, token_cap + row_cap :].reshape(1, -1)
    fetched, means, share, got_places, late_places = lax.optimization_barrier(
        (fetched, means, share, got_places, late_places)
    )

    passage_embed, spread = encode(
        peer_count,
        token_slot,
        fetched,
        lengths,
        pos_table,
        emb_gain,
        emb_bias,
        w_qkv,
        w_out,
        out_bias,
        norm_gain,
        norm_bias,
    )
    all_embeds = lax.all_to_all(
        spread, "dp", split_axis=0, concat_axis=0, tiled=True
    )
    pieces = own_half[2:] + other_half
    new_centroids = late_update(got_places, late_places, all_embeds, share, means, pieces)
    return (passage_embed, new_centroids)


def solution(mesh):
    return jax.shard_map(
        shards,
        mesh=mesh,
        in_specs=(
            P(("groups", "dp"), None),
            P(("groups", "dp")),
            P("dp", None),
            P(),
            P(),
            P(),
            P(),
            P(),
            P(),
            P(),
            P(),
            P(("groups", "dp"), None),
            P(("groups", "dp"), None),
            P(("groups", "dp")),
            P(("groups", "dp"), None),
        ),
        out_specs=(P(("groups", "dp"), None), P(("groups", "dp"), None)),
        check_vma=False,
    )
```

```python
import functools

import jax
import jax.numpy as jnp
from jax import lax
from jax.experimental import pallas as pl
from jax.experimental.pallas import tpu as pltpu
from jax.sharding import PartitionSpec as P

HEADS = 8
HD = 64


def normed(values, gain, shift):
    center = values - jnp.mean(values, axis=-1, keepdims=True)
    spread = jnp.mean(center * center, axis=-1, keepdims=True)
    return center * lax.rsqrt(spread + 1e-12) * gain + shift


def head_sums(weights, seq):
    rows, columns = weights.shape
    lane = lax.broadcasted_iota(jnp.int32, (rows, 2 * seq), 1)
    sums = []
    for start in range(0, columns, 2 * seq):
        pair = weights[:, start : start + 2 * seq]
        first = jnp.sum(jnp.where(lane < seq, pair, 0.0), axis=1, keepdims=True)
        second = jnp.sum(jnp.where(lane < seq, 0.0, pair), axis=1, keepdims=True)
        sums.append(jnp.where(lane < seq, first, second))
    return jnp.concatenate(sums, axis=1)


def encode_kernel(*refs):
    count = (len(refs) - 3) // 2
    far, (out, spread), near, arrived = refs[:count], refs[count : count + 2], refs[-count - 1 : -1], refs[-1]
    w_qkv_far, inner = far[-2], HEADS * HD
    copies = [
        pltpu.make_async_copy(source, target, arrived.at[at])
        for at, (source, target) in enumerate(zip(far, near))
        if source is not w_qkv_far
    ]
    lengths, slots, fetched, pos, emb_gain, emb_bias, out_bias, norm_gain, norm_bias, w_qkv, w_out = near
    out_copy = copies.pop()
    thirds = []
    for third in range(3):
        columns = pl.ds(third * inner, inner)
        thirds.append(
            pltpu.make_async_copy(
                w_qkv_far.at[:, columns], w_qkv.at[:, columns], arrived.at[count + third]
            )
        )
    for copy in copies + thirds + [out_copy]:
        copy.start()
    for copy in copies:
        copy.wait()
    passes = out.shape[0]
    size = [lengths[:, p : p + 1] for p in range(passes)]
    tokens, slot_count = slots.shape[0], fetched.shape[0]
    seq = tokens // passes
    spot = lax.broadcasted_iota(jnp.int32, (tokens, slot_count), 1)
    picker = jnp.where(slots[...] == spot, 1.0, 0.0).astype(jnp.bfloat16)
    tok = jnp.dot(picker, fetched[...], preferred_element_type=jnp.float32)
    where_at = pos[...].astype(jnp.float32)
    summed = tok + jnp.concatenate([where_at] * passes, axis=0)
    embedded = normed(summed, emb_gain[...], emb_bias[...]).astype(jnp.bfloat16)
    parts = []
    for third in range(3):
        thirds[third].wait()
        weights = w_qkv[:, third * inner : (third + 1) * inner]
        part = jnp.dot(embedded, weights, preferred_element_type=jnp.float32)
        parts.append(part.astype(jnp.bfloat16))

    block_row = lax.broadcasted_iota(jnp.int32, (HEADS * seq, inner), 0) // seq
    block_col = lax.broadcasted_iota(jnp.int32, (HEADS * seq, inner), 1) // HD
    same = block_row == block_col
    lane = lax.broadcasted_iota(jnp.int32, (seq, HEADS * seq), 1) % seq
    contexts = []
    for p in range(passes):
        query, keys, vals = (part[p * seq : (p + 1) * seq] for part in parts)
        zero = jnp.zeros((), jnp.bfloat16)
        keys = jnp.where(same, jnp.concatenate([keys] * HEADS, axis=0), zero)
        vals = jnp.where(same, jnp.concatenate([vals] * HEADS, axis=0), zero)
        scores = lax.dot_general(
            query, keys, (((1,), (1,)), ((), ())), preferred_element_type=jnp.float32
        ) * HD ** (-0.5)
        weights = jnp.where(lane < size[p], jnp.exp(scores), 0.0)
        probs = (weights / head_sums(weights, seq)).astype(jnp.bfloat16)
        contexts.append(jnp.dot(probs, vals, preferred_element_type=jnp.float32))
    context = jnp.concatenate(contexts, axis=0).astype(jnp.bfloat16)
    out_copy.wait()
    attended = jnp.dot(context, w_out[...], preferred_element_type=jnp.float32) + out_bias[...]
    hidden = normed(embedded.astype(jnp.float32) + attended, norm_gain[...], norm_bias[...])
    row = lax.broadcasted_iota(jnp.int32, (seq, 1), 0)
    for p in range(passes):
        kept = jnp.where(row < size[p], hidden[p * seq : (p + 1) * seq], 0.0)
        pooled = jnp.sum(kept, axis=0, keepdims=True) / size[p].astype(jnp.float32)
        scale = lax.rsqrt(jnp.mean(pooled * pooled, axis=-1, keepdims=True) + 1e-06)
        out[p : p + 1, :] = (pooled * scale).astype(jnp.bfloat16)
    spread[...] = jnp.broadcast_to(out[...][None], spread.shape)


def encode(
    peers, slots, fetched, lengths, pos_table, emb_gain, emb_bias, w_qkv, w_out, out_bias, norm_gain, norm_bias
):
    width = fetched.shape[1]
    tokens = slots.shape[0]
    passes = lengths.shape[0]
    macs = tokens * width * (fetched.shape[0] + 4 * HEADS * HD)
    operands = (
        lengths[None],
        slots,
        fetched,
        pos_table,
        emb_gain[None],
        emb_bias[None],
        out_bias[None],
        norm_gain[None],
        norm_bias[None],
        w_qkv,
        w_out,
    )
    return pl.pallas_call(
        encode_kernel,
        out_shape=[
            jax.ShapeDtypeStruct((passes, width), jnp.bfloat16),
            jax.ShapeDtypeStruct((peers, passes, width), jnp.bfloat16),
        ],
        in_specs=[pl.BlockSpec(memory_space=pltpu.HBM)] * len(operands),
        out_specs=[pl.BlockSpec(memory_space=pltpu.VMEM)] * 2,
        scratch_shapes=[pltpu.VMEM(operand.shape, operand.dtype) for operand in operands]
        + [pltpu.SemaphoreType.DMA((len(operands) + 3,))],
        compiler_params=pltpu.CompilerParams(vmem_limit_bytes=60 * 1024 * 1024),
        cost_estimate=pl.CostEstimate(
            flops=2 * macs, bytes_accessed=6 * 1024 * 1024, transcendentals=0
        ),
        name="encode",
    )(*operands)


def padded(rows):
    return -(-rows // 16) * 16


def rank_bits(count):
    return max(1, (count - 1).bit_length())


def ranks(kind):
    count = kind.shape[1]
    at = lax.broadcasted_iota(jnp.int32, (count, count), 0)
    by = lax.broadcasted_iota(jnp.int32, (count, count), 1)
    across = jnp.broadcast_to(kind, (count, count))
    down = jnp.sum(jnp.where(at == by, across, 0), axis=1, keepdims=True)
    same = down == across
    rank_row = jnp.sum(jnp.where(same & (at < by), 1, 0), axis=0, keepdims=True)
    rank_col = jnp.sum(jnp.where(same & (by < at), 1, 0), axis=1, keepdims=True)
    return down, rank_row, rank_col


def route_kernel(
    sizes,
    token_ids_far,
    owners_far,
    row_slot_far,
    sibling_far,
    plan,
    token_slot_far,
    code,
    sibling_code,
    *near,
):
    peers, vocab_rows, token_cap, row_cap, pooled = sizes
    token_ids, owners, row_slot, sibling, token_slot, arrived = near
    copies = [
        pltpu.make_async_copy(source, target, arrived.at[at])
        for at, (source, target) in enumerate(
            (
                (token_ids_far, token_ids),
                (owners_far, owners),
                (row_slot_far, row_slot),
                (sibling_far, sibling),
            )
        )
    ]
    for copy in copies:
        copy.start()
    for copy in copies:
        copy.wait()
    ids = jnp.concatenate([token_ids[p : p + 1, :] for p in range(token_ids.shape[0])], axis=1)
    tokens, rows = ids.shape[1], owners.shape[1]
    count = tokens + rows
    edge = (lax.broadcasted_iota(jnp.int32, (peers, tokens), 0) + 1) * vocab_rows
    holder = jnp.sum(jnp.where(ids >= edge, 1, 0), axis=0, keepdims=True)
    values = jnp.concatenate([ids - holder * vocab_rows, row_slot[...]], axis=1)

    kind = jnp.concatenate([holder, owners[...] + peers], axis=1)
    down, rank_row, rank_col = ranks(kind)

    code[...] = owners[...] * 2 ** rank_bits(rows) + rank_row[:, tokens:]
    sibling_code[...] = sibling[...] * 2 ** rank_bits(rows) + ranks(sibling[...])[1]
    goal = jnp.concatenate([holder, owners[...]], axis=1)
    peer = lax.broadcasted_iota(jnp.int32, (peers, count), 0)
    left = jnp.where(peer == goal, values + 1, 0).astype(jnp.float32)
    columns = token_cap + row_cap + pooled
    column = lax.broadcasted_iota(jnp.int32, (count, columns), 1)
    entry = lax.broadcasted_iota(jnp.int32, (count, 1), 0)
    first = jnp.where(entry < tokens, rank_col, rank_col + token_cap)
    second = entry - (count - pooled) + token_cap + row_cap
    second = jnp.where(entry < count - pooled, -1, second)
    right = jnp.where((column == first) | (column == second), 1.0, 0.0)
    filled = jnp.dot(
        left, right, preferred_element_type=jnp.float32, precision=lax.Precision.HIGHEST
    )
    filled = filled.astype(jnp.int32) - 1
    for p in range(peers):
        plan[p, :, :rows] = code[...]
        plan[p, :, rows:] = filled[p : p + 1]
    token_slot[...] = down[:tokens] * token_cap + rank_col[:tokens]
    send = pltpu.make_async_copy(token_slot, token_slot_far, arrived.at[4])
    send.start()
    send.wait()


def route(token_ids, owners, row_slot, sibling_owners, sizes):
    peers, _, token_cap, row_cap, pooled = sizes
    passes, seq_len = token_ids.shape
    rows = owners.shape[1]
    ints = lambda *shape: jax.ShapeDtypeStruct(shape, jnp.int32)
    return pl.pallas_call(
        functools.partial(route_kernel, sizes),
        out_shape=[
            ints(peers, 1, rows + token_cap + row_cap + pooled),
            ints(passes * seq_len, 1),
            ints(1, rows),
            ints(1, rows),
        ],
        in_specs=[pl.BlockSpec(memory_space=pltpu.HBM)] * 4,
        out_specs=[
            pl.BlockSpec(memory_space=pltpu.VMEM),
            pl.BlockSpec(memory_space=pltpu.HBM),
            pl.BlockSpec(memory_space=pltpu.VMEM),
            pl.BlockSpec(memory_space=pltpu.VMEM),
        ],
        scratch_shapes=[
            pltpu.VMEM(token_ids.shape, jnp.int32),
            pltpu.VMEM(owners.shape, jnp.int32),
            pltpu.VMEM(row_slot.shape, jnp.int32),
            pltpu.VMEM(owners.shape, jnp.int32),
            pltpu.VMEM((passes * seq_len, 1), jnp.int32),
            pltpu.SemaphoreType.DMA((5,)),
        ],
        compiler_params=pltpu.CompilerParams(vmem_limit_bytes=60 * 1024 * 1024),
        name="route",
    )(token_ids, owners, row_slot, sibling_owners)


def pack_kernel(half, row_cap, count, picks, pieces, rest, *refs):
    me = lax.axis_index("dp")
    operands = 2 + 2 * pieces
    far, refs = refs[:operands], refs[operands:]
    steps = half // 2
    outs, refs = refs[: steps + bool(rest)], refs[steps + bool(rest) :]
    near, (blocks, tail, arrived, left) = refs[:operands], refs[operands:]
    size = blocks.shape[0] // steps
    copies = [
        pltpu.make_async_copy(far[at], near[at], arrived.at[at]) for at in range(operands)
    ]
    for copy in copies:
        copy.start()
    for copy in copies[:2]:
        copy.wait()
    if size > 2 * row_cap:
        blocks[...] = jnp.zeros(blocks.shape, blocks.dtype)
    for source in range(2):
        if picks is None:
            code = near[source][...]
        else:
            code = near[source][me ^ picks[source], :, :count]
        bits = rank_bits(count)
        owner, rank = code >> bits, code & (2**bits - 1)
        fits = ((owner ^ me) & (1 | half)) == 0
        chip = ((owner ^ me) & (half - 1)) >> 1
        slot = jnp.where(fits, chip * row_cap + rank, -1)
        packed, at = 0.0, 0
        for piece in range(2 + source * pieces, 2 + (source + 1) * pieces):
            rows = near[piece]
            spot = lax.broadcasted_iota(jnp.int32, (steps * row_cap, rows.shape[0]), 0)
            table = jnp.where(slot[:, at : at + rows.shape[0]] == spot, 1.0, 0.0)
            copies[piece].wait()
            packed += jnp.dot(
                table.astype(jnp.bfloat16), rows[...], preferred_element_type=jnp.float32
            )
            at += rows.shape[0]
        packed = packed.astype(jnp.bfloat16)
        for step in range(steps):
            first = step * size + source * row_cap
            blocks[first : first + row_cap, :] = packed[step * row_cap : (step + 1) * row_cap]
    sends = [
        pltpu.make_async_copy(
            blocks.at[pl.ds(step * size, size)], outs[step], left.at[step]
        )
        for step in range(steps)
    ]
    if rest:
        tail[...] = near[2][near[2].shape[0] - rest :, :]
        sends.append(pltpu.make_async_copy(tail, outs[steps], left.at[steps]))
    for send in sends:
        send.start()
    for send in sends:
        send.wait()


def pack_rows(codes_a, codes_b, rows_a, rows_b, half, row_cap, count, picks=None, rest=0):
    width = rows_a[0].shape[1]
    total = sum(piece.shape[0] for piece in rows_a)
    steps = half // 2
    size = padded(2 * row_cap)
    operands = (codes_a, codes_b, *rows_a, *rows_b)
    shapes = [(size, width)] * steps + [(rest, width)] * bool(rest)
    return pl.pallas_call(
        functools.partial(pack_kernel, half, row_cap, count, picks, len(rows_a), rest),
        out_shape=[jax.ShapeDtypeStruct(shape, jnp.bfloat16) for shape in shapes],
        in_specs=[pl.BlockSpec(memory_space=pltpu.HBM)] * len(operands),
        out_specs=[pl.BlockSpec(memory_space=pltpu.HBM)] * len(shapes),
        scratch_shapes=[
            *(pltpu.VMEM(operand.shape, operand.dtype) for operand in operands),
            pltpu.VMEM((steps * size, width), jnp.bfloat16),
            pltpu.VMEM((max(rest, 16), width), jnp.bfloat16),
            pltpu.SemaphoreType.DMA((len(operands),)),
            pltpu.SemaphoreType.DMA((len(shapes),)),
        ],
        compiler_params=pltpu.CompilerParams(vmem_limit_bytes=60 * 1024 * 1024),
        cost_estimate=pl.CostEstimate(
            flops=4 * steps * row_cap * width * total,
            bytes_accessed=4 * width * (total + steps * row_cap),
            transcendentals=0,
        ),
        name="pack",
    )(*operands)


def onehot(where_to, first, count):
    centre = lax.broadcasted_iota(jnp.int32, (count, where_to.shape[1]), 0) + first
    return jnp.where(centre == where_to, 1.0, 0.0)


BLOCK = 128


def early_kernel(places_far, centroids_far, *rest):
    pieces, (out_far, share_far, places, rows, centroids, out, share, arrived, left) = rest[:-9], rest[-9:]
    size = pieces[0].shape[0]
    steps = centroids.shape[0] // BLOCK
    copies = [pltpu.make_async_copy(places_far, places, arrived.at[0])]
    for at, piece in enumerate(pieces):
        copies.append(
            pltpu.make_async_copy(piece, rows.at[pl.ds(at * size, size)], arrived.at[1 + at])
        )
    loads = []
    for step in range(steps):
        block = pl.ds(step * BLOCK, BLOCK)
        loads.append(
            pltpu.make_async_copy(
                centroids_far.at[block], centroids.at[block], arrived.at[1 + len(pieces) + step]
            )
        )
    for copy in copies + loads:
        copy.start()
    for copy in copies:
        copy.wait()
    sends = []
    for step in range(steps):
        block = pl.ds(step * BLOCK, BLOCK)
        hot = onehot(places[...], step * BLOCK, BLOCK)
        counts = jnp.sum(hot, axis=1, keepdims=True)
        scale = jnp.where(counts > 0, 1.0 / jnp.maximum(counts, 1.0), 0.0)
        sums = jnp.dot(
            hot[:, : rows.shape[0]].astype(jnp.bfloat16),
            rows[...],
            preferred_element_type=jnp.float32,
        )
        loads[step].wait()
        out[block, :] = jnp.where(counts > 0, sums * scale, centroids[block, :])
        share[block, :] = jnp.broadcast_to(scale, (BLOCK, share.shape[1]))
        sends.append(pltpu.make_async_copy(out.at[block], out_far.at[block], left.at[step]))
        sends[-1].start()
    sends.append(pltpu.make_async_copy(share, share_far, left.at[steps]))
    sends[-1].start()
    for send in sends:
        send.wait()


def late_kernel(places_far, late_far, spread_far, share_far, early_far, *rest):
    pieces, rest = rest[:-10], rest[-10:]
    out_far, places, late, spread, share, rows, early, out, arrived, left = rest
    size, passes = pieces[0].shape[0], spread.shape[1]
    steps = early.shape[0] // BLOCK
    loads = [
        pltpu.make_async_copy(source, target, arrived.at[at])
        for at, (source, target) in enumerate(
            ((places_far, places), (late_far, late), (spread_far, spread), (share_far, share))
        )
    ]
    for at, piece in enumerate(pieces):
        loads.append(
            pltpu.make_async_copy(piece, rows.at[pl.ds(at * size, size)], arrived.at[4 + at])
        )
    starts = []
    for step in range(steps):
        block = pl.ds(step * BLOCK, BLOCK)
        starts.append(
            pltpu.make_async_copy(
                early_far.at[block], early.at[block], arrived.at[len(loads) + step]
            )
        )
    for copy in loads + starts:
        copy.start()
    for copy in loads:
        copy.wait()
    top = len(pieces) * size
    for peer in range(spread.shape[0]):
        rows[top + peer * passes : top + (peer + 1) * passes, :] = spread[peer]
    where_to = jnp.concatenate([places[:, places.shape[1] - top :], late[...]], axis=1)
    sends = []
    for step in range(steps):
        block = pl.ds(step * BLOCK, BLOCK)
        hot = onehot(where_to, step * BLOCK, BLOCK).astype(jnp.bfloat16)
        sums = jnp.dot(hot, rows[...], preferred_element_type=jnp.float32)
        starts[step].wait()
        out[block, :] = early[block, :] + sums * share[block, :1]
        sends.append(pltpu.make_async_copy(out.at[block], out_far.at[block], left.at[step]))
        sends[-1].start()
    for send in sends:
        send.wait()


def early_update(places, centroids, pieces):
    centre_count, width = centroids.shape
    row_total = sum(piece.shape[0] for piece in pieces)
    wide = pltpu.VMEM(centroids.shape, jnp.float32)
    thin = (centre_count, 128)
    steps = centre_count // BLOCK
    return pl.pallas_call(
        early_kernel,
        out_shape=[
            jax.ShapeDtypeStruct(centroids.shape, jnp.float32),
            jax.ShapeDtypeStruct(thin, jnp.float32),
        ],
        in_specs=[pl.BlockSpec(memory_space=pl.ANY)] * (2 + len(pieces)),
        out_specs=[pl.BlockSpec(memory_space=pltpu.HBM)] * 2,
        scratch_shapes=[
            pltpu.VMEM(places.shape, jnp.int32),
            pltpu.VMEM((row_total, width), jnp.bfloat16),
            wide,
            wide,
            pltpu.VMEM(thin, jnp.float32),
            pltpu.SemaphoreType.DMA((1 + len(pieces) + steps,)),
            pltpu.SemaphoreType.DMA((steps + 1,)),
        ],
        compiler_params=pltpu.CompilerParams(vmem_limit_bytes=60 * 1024 * 1024),
        cost_estimate=pl.CostEstimate(
            flops=100 * centre_count * width * row_total,
            bytes_accessed=200 * centre_count * width,
            transcendentals=0,
        ),
        name="early",
    )(places, centroids, *pieces)


def late_update(places, late, spread, share, early, pieces):
    centre_count, width = early.shape
    row_total = sum(piece.shape[0] for piece in pieces) + late.shape[1]
    wide = pltpu.VMEM(early.shape, jnp.float32)
    steps = centre_count // BLOCK
    return pl.pallas_call(
        late_kernel,
        out_shape=jax.ShapeDtypeStruct(early.shape, jnp.float32),
        in_specs=[pl.BlockSpec(memory_space=pltpu.HBM)] * (5 + len(pieces)),
        out_specs=pl.BlockSpec(memory_space=pltpu.HBM),
        scratch_shapes=[
            pltpu.VMEM(places.shape, jnp.int32),
            pltpu.VMEM(late.shape, jnp.int32),
            pltpu.VMEM(spread.shape, jnp.bfloat16),
            pltpu.VMEM(share.shape, jnp.float32),
            pltpu.VMEM((row_total, width), jnp.bfloat16),
            wide,
            wide,
            pltpu.SemaphoreType.DMA((4 + len(pieces) + steps,)),
            pltpu.SemaphoreType.DMA((steps,)),
        ],
        compiler_params=pltpu.CompilerParams(vmem_limit_bytes=60 * 1024 * 1024),
        cost_estimate=pl.CostEstimate(
            flops=2 * centre_count * width * row_total,
            bytes_accessed=8 * centre_count * width,
            transcendentals=0,
        ),
        name="late",
    )(places, late, spread, share, early, *pieces)


def shards(
    token_ids,
    lengths,
    word_table,
    pos_table,
    emb_gain,
    emb_bias,
    w_qkv,
    w_out,
    out_bias,
    norm_gain,
    norm_bias,
    stored_rows,
    row_owner,
    row_slot,
    centroids,
):
    peer_count = lax.axis_size("dp")
    half = peer_count // 2
    width = word_table.shape[1]
    vocab_rows = word_table.shape[0]
    passes, seq_len = token_ids.shape
    token_count = passes * seq_len
    row_count = row_slot.shape[0]
    store_count = stored_rows.shape[0]
    token_cap = max(2, 3 * token_count // peer_count)
    row_cap = max(2, 3 * row_count // peer_count)

    across = [(i, i ^ half) for i in range(peer_count)]
    beside = [(i, i ^ 1) for i in range(peer_count)]

    def hand_on(blocks):
        got = [blocks[0]]
        for step in range(1, len(blocks)):
            moves = [(i, i ^ (2 * step)) for i in range(peer_count)]
            got.append(lax.ppermute(blocks[step], "dp", moves))
        return got

    ahead = store_count * 3 // 4 // 16 * 16
    sibling_rows = lax.ppermute(stored_rows, "dp", beside)
    first_rows = lax.ppermute(stored_rows[:ahead], "dp", across)
    sizes = (peer_count, vocab_rows, token_cap, row_cap, row_count - store_count)
    owners = row_owner.reshape(1, row_count)
    sibling_owners = lax.ppermute(owners, "dp", beside)
    plan, token_slot, code, sibling_code = route(
        token_ids, owners, row_slot[None], sibling_owners, sizes
    )
    plan, sibling_rows = lax.optimization_barrier((plan, sibling_rows))
    codes = lax.all_to_all(plan, "dp", split_axis=0, concat_axis=0, tiled=True)
    *blocks, last_rows = pack_rows(
        code,
        sibling_code,
        [stored_rows],
        [sibling_rows],
        half,
        row_cap,
        row_count,
        rest=store_count - ahead,
    )
    codes, last_rows = lax.optimization_barrier((codes, last_rows))
    last_rows = lax.ppermute(last_rows, "dp", across)
    own_half = hand_on(blocks)
    plan = codes[:, 0, row_count:]
    wanted = plan[:, :token_cap].reshape(peer_count * token_cap)
    chosen = wanted[:, None] == jnp.arange(vocab_rows, dtype=jnp.int32)[None, :]
    found = jnp.dot(
        chosen.astype(jnp.bfloat16), word_table, preferred_element_type=jnp.float32
    ).astype(jnp.bfloat16)
    found, first_rows, own_half[:2] = lax.optimization_barrier(
        (found, first_rows, own_half[:2])
    )
    fetched = lax.all_to_all(
        found.reshape(peer_count, token_cap, width), "dp", split_axis=0, concat_axis=0, tiled=True
    ).reshape(peer_count * token_cap, width)

    sources = lax.axis_index("dp") ^ jnp.arange(peer_count, dtype=jnp.int32)
    got_places = plan[:, token_cap : token_cap + row_cap][sources].reshape(half, 2 * row_cap)
    spare = padded(2 * row_cap) - 2 * row_cap
    got_places = jnp.pad(got_places, ((0, 0), (0, spare)), constant_values=-1).reshape(1, -1)
    near_rows, last_rows = lax.optimization_barrier((own_half, last_rows))
    means, share = early_update(got_places, centroids, near_rows)
    first_rows, last_rows, means = lax.optimization_barrier((first_rows, last_rows, means))
    partner_rows = [first_rows, last_rows]
    far_rows = [lax.ppermute(rows, "dp", beside) for rows in partner_rows]
    picks = (half, half ^ 1)
    blocks = pack_rows(codes, codes, partner_rows, far_rows, half, row_cap, row_count, picks)
    other_half = hand_on(blocks)
    late_places = plan[:, token_cap + row_cap :].reshape(1, -1)
    fetched, means, share, got_places, late_places = lax.optimization_barrier(
        (fetched, means, share, got_places, late_places)
    )

    passage_embed, spread = encode(
        peer_count,
        token_slot,
        fetched,
        lengths,
        pos_table,
        emb_gain,
        emb_bias,
        w_qkv,
        w_out,
        out_bias,
        norm_gain,
        norm_bias,
    )
    all_embeds = lax.all_to_all(
        spread, "dp", split_axis=0, concat_axis=0, tiled=True
    )
    new_centroids = late_update(got_places, late_places, all_embeds, share, means, other_half)
    return (passage_embed, new_centroids)


def solution(mesh):
    return jax.shard_map(
        shards,
        mesh=mesh,
        in_specs=(
            P(("groups", "dp"), None),
            P(("groups", "dp")),
            P("dp", None),
            P(),
            P(),
            P(),
            P(),
            P(),
            P(),
            P(),
            P(),
            P(("groups", "dp"), None),
            P(("groups", "dp"), None),
            P(("groups", "dp")),
            P(("groups", "dp"), None),
        ),
        out_specs=(P(("groups", "dp"), None), P(("groups", "dp"), None)),
        check_vma=False,
    )
```

```python
import functools

import jax
import jax.numpy as jnp
from jax import lax
from jax.experimental import pallas as pl
from jax.experimental.pallas import tpu as pltpu
from jax.sharding import PartitionSpec as P

HEADS = 8
HD = 64


def normed(values, gain, shift):
    center = values - jnp.mean(values, axis=-1, keepdims=True)
    spread = jnp.mean(center * center, axis=-1, keepdims=True)
    return center * lax.rsqrt(spread + 1e-12) * gain + shift


def head_sums(weights, seq):
    rows, columns = weights.shape
    lane = lax.broadcasted_iota(jnp.int32, (rows, 2 * seq), 1)
    sums = []
    for start in range(0, columns, 2 * seq):
        pair = weights[:, start : start + 2 * seq]
        first = jnp.sum(jnp.where(lane < seq, pair, 0.0), axis=1, keepdims=True)
        second = jnp.sum(jnp.where(lane < seq, 0.0, pair), axis=1, keepdims=True)
        sums.append(jnp.where(lane < seq, first, second))
    return jnp.concatenate(sums, axis=1)


def encode_kernel(*refs):
    count = (len(refs) - 3) // 2
    far, (out, spread), near, arrived = refs[:count], refs[count : count + 2], refs[-count - 1 : -1], refs[-1]
    w_qkv_far, inner = far[-2], HEADS * HD
    copies = [
        pltpu.make_async_copy(source, target, arrived.at[at])
        for at, (source, target) in enumerate(zip(far, near))
        if source is not w_qkv_far
    ]
    lengths, slots, fetched, pos, emb_gain, emb_bias, out_bias, norm_gain, norm_bias, w_qkv, w_out = near
    out_copy = copies.pop()
    thirds = []
    for third in range(3):
        columns = pl.ds(third * inner, inner)
        thirds.append(
            pltpu.make_async_copy(
                w_qkv_far.at[:, columns], w_qkv.at[:, columns], arrived.at[count + third]
            )
        )
    for copy in copies + thirds + [out_copy]:
        copy.start()
    for copy in copies:
        copy.wait()
    passes = out.shape[0]
    size = [lengths[:, p : p + 1] for p in range(passes)]
    tokens, slot_count = slots.shape[0], fetched.shape[0]
    seq = tokens // passes
    spot = lax.broadcasted_iota(jnp.int32, (tokens, slot_count), 1)
    picker = jnp.where(slots[...] == spot, 1.0, 0.0).astype(jnp.bfloat16)
    tok = jnp.dot(picker, fetched[...], preferred_element_type=jnp.float32)
    where_at = pos[...].astype(jnp.float32)
    summed = tok + jnp.concatenate([where_at] * passes, axis=0)
    embedded = normed(summed, emb_gain[...], emb_bias[...]).astype(jnp.bfloat16)
    parts = []
    for third in range(3):
        thirds[third].wait()
        weights = w_qkv[:, third * inner : (third + 1) * inner]
        part = jnp.dot(embedded, weights, preferred_element_type=jnp.float32)
        parts.append(part.astype(jnp.bfloat16))

    block_row = lax.broadcasted_iota(jnp.int32, (HEADS * seq, inner), 0) // seq
    block_col = lax.broadcasted_iota(jnp.int32, (HEADS * seq, inner), 1) // HD
    same = block_row == block_col
    lane = lax.broadcasted_iota(jnp.int32, (seq, HEADS * seq), 1) % seq
    contexts = []
    for p in range(passes):
        query, keys, vals = (part[p * seq : (p + 1) * seq] for part in parts)
        zero = jnp.zeros((), jnp.bfloat16)
        keys = jnp.where(same, jnp.concatenate([keys] * HEADS, axis=0), zero)
        vals = jnp.where(same, jnp.concatenate([vals] * HEADS, axis=0), zero)
        scores = lax.dot_general(
            query, keys, (((1,), (1,)), ((), ())), preferred_element_type=jnp.float32
        ) * HD ** (-0.5)
        weights = jnp.where(lane < size[p], jnp.exp(scores), 0.0)
        probs = (weights / head_sums(weights, seq)).astype(jnp.bfloat16)
        contexts.append(jnp.dot(probs, vals, preferred_element_type=jnp.float32))
    context = jnp.concatenate(contexts, axis=0).astype(jnp.bfloat16)
    out_copy.wait()
    attended = jnp.dot(context, w_out[...], preferred_element_type=jnp.float32) + out_bias[...]
    hidden = normed(embedded.astype(jnp.float32) + attended, norm_gain[...], norm_bias[...])
    row = lax.broadcasted_iota(jnp.int32, (seq, 1), 0)
    for p in range(passes):
        kept = jnp.where(row < size[p], hidden[p * seq : (p + 1) * seq], 0.0)
        pooled = jnp.sum(kept, axis=0, keepdims=True) / size[p].astype(jnp.float32)
        scale = lax.rsqrt(jnp.mean(pooled * pooled, axis=-1, keepdims=True) + 1e-06)
        out[p : p + 1, :] = (pooled * scale).astype(jnp.bfloat16)
    spread[...] = jnp.broadcast_to(out[...][None], spread.shape)


def encode(
    peers, slots, fetched, lengths, pos_table, emb_gain, emb_bias, w_qkv, w_out, out_bias, norm_gain, norm_bias
):
    width = fetched.shape[1]
    tokens = slots.shape[0]
    passes = lengths.shape[0]
    macs = tokens * width * (fetched.shape[0] + 4 * HEADS * HD)
    operands = (
        lengths[None],
        slots,
        fetched,
        pos_table,
        emb_gain[None],
        emb_bias[None],
        out_bias[None],
        norm_gain[None],
        norm_bias[None],
        w_qkv,
        w_out,
    )
    return pl.pallas_call(
        encode_kernel,
        out_shape=[
            jax.ShapeDtypeStruct((passes, width), jnp.bfloat16),
            jax.ShapeDtypeStruct((peers, passes, width), jnp.bfloat16),
        ],
        in_specs=[pl.BlockSpec(memory_space=pl.ANY)] * len(operands),
        out_specs=[pl.BlockSpec(memory_space=pltpu.VMEM)] * 2,
        scratch_shapes=[pltpu.VMEM(operand.shape, operand.dtype) for operand in operands]
        + [pltpu.SemaphoreType.DMA((len(operands) + 3,))],
        compiler_params=pltpu.CompilerParams(vmem_limit_bytes=40 * 1024 * 1024),
        cost_estimate=pl.CostEstimate(
            flops=2 * macs, bytes_accessed=6 * 1024 * 1024, transcendentals=0
        ),
        name="encode",
    )(*operands)


def padded(rows):
    return -(-rows // 16) * 16


def rank_bits(count):
    return max(1, (count - 1).bit_length())


def ranks(kind):
    count = kind.shape[1]
    at = lax.broadcasted_iota(jnp.int32, (count, count), 0)
    by = lax.broadcasted_iota(jnp.int32, (count, count), 1)
    across = jnp.broadcast_to(kind, (count, count))
    down = jnp.sum(jnp.where(at == by, across, 0), axis=1, keepdims=True)
    same = down == across
    rank_row = jnp.sum(jnp.where(same & (at < by), 1, 0), axis=0, keepdims=True)
    rank_col = jnp.sum(jnp.where(same & (by < at), 1, 0), axis=1, keepdims=True)
    return down, rank_row, rank_col


def route_kernel(
    sizes,
    token_ids_far,
    owners_far,
    row_slot_far,
    sibling_far,
    plan,
    token_slot_far,
    code,
    sibling_code,
    *near,
):
    peers, vocab_rows, token_cap, row_cap, pooled = sizes
    token_ids, owners, row_slot, sibling, token_slot, arrived = near
    copies = [
        pltpu.make_async_copy(source, target, arrived.at[at])
        for at, (source, target) in enumerate(
            (
                (token_ids_far, token_ids),
                (owners_far, owners),
                (row_slot_far, row_slot),
                (sibling_far, sibling),
            )
        )
    ]
    for copy in copies:
        copy.start()
    for copy in copies:
        copy.wait()
    ids = jnp.concatenate([token_ids[p : p + 1, :] for p in range(token_ids.shape[0])], axis=1)
    tokens, rows = ids.shape[1], owners.shape[1]
    count = tokens + rows
    edge = (lax.broadcasted_iota(jnp.int32, (peers, tokens), 0) + 1) * vocab_rows
    holder = jnp.sum(jnp.where(ids >= edge, 1, 0), axis=0, keepdims=True)
    values = jnp.concatenate([ids - holder * vocab_rows, row_slot[...]], axis=1)

    kind = jnp.concatenate([holder, owners[...] + peers], axis=1)
    down, rank_row, rank_col = ranks(kind)

    code[...] = owners[...] * 2 ** rank_bits(rows) + rank_row[:, tokens:]
    sibling_code[...] = sibling[...] * 2 ** rank_bits(rows) + ranks(sibling[...])[1]
    goal = jnp.concatenate([holder, owners[...]], axis=1)
    peer = lax.broadcasted_iota(jnp.int32, (peers, count), 0)
    left = jnp.where(peer == goal, values + 1, 0).astype(jnp.float32)
    columns = token_cap + row_cap + pooled
    column = lax.broadcasted_iota(jnp.int32, (count, columns), 1)
    entry = lax.broadcasted_iota(jnp.int32, (count, 1), 0)
    first = jnp.where(entry < tokens, rank_col, rank_col + token_cap)
    second = entry - (count - pooled) + token_cap + row_cap
    second = jnp.where(entry < count - pooled, -1, second)
    right = jnp.where((column == first) | (column == second), 1.0, 0.0)
    filled = jnp.dot(
        left, right, preferred_element_type=jnp.float32, precision=lax.Precision.HIGHEST
    )
    filled = filled.astype(jnp.int32) - 1
    for p in range(peers):
        plan[p, :, :rows] = code[...]
        plan[p, :, rows:] = filled[p : p + 1]
    token_slot[...] = down[:tokens] * token_cap + rank_col[:tokens]
    send = pltpu.make_async_copy(token_slot, token_slot_far, arrived.at[4])
    send.start()
    send.wait()


def route(token_ids, owners, row_slot, sibling_owners, sizes):
    peers, _, token_cap, row_cap, pooled = sizes
    passes, seq_len = token_ids.shape
    rows = owners.shape[1]
    ints = lambda *shape: jax.ShapeDtypeStruct(shape, jnp.int32)
    return pl.pallas_call(
        functools.partial(route_kernel, sizes),
        out_shape=[
            ints(peers, 1, rows + token_cap + row_cap + pooled),
            ints(passes * seq_len, 1),
            ints(1, rows),
            ints(1, rows),
        ],
        in_specs=[pl.BlockSpec(memory_space=pltpu.HBM)] * 4,
        out_specs=[
            pl.BlockSpec(memory_space=pltpu.VMEM),
            pl.BlockSpec(memory_space=pltpu.HBM),
            pl.BlockSpec(memory_space=pltpu.VMEM),
            pl.BlockSpec(memory_space=pltpu.VMEM),
        ],
        scratch_shapes=[
            pltpu.VMEM(token_ids.shape, jnp.int32),
            pltpu.VMEM(owners.shape, jnp.int32),
            pltpu.VMEM(row_slot.shape, jnp.int32),
            pltpu.VMEM(owners.shape, jnp.int32),
            pltpu.VMEM((passes * seq_len, 1), jnp.int32),
            pltpu.SemaphoreType.DMA((5,)),
        ],
        compiler_params=pltpu.CompilerParams(vmem_limit_bytes=60 * 1024 * 1024),
        name="route",
    )(token_ids, owners, row_slot, sibling_owners)


def pack_kernel(half, row_cap, count, picks, pieces, rest, *refs):
    me = lax.axis_index("dp")
    operands = 2 + 2 * pieces
    far, refs = refs[:operands], refs[operands:]
    steps = half // 2
    outs, refs = refs[: steps + bool(rest)], refs[steps + bool(rest) :]
    near, (blocks, tail, arrived, left) = refs[:operands], refs[operands:]
    size = blocks.shape[0] // steps
    copies = [
        pltpu.make_async_copy(far[at], near[at], arrived.at[at]) for at in range(operands)
    ]
    for copy in copies:
        copy.start()
    for copy in copies[:2]:
        copy.wait()
    if size > 2 * row_cap:
        blocks[...] = jnp.zeros(blocks.shape, blocks.dtype)
    for source in range(2):
        if picks is None:
            code = near[source][...]
        else:
            code = near[source][me ^ picks[source], :, :count]
        bits = rank_bits(count)
        owner, rank = code >> bits, code & (2**bits - 1)
        fits = ((owner ^ me) & (1 | half)) == 0
        chip = ((owner ^ me) & (half - 1)) >> 1
        slot = jnp.where(fits, chip * row_cap + rank, -1)
        packed, at = 0.0, 0
        for piece in range(2 + source * pieces, 2 + (source + 1) * pieces):
            rows = near[piece]
            spot = lax.broadcasted_iota(jnp.int32, (steps * row_cap, rows.shape[0]), 0)
            table = jnp.where(slot[:, at : at + rows.shape[0]] == spot, 1.0, 0.0)
            copies[piece].wait()
            packed += jnp.dot(
                table.astype(jnp.bfloat16), rows[...], preferred_element_type=jnp.float32
            )
            at += rows.shape[0]
        packed = packed.astype(jnp.bfloat16)
        for step in range(steps):
            first = step * size + source * row_cap
            blocks[first : first + row_cap, :] = packed[step * row_cap : (step + 1) * row_cap]
    sends = [
        pltpu.make_async_copy(
            blocks.at[pl.ds(step * size, size)], outs[step], left.at[step]
        )
        for step in range(steps)
    ]
    if rest:
        tail[...] = near[2][near[2].shape[0] - rest :, :]
        sends.append(pltpu.make_async_copy(tail, outs[steps], left.at[steps]))
    for send in sends:
        send.start()
    for send in sends:
        send.wait()


def pack_rows(codes_a, codes_b, rows_a, rows_b, half, row_cap, count, picks=None, rest=0):
    width = rows_a[0].shape[1]
    total = sum(piece.shape[0] for piece in rows_a)
    steps = half // 2
    size = padded(2 * row_cap)
    operands = (codes_a, codes_b, *rows_a, *rows_b)
    shapes = [(size, width)] * steps + [(rest, width)] * bool(rest)
    return pl.pallas_call(
        functools.partial(pack_kernel, half, row_cap, count, picks, len(rows_a), rest),
        out_shape=[jax.ShapeDtypeStruct(shape, jnp.bfloat16) for shape in shapes],
        in_specs=[pl.BlockSpec(memory_space=pltpu.HBM)] * len(operands),
        out_specs=[pl.BlockSpec(memory_space=pltpu.HBM)] * len(shapes),
        scratch_shapes=[
            *(pltpu.VMEM(operand.shape, operand.dtype) for operand in operands),
            pltpu.VMEM((steps * size, width), jnp.bfloat16),
            pltpu.VMEM((max(rest, 16), width), jnp.bfloat16),
            pltpu.SemaphoreType.DMA((len(operands),)),
            pltpu.SemaphoreType.DMA((len(shapes),)),
        ],
        compiler_params=pltpu.CompilerParams(vmem_limit_bytes=60 * 1024 * 1024),
        cost_estimate=pl.CostEstimate(
            flops=4 * steps * row_cap * width * total,
            bytes_accessed=4 * width * (total + steps * row_cap),
            transcendentals=0,
        ),
        name="pack",
    )(*operands)


def onehot(where_to, first, count):
    centre = lax.broadcasted_iota(jnp.int32, (count, where_to.shape[1]), 0) + first
    return jnp.where(centre == where_to, 1.0, 0.0)


BLOCK = 128


def early_kernel(places_far, centroids_far, *rest):
    pieces, (out_far, share_far, places, rows, centroids, out, share, arrived, left) = rest[:-9], rest[-9:]
    size = pieces[0].shape[0]
    steps = centroids.shape[0] // BLOCK
    copies = [pltpu.make_async_copy(places_far, places, arrived.at[0])]
    for at, piece in enumerate(pieces):
        copies.append(
            pltpu.make_async_copy(piece, rows.at[pl.ds(at * size, size)], arrived.at[1 + at])
        )
    loads = []
    for step in range(steps):
        block = pl.ds(step * BLOCK, BLOCK)
        loads.append(
            pltpu.make_async_copy(
                centroids_far.at[block], centroids.at[block], arrived.at[1 + len(pieces) + step]
            )
        )
    for copy in copies + loads:
        copy.start()
    for copy in copies:
        copy.wait()
    sends = []
    for step in range(steps):
        block = pl.ds(step * BLOCK, BLOCK)
        hot = onehot(places[...], step * BLOCK, BLOCK)
        counts = jnp.sum(hot, axis=1, keepdims=True)
        scale = jnp.where(counts > 0, 1.0 / jnp.maximum(counts, 1.0), 0.0)
        sums = jnp.dot(
            hot[:, : rows.shape[0]].astype(jnp.bfloat16),
            rows[...],
            preferred_element_type=jnp.float32,
        )
        loads[step].wait()
        out[block, :] = jnp.where(counts > 0, sums * scale, centroids[block, :])
        share[block, :] = jnp.broadcast_to(scale, (BLOCK, share.shape[1]))
        sends.append(pltpu.make_async_copy(out.at[block], out_far.at[block], left.at[step]))
        sends[-1].start()
    sends.append(pltpu.make_async_copy(share, share_far, left.at[steps]))
    sends[-1].start()
    for send in sends:
        send.wait()


def late_kernel(places_far, late_far, spread_far, share_far, early_far, *rest):
    pieces, rest = rest[:-10], rest[-10:]
    out_far, places, late, spread, share, rows, early, out, arrived, left = rest
    size, passes = pieces[0].shape[0], spread.shape[1]
    steps = early.shape[0] // BLOCK
    loads = [
        pltpu.make_async_copy(source, target, arrived.at[at])
        for at, (source, target) in enumerate(
            ((places_far, places), (late_far, late), (spread_far, spread), (share_far, share))
        )
    ]
    for at, piece in enumerate(pieces):
        loads.append(
            pltpu.make_async_copy(piece, rows.at[pl.ds(at * size, size)], arrived.at[4 + at])
        )
    starts = []
    for step in range(steps):
        block = pl.ds(step * BLOCK, BLOCK)
        starts.append(
            pltpu.make_async_copy(
                early_far.at[block], early.at[block], arrived.at[len(loads) + step]
            )
        )
    for copy in loads + starts:
        copy.start()
    for copy in loads:
        copy.wait()
    top = len(pieces) * size
    for peer in range(spread.shape[0]):
        rows[top + peer * passes : top + (peer + 1) * passes, :] = spread[peer]
    where_to = jnp.concatenate([places[:, places.shape[1] - top :], late[...]], axis=1)
    sends = []
    for step in range(steps):
        block = pl.ds(step * BLOCK, BLOCK)
        hot = onehot(where_to, step * BLOCK, BLOCK).astype(jnp.bfloat16)
        sums = jnp.dot(hot, rows[...], preferred_element_type=jnp.float32)
        starts[step].wait()
        out[block, :] = early[block, :] + sums * share[block, :1]
        sends.append(pltpu.make_async_copy(out.at[block], out_far.at[block], left.at[step]))
        sends[-1].start()
    for send in sends:
        send.wait()


def early_update(places, centroids, pieces):
    centre_count, width = centroids.shape
    row_total = sum(piece.shape[0] for piece in pieces)
    wide = pltpu.VMEM(centroids.shape, jnp.float32)
    thin = (centre_count, 128)
    steps = centre_count // BLOCK
    return pl.pallas_call(
        early_kernel,
        out_shape=[
            jax.ShapeDtypeStruct(centroids.shape, jnp.float32),
            jax.ShapeDtypeStruct(thin, jnp.float32),
        ],
        in_specs=[pl.BlockSpec(memory_space=pl.ANY)] * (2 + len(pieces)),
        out_specs=[pl.BlockSpec(memory_space=pltpu.HBM)] * 2,
        scratch_shapes=[
            pltpu.VMEM(places.shape, jnp.int32),
            pltpu.VMEM((row_total, width), jnp.bfloat16),
            wide,
            wide,
            pltpu.VMEM(thin, jnp.float32),
            pltpu.SemaphoreType.DMA((1 + len(pieces) + steps,)),
            pltpu.SemaphoreType.DMA((steps + 1,)),
        ],
        compiler_params=pltpu.CompilerParams(vmem_limit_bytes=60 * 1024 * 1024),
        cost_estimate=pl.CostEstimate(
            flops=100 * centre_count * width * row_total,
            bytes_accessed=200 * centre_count * width,
            transcendentals=0,
        ),
        name="early",
    )(places, centroids, *pieces)


def late_update(places, late, spread, share, early, pieces):
    centre_count, width = early.shape
    row_total = sum(piece.shape[0] for piece in pieces) + late.shape[1]
    wide = pltpu.VMEM(early.shape, jnp.float32)
    steps = centre_count // BLOCK
    return pl.pallas_call(
        late_kernel,
        out_shape=jax.ShapeDtypeStruct(early.shape, jnp.float32),
        in_specs=[pl.BlockSpec(memory_space=pltpu.HBM)] * (5 + len(pieces)),
        out_specs=pl.BlockSpec(memory_space=pltpu.HBM),
        scratch_shapes=[
            pltpu.VMEM(places.shape, jnp.int32),
            pltpu.VMEM(late.shape, jnp.int32),
            pltpu.VMEM(spread.shape, jnp.bfloat16),
            pltpu.VMEM(share.shape, jnp.float32),
            pltpu.VMEM((row_total, width), jnp.bfloat16),
            wide,
            wide,
            pltpu.SemaphoreType.DMA((4 + len(pieces) + steps,)),
            pltpu.SemaphoreType.DMA((steps,)),
        ],
        compiler_params=pltpu.CompilerParams(vmem_limit_bytes=60 * 1024 * 1024),
        cost_estimate=pl.CostEstimate(
            flops=2 * centre_count * width * row_total,
            bytes_accessed=8 * centre_count * width,
            transcendentals=0,
        ),
        name="late",
    )(places, late, spread, share, early, *pieces)


def shards(
    token_ids,
    lengths,
    word_table,
    pos_table,
    emb_gain,
    emb_bias,
    w_qkv,
    w_out,
    out_bias,
    norm_gain,
    norm_bias,
    stored_rows,
    row_owner,
    row_slot,
    centroids,
):
    peer_count = lax.axis_size("dp")
    half = peer_count // 2
    width = word_table.shape[1]
    vocab_rows = word_table.shape[0]
    passes, seq_len = token_ids.shape
    token_count = passes * seq_len
    row_count = row_slot.shape[0]
    store_count = stored_rows.shape[0]
    token_cap = max(2, 3 * token_count // peer_count)
    row_cap = max(2, 3 * row_count // peer_count)

    across = [(i, i ^ half) for i in range(peer_count)]
    beside = [(i, i ^ 1) for i in range(peer_count)]

    def hand_on(blocks):
        got = [blocks[0]]
        for step in range(1, len(blocks)):
            moves = [(i, i ^ (2 * step)) for i in range(peer_count)]
            got.append(lax.ppermute(blocks[step], "dp", moves))
        return got

    ahead = store_count * 3 // 4 // 16 * 16
    sibling_rows = lax.ppermute(stored_rows, "dp", beside)
    first_rows = lax.ppermute(stored_rows[:ahead], "dp", across)
    sizes = (peer_count, vocab_rows, token_cap, row_cap, row_count - store_count)
    owners = row_owner.reshape(1, row_count)
    sibling_owners = lax.ppermute(owners, "dp", beside)
    plan, token_slot, code, sibling_code = route(
        token_ids, owners, row_slot[None], sibling_owners, sizes
    )
    plan, sibling_rows = lax.optimization_barrier((plan, sibling_rows))
    codes = lax.all_to_all(plan, "dp", split_axis=0, concat_axis=0, tiled=True)
    *blocks, last_rows = pack_rows(
        code,
        sibling_code,
        [stored_rows],
        [sibling_rows],
        half,
        row_cap,
        row_count,
        rest=store_count - ahead,
    )
    codes, last_rows = lax.optimization_barrier((codes, last_rows))
    last_rows = lax.ppermute(last_rows, "dp", across)
    own_half = hand_on(blocks)
    plan = codes[:, 0, row_count:]
    wanted = plan[:, :token_cap].reshape(peer_count * token_cap)
    chosen = wanted[:, None] == jnp.arange(vocab_rows, dtype=jnp.int32)[None, :]
    found = jnp.dot(
        chosen.astype(jnp.bfloat16), word_table, preferred_element_type=jnp.float32
    ).astype(jnp.bfloat16)
    found, first_rows, own_half[:2] = lax.optimization_barrier(
        (found, first_rows, own_half[:2])
    )
    fetched = lax.all_to_all(
        found.reshape(peer_count, token_cap, width), "dp", split_axis=0, concat_axis=0, tiled=True
    ).reshape(peer_count * token_cap, width)

    sources = lax.axis_index("dp") ^ jnp.arange(peer_count, dtype=jnp.int32)
    got_places = plan[:, token_cap : token_cap + row_cap][sources].reshape(half, 2 * row_cap)
    spare = padded(2 * row_cap) - 2 * row_cap
    got_places = jnp.pad(got_places, ((0, 0), (0, spare)), constant_values=-1).reshape(1, -1)
    near_rows, last_rows = lax.optimization_barrier((own_half[:2], last_rows))
    means, share = early_update(got_places, centroids, near_rows)
    first_rows, last_rows, means = lax.optimization_barrier((first_rows, last_rows, means))
    partner_rows = [first_rows, last_rows]
    far_rows = [lax.ppermute(rows, "dp", beside) for rows in partner_rows]
    picks = (half, half ^ 1)
    blocks = pack_rows(codes, codes, partner_rows, far_rows, half, row_cap, row_count, picks)
    other_half = hand_on(blocks)
    late_places = plan[:, token_cap + row_cap :].reshape(1, -1)
    fetched, means, share, got_places, late_places = lax.optimization_barrier(
        (fetched, means, share, got_places, late_places)
    )

    passage_embed, spread = encode(
        peer_count,
        token_slot,
        fetched,
        lengths,
        pos_table,
        emb_gain,
        emb_bias,
        w_qkv,
        w_out,
        out_bias,
        norm_gain,
        norm_bias,
    )
    all_embeds = lax.all_to_all(
        spread, "dp", split_axis=0, concat_axis=0, tiled=True
    )
    pieces = own_half[2:] + other_half
    new_centroids = late_update(got_places, late_places, all_embeds, share, means, pieces)
    return (passage_embed, new_centroids)


def solution(mesh):
    return jax.shard_map(
        shards,
        mesh=mesh,
        in_specs=(
            P(("groups", "dp"), None),
            P(("groups", "dp")),
            P("dp", None),
            P(),
            P(),
            P(),
            P(),
            P(),
            P(),
            P(),
            P(),
            P(("groups", "dp"), None),
            P(("groups", "dp"), None),
            P(("groups", "dp")),
            P(("groups", "dp"), None),
        ),
        out_specs=(P(("groups", "dp"), None), P(("groups", "dp"), None)),
        check_vma=False,
    )
```

```python
import functools

import jax
import jax.numpy as jnp
from jax import lax
from jax.experimental import pallas as pl
from jax.experimental.pallas import tpu as pltpu
from jax.sharding import PartitionSpec as P

HEADS = 8
HD = 64


def normed(values, gain, shift):
    center = values - jnp.mean(values, axis=-1, keepdims=True)
    spread = jnp.mean(center * center, axis=-1, keepdims=True)
    return center * lax.rsqrt(spread + 1e-12) * gain + shift


def head_sums(weights, seq):
    rows, columns = weights.shape
    lane = lax.broadcasted_iota(jnp.int32, (rows, 2 * seq), 1)
    sums = []
    for start in range(0, columns, 2 * seq):
        pair = weights[:, start : start + 2 * seq]
        first = jnp.sum(jnp.where(lane < seq, pair, 0.0), axis=1, keepdims=True)
        second = jnp.sum(jnp.where(lane < seq, 0.0, pair), axis=1, keepdims=True)
        sums.append(jnp.where(lane < seq, first, second))
    return jnp.concatenate(sums, axis=1)


def encode_kernel(*refs):
    *refs, same, arrived = refs
    count = (len(refs) - 2) // 2
    far, (out, spread), near = refs[:count], refs[count : count + 2], refs[-count:]
    w_qkv_far, inner = far[-2], HEADS * HD
    copies = [
        pltpu.make_async_copy(source, target, arrived.at[at])
        for at, (source, target) in enumerate(zip(far, near))
        if source is not w_qkv_far
    ]
    lengths, slots, fetched, pos, emb_gain, emb_bias, out_bias, norm_gain, norm_bias, w_qkv, w_out = near
    out_copy = copies.pop()
    thirds = []
    for third in range(3):
        columns = pl.ds(third * inner, inner)
        thirds.append(
            pltpu.make_async_copy(
                w_qkv_far.at[:, columns], w_qkv.at[:, columns], arrived.at[count + third]
            )
        )
    for copy in copies + thirds + [out_copy]:
        copy.start()
    passes = out.shape[0]
    tokens, slot_count = slots.shape[0], fetched.shape[0]
    seq = tokens // passes
    block_row = lax.broadcasted_iota(jnp.int32, (HEADS * seq, inner), 0) // seq
    block_col = lax.broadcasted_iota(jnp.int32, (HEADS * seq, inner), 1) // HD
    same[...] = jnp.where(block_row == block_col, 1.0, 0.0).astype(jnp.bfloat16)
    spot = lax.broadcasted_iota(jnp.int32, (tokens, slot_count), 1)
    lane = lax.broadcasted_iota(jnp.int32, (seq, HEADS * seq), 1) % seq
    for copy in copies[:2]:
        copy.wait()
    size = [lengths[:, p : p + 1] for p in range(passes)]
    picker = jnp.where(slots[...] == spot, 1.0, 0.0).astype(jnp.bfloat16)
    for copy in copies[2:]:
        copy.wait()
    tok = jnp.dot(picker, fetched[...], preferred_element_type=jnp.float32)
    where_at = pos[...].astype(jnp.float32)
    summed = tok + jnp.concatenate([where_at] * passes, axis=0)
    embedded = normed(summed, emb_gain[...], emb_bias[...]).astype(jnp.bfloat16)
    parts = []
    for third in range(3):
        thirds[third].wait()
        weights = w_qkv[:, third * inner : (third + 1) * inner]
        part = jnp.dot(embedded, weights, preferred_element_type=jnp.float32)
        parts.append(part.astype(jnp.bfloat16))

    contexts = []
    for p in range(passes):
        query, keys, vals = (part[p * seq : (p + 1) * seq] for part in parts)
        keys = jnp.concatenate([keys] * HEADS, axis=0) * same[...]
        vals = jnp.concatenate([vals] * HEADS, axis=0) * same[...]
        scores = lax.dot_general(
            query, keys, (((1,), (1,)), ((), ())), preferred_element_type=jnp.float32
        ) * HD ** (-0.5)
        weights = jnp.where(lane < size[p], jnp.exp(scores), 0.0)
        probs = (weights / head_sums(weights, seq)).astype(jnp.bfloat16)
        contexts.append(jnp.dot(probs, vals, preferred_element_type=jnp.float32))
    context = jnp.concatenate(contexts, axis=0).astype(jnp.bfloat16)
    out_copy.wait()
    attended = jnp.dot(context, w_out[...], preferred_element_type=jnp.float32) + out_bias[...]
    hidden = normed(embedded.astype(jnp.float32) + attended, norm_gain[...], norm_bias[...])
    row = lax.broadcasted_iota(jnp.int32, (seq, 1), 0)
    for p in range(passes):
        kept = jnp.where(row < size[p], hidden[p * seq : (p + 1) * seq], 0.0)
        pooled = jnp.sum(kept, axis=0, keepdims=True) / size[p].astype(jnp.float32)
        scale = lax.rsqrt(jnp.mean(pooled * pooled, axis=-1, keepdims=True) + 1e-06)
        out[p : p + 1, :] = (pooled * scale).astype(jnp.bfloat16)
    spread[...] = jnp.broadcast_to(out[...][None], spread.shape)


def encode(
    peers, slots, fetched, lengths, pos_table, emb_gain, emb_bias, w_qkv, w_out, out_bias, norm_gain, norm_bias
):
    width = fetched.shape[1]
    tokens = slots.shape[0]
    passes = lengths.shape[0]
    macs = tokens * width * (fetched.shape[0] + 4 * HEADS * HD)
    operands = (
        lengths[None],
        slots,
        fetched,
        pos_table,
        emb_gain[None],
        emb_bias[None],
        out_bias[None],
        norm_gain[None],
        norm_bias[None],
        w_qkv,
        w_out,
    )
    return pl.pallas_call(
        encode_kernel,
        out_shape=[
            jax.ShapeDtypeStruct((passes, width), jnp.bfloat16),
            jax.ShapeDtypeStruct((peers, passes, width), jnp.bfloat16),
        ],
        in_specs=[pl.BlockSpec(memory_space=pltpu.HBM)] * len(operands),
        out_specs=[pl.BlockSpec(memory_space=pltpu.VMEM)] * 2,
        scratch_shapes=[pltpu.VMEM(operand.shape, operand.dtype) for operand in operands]
        + [
            pltpu.VMEM((HEADS * tokens // passes, HEADS * HD), jnp.bfloat16),
            pltpu.SemaphoreType.DMA((len(operands) + 3,)),
        ],
        compiler_params=pltpu.CompilerParams(vmem_limit_bytes=60 * 1024 * 1024),
        cost_estimate=pl.CostEstimate(
            flops=2 * macs, bytes_accessed=6 * 1024 * 1024, transcendentals=0
        ),
        name="encode",
    )(*operands)


def padded(rows):
    return -(-rows // 16) * 16


def rank_bits(count):
    return max(1, (count - 1).bit_length())


def ranks(kind):
    count = kind.shape[1]
    at = lax.broadcasted_iota(jnp.int32, (count, count), 0)
    by = lax.broadcasted_iota(jnp.int32, (count, count), 1)
    across = jnp.broadcast_to(kind, (count, count))
    down = jnp.sum(jnp.where(at == by, across, 0), axis=1, keepdims=True)
    same = down == across
    rank_row = jnp.sum(jnp.where(same & (at < by), 1, 0), axis=0, keepdims=True)
    rank_col = jnp.sum(jnp.where(same & (by < at), 1, 0), axis=1, keepdims=True)
    return down, rank_row, rank_col


def route_kernel(
    sizes,
    token_ids_far,
    owners_far,
    row_slot_far,
    sibling_far,
    plan,
    token_slot_far,
    code,
    sibling_code,
    *near,
):
    peers, vocab_rows, token_cap, row_cap, pooled = sizes
    token_ids, owners, row_slot, sibling, token_slot, arrived = near
    copies = [
        pltpu.make_async_copy(source, target, arrived.at[at])
        for at, (source, target) in enumerate(
            (
                (token_ids_far, token_ids),
                (owners_far, owners),
                (row_slot_far, row_slot),
                (sibling_far, sibling),
            )
        )
    ]
    for copy in copies:
        copy.start()
    for copy in copies:
        copy.wait()
    ids = jnp.concatenate([token_ids[p : p + 1, :] for p in range(token_ids.shape[0])], axis=1)
    tokens, rows = ids.shape[1], owners.shape[1]
    count = tokens + rows
    edge = (lax.broadcasted_iota(jnp.int32, (peers, tokens), 0) + 1) * vocab_rows
    holder = jnp.sum(jnp.where(ids >= edge, 1, 0), axis=0, keepdims=True)
    values = jnp.concatenate([ids - holder * vocab_rows, row_slot[...]], axis=1)

    kind = jnp.concatenate([holder, owners[...] + peers], axis=1)
    down, rank_row, rank_col = ranks(kind)

    code[...] = owners[...] * 2 ** rank_bits(rows) + rank_row[:, tokens:]
    sibling_code[...] = sibling[...] * 2 ** rank_bits(rows) + ranks(sibling[...])[1]
    goal = jnp.concatenate([holder, owners[...]], axis=1)
    peer = lax.broadcasted_iota(jnp.int32, (peers, count), 0)
    left = jnp.where(peer == goal, values + 1, 0).astype(jnp.float32)
    columns = token_cap + row_cap + pooled
    column = lax.broadcasted_iota(jnp.int32, (count, columns), 1)
    entry = lax.broadcasted_iota(jnp.int32, (count, 1), 0)
    first = jnp.where(entry < tokens, rank_col, rank_col + token_cap)
    second = entry - (count - pooled) + token_cap + row_cap
    second = jnp.where(entry < count - pooled, -1, second)
    right = jnp.where((column == first) | (column == second), 1.0, 0.0)
    filled = jnp.dot(
        left, right, preferred_element_type=jnp.float32, precision=lax.Precision.HIGHEST
    )
    filled = filled.astype(jnp.int32) - 1
    for p in range(peers):
        plan[p, :, :rows] = code[...]
        plan[p, :, rows:] = filled[p : p + 1]
    token_slot[...] = down[:tokens] * token_cap + rank_col[:tokens]
    send = pltpu.make_async_copy(token_slot, token_slot_far, arrived.at[4])
    send.start()
    send.wait()


def route(token_ids, owners, row_slot, sibling_owners, sizes):
    peers, _, token_cap, row_cap, pooled = sizes
    passes, seq_len = token_ids.shape
    rows = owners.shape[1]
    ints = lambda *shape: jax.ShapeDtypeStruct(shape, jnp.int32)
    return pl.pallas_call(
        functools.partial(route_kernel, sizes),
        out_shape=[
            ints(peers, 1, rows + token_cap + row_cap + pooled),
            ints(passes * seq_len, 1),
            ints(1, rows),
            ints(1, rows),
        ],
        in_specs=[pl.BlockSpec(memory_space=pltpu.HBM)] * 4,
        out_specs=[
            pl.BlockSpec(memory_space=pltpu.VMEM),
            pl.BlockSpec(memory_space=pltpu.HBM),
            pl.BlockSpec(memory_space=pltpu.VMEM),
            pl.BlockSpec(memory_space=pltpu.VMEM),
        ],
        scratch_shapes=[
            pltpu.VMEM(token_ids.shape, jnp.int32),
            pltpu.VMEM(owners.shape, jnp.int32),
            pltpu.VMEM(row_slot.shape, jnp.int32),
            pltpu.VMEM(owners.shape, jnp.int32),
            pltpu.VMEM((passes * seq_len, 1), jnp.int32),
            pltpu.SemaphoreType.DMA((5,)),
        ],
        compiler_params=pltpu.CompilerParams(vmem_limit_bytes=60 * 1024 * 1024),
        name="route",
    )(token_ids, owners, row_slot, sibling_owners)


def pack_kernel(half, row_cap, count, picks, pieces, rest, *refs):
    me = lax.axis_index("dp")
    operands = 2 + 2 * pieces
    far, refs = refs[:operands], refs[operands:]
    steps = half // 2
    outs, refs = refs[: steps + bool(rest)], refs[steps + bool(rest) :]
    near, (blocks, tail, arrived, left) = refs[:operands], refs[operands:]
    size = blocks.shape[0] // steps
    copies = [
        pltpu.make_async_copy(far[at], near[at], arrived.at[at]) for at in range(operands)
    ]
    for copy in copies:
        copy.start()
    for copy in copies[:2]:
        copy.wait()
    if size > 2 * row_cap:
        blocks[...] = jnp.zeros(blocks.shape, blocks.dtype)
    for source in range(2):
        if picks is None:
            code = near[source][...]
        else:
            code = near[source][me ^ picks[source], :, :count]
        bits = rank_bits(count)
        owner, rank = code >> bits, code & (2**bits - 1)
        fits = ((owner ^ me) & (1 | half)) == 0
        chip = ((owner ^ me) & (half - 1)) >> 1
        slot = jnp.where(fits, chip * row_cap + rank, -1)
        packed, at = 0.0, 0
        for piece in range(2 + source * pieces, 2 + (source + 1) * pieces):
            rows = near[piece]
            spot = lax.broadcasted_iota(jnp.int32, (steps * row_cap, rows.shape[0]), 0)
            table = jnp.where(slot[:, at : at + rows.shape[0]] == spot, 1.0, 0.0)
            copies[piece].wait()
            packed += jnp.dot(
                table.astype(jnp.bfloat16), rows[...], preferred_element_type=jnp.float32
            )
            at += rows.shape[0]
        packed = packed.astype(jnp.bfloat16)
        for step in range(steps):
            first = step * size + source * row_cap
            blocks[first : first + row_cap, :] = packed[step * row_cap : (step + 1) * row_cap]
    sends = [
        pltpu.make_async_copy(
            blocks.at[pl.ds(step * size, size)], outs[step], left.at[step]
        )
        for step in range(steps)
    ]
    if rest:
        tail[...] = near[2][near[2].shape[0] - rest :, :]
        sends.append(pltpu.make_async_copy(tail, outs[steps], left.at[steps]))
    for send in sends:
        send.start()
    for send in sends:
        send.wait()


def pack_rows(codes_a, codes_b, rows_a, rows_b, half, row_cap, count, picks=None, rest=0):
    width = rows_a[0].shape[1]
    total = sum(piece.shape[0] for piece in rows_a)
    steps = half // 2
    size = padded(2 * row_cap)
    operands = (codes_a, codes_b, *rows_a, *rows_b)
    shapes = [(size, width)] * steps + [(rest, width)] * bool(rest)
    return pl.pallas_call(
        functools.partial(pack_kernel, half, row_cap, count, picks, len(rows_a), rest),
        out_shape=[jax.ShapeDtypeStruct(shape, jnp.bfloat16) for shape in shapes],
        in_specs=[pl.BlockSpec(memory_space=pltpu.HBM)] * len(operands),
        out_specs=[pl.BlockSpec(memory_space=pltpu.HBM)] * len(shapes),
        scratch_shapes=[
            *(pltpu.VMEM(operand.shape, operand.dtype) for operand in operands),
            pltpu.VMEM((steps * size, width), jnp.bfloat16),
            pltpu.VMEM((max(rest, 16), width), jnp.bfloat16),
            pltpu.SemaphoreType.DMA((len(operands),)),
            pltpu.SemaphoreType.DMA((len(shapes),)),
        ],
        compiler_params=pltpu.CompilerParams(vmem_limit_bytes=60 * 1024 * 1024),
        cost_estimate=pl.CostEstimate(
            flops=4 * steps * row_cap * width * total,
            bytes_accessed=4 * width * (total + steps * row_cap),
            transcendentals=0,
        ),
        name="pack",
    )(*operands)


def onehot(where_to, first, count):
    centre = lax.broadcasted_iota(jnp.int32, (count, where_to.shape[1]), 0) + first
    return jnp.where(centre == where_to, 1.0, 0.0)


BLOCK = 128


def early_kernel(places_far, centroids_far, *rest):
    pieces, (out_far, share_far, places, rows, centroids, out, share, arrived, left) = rest[:-9], rest[-9:]
    size = pieces[0].shape[0]
    steps = centroids.shape[0] // BLOCK
    copies = [pltpu.make_async_copy(places_far, places, arrived.at[0])]
    for at, piece in enumerate(pieces):
        copies.append(
            pltpu.make_async_copy(piece, rows.at[pl.ds(at * size, size)], arrived.at[1 + at])
        )
    loads = []
    for step in range(steps):
        block = pl.ds(step * BLOCK, BLOCK)
        loads.append(
            pltpu.make_async_copy(
                centroids_far.at[block], centroids.at[block], arrived.at[1 + len(pieces) + step]
            )
        )
    for copy in copies + loads:
        copy.start()
    for copy in copies:
        copy.wait()
    sends = []
    for step in range(steps):
        block = pl.ds(step * BLOCK, BLOCK)
        hot = onehot(places[...], step * BLOCK, BLOCK)
        counts = jnp.sum(hot, axis=1, keepdims=True)
        scale = jnp.where(counts > 0, 1.0 / jnp.maximum(counts, 1.0), 0.0)
        sums = jnp.dot(
            hot[:, : rows.shape[0]].astype(jnp.bfloat16),
            rows[...],
            preferred_element_type=jnp.float32,
        )
        loads[step].wait()
        out[block, :] = jnp.where(counts > 0, sums * scale, centroids[block, :])
        share[block, :] = jnp.broadcast_to(scale, (BLOCK, share.shape[1]))
        sends.append(pltpu.make_async_copy(out.at[block], out_far.at[block], left.at[step]))
        sends[-1].start()
    sends.append(pltpu.make_async_copy(share, share_far, left.at[steps]))
    sends[-1].start()
    for send in sends:
        send.wait()


def late_kernel(places_far, late_far, spread_far, share_far, early_far, *rest):
    pieces, rest = rest[:-10], rest[-10:]
    out_far, places, late, spread, share, rows, early, out, arrived, left = rest
    size, passes = pieces[0].shape[0], spread.shape[1]
    steps = early.shape[0] // BLOCK
    loads = [
        pltpu.make_async_copy(source, target, arrived.at[at])
        for at, (source, target) in enumerate(
            ((places_far, places), (late_far, late), (spread_far, spread), (share_far, share))
        )
    ]
    for at, piece in enumerate(pieces):
        loads.append(
            pltpu.make_async_copy(piece, rows.at[pl.ds(at * size, size)], arrived.at[4 + at])
        )
    starts = []
    for step in range(steps):
        block = pl.ds(step * BLOCK, BLOCK)
        starts.append(
            pltpu.make_async_copy(
                early_far.at[block], early.at[block], arrived.at[len(loads) + step]
            )
        )
    for copy in loads + starts:
        copy.start()
    for copy in loads:
        copy.wait()
    top = len(pieces) * size
    for peer in range(spread.shape[0]):
        rows[top + peer * passes : top + (peer + 1) * passes, :] = spread[peer]
    where_to = jnp.concatenate([places[:, places.shape[1] - top :], late[...]], axis=1)
    sends = []
    for step in range(steps):
        block = pl.ds(step * BLOCK, BLOCK)
        hot = onehot(where_to, step * BLOCK, BLOCK).astype(jnp.bfloat16)
        sums = jnp.dot(hot, rows[...], preferred_element_type=jnp.float32)
        starts[step].wait()
        out[block, :] = early[block, :] + sums * share[block, :1]
        sends.append(pltpu.make_async_copy(out.at[block], out_far.at[block], left.at[step]))
        sends[-1].start()
    for send in sends:
        send.wait()


def early_update(places, centroids, pieces):
    centre_count, width = centroids.shape
    row_total = sum(piece.shape[0] for piece in pieces)
    wide = pltpu.VMEM(centroids.shape, jnp.float32)
    thin = (centre_count, 128)
    steps = centre_count // BLOCK
    return pl.pallas_call(
        early_kernel,
        out_shape=[
            jax.ShapeDtypeStruct(centroids.shape, jnp.float32),
            jax.ShapeDtypeStruct(thin, jnp.float32),
        ],
        in_specs=[pl.BlockSpec(memory_space=pl.ANY)] * (2 + len(pieces)),
        out_specs=[pl.BlockSpec(memory_space=pltpu.HBM)] * 2,
        scratch_shapes=[
            pltpu.VMEM(places.shape, jnp.int32),
            pltpu.VMEM((row_total, width), jnp.bfloat16),
            wide,
            wide,
            pltpu.VMEM(thin, jnp.float32),
            pltpu.SemaphoreType.DMA((1 + len(pieces) + steps,)),
            pltpu.SemaphoreType.DMA((steps + 1,)),
        ],
        compiler_params=pltpu.CompilerParams(vmem_limit_bytes=60 * 1024 * 1024),
        cost_estimate=pl.CostEstimate(
            flops=100 * centre_count * width * row_total,
            bytes_accessed=200 * centre_count * width,
            transcendentals=0,
        ),
        name="early",
    )(places, centroids, *pieces)


def late_update(places, late, spread, share, early, pieces):
    centre_count, width = early.shape
    row_total = sum(piece.shape[0] for piece in pieces) + late.shape[1]
    wide = pltpu.VMEM(early.shape, jnp.float32)
    steps = centre_count // BLOCK
    return pl.pallas_call(
        late_kernel,
        out_shape=jax.ShapeDtypeStruct(early.shape, jnp.float32),
        in_specs=[pl.BlockSpec(memory_space=pltpu.HBM)] * (5 + len(pieces)),
        out_specs=pl.BlockSpec(memory_space=pltpu.HBM),
        scratch_shapes=[
            pltpu.VMEM(places.shape, jnp.int32),
            pltpu.VMEM(late.shape, jnp.int32),
            pltpu.VMEM(spread.shape, jnp.bfloat16),
            pltpu.VMEM(share.shape, jnp.float32),
            pltpu.VMEM((row_total, width), jnp.bfloat16),
            wide,
            wide,
            pltpu.SemaphoreType.DMA((4 + len(pieces) + steps,)),
            pltpu.SemaphoreType.DMA((steps,)),
        ],
        compiler_params=pltpu.CompilerParams(vmem_limit_bytes=60 * 1024 * 1024),
        cost_estimate=pl.CostEstimate(
            flops=2 * centre_count * width * row_total,
            bytes_accessed=8 * centre_count * width,
            transcendentals=0,
        ),
        name="late",
    )(places, late, spread, share, early, *pieces)


def shards(
    token_ids,
    lengths,
    word_table,
    pos_table,
    emb_gain,
    emb_bias,
    w_qkv,
    w_out,
    out_bias,
    norm_gain,
    norm_bias,
    stored_rows,
    row_owner,
    row_slot,
    centroids,
):
    peer_count = lax.axis_size("dp")
    half = peer_count // 2
    width = word_table.shape[1]
    vocab_rows = word_table.shape[0]
    passes, seq_len = token_ids.shape
    token_count = passes * seq_len
    row_count = row_slot.shape[0]
    store_count = stored_rows.shape[0]
    token_cap = max(2, 3 * token_count // peer_count)
    row_cap = max(2, 3 * row_count // peer_count)

    across = [(i, i ^ half) for i in range(peer_count)]
    beside = [(i, i ^ 1) for i in range(peer_count)]

    def hand_on(blocks):
        got = [blocks[0]]
        for step in range(1, len(blocks)):
            moves = [(i, i ^ (2 * step)) for i in range(peer_count)]
            got.append(lax.ppermute(blocks[step], "dp", moves))
        return got

    ahead = store_count * 3 // 4 // 16 * 16
    sibling_rows = lax.ppermute(stored_rows, "dp", beside)
    first_rows = lax.ppermute(stored_rows[:ahead], "dp", across)
    sizes = (peer_count, vocab_rows, token_cap, row_cap, row_count - store_count)
    owners = row_owner.reshape(1, row_count)
    sibling_owners = lax.ppermute(owners, "dp", beside)
    plan, token_slot, code, sibling_code = route(
        token_ids, owners, row_slot[None], sibling_owners, sizes
    )
    plan, sibling_rows = lax.optimization_barrier((plan, sibling_rows))
    codes = lax.all_to_all(plan, "dp", split_axis=0, concat_axis=0, tiled=True)
    *blocks, last_rows = pack_rows(
        code,
        sibling_code,
        [stored_rows],
        [sibling_rows],
        half,
        row_cap,
        row_count,
        rest=store_count - ahead,
    )
    own_half = hand_on(blocks)
    plan = codes[:, 0, row_count:]
    wanted = plan[:, :token_cap].reshape(peer_count * token_cap)
    chosen = wanted[:, None] == jnp.arange(vocab_rows, dtype=jnp.int32)[None, :]
    found = jnp.dot(
        chosen.astype(jnp.bfloat16), word_table, preferred_element_type=jnp.float32
    ).astype(jnp.bfloat16)
    found, last_rows = lax.optimization_barrier((found, last_rows))
    last_rows = lax.ppermute(last_rows, "dp", across)
    found, first_rows, own_half[:2] = lax.optimization_barrier(
        (found, first_rows, own_half[:2])
    )
    fetched = lax.all_to_all(
        found.reshape(peer_count, token_cap, width), "dp", split_axis=0, concat_axis=0, tiled=True
    ).reshape(peer_count * token_cap, width)

    sources = lax.axis_index("dp") ^ jnp.arange(peer_count, dtype=jnp.int32)
    got_places = plan[:, token_cap : token_cap + row_cap][sources].reshape(half, 2 * row_cap)
    spare = padded(2 * row_cap) - 2 * row_cap
    got_places = jnp.pad(got_places, ((0, 0), (0, spare)), constant_values=-1).reshape(1, -1)
    near_rows, last_rows = lax.optimization_barrier((own_half[:2], last_rows))
    means, share = early_update(got_places, centroids, near_rows)
    first_rows, last_rows, means = lax.optimization_barrier((first_rows, last_rows, means))
    partner_rows = [first_rows, last_rows]
    far_rows = [lax.ppermute(rows, "dp", beside) for rows in partner_rows]
    picks = (half, half ^ 1)
    blocks = pack_rows(codes, codes, partner_rows, far_rows, half, row_cap, row_count, picks)
    other_half = hand_on(blocks)
    late_places = plan[:, token_cap + row_cap :].reshape(1, -1)
    fetched, means, share, got_places, late_places = lax.optimization_barrier(
        (fetched, means, share, got_places, late_places)
    )

    passage_embed, spread = encode(
        peer_count,
        token_slot,
        fetched,
        lengths,
        pos_table,
        emb_gain,
        emb_bias,
        w_qkv,
        w_out,
        out_bias,
        norm_gain,
        norm_bias,
    )
    all_embeds = lax.all_to_all(
        spread, "dp", split_axis=0, concat_axis=0, tiled=True
    )
    pieces = own_half[2:] + other_half
    new_centroids = late_update(got_places, late_places, all_embeds, share, means, pieces)
    return (passage_embed, new_centroids)


def solution(mesh):
    return jax.shard_map(
        shards,
        mesh=mesh,
        in_specs=(
            P(("groups", "dp"), None),
            P(("groups", "dp")),
            P("dp", None),
            P(),
            P(),
            P(),
            P(),
            P(),
            P(),
            P(),
            P(),
            P(("groups", "dp"), None),
            P(("groups", "dp"), None),
            P(("groups", "dp")),
            P(("groups", "dp"), None),
        ),
        out_specs=(P(("groups", "dp"), None), P(("groups", "dp"), None)),
        check_vma=False,
    )
```

```python
import functools

import jax
import jax.numpy as jnp
from jax import lax
from jax.experimental import pallas as pl
from jax.experimental.pallas import tpu as pltpu
from jax.sharding import PartitionSpec as P

HEADS = 8
HD = 64


def normed(values, gain, shift):
    center = values - jnp.mean(values, axis=-1, keepdims=True)
    spread = jnp.mean(center * center, axis=-1, keepdims=True)
    return center * lax.rsqrt(spread + 1e-12) * gain + shift


def head_sums(weights, seq):
    rows, columns = weights.shape
    lane = lax.broadcasted_iota(jnp.int32, (rows, 2 * seq), 1)
    sums = []
    for start in range(0, columns, 2 * seq):
        pair = weights[:, start : start + 2 * seq]
        first = jnp.sum(jnp.where(lane < seq, pair, 0.0), axis=1, keepdims=True)
        second = jnp.sum(jnp.where(lane < seq, 0.0, pair), axis=1, keepdims=True)
        sums.append(jnp.where(lane < seq, first, second))
    return jnp.concatenate(sums, axis=1)


def encode_kernel(*refs):
    count = (len(refs) - 3) // 2
    far, (out, spread), near, arrived = refs[:count], refs[count : count + 2], refs[-count - 1 : -1], refs[-1]
    w_qkv_far, inner = far[-2], HEADS * HD
    copies = [
        pltpu.make_async_copy(source, target, arrived.at[at])
        for at, (source, target) in enumerate(zip(far, near))
        if source is not w_qkv_far
    ]
    lengths, slots, fetched, pos, emb_gain, emb_bias, out_bias, norm_gain, norm_bias, w_qkv, w_out = near
    out_copy = copies.pop()
    thirds = []
    for third in range(3):
        columns = pl.ds(third * inner, inner)
        thirds.append(
            pltpu.make_async_copy(
                w_qkv_far.at[:, columns], w_qkv.at[:, columns], arrived.at[count + third]
            )
        )
    for copy in copies + thirds + [out_copy]:
        copy.start()
    for copy in copies:
        copy.wait()
    passes = out.shape[0]
    size = [lengths[:, p : p + 1] for p in range(passes)]
    tokens, slot_count = slots.shape[0], fetched.shape[0]
    seq = tokens // passes
    spot = lax.broadcasted_iota(jnp.int32, (tokens, slot_count), 1)
    picker = jnp.where(slots[...] == spot, 1.0, 0.0).astype(jnp.bfloat16)
    tok = jnp.dot(picker, fetched[...], preferred_element_type=jnp.float32)
    where_at = pos[...].astype(jnp.float32)
    summed = tok + jnp.concatenate([where_at] * passes, axis=0)
    embedded = normed(summed, emb_gain[...], emb_bias[...]).astype(jnp.bfloat16)
    parts = []
    for third in range(3):
        thirds[third].wait()
        weights = w_qkv[:, third * inner : (third + 1) * inner]
        part = jnp.dot(embedded, weights, preferred_element_type=jnp.float32)
        parts.append(part.astype(jnp.bfloat16))

    block_row = lax.broadcasted_iota(jnp.int32, (HEADS * seq, inner), 0) // seq
    block_col = lax.broadcasted_iota(jnp.int32, (HEADS * seq, inner), 1) // HD
    same = block_row == block_col
    lane = lax.broadcasted_iota(jnp.int32, (seq, HEADS * seq), 1) % seq
    contexts = []
    for p in range(passes):
        query, keys, vals = (part[p * seq : (p + 1) * seq] for part in parts)
        zero = jnp.zeros((), jnp.bfloat16)
        keys = jnp.where(same, jnp.concatenate([keys] * HEADS, axis=0), zero)
        vals = jnp.where(same, jnp.concatenate([vals] * HEADS, axis=0), zero)
        scores = lax.dot_general(
            query, keys, (((1,), (1,)), ((), ())), preferred_element_type=jnp.float32
        ) * HD ** (-0.5)
        weights = jnp.where(lane < size[p], jnp.exp(scores), 0.0)
        probs = (weights / head_sums(weights, seq)).astype(jnp.bfloat16)
        contexts.append(jnp.dot(probs, vals, preferred_element_type=jnp.float32))
    context = jnp.concatenate(contexts, axis=0).astype(jnp.bfloat16)
    out_copy.wait()
    attended = jnp.dot(context, w_out[...], preferred_element_type=jnp.float32) + out_bias[...]
    hidden = normed(embedded.astype(jnp.float32) + attended, norm_gain[...], norm_bias[...])
    row = lax.broadcasted_iota(jnp.int32, (seq, 1), 0)
    for p in range(passes):
        kept = jnp.where(row < size[p], hidden[p * seq : (p + 1) * seq], 0.0)
        pooled = jnp.sum(kept, axis=0, keepdims=True) / size[p].astype(jnp.float32)
        scale = lax.rsqrt(jnp.mean(pooled * pooled, axis=-1, keepdims=True) + 1e-06)
        out[p : p + 1, :] = (pooled * scale).astype(jnp.bfloat16)
    spread[...] = jnp.broadcast_to(out[...][None], spread.shape)


def encode(
    peers, slots, fetched, lengths, pos_table, emb_gain, emb_bias, w_qkv, w_out, out_bias, norm_gain, norm_bias
):
    width = fetched.shape[1]
    tokens = slots.shape[0]
    passes = lengths.shape[0]
    macs = tokens * width * (fetched.shape[0] + 4 * HEADS * HD)
    operands = (
        lengths[None],
        slots,
        fetched,
        pos_table,
        emb_gain[None],
        emb_bias[None],
        out_bias[None],
        norm_gain[None],
        norm_bias[None],
        w_qkv,
        w_out,
    )
    return pl.pallas_call(
        encode_kernel,
        out_shape=[
            jax.ShapeDtypeStruct((passes, width), jnp.bfloat16),
            jax.ShapeDtypeStruct((peers, passes, width), jnp.bfloat16),
        ],
        in_specs=[pl.BlockSpec(memory_space=pltpu.HBM)] * len(operands),
        out_specs=[pl.BlockSpec(memory_space=pltpu.VMEM)] * 2,
        scratch_shapes=[pltpu.VMEM(operand.shape, operand.dtype) for operand in operands]
        + [pltpu.SemaphoreType.DMA((len(operands) + 3,))],
        compiler_params=pltpu.CompilerParams(vmem_limit_bytes=60 * 1024 * 1024),
        cost_estimate=pl.CostEstimate(
            flops=2 * macs, bytes_accessed=6 * 1024 * 1024, transcendentals=0
        ),
        name="encode",
    )(*operands)


def padded(rows):
    return -(-rows // 16) * 16


def rank_bits(count):
    return max(1, (count - 1).bit_length())


def ranks(kind):
    count = kind.shape[1]
    at = lax.broadcasted_iota(jnp.int32, (count, count), 0)
    by = lax.broadcasted_iota(jnp.int32, (count, count), 1)
    across = jnp.broadcast_to(kind, (count, count))
    down = jnp.sum(jnp.where(at == by, across, 0), axis=1, keepdims=True)
    same = down == across
    rank_row = jnp.sum(jnp.where(same & (at < by), 1, 0), axis=0, keepdims=True)
    rank_col = jnp.sum(jnp.where(same & (by < at), 1, 0), axis=1, keepdims=True)
    return down, rank_row, rank_col


def route_kernel(
    sizes,
    token_ids_far,
    owners_far,
    row_slot_far,
    sibling_far,
    plan,
    token_slot_far,
    code,
    sibling_code,
    *near,
):
    peers, vocab_rows, token_cap, row_cap, pooled = sizes
    token_ids, owners, row_slot, sibling, token_slot, arrived = near
    copies = [
        pltpu.make_async_copy(source, target, arrived.at[at])
        for at, (source, target) in enumerate(
            (
                (token_ids_far, token_ids),
                (owners_far, owners),
                (row_slot_far, row_slot),
                (sibling_far, sibling),
            )
        )
    ]
    for copy in copies:
        copy.start()
    for copy in copies:
        copy.wait()
    ids = jnp.concatenate([token_ids[p : p + 1, :] for p in range(token_ids.shape[0])], axis=1)
    tokens, rows = ids.shape[1], owners.shape[1]
    count = tokens + rows
    edge = (lax.broadcasted_iota(jnp.int32, (peers, tokens), 0) + 1) * vocab_rows
    holder = jnp.sum(jnp.where(ids >= edge, 1, 0), axis=0, keepdims=True)
    values = jnp.concatenate([ids - holder * vocab_rows, row_slot[...]], axis=1)

    kind = jnp.concatenate([holder, owners[...] + peers], axis=1)
    down, rank_row, rank_col = ranks(kind)

    code[...] = owners[...] * 2 ** rank_bits(rows) + rank_row[:, tokens:]
    sibling_code[...] = sibling[...] * 2 ** rank_bits(rows) + ranks(sibling[...])[1]
    goal = jnp.concatenate([holder, owners[...]], axis=1)
    peer = lax.broadcasted_iota(jnp.int32, (peers, count), 0)
    left = jnp.where(peer == goal, values + 1, 0).astype(jnp.float32)
    columns = token_cap + row_cap + pooled
    column = lax.broadcasted_iota(jnp.int32, (count, columns), 1)
    entry = lax.broadcasted_iota(jnp.int32, (count, 1), 0)
    first = jnp.where(entry < tokens, rank_col, rank_col + token_cap)
    second = entry - (count - pooled) + token_cap + row_cap
    second = jnp.where(entry < count - pooled, -1, second)
    right = jnp.where((column == first) | (column == second), 1.0, 0.0)
    filled = jnp.dot(
        left, right, preferred_element_type=jnp.float32, precision=lax.Precision.HIGHEST
    )
    filled = filled.astype(jnp.int32) - 1
    for p in range(peers):
        plan[p, :, :rows] = code[...]
        plan[p, :, rows:] = filled[p : p + 1]
    token_slot[...] = down[:tokens] * token_cap + rank_col[:tokens]
    send = pltpu.make_async_copy(token_slot, token_slot_far, arrived.at[4])
    send.start()
    send.wait()


def route(token_ids, owners, row_slot, sibling_owners, sizes):
    peers, _, token_cap, row_cap, pooled = sizes
    passes, seq_len = token_ids.shape
    rows = owners.shape[1]
    ints = lambda *shape: jax.ShapeDtypeStruct(shape, jnp.int32)
    return pl.pallas_call(
        functools.partial(route_kernel, sizes),
        out_shape=[
            ints(peers, 1, rows + token_cap + row_cap + pooled),
            ints(passes * seq_len, 1),
            ints(1, rows),
            ints(1, rows),
        ],
        in_specs=[pl.BlockSpec(memory_space=pltpu.HBM)] * 4,
        out_specs=[
            pl.BlockSpec(memory_space=pltpu.VMEM),
            pl.BlockSpec(memory_space=pltpu.HBM),
            pl.BlockSpec(memory_space=pltpu.VMEM),
            pl.BlockSpec(memory_space=pltpu.VMEM),
        ],
        scratch_shapes=[
            pltpu.VMEM(token_ids.shape, jnp.int32),
            pltpu.VMEM(owners.shape, jnp.int32),
            pltpu.VMEM(row_slot.shape, jnp.int32),
            pltpu.VMEM(owners.shape, jnp.int32),
            pltpu.VMEM((passes * seq_len, 1), jnp.int32),
            pltpu.SemaphoreType.DMA((5,)),
        ],
        compiler_params=pltpu.CompilerParams(vmem_limit_bytes=60 * 1024 * 1024),
        name="route",
    )(token_ids, owners, row_slot, sibling_owners)


def pack_kernel(half, row_cap, count, picks, pieces, rest, *refs):
    me = lax.axis_index("dp")
    operands = 2 + 2 * pieces
    far, refs = refs[:operands], refs[operands:]
    steps = half // 2
    outs, refs = refs[: steps + bool(rest)], refs[steps + bool(rest) :]
    near, (blocks, tail, arrived, left) = refs[:operands], refs[operands:]
    size = blocks.shape[0] // steps
    copies = [
        pltpu.make_async_copy(far[at], near[at], arrived.at[at]) for at in range(operands)
    ]
    for copy in copies:
        copy.start()
    for copy in copies[:2]:
        copy.wait()
    if size > 2 * row_cap:
        blocks[...] = jnp.zeros(blocks.shape, blocks.dtype)
    for source in range(2):
        if picks is None:
            code = near[source][...]
        else:
            code = near[source][me ^ picks[source], :, :count]
        bits = rank_bits(count)
        owner, rank = code >> bits, code & (2**bits - 1)
        fits = ((owner ^ me) & (1 | half)) == 0
        chip = ((owner ^ me) & (half - 1)) >> 1
        slot = jnp.where(fits, chip * row_cap + rank, -1)
        packed, at = 0.0, 0
        for piece in range(2 + source * pieces, 2 + (source + 1) * pieces):
            rows = near[piece]
            spot = lax.broadcasted_iota(jnp.int32, (steps * row_cap, rows.shape[0]), 0)
            table = jnp.where(slot[:, at : at + rows.shape[0]] == spot, 1.0, 0.0)
            copies[piece].wait()
            packed += jnp.dot(
                table.astype(jnp.bfloat16), rows[...], preferred_element_type=jnp.float32
            )
            at += rows.shape[0]
        packed = packed.astype(jnp.bfloat16)
        for step in range(steps):
            first = step * size + source * row_cap
            blocks[first : first + row_cap, :] = packed[step * row_cap : (step + 1) * row_cap]
    sends = [
        pltpu.make_async_copy(
            blocks.at[pl.ds(step * size, size)], outs[step], left.at[step]
        )
        for step in range(steps)
    ]
    if rest:
        tail[...] = near[2][near[2].shape[0] - rest :, :]
        sends.append(pltpu.make_async_copy(tail, outs[steps], left.at[steps]))
    for send in sends:
        send.start()
    for send in sends:
        send.wait()


def pack_rows(codes_a, codes_b, rows_a, rows_b, half, row_cap, count, picks=None, rest=0):
    width = rows_a[0].shape[1]
    total = sum(piece.shape[0] for piece in rows_a)
    steps = half // 2
    size = padded(2 * row_cap)
    operands = (codes_a, codes_b, *rows_a, *rows_b)
    shapes = [(size, width)] * steps + [(rest, width)] * bool(rest)
    return pl.pallas_call(
        functools.partial(pack_kernel, half, row_cap, count, picks, len(rows_a), rest),
        out_shape=[jax.ShapeDtypeStruct(shape, jnp.bfloat16) for shape in shapes],
        in_specs=[pl.BlockSpec(memory_space=pltpu.HBM)] * len(operands),
        out_specs=[pl.BlockSpec(memory_space=pltpu.HBM)] * len(shapes),
        scratch_shapes=[
            *(pltpu.VMEM(operand.shape, operand.dtype) for operand in operands),
            pltpu.VMEM((steps * size, width), jnp.bfloat16),
            pltpu.VMEM((max(rest, 16), width), jnp.bfloat16),
            pltpu.SemaphoreType.DMA((len(operands),)),
            pltpu.SemaphoreType.DMA((len(shapes),)),
        ],
        compiler_params=pltpu.CompilerParams(vmem_limit_bytes=60 * 1024 * 1024),
        cost_estimate=pl.CostEstimate(
            flops=4 * steps * row_cap * width * total,
            bytes_accessed=4 * width * (total + steps * row_cap),
            transcendentals=0,
        ),
        name="pack",
    )(*operands)


def onehot(where_to, first, count):
    centre = lax.broadcasted_iota(jnp.int32, (count, where_to.shape[1]), 0) + first
    return jnp.where(centre == where_to, 1.0, 0.0)


BLOCK = 128


def early_kernel(places_far, centroids_far, *rest):
    pieces, (out_far, share_far, places, rows, centroids, out, share, arrived, left) = rest[:-9], rest[-9:]
    size = pieces[0].shape[0]
    steps = centroids.shape[0] // BLOCK
    copies = [pltpu.make_async_copy(places_far, places, arrived.at[0])]
    for at, piece in enumerate(pieces):
        copies.append(
            pltpu.make_async_copy(piece, rows.at[pl.ds(at * size, size)], arrived.at[1 + at])
        )
    loads = []
    for step in range(steps):
        block = pl.ds(step * BLOCK, BLOCK)
        loads.append(
            pltpu.make_async_copy(
                centroids_far.at[block], centroids.at[block], arrived.at[1 + len(pieces) + step]
            )
        )
    for copy in copies + loads:
        copy.start()
    for copy in copies:
        copy.wait()
    sends = []
    for step in range(steps):
        block = pl.ds(step * BLOCK, BLOCK)
        hot = onehot(places[...], step * BLOCK, BLOCK)
        counts = jnp.sum(hot, axis=1, keepdims=True)
        scale = jnp.where(counts > 0, 1.0 / jnp.maximum(counts, 1.0), 0.0)
        sums = jnp.dot(
            hot[:, : rows.shape[0]].astype(jnp.bfloat16),
            rows[...],
            preferred_element_type=jnp.float32,
        )
        loads[step].wait()
        out[block, :] = jnp.where(counts > 0, sums * scale, centroids[block, :])
        share[block, :] = jnp.broadcast_to(scale, (BLOCK, share.shape[1]))
        sends.append(pltpu.make_async_copy(out.at[block], out_far.at[block], left.at[step]))
        sends[-1].start()
    sends.append(pltpu.make_async_copy(share, share_far, left.at[steps]))
    sends[-1].start()
    for send in sends:
        send.wait()


def late_kernel(places_far, late_far, spread_far, share_far, early_far, *rest):
    pieces, rest = rest[:-10], rest[-10:]
    out_far, places, late, spread, share, rows, early, out, arrived, left = rest
    size, passes = pieces[0].shape[0], spread.shape[1]
    steps = early.shape[0] // BLOCK
    loads = [
        pltpu.make_async_copy(source, target, arrived.at[at])
        for at, (source, target) in enumerate(
            ((places_far, places), (late_far, late), (spread_far, spread), (share_far, share))
        )
    ]
    for at, piece in enumerate(pieces):
        loads.append(
            pltpu.make_async_copy(piece, rows.at[pl.ds(at * size, size)], arrived.at[4 + at])
        )
    starts = []
    for step in range(steps):
        block = pl.ds(step * BLOCK, BLOCK)
        starts.append(
            pltpu.make_async_copy(
                early_far.at[block], early.at[block], arrived.at[len(loads) + step]
            )
        )
    for copy in loads + starts:
        copy.start()
    for copy in loads:
        copy.wait()
    top = len(pieces) * size
    for peer in range(spread.shape[0]):
        rows[top + peer * passes : top + (peer + 1) * passes, :] = spread[peer]
    where_to = jnp.concatenate([places[:, places.shape[1] - top :], late[...]], axis=1)
    sends = []
    for step in range(steps):
        block = pl.ds(step * BLOCK, BLOCK)
        hot = onehot(where_to, step * BLOCK, BLOCK).astype(jnp.bfloat16)
        sums = jnp.dot(hot, rows[...], preferred_element_type=jnp.float32)
        starts[step].wait()
        out[block, :] = early[block, :] + sums * share[block, :1]
        sends.append(pltpu.make_async_copy(out.at[block], out_far.at[block], left.at[step]))
        sends[-1].start()
    for send in sends:
        send.wait()


def early_update(places, centroids, pieces):
    centre_count, width = centroids.shape
    row_total = sum(piece.shape[0] for piece in pieces)
    wide = pltpu.VMEM(centroids.shape, jnp.float32)
    thin = (centre_count, 128)
    steps = centre_count // BLOCK
    return pl.pallas_call(
        early_kernel,
        out_shape=[
            jax.ShapeDtypeStruct(centroids.shape, jnp.float32),
            jax.ShapeDtypeStruct(thin, jnp.float32),
        ],
        in_specs=[pl.BlockSpec(memory_space=pl.ANY)] * (2 + len(pieces)),
        out_specs=[pl.BlockSpec(memory_space=pltpu.HBM)] * 2,
        scratch_shapes=[
            pltpu.VMEM(places.shape, jnp.int32),
            pltpu.VMEM((row_total, width), jnp.bfloat16),
            wide,
            wide,
            pltpu.VMEM(thin, jnp.float32),
            pltpu.SemaphoreType.DMA((1 + len(pieces) + steps,)),
            pltpu.SemaphoreType.DMA((steps + 1,)),
        ],
        compiler_params=pltpu.CompilerParams(vmem_limit_bytes=60 * 1024 * 1024),
        cost_estimate=pl.CostEstimate(
            flops=100 * centre_count * width * row_total,
            bytes_accessed=200 * centre_count * width,
            transcendentals=0,
        ),
        name="early",
    )(places, centroids, *pieces)


def late_update(places, late, spread, share, early, pieces):
    centre_count, width = early.shape
    row_total = sum(piece.shape[0] for piece in pieces) + late.shape[1]
    wide = pltpu.VMEM(early.shape, jnp.float32)
    steps = centre_count // BLOCK
    return pl.pallas_call(
        late_kernel,
        out_shape=jax.ShapeDtypeStruct(early.shape, jnp.float32),
        in_specs=[pl.BlockSpec(memory_space=pltpu.HBM)] * (5 + len(pieces)),
        out_specs=pl.BlockSpec(memory_space=pltpu.HBM),
        scratch_shapes=[
            pltpu.VMEM(places.shape, jnp.int32),
            pltpu.VMEM(late.shape, jnp.int32),
            pltpu.VMEM(spread.shape, jnp.bfloat16),
            pltpu.VMEM(share.shape, jnp.float32),
            pltpu.VMEM((row_total, width), jnp.bfloat16),
            wide,
            wide,
            pltpu.SemaphoreType.DMA((4 + len(pieces) + steps,)),
            pltpu.SemaphoreType.DMA((steps,)),
        ],
        compiler_params=pltpu.CompilerParams(vmem_limit_bytes=60 * 1024 * 1024),
        cost_estimate=pl.CostEstimate(
            flops=2 * centre_count * width * row_total,
            bytes_accessed=8 * centre_count * width,
            transcendentals=0,
        ),
        name="late",
    )(places, late, spread, share, early, *pieces)


def shards(
    token_ids,
    lengths,
    word_table,
    pos_table,
    emb_gain,
    emb_bias,
    w_qkv,
    w_out,
    out_bias,
    norm_gain,
    norm_bias,
    stored_rows,
    row_owner,
    row_slot,
    centroids,
):
    peer_count = lax.axis_size("dp")
    half = peer_count // 2
    width = word_table.shape[1]
    vocab_rows = word_table.shape[0]
    passes, seq_len = token_ids.shape
    token_count = passes * seq_len
    row_count = row_slot.shape[0]
    store_count = stored_rows.shape[0]
    token_cap = max(2, 3 * token_count // peer_count)
    row_cap = max(2, 3 * row_count // peer_count)

    across = [(i, i ^ half) for i in range(peer_count)]
    beside = [(i, i ^ 1) for i in range(peer_count)]

    def hand_on(blocks):
        got = [blocks[0]]
        for step in range(1, len(blocks)):
            moves = [(i, i ^ (2 * step)) for i in range(peer_count)]
            got.append(lax.ppermute(blocks[step], "dp", moves))
        return got

    ahead = store_count * 3 // 4 // 16 * 16
    sibling_rows = lax.ppermute(stored_rows, "dp", beside)
    first_rows = lax.ppermute(stored_rows[:ahead], "dp", across)
    sizes = (peer_count, vocab_rows, token_cap, row_cap, row_count - store_count)
    owners = row_owner.reshape(1, row_count)
    sibling_owners = lax.ppermute(owners, "dp", beside)
    plan, token_slot, code, sibling_code = route(
        token_ids, owners, row_slot[None], sibling_owners, sizes
    )
    plan, sibling_rows = lax.optimization_barrier((plan, sibling_rows))
    codes = lax.all_to_all(plan, "dp", split_axis=0, concat_axis=0, tiled=True)
    *blocks, last_rows = pack_rows(
        code,
        sibling_code,
        [stored_rows],
        [sibling_rows],
        half,
        row_cap,
        row_count,
        rest=store_count - ahead,
    )
    codes, last_rows = lax.optimization_barrier((codes, last_rows))
    last_rows = lax.ppermute(last_rows, "dp", across)
    own_half = hand_on(blocks)
    plan = codes[:, 0, row_count:]
    wanted = plan[:, :token_cap].reshape(peer_count * token_cap)
    chosen = wanted[:, None] == jnp.arange(vocab_rows, dtype=jnp.int32)[None, :]
    found = jnp.dot(
        chosen.astype(jnp.bfloat16), word_table, preferred_element_type=jnp.float32
    ).astype(jnp.bfloat16)
    found, plan, first_rows, own_half[:2] = lax.optimization_barrier(
        (found, plan, first_rows, own_half[:2])
    )
    fetched = lax.all_to_all(
        found.reshape(peer_count, token_cap, width), "dp", split_axis=0, concat_axis=0, tiled=True
    ).reshape(peer_count * token_cap, width)

    sources = lax.axis_index("dp") ^ jnp.arange(peer_count, dtype=jnp.int32)
    got_places = plan[:, token_cap : token_cap + row_cap][sources].reshape(half, 2 * row_cap)
    spare = padded(2 * row_cap) - 2 * row_cap
    got_places = jnp.pad(got_places, ((0, 0), (0, spare)), constant_values=-1).reshape(1, -1)
    near_rows, last_rows = lax.optimization_barrier((own_half, last_rows))
    means, share = early_update(got_places, centroids, near_rows)
    first_rows, last_rows, means = lax.optimization_barrier((first_rows, last_rows, means))
    partner_rows = [first_rows, last_rows]
    far_rows = [lax.ppermute(rows, "dp", beside) for rows in partner_rows]
    picks = (half, half ^ 1)
    blocks = pack_rows(codes, codes, partner_rows, far_rows, half, row_cap, row_count, picks)
    other_half = hand_on(blocks)
    late_places = plan[:, token_cap + row_cap :].reshape(1, -1)
    fetched, means, share, got_places, late_places = lax.optimization_barrier(
        (fetched, means, share, got_places, late_places)
    )

    passage_embed, spread = encode(
        peer_count,
        token_slot,
        fetched,
        lengths,
        pos_table,
        emb_gain,
        emb_bias,
        w_qkv,
        w_out,
        out_bias,
        norm_gain,
        norm_bias,
    )
    all_embeds = lax.all_to_all(
        spread, "dp", split_axis=0, concat_axis=0, tiled=True
    )
    new_centroids = late_update(got_places, late_places, all_embeds, share, means, other_half)
    return (passage_embed, new_centroids)


def solution(mesh):
    return jax.shard_map(
        shards,
        mesh=mesh,
        in_specs=(
            P(("groups", "dp"), None),
            P(("groups", "dp")),
            P("dp", None),
            P(),
            P(),
            P(),
            P(),
            P(),
            P(),
            P(),
            P(),
            P(("groups", "dp"), None),
            P(("groups", "dp"), None),
            P(("groups", "dp")),
            P(("groups", "dp"), None),
        ),
        out_specs=(P(("groups", "dp"), None), P(("groups", "dp"), None)),
        check_vma=False,
    )
```

```python
import functools

import jax
import jax.numpy as jnp
from jax import lax
from jax.experimental import pallas as pl
from jax.experimental.pallas import tpu as pltpu
from jax.sharding import PartitionSpec as P

HEADS = 8
HD = 64


def normed(values, gain, shift):
    center = values - jnp.mean(values, axis=-1, keepdims=True)
    spread = jnp.mean(center * center, axis=-1, keepdims=True)
    return center * lax.rsqrt(spread + 1e-12) * gain + shift


def head_sums(weights, seq):
    rows, columns = weights.shape
    lane = lax.broadcasted_iota(jnp.int32, (rows, 2 * seq), 1)
    sums = []
    for start in range(0, columns, 2 * seq):
        pair = weights[:, start : start + 2 * seq]
        first = jnp.sum(jnp.where(lane < seq, pair, 0.0), axis=1, keepdims=True)
        second = jnp.sum(jnp.where(lane < seq, 0.0, pair), axis=1, keepdims=True)
        sums.append(jnp.where(lane < seq, first, second))
    return jnp.concatenate(sums, axis=1)


def encode_kernel(*refs):
    count = (len(refs) - 3) // 2
    far, (out, spread), near, arrived = refs[:count], refs[count : count + 2], refs[-count - 1 : -1], refs[-1]
    w_qkv_far, inner = far[-2], HEADS * HD
    copies = [
        pltpu.make_async_copy(source, target, arrived.at[at])
        for at, (source, target) in enumerate(zip(far, near))
        if source is not w_qkv_far
    ]
    lengths, slots, fetched, pos, emb_gain, emb_bias, out_bias, norm_gain, norm_bias, w_qkv, w_out = near
    out_copy = copies.pop()
    thirds = []
    for third in range(3):
        columns = pl.ds(third * inner, inner)
        thirds.append(
            pltpu.make_async_copy(
                w_qkv_far.at[:, columns], w_qkv.at[:, columns], arrived.at[count + third]
            )
        )
    for copy in copies + thirds + [out_copy]:
        copy.start()
    for copy in copies:
        copy.wait()
    passes = out.shape[0]
    size = [lengths[:, p : p + 1] for p in range(passes)]
    tokens, slot_count = slots.shape[0], fetched.shape[0]
    seq = tokens // passes
    spot = lax.broadcasted_iota(jnp.int32, (tokens, slot_count), 1)
    picker = jnp.where(slots[...] == spot, 1.0, 0.0).astype(jnp.bfloat16)
    tok = jnp.dot(picker, fetched[...], preferred_element_type=jnp.float32)
    where_at = pos[...].astype(jnp.float32)
    summed = tok + jnp.concatenate([where_at] * passes, axis=0)
    embedded = normed(summed, emb_gain[...], emb_bias[...]).astype(jnp.bfloat16)
    parts = []
    for third in range(3):
        thirds[third].wait()
        weights = w_qkv[:, third * inner : (third + 1) * inner]
        part = jnp.dot(embedded, weights, preferred_element_type=jnp.float32)
        parts.append(part.astype(jnp.bfloat16))

    block_row = lax.broadcasted_iota(jnp.int32, (HEADS * seq, inner), 0) // seq
    block_col = lax.broadcasted_iota(jnp.int32, (HEADS * seq, inner), 1) // HD
    same = block_row == block_col
    lane = lax.broadcasted_iota(jnp.int32, (seq, HEADS * seq), 1) % seq
    contexts = []
    for p in range(passes):
        query, keys, vals = (part[p * seq : (p + 1) * seq] for part in parts)
        zero = jnp.zeros((), jnp.bfloat16)
        keys = jnp.where(same, jnp.concatenate([keys] * HEADS, axis=0), zero)
        vals = jnp.where(same, jnp.concatenate([vals] * HEADS, axis=0), zero)
        scores = lax.dot_general(
            query, keys, (((1,), (1,)), ((), ())), preferred_element_type=jnp.float32
        ) * HD ** (-0.5)
        weights = jnp.where(lane < size[p], jnp.exp(scores), 0.0)
        probs = (weights / head_sums(weights, seq)).astype(jnp.bfloat16)
        contexts.append(jnp.dot(probs, vals, preferred_element_type=jnp.float32))
    context = jnp.concatenate(contexts, axis=0).astype(jnp.bfloat16)
    out_copy.wait()
    attended = jnp.dot(context, w_out[...], preferred_element_type=jnp.float32) + out_bias[...]
    hidden = normed(embedded.astype(jnp.float32) + attended, norm_gain[...], norm_bias[...])
    row = lax.broadcasted_iota(jnp.int32, (seq, 1), 0)
    for p in range(passes):
        kept = jnp.where(row < size[p], hidden[p * seq : (p + 1) * seq], 0.0)
        pooled = jnp.sum(kept, axis=0, keepdims=True) / size[p].astype(jnp.float32)
        scale = lax.rsqrt(jnp.mean(pooled * pooled, axis=-1, keepdims=True) + 1e-06)
        out[p : p + 1, :] = (pooled * scale).astype(jnp.bfloat16)
    spread[...] = jnp.broadcast_to(out[...][None], spread.shape)


def encode(
    peers, slots, fetched, lengths, pos_table, emb_gain, emb_bias, w_qkv, w_out, out_bias, norm_gain, norm_bias
):
    width = fetched.shape[1]
    tokens = slots.shape[0]
    passes = lengths.shape[0]
    macs = tokens * width * (fetched.shape[0] + 4 * HEADS * HD)
    operands = (
        lengths[None],
        slots,
        fetched,
        pos_table,
        emb_gain[None],
        emb_bias[None],
        out_bias[None],
        norm_gain[None],
        norm_bias[None],
        w_qkv,
        w_out,
    )
    return pl.pallas_call(
        encode_kernel,
        out_shape=[
            jax.ShapeDtypeStruct((passes, width), jnp.bfloat16),
            jax.ShapeDtypeStruct((peers, passes, width), jnp.bfloat16),
        ],
        in_specs=[pl.BlockSpec(memory_space=pltpu.HBM)] * len(operands),
        out_specs=[pl.BlockSpec(memory_space=pltpu.VMEM)] * 2,
        scratch_shapes=[pltpu.VMEM(operand.shape, operand.dtype) for operand in operands]
        + [pltpu.SemaphoreType.DMA((len(operands) + 3,))],
        compiler_params=pltpu.CompilerParams(vmem_limit_bytes=60 * 1024 * 1024),
        cost_estimate=pl.CostEstimate(
            flops=2 * macs, bytes_accessed=6 * 1024 * 1024, transcendentals=0
        ),
        name="encode",
    )(*operands)


def padded(rows):
    return -(-rows // 16) * 16


def rank_bits(count):
    return max(1, (count - 1).bit_length())


def ranks(kind):
    count = kind.shape[1]
    at = lax.broadcasted_iota(jnp.int32, (count, count), 0)
    by = lax.broadcasted_iota(jnp.int32, (count, count), 1)
    across = jnp.broadcast_to(kind, (count, count))
    down = jnp.sum(jnp.where(at == by, across, 0), axis=1, keepdims=True)
    same = down == across
    rank_row = jnp.sum(jnp.where(same & (at < by), 1, 0), axis=0, keepdims=True)
    rank_col = jnp.sum(jnp.where(same & (by < at), 1, 0), axis=1, keepdims=True)
    return down, rank_row, rank_col


def route_kernel(
    sizes,
    token_ids_far,
    owners_far,
    row_slot_far,
    sibling_far,
    plan,
    token_slot_far,
    code,
    sibling_code,
    *near,
):
    peers, vocab_rows, token_cap, row_cap, pooled = sizes
    token_ids, owners, row_slot, sibling, token_slot, arrived = near
    copies = [
        pltpu.make_async_copy(source, target, arrived.at[at])
        for at, (source, target) in enumerate(
            (
                (token_ids_far, token_ids),
                (owners_far, owners),
                (row_slot_far, row_slot),
                (sibling_far, sibling),
            )
        )
    ]
    for copy in copies:
        copy.start()
    for copy in copies:
        copy.wait()
    ids = jnp.concatenate([token_ids[p : p + 1, :] for p in range(token_ids.shape[0])], axis=1)
    tokens, rows = ids.shape[1], owners.shape[1]
    count = tokens + rows
    edge = (lax.broadcasted_iota(jnp.int32, (peers, tokens), 0) + 1) * vocab_rows
    holder = jnp.sum(jnp.where(ids >= edge, 1, 0), axis=0, keepdims=True)
    values = jnp.concatenate([ids - holder * vocab_rows, row_slot[...]], axis=1)

    kind = jnp.concatenate([holder, owners[...] + peers], axis=1)
    down, rank_row, rank_col = ranks(kind)

    code[...] = owners[...] * 2 ** rank_bits(rows) + rank_row[:, tokens:]
    sibling_code[...] = sibling[...] * 2 ** rank_bits(rows) + ranks(sibling[...])[1]
    goal = jnp.concatenate([holder, owners[...]], axis=1)
    peer = lax.broadcasted_iota(jnp.int32, (peers, count), 0)
    left = jnp.where(peer == goal, values + 1, 0).astype(jnp.float32)
    columns = token_cap + row_cap + pooled
    column = lax.broadcasted_iota(jnp.int32, (count, columns), 1)
    entry = lax.broadcasted_iota(jnp.int32, (count, 1), 0)
    first = jnp.where(entry < tokens, rank_col, rank_col + token_cap)
    second = entry - (count - pooled) + token_cap + row_cap
    second = jnp.where(entry < count - pooled, -1, second)
    right = jnp.where((column == first) | (column == second), 1.0, 0.0)
    filled = jnp.dot(
        left, right, preferred_element_type=jnp.float32, precision=lax.Precision.HIGHEST
    )
    filled = filled.astype(jnp.int32) - 1
    for p in range(peers):
        plan[p, :, :rows] = code[...]
        plan[p, :, rows:] = filled[p : p + 1]
    token_slot[...] = down[:tokens] * token_cap + rank_col[:tokens]
    send = pltpu.make_async_copy(token_slot, token_slot_far, arrived.at[4])
    send.start()
    send.wait()


def route(token_ids, owners, row_slot, sibling_owners, sizes):
    peers, _, token_cap, row_cap, pooled = sizes
    passes, seq_len = token_ids.shape
    rows = owners.shape[1]
    ints = lambda *shape: jax.ShapeDtypeStruct(shape, jnp.int32)
    return pl.pallas_call(
        functools.partial(route_kernel, sizes),
        out_shape=[
            ints(peers, 1, rows + token_cap + row_cap + pooled),
            ints(passes * seq_len, 1),
            ints(1, rows),
            ints(1, rows),
        ],
        in_specs=[pl.BlockSpec(memory_space=pltpu.HBM)] * 4,
        out_specs=[
            pl.BlockSpec(memory_space=pltpu.VMEM),
            pl.BlockSpec(memory_space=pltpu.HBM),
            pl.BlockSpec(memory_space=pltpu.VMEM),
            pl.BlockSpec(memory_space=pltpu.VMEM),
        ],
        scratch_shapes=[
            pltpu.VMEM(token_ids.shape, jnp.int32),
            pltpu.VMEM(owners.shape, jnp.int32),
            pltpu.VMEM(row_slot.shape, jnp.int32),
            pltpu.VMEM(owners.shape, jnp.int32),
            pltpu.VMEM((passes * seq_len, 1), jnp.int32),
            pltpu.SemaphoreType.DMA((5,)),
        ],
        compiler_params=pltpu.CompilerParams(vmem_limit_bytes=60 * 1024 * 1024),
        name="route",
    )(token_ids, owners, row_slot, sibling_owners)


def pack_kernel(half, row_cap, count, picks, pieces, rest, *refs):
    me = lax.axis_index("dp")
    operands = 2 + 2 * pieces
    far, refs = refs[:operands], refs[operands:]
    steps = half // 2
    outs, refs = refs[: steps + bool(rest)], refs[steps + bool(rest) :]
    near, (blocks, tail, arrived, left) = refs[:operands], refs[operands:]
    size = blocks.shape[0] // steps
    copies = [
        pltpu.make_async_copy(far[at], near[at], arrived.at[at]) for at in range(operands)
    ]
    for copy in copies:
        copy.start()
    for copy in copies[:2]:
        copy.wait()
    if size > 2 * row_cap:
        blocks[...] = jnp.zeros(blocks.shape, blocks.dtype)
    for source in range(2):
        if picks is None:
            code = near[source][...]
        else:
            code = near[source][me ^ picks[source], :, :count]
        bits = rank_bits(count)
        owner, rank = code >> bits, code & (2**bits - 1)
        fits = ((owner ^ me) & (1 | half)) == 0
        chip = ((owner ^ me) & (half - 1)) >> 1
        slot = jnp.where(fits, chip * row_cap + rank, -1)
        packed, at = 0.0, 0
        for piece in range(2 + source * pieces, 2 + (source + 1) * pieces):
            rows = near[piece]
            spot = lax.broadcasted_iota(jnp.int32, (steps * row_cap, rows.shape[0]), 0)
            table = jnp.where(slot[:, at : at + rows.shape[0]] == spot, 1.0, 0.0)
            copies[piece].wait()
            packed += jnp.dot(
                table.astype(jnp.bfloat16), rows[...], preferred_element_type=jnp.float32
            )
            at += rows.shape[0]
        packed = packed.astype(jnp.bfloat16)
        for step in range(steps):
            first = step * size + source * row_cap
            blocks[first : first + row_cap, :] = packed[step * row_cap : (step + 1) * row_cap]
    sends = [
        pltpu.make_async_copy(
            blocks.at[pl.ds(step * size, size)], outs[step], left.at[step]
        )
        for step in range(steps)
    ]
    if rest:
        tail[...] = near[2][near[2].shape[0] - rest :, :]
        sends.append(pltpu.make_async_copy(tail, outs[steps], left.at[steps]))
    for send in sends:
        send.start()
    for send in sends:
        send.wait()


def pack_rows(codes_a, codes_b, rows_a, rows_b, half, row_cap, count, picks=None, rest=0):
    width = rows_a[0].shape[1]
    total = sum(piece.shape[0] for piece in rows_a)
    steps = half // 2
    size = padded(2 * row_cap)
    operands = (codes_a, codes_b, *rows_a, *rows_b)
    shapes = [(size, width)] * steps + [(rest, width)] * bool(rest)
    return pl.pallas_call(
        functools.partial(pack_kernel, half, row_cap, count, picks, len(rows_a), rest),
        out_shape=[jax.ShapeDtypeStruct(shape, jnp.bfloat16) for shape in shapes],
        in_specs=[pl.BlockSpec(memory_space=pltpu.HBM)] * len(operands),
        out_specs=[pl.BlockSpec(memory_space=pltpu.HBM)] * len(shapes),
        scratch_shapes=[
            *(pltpu.VMEM(operand.shape, operand.dtype) for operand in operands),
            pltpu.VMEM((steps * size, width), jnp.bfloat16),
            pltpu.VMEM((max(rest, 16), width), jnp.bfloat16),
            pltpu.SemaphoreType.DMA((len(operands),)),
            pltpu.SemaphoreType.DMA((len(shapes),)),
        ],
        compiler_params=pltpu.CompilerParams(vmem_limit_bytes=60 * 1024 * 1024),
        cost_estimate=pl.CostEstimate(
            flops=4 * steps * row_cap * width * total,
            bytes_accessed=4 * width * (total + steps * row_cap),
            transcendentals=0,
        ),
        name="pack",
    )(*operands)


def onehot(where_to, first, count):
    centre = lax.broadcasted_iota(jnp.int32, (count, where_to.shape[1]), 0) + first
    return jnp.where(centre == where_to, 1.0, 0.0)


BLOCK = 128


def early_kernel(places_far, centroids_far, *rest):
    pieces, (out_far, share_far, places, rows, centroids, out, share, arrived, left) = rest[:-9], rest[-9:]
    size = pieces[0].shape[0]
    steps = centroids.shape[0] // BLOCK
    copies = [pltpu.make_async_copy(places_far, places, arrived.at[0])]
    for at, piece in enumerate(pieces):
        copies.append(
            pltpu.make_async_copy(piece, rows.at[pl.ds(at * size, size)], arrived.at[1 + at])
        )
    loads = []
    for step in range(steps):
        block = pl.ds(step * BLOCK, BLOCK)
        loads.append(
            pltpu.make_async_copy(
                centroids_far.at[block], centroids.at[block], arrived.at[1 + len(pieces) + step]
            )
        )
    for copy in copies + loads:
        copy.start()
    for copy in copies:
        copy.wait()
    sends = []
    for step in range(steps):
        block = pl.ds(step * BLOCK, BLOCK)
        hot = onehot(places[...], step * BLOCK, BLOCK)
        counts = jnp.sum(hot, axis=1, keepdims=True)
        scale = jnp.where(counts > 0, 1.0 / jnp.maximum(counts, 1.0), 0.0)
        sums = jnp.dot(
            hot[:, : rows.shape[0]].astype(jnp.bfloat16),
            rows[...],
            preferred_element_type=jnp.float32,
        )
        loads[step].wait()
        out[block, :] = jnp.where(counts > 0, sums * scale, centroids[block, :])
        share[block, :] = jnp.broadcast_to(scale, (BLOCK, share.shape[1]))
        sends.append(pltpu.make_async_copy(out.at[block], out_far.at[block], left.at[step]))
        sends[-1].start()
    sends.append(pltpu.make_async_copy(share, share_far, left.at[steps]))
    sends[-1].start()
    for send in sends:
        send.wait()


def late_kernel(places_far, late_far, spread_far, share_far, early_far, *rest):
    pieces, rest = rest[:-10], rest[-10:]
    out_far, places, late, spread, share, rows, early, out, arrived, left = rest
    size, passes = pieces[0].shape[0], spread.shape[1]
    steps = early.shape[0] // BLOCK
    loads = [
        pltpu.make_async_copy(source, target, arrived.at[at])
        for at, (source, target) in enumerate(
            ((places_far, places), (late_far, late), (spread_far, spread), (share_far, share))
        )
    ]
    for at, piece in enumerate(pieces):
        loads.append(
            pltpu.make_async_copy(piece, rows.at[pl.ds(at * size, size)], arrived.at[4 + at])
        )
    starts = []
    for step in range(steps):
        block = pl.ds(step * BLOCK, BLOCK)
        starts.append(
            pltpu.make_async_copy(
                early_far.at[block], early.at[block], arrived.at[len(loads) + step]
            )
        )
    for copy in loads + starts:
        copy.start()
    for copy in loads:
        copy.wait()
    top = len(pieces) * size
    for peer in range(spread.shape[0]):
        rows[top + peer * passes : top + (peer + 1) * passes, :] = spread[peer]
    where_to = jnp.concatenate([places[:, places.shape[1] - top :], late[...]], axis=1)
    sends = []
    for step in range(steps):
        block = pl.ds(step * BLOCK, BLOCK)
        hot = onehot(where_to, step * BLOCK, BLOCK).astype(jnp.bfloat16)
        sums = jnp.dot(hot, rows[...], preferred_element_type=jnp.float32)
        starts[step].wait()
        out[block, :] = early[block, :] + sums * share[block, :1]
        sends.append(pltpu.make_async_copy(out.at[block], out_far.at[block], left.at[step]))
        sends[-1].start()
    for send in sends:
        send.wait()


def early_update(places, centroids, pieces):
    centre_count, width = centroids.shape
    row_total = sum(piece.shape[0] for piece in pieces)
    wide = pltpu.VMEM(centroids.shape, jnp.float32)
    thin = (centre_count, 128)
    steps = centre_count // BLOCK
    return pl.pallas_call(
        early_kernel,
        out_shape=[
            jax.ShapeDtypeStruct(centroids.shape, jnp.float32),
            jax.ShapeDtypeStruct(thin, jnp.float32),
        ],
        in_specs=[pl.BlockSpec(memory_space=pl.ANY)] * (2 + len(pieces)),
        out_specs=[pl.BlockSpec(memory_space=pltpu.HBM)] * 2,
        scratch_shapes=[
            pltpu.VMEM(places.shape, jnp.int32),
            pltpu.VMEM((row_total, width), jnp.bfloat16),
            wide,
            wide,
            pltpu.VMEM(thin, jnp.float32),
            pltpu.SemaphoreType.DMA((1 + len(pieces) + steps,)),
            pltpu.SemaphoreType.DMA((steps + 1,)),
        ],
        compiler_params=pltpu.CompilerParams(vmem_limit_bytes=60 * 1024 * 1024),
        cost_estimate=pl.CostEstimate(
            flops=100 * centre_count * width * row_total,
            bytes_accessed=200 * centre_count * width,
            transcendentals=0,
        ),
        name="early",
    )(places, centroids, *pieces)


def late_update(places, late, spread, share, early, pieces):
    centre_count, width = early.shape
    row_total = sum(piece.shape[0] for piece in pieces) + late.shape[1]
    wide = pltpu.VMEM(early.shape, jnp.float32)
    steps = centre_count // BLOCK
    return pl.pallas_call(
        late_kernel,
        out_shape=jax.ShapeDtypeStruct(early.shape, jnp.float32),
        in_specs=[pl.BlockSpec(memory_space=pltpu.HBM)] * (5 + len(pieces)),
        out_specs=pl.BlockSpec(memory_space=pltpu.HBM),
        scratch_shapes=[
            pltpu.VMEM(places.shape, jnp.int32),
            pltpu.VMEM(late.shape, jnp.int32),
            pltpu.VMEM(spread.shape, jnp.bfloat16),
            pltpu.VMEM(share.shape, jnp.float32),
            pltpu.VMEM((row_total, width), jnp.bfloat16),
            wide,
            wide,
            pltpu.SemaphoreType.DMA((4 + len(pieces) + steps,)),
            pltpu.SemaphoreType.DMA((steps,)),
        ],
        compiler_params=pltpu.CompilerParams(vmem_limit_bytes=60 * 1024 * 1024),
        cost_estimate=pl.CostEstimate(
            flops=2 * centre_count * width * row_total,
            bytes_accessed=8 * centre_count * width,
            transcendentals=0,
        ),
        name="late",
    )(places, late, spread, share, early, *pieces)


def shards(
    token_ids,
    lengths,
    word_table,
    pos_table,
    emb_gain,
    emb_bias,
    w_qkv,
    w_out,
    out_bias,
    norm_gain,
    norm_bias,
    stored_rows,
    row_owner,
    row_slot,
    centroids,
):
    peer_count = lax.axis_size("dp")
    half = peer_count // 2
    width = word_table.shape[1]
    vocab_rows = word_table.shape[0]
    passes, seq_len = token_ids.shape
    token_count = passes * seq_len
    row_count = row_slot.shape[0]
    store_count = stored_rows.shape[0]
    token_cap = max(2, 3 * token_count // peer_count)
    row_cap = max(2, 3 * row_count // peer_count)

    across = [(i, i ^ half) for i in range(peer_count)]
    beside = [(i, i ^ 1) for i in range(peer_count)]

    def hand_on(blocks):
        got = [blocks[0]]
        for step in range(1, len(blocks)):
            moves = [(i, i ^ (2 * step)) for i in range(peer_count)]
            got.append(lax.ppermute(blocks[step], "dp", moves))
        return got

    ahead = store_count * 3 // 4 // 16 * 16
    sibling_rows = lax.ppermute(stored_rows, "dp", beside)
    first_rows = lax.ppermute(stored_rows[:ahead], "dp", across)
    sizes = (peer_count, vocab_rows, token_cap, row_cap, row_count - store_count)
    owners = row_owner.reshape(1, row_count)
    sibling_owners = lax.ppermute(owners, "dp", beside)
    plan, token_slot, code, sibling_code = route(
        token_ids, owners, row_slot[None], sibling_owners, sizes
    )
    plan, sibling_rows = lax.optimization_barrier((plan, sibling_rows))
    codes = lax.all_to_all(plan, "dp", split_axis=0, concat_axis=0, tiled=True)
    *blocks, last_rows = pack_rows(
        code,
        sibling_code,
        [stored_rows],
        [sibling_rows],
        half,
        row_cap,
        row_count,
        rest=store_count - ahead,
    )
    codes, last_rows = lax.optimization_barrier((codes, last_rows))
    last_rows = lax.ppermute(last_rows, "dp", across)
    own_half = hand_on(blocks)
    plan = codes[:, 0, row_count:]
    wanted = plan[:, :token_cap].reshape(peer_count * token_cap)
    chosen = wanted[:, None] == jnp.arange(vocab_rows, dtype=jnp.int32)[None, :]
    found = jnp.dot(
        chosen.astype(jnp.bfloat16), word_table, preferred_element_type=jnp.float32
    ).astype(jnp.bfloat16)
    found, first_rows, own_half[:2] = lax.optimization_barrier(
        (found, first_rows, own_half[:2])
    )
    plan_behind, last_rows = lax.optimization_barrier((plan, last_rows))
    fetched = lax.all_to_all(
        found.reshape(peer_count, token_cap, width), "dp", split_axis=0, concat_axis=0, tiled=True
    ).reshape(peer_count * token_cap, width)

    sources = lax.axis_index("dp") ^ jnp.arange(peer_count, dtype=jnp.int32)
    got_places = plan_behind[:, token_cap : token_cap + row_cap][sources].reshape(half, 2 * row_cap)
    spare = padded(2 * row_cap) - 2 * row_cap
    got_places = jnp.pad(got_places, ((0, 0), (0, spare)), constant_values=-1).reshape(1, -1)
    near_rows, last_rows = lax.optimization_barrier((own_half, last_rows))
    means, share = early_update(got_places, centroids, near_rows)
    first_rows, last_rows, means = lax.optimization_barrier((first_rows, last_rows, means))
    partner_rows = [first_rows, last_rows]
    far_rows = [lax.ppermute(rows, "dp", beside) for rows in partner_rows]
    picks = (half, half ^ 1)
    blocks = pack_rows(codes, codes, partner_rows, far_rows, half, row_cap, row_count, picks)
    other_half = hand_on(blocks)
    late_places = plan[:, token_cap + row_cap :].reshape(1, -1)
    fetched, means, share, got_places = lax.optimization_barrier(
        (fetched, means, share, got_places)
    )

    passage_embed, spread = encode(
        peer_count,
        token_slot,
        fetched,
        lengths,
        pos_table,
        emb_gain,
        emb_bias,
        w_qkv,
        w_out,
        out_bias,
        norm_gain,
        norm_bias,
    )
    all_embeds = lax.all_to_all(
        spread, "dp", split_axis=0, concat_axis=0, tiled=True
    )
    new_centroids = late_update(got_places, late_places, all_embeds, share, means, other_half)
    return (passage_embed, new_centroids)


def solution(mesh):
    return jax.shard_map(
        shards,
        mesh=mesh,
        in_specs=(
            P(("groups", "dp"), None),
            P(("groups", "dp")),
            P("dp", None),
            P(),
            P(),
            P(),
            P(),
            P(),
            P(),
            P(),
            P(),
            P(("groups", "dp"), None),
            P(("groups", "dp"), None),
            P(("groups", "dp")),
            P(("groups", "dp"), None),
        ),
        out_specs=(P(("groups", "dp"), None), P(("groups", "dp"), None)),
        check_vma=False,
    )
```

```python
import functools

import jax
import jax.numpy as jnp
from jax import lax
from jax.experimental import pallas as pl
from jax.experimental.pallas import tpu as pltpu
from jax.sharding import PartitionSpec as P

HEADS = 8
HD = 64


def normed(values, gain, shift):
    center = values - jnp.mean(values, axis=-1, keepdims=True)
    spread = jnp.mean(center * center, axis=-1, keepdims=True)
    return center * lax.rsqrt(spread + 1e-12) * gain + shift


def head_sums(weights, seq):
    rows, columns = weights.shape
    lane = lax.broadcasted_iota(jnp.int32, (rows, 2 * seq), 1)
    sums = []
    for start in range(0, columns, 2 * seq):
        pair = weights[:, start : start + 2 * seq]
        first = jnp.sum(jnp.where(lane < seq, pair, 0.0), axis=1, keepdims=True)
        second = jnp.sum(jnp.where(lane < seq, 0.0, pair), axis=1, keepdims=True)
        sums.append(jnp.where(lane < seq, first, second))
    return jnp.concatenate(sums, axis=1)


def encode_kernel(*refs):
    count = (len(refs) - 3) // 2
    far, (out, spread), near, arrived = refs[:count], refs[count : count + 2], refs[-count - 1 : -1], refs[-1]
    w_qkv_far, inner = far[-2], HEADS * HD
    copies = [
        pltpu.make_async_copy(source, target, arrived.at[at])
        for at, (source, target) in enumerate(zip(far, near))
        if source is not w_qkv_far
    ]
    lengths, slots, fetched, pos, emb_gain, emb_bias, out_bias, norm_gain, norm_bias, w_qkv, w_out = near
    out_copy = copies.pop()
    thirds = []
    for third in range(3):
        columns = pl.ds(third * inner, inner)
        thirds.append(
            pltpu.make_async_copy(
                w_qkv_far.at[:, columns], w_qkv.at[:, columns], arrived.at[count + third]
            )
        )
    for copy in copies + thirds + [out_copy]:
        copy.start()
    for copy in copies:
        copy.wait()
    passes = out.shape[0]
    size = [lengths[:, p : p + 1] for p in range(passes)]
    tokens, slot_count = slots.shape[0], fetched.shape[0]
    seq = tokens // passes
    spot = lax.broadcasted_iota(jnp.int32, (tokens, slot_count), 1)
    picker = jnp.where(slots[...] == spot, 1.0, 0.0).astype(jnp.bfloat16)
    tok = jnp.dot(picker, fetched[...], preferred_element_type=jnp.float32)
    where_at = pos[...].astype(jnp.float32)
    summed = tok + jnp.concatenate([where_at] * passes, axis=0)
    embedded = normed(summed, emb_gain[...], emb_bias[...]).astype(jnp.bfloat16)
    parts = []
    for third in range(3):
        thirds[third].wait()
        weights = w_qkv[:, third * inner : (third + 1) * inner]
        part = jnp.dot(embedded, weights, preferred_element_type=jnp.float32)
        parts.append(part.astype(jnp.bfloat16))

    block_row = lax.broadcasted_iota(jnp.int32, (HEADS * seq, inner), 0) // seq
    block_col = lax.broadcasted_iota(jnp.int32, (HEADS * seq, inner), 1) // HD
    same = block_row == block_col
    lane = lax.broadcasted_iota(jnp.int32, (seq, HEADS * seq), 1) % seq
    contexts = []
    for p in range(passes):
        query, keys, vals = (part[p * seq : (p + 1) * seq] for part in parts)
        zero = jnp.zeros((), jnp.bfloat16)
        keys = jnp.where(same, jnp.concatenate([keys] * HEADS, axis=0), zero)
        vals = jnp.where(same, jnp.concatenate([vals] * HEADS, axis=0), zero)
        scores = lax.dot_general(
            query, keys, (((1,), (1,)), ((), ())), preferred_element_type=jnp.float32
        ) * HD ** (-0.5)
        weights = jnp.where(lane < size[p], jnp.exp(scores), 0.0)
        probs = (weights / head_sums(weights, seq)).astype(jnp.bfloat16)
        contexts.append(jnp.dot(probs, vals, preferred_element_type=jnp.float32))
    context = jnp.concatenate(contexts, axis=0).astype(jnp.bfloat16)
    out_copy.wait()
    attended = jnp.dot(context, w_out[...], preferred_element_type=jnp.float32) + out_bias[...]
    hidden = normed(embedded.astype(jnp.float32) + attended, norm_gain[...], norm_bias[...])
    row = lax.broadcasted_iota(jnp.int32, (seq, 1), 0)
    for p in range(passes):
        kept = jnp.where(row < size[p], hidden[p * seq : (p + 1) * seq], 0.0)
        pooled = jnp.sum(kept, axis=0, keepdims=True) / size[p].astype(jnp.float32)
        scale = lax.rsqrt(jnp.mean(pooled * pooled, axis=-1, keepdims=True) + 1e-06)
        out[p : p + 1, :] = (pooled * scale).astype(jnp.bfloat16)
    spread[...] = jnp.broadcast_to(out[...][None], spread.shape)


def encode(
    peers, slots, fetched, lengths, pos_table, emb_gain, emb_bias, w_qkv, w_out, out_bias, norm_gain, norm_bias
):
    width = fetched.shape[1]
    tokens = slots.shape[0]
    passes = lengths.shape[0]
    macs = tokens * width * (fetched.shape[0] + 4 * HEADS * HD)
    operands = (
        lengths[None],
        slots,
        fetched,
        pos_table,
        emb_gain[None],
        emb_bias[None],
        out_bias[None],
        norm_gain[None],
        norm_bias[None],
        w_qkv,
        w_out,
    )
    return pl.pallas_call(
        encode_kernel,
        out_shape=[
            jax.ShapeDtypeStruct((passes, width), jnp.bfloat16),
            jax.ShapeDtypeStruct((peers, passes, width), jnp.bfloat16),
        ],
        in_specs=[pl.BlockSpec(memory_space=pltpu.HBM)] * len(operands),
        out_specs=[pl.BlockSpec(memory_space=pltpu.VMEM)] * 2,
        scratch_shapes=[pltpu.VMEM(operand.shape, operand.dtype) for operand in operands]
        + [pltpu.SemaphoreType.DMA((len(operands) + 3,))],
        compiler_params=pltpu.CompilerParams(vmem_limit_bytes=60 * 1024 * 1024),
        cost_estimate=pl.CostEstimate(
            flops=2 * macs, bytes_accessed=6 * 1024 * 1024, transcendentals=0
        ),
        name="encode",
    )(*operands)


def padded(rows):
    return -(-rows // 16) * 16


def rank_bits(count):
    return max(1, (count - 1).bit_length())


def ranks(kind):
    count = kind.shape[1]
    at = lax.broadcasted_iota(jnp.int32, (count, count), 0)
    by = lax.broadcasted_iota(jnp.int32, (count, count), 1)
    across = jnp.broadcast_to(kind, (count, count))
    down = jnp.sum(jnp.where(at == by, across, 0), axis=1, keepdims=True)
    same = down == across
    rank_row = jnp.sum(jnp.where(same & (at < by), 1, 0), axis=0, keepdims=True)
    rank_col = jnp.sum(jnp.where(same & (by < at), 1, 0), axis=1, keepdims=True)
    return down, rank_row, rank_col


def route_kernel(
    sizes,
    token_ids_far,
    owners_far,
    row_slot_far,
    sibling_far,
    plan,
    token_slot_far,
    code,
    sibling_code,
    *near,
):
    peers, vocab_rows, token_cap, row_cap, pooled = sizes
    token_ids, owners, row_slot, sibling, token_slot, arrived = near
    copies = [
        pltpu.make_async_copy(source, target, arrived.at[at])
        for at, (source, target) in enumerate(
            (
                (token_ids_far, token_ids),
                (owners_far, owners),
                (row_slot_far, row_slot),
                (sibling_far, sibling),
            )
        )
    ]
    for copy in copies:
        copy.start()
    for copy in copies:
        copy.wait()
    ids = jnp.concatenate([token_ids[p : p + 1, :] for p in range(token_ids.shape[0])], axis=1)
    tokens, rows = ids.shape[1], owners.shape[1]
    count = tokens + rows
    edge = (lax.broadcasted_iota(jnp.int32, (peers, tokens), 0) + 1) * vocab_rows
    holder = jnp.sum(jnp.where(ids >= edge, 1, 0), axis=0, keepdims=True)
    values = jnp.concatenate([ids - holder * vocab_rows, row_slot[...]], axis=1)

    kind = jnp.concatenate([holder, owners[...] + peers], axis=1)
    down, rank_row, rank_col = ranks(kind)

    code[...] = owners[...] * 2 ** rank_bits(rows) + rank_row[:, tokens:]
    sibling_code[...] = sibling[...] * 2 ** rank_bits(rows) + ranks(sibling[...])[1]
    goal = jnp.concatenate([holder, owners[...]], axis=1)
    peer = lax.broadcasted_iota(jnp.int32, (peers, count), 0)
    left = jnp.where(peer == goal, values + 1, 0).astype(jnp.float32)
    columns = token_cap + row_cap + pooled
    column = lax.broadcasted_iota(jnp.int32, (count, columns), 1)
    entry = lax.broadcasted_iota(jnp.int32, (count, 1), 0)
    first = jnp.where(entry < tokens, rank_col, rank_col + token_cap)
    second = entry - (count - pooled) + token_cap + row_cap
    second = jnp.where(entry < count - pooled, -1, second)
    right = jnp.where((column == first) | (column == second), 1.0, 0.0)
    filled = jnp.dot(
        left, right, preferred_element_type=jnp.float32, precision=lax.Precision.HIGHEST
    )
    filled = filled.astype(jnp.int32) - 1
    for p in range(peers):
        plan[p, :, :rows] = code[...]
        plan[p, :, rows:] = filled[p : p + 1]
    token_slot[...] = down[:tokens] * token_cap + rank_col[:tokens]
    send = pltpu.make_async_copy(token_slot, token_slot_far, arrived.at[4])
    send.start()
    send.wait()


def route(token_ids, owners, row_slot, sibling_owners, sizes):
    peers, _, token_cap, row_cap, pooled = sizes
    passes, seq_len = token_ids.shape
    rows = owners.shape[1]
    ints = lambda *shape: jax.ShapeDtypeStruct(shape, jnp.int32)
    return pl.pallas_call(
        functools.partial(route_kernel, sizes),
        out_shape=[
            ints(peers, 1, rows + token_cap + row_cap + pooled),
            ints(passes * seq_len, 1),
            ints(1, rows),
            ints(1, rows),
        ],
        in_specs=[pl.BlockSpec(memory_space=pltpu.HBM)] * 4,
        out_specs=[
            pl.BlockSpec(memory_space=pltpu.VMEM),
            pl.BlockSpec(memory_space=pltpu.HBM),
            pl.BlockSpec(memory_space=pltpu.VMEM),
            pl.BlockSpec(memory_space=pltpu.VMEM),
        ],
        scratch_shapes=[
            pltpu.VMEM(token_ids.shape, jnp.int32),
            pltpu.VMEM(owners.shape, jnp.int32),
            pltpu.VMEM(row_slot.shape, jnp.int32),
            pltpu.VMEM(owners.shape, jnp.int32),
            pltpu.VMEM((passes * seq_len, 1), jnp.int32),
            pltpu.SemaphoreType.DMA((5,)),
        ],
        compiler_params=pltpu.CompilerParams(vmem_limit_bytes=60 * 1024 * 1024),
        name="route",
    )(token_ids, owners, row_slot, sibling_owners)


def pack_kernel(half, row_cap, count, picks, pieces, rest, *refs):
    me = lax.axis_index("dp")
    operands = 2 + 2 * pieces
    far, refs = refs[:operands], refs[operands:]
    steps = half // 2
    outs, refs = refs[: steps + bool(rest)], refs[steps + bool(rest) :]
    near, (blocks, tail, arrived, left) = refs[:operands], refs[operands:]
    size = blocks.shape[0] // steps
    copies = [
        pltpu.make_async_copy(far[at], near[at], arrived.at[at]) for at in range(operands)
    ]
    for copy in copies:
        copy.start()
    for copy in copies[:2]:
        copy.wait()
    if size > 2 * row_cap:
        blocks[...] = jnp.zeros(blocks.shape, blocks.dtype)
    for source in range(2):
        if picks is None:
            code = near[source][...]
        else:
            code = near[source][me ^ picks[source], :, :count]
        bits = rank_bits(count)
        owner, rank = code >> bits, code & (2**bits - 1)
        fits = ((owner ^ me) & (1 | half)) == 0
        chip = ((owner ^ me) & (half - 1)) >> 1
        slot = jnp.where(fits, chip * row_cap + rank, -1)
        packed, at = 0.0, 0
        for piece in range(2 + source * pieces, 2 + (source + 1) * pieces):
            rows = near[piece]
            spot = lax.broadcasted_iota(jnp.int32, (steps * row_cap, rows.shape[0]), 0)
            table = jnp.where(slot[:, at : at + rows.shape[0]] == spot, 1.0, 0.0)
            copies[piece].wait()
            packed += jnp.dot(
                table.astype(jnp.bfloat16), rows[...], preferred_element_type=jnp.float32
            )
            at += rows.shape[0]
        packed = packed.astype(jnp.bfloat16)
        for step in range(steps):
            first = step * size + source * row_cap
            blocks[first : first + row_cap, :] = packed[step * row_cap : (step + 1) * row_cap]
    sends = [
        pltpu.make_async_copy(
            blocks.at[pl.ds(step * size, size)], outs[step], left.at[step]
        )
        for step in range(steps)
    ]
    if rest:
        tail[...] = near[2][near[2].shape[0] - rest :, :]
        sends.append(pltpu.make_async_copy(tail, outs[steps], left.at[steps]))
    for send in sends:
        send.start()
    for send in sends:
        send.wait()


def pack_rows(codes_a, codes_b, rows_a, rows_b, half, row_cap, count, picks=None, rest=0):
    width = rows_a[0].shape[1]
    total = sum(piece.shape[0] for piece in rows_a)
    steps = half // 2
    size = padded(2 * row_cap)
    operands = (codes_a, codes_b, *rows_a, *rows_b)
    shapes = [(size, width)] * steps + [(rest, width)] * bool(rest)
    return pl.pallas_call(
        functools.partial(pack_kernel, half, row_cap, count, picks, len(rows_a), rest),
        out_shape=[jax.ShapeDtypeStruct(shape, jnp.bfloat16) for shape in shapes],
        in_specs=[pl.BlockSpec(memory_space=pltpu.HBM)] * len(operands),
        out_specs=[pl.BlockSpec(memory_space=pltpu.HBM)] * len(shapes),
        scratch_shapes=[
            *(pltpu.VMEM(operand.shape, operand.dtype) for operand in operands),
            pltpu.VMEM((steps * size, width), jnp.bfloat16),
            pltpu.VMEM((max(rest, 16), width), jnp.bfloat16),
            pltpu.SemaphoreType.DMA((len(operands),)),
            pltpu.SemaphoreType.DMA((len(shapes),)),
        ],
        compiler_params=pltpu.CompilerParams(vmem_limit_bytes=60 * 1024 * 1024),
        cost_estimate=pl.CostEstimate(
            flops=4 * steps * row_cap * width * total,
            bytes_accessed=4 * width * (total + steps * row_cap),
            transcendentals=0,
        ),
        name="pack",
    )(*operands)


def onehot(where_to, first, count):
    centre = lax.broadcasted_iota(jnp.int32, (count, where_to.shape[1]), 0) + first
    return jnp.where(centre == where_to, 1.0, 0.0)


BLOCK = 256


def early_kernel(places_far, centroids_far, *rest):
    pieces, (out_far, share_far, places, rows, centroids, out, share, arrived, left) = rest[:-9], rest[-9:]
    size = pieces[0].shape[0]
    steps = centroids.shape[0] // BLOCK
    copies = [pltpu.make_async_copy(places_far, places, arrived.at[0])]
    for at, piece in enumerate(pieces):
        copies.append(
            pltpu.make_async_copy(piece, rows.at[pl.ds(at * size, size)], arrived.at[1 + at])
        )
    loads = []
    for step in range(steps):
        block = pl.ds(step * BLOCK, BLOCK)
        loads.append(
            pltpu.make_async_copy(
                centroids_far.at[block], centroids.at[block], arrived.at[1 + len(pieces) + step]
            )
        )
    for copy in copies + loads:
        copy.start()
    for copy in copies:
        copy.wait()
    sends = []
    for step in range(steps):
        block = pl.ds(step * BLOCK, BLOCK)
        hot = onehot(places[...], step * BLOCK, BLOCK)
        counts = jnp.sum(hot, axis=1, keepdims=True)
        scale = jnp.where(counts > 0, 1.0 / jnp.maximum(counts, 1.0), 0.0)
        sums = jnp.dot(
            hot[:, : rows.shape[0]].astype(jnp.bfloat16),
            rows[...],
            preferred_element_type=jnp.float32,
        )
        loads[step].wait()
        out[block, :] = jnp.where(counts > 0, sums * scale, centroids[block, :])
        share[block, :] = jnp.broadcast_to(scale, (BLOCK, share.shape[1]))
        sends.append(pltpu.make_async_copy(out.at[block], out_far.at[block], left.at[step]))
        sends[-1].start()
    sends.append(pltpu.make_async_copy(share, share_far, left.at[steps]))
    sends[-1].start()
    for send in sends:
        send.wait()


def late_kernel(places_far, late_far, spread_far, share_far, early_far, *rest):
    pieces, rest = rest[:-10], rest[-10:]
    out_far, places, late, spread, share, rows, early, out, arrived, left = rest
    size, passes = pieces[0].shape[0], spread.shape[1]
    steps = early.shape[0] // BLOCK
    loads = [
        pltpu.make_async_copy(source, target, arrived.at[at])
        for at, (source, target) in enumerate(
            ((places_far, places), (late_far, late), (spread_far, spread), (share_far, share))
        )
    ]
    for at, piece in enumerate(pieces):
        loads.append(
            pltpu.make_async_copy(piece, rows.at[pl.ds(at * size, size)], arrived.at[4 + at])
        )
    starts = []
    for step in range(steps):
        block = pl.ds(step * BLOCK, BLOCK)
        starts.append(
            pltpu.make_async_copy(
                early_far.at[block], early.at[block], arrived.at[len(loads) + step]
            )
        )
    for copy in loads + starts:
        copy.start()
    for copy in loads:
        copy.wait()
    top = len(pieces) * size
    for peer in range(spread.shape[0]):
        rows[top + peer * passes : top + (peer + 1) * passes, :] = spread[peer]
    where_to = jnp.concatenate([places[:, places.shape[1] - top :], late[...]], axis=1)
    sends = []
    for step in range(steps):
        block = pl.ds(step * BLOCK, BLOCK)
        hot = onehot(where_to, step * BLOCK, BLOCK).astype(jnp.bfloat16)
        sums = jnp.dot(hot, rows[...], preferred_element_type=jnp.float32)
        starts[step].wait()
        out[block, :] = early[block, :] + sums * share[block, :1]
        sends.append(pltpu.make_async_copy(out.at[block], out_far.at[block], left.at[step]))
        sends[-1].start()
    for send in sends:
        send.wait()


def early_update(places, centroids, pieces):
    centre_count, width = centroids.shape
    row_total = sum(piece.shape[0] for piece in pieces)
    wide = pltpu.VMEM(centroids.shape, jnp.float32)
    thin = (centre_count, 128)
    steps = centre_count // BLOCK
    return pl.pallas_call(
        early_kernel,
        out_shape=[
            jax.ShapeDtypeStruct(centroids.shape, jnp.float32),
            jax.ShapeDtypeStruct(thin, jnp.float32),
        ],
        in_specs=[pl.BlockSpec(memory_space=pl.ANY)] * (2 + len(pieces)),
        out_specs=[pl.BlockSpec(memory_space=pltpu.HBM)] * 2,
        scratch_shapes=[
            pltpu.VMEM(places.shape, jnp.int32),
            pltpu.VMEM((row_total, width), jnp.bfloat16),
            wide,
            wide,
            pltpu.VMEM(thin, jnp.float32),
            pltpu.SemaphoreType.DMA((1 + len(pieces) + steps,)),
            pltpu.SemaphoreType.DMA((steps + 1,)),
        ],
        compiler_params=pltpu.CompilerParams(vmem_limit_bytes=60 * 1024 * 1024),
        cost_estimate=pl.CostEstimate(
            flops=100 * centre_count * width * row_total,
            bytes_accessed=200 * centre_count * width,
            transcendentals=0,
        ),
        name="early",
    )(places, centroids, *pieces)


def late_update(places, late, spread, share, early, pieces):
    centre_count, width = early.shape
    row_total = sum(piece.shape[0] for piece in pieces) + late.shape[1]
    wide = pltpu.VMEM(early.shape, jnp.float32)
    steps = centre_count // BLOCK
    return pl.pallas_call(
        late_kernel,
        out_shape=jax.ShapeDtypeStruct(early.shape, jnp.float32),
        in_specs=[pl.BlockSpec(memory_space=pltpu.HBM)] * (5 + len(pieces)),
        out_specs=pl.BlockSpec(memory_space=pltpu.HBM),
        scratch_shapes=[
            pltpu.VMEM(places.shape, jnp.int32),
            pltpu.VMEM(late.shape, jnp.int32),
            pltpu.VMEM(spread.shape, jnp.bfloat16),
            pltpu.VMEM(share.shape, jnp.float32),
            pltpu.VMEM((row_total, width), jnp.bfloat16),
            wide,
            wide,
            pltpu.SemaphoreType.DMA((4 + len(pieces) + steps,)),
            pltpu.SemaphoreType.DMA((steps,)),
        ],
        compiler_params=pltpu.CompilerParams(vmem_limit_bytes=60 * 1024 * 1024),
        cost_estimate=pl.CostEstimate(
            flops=2 * centre_count * width * row_total,
            bytes_accessed=8 * centre_count * width,
            transcendentals=0,
        ),
        name="late",
    )(places, late, spread, share, early, *pieces)


def shards(
    token_ids,
    lengths,
    word_table,
    pos_table,
    emb_gain,
    emb_bias,
    w_qkv,
    w_out,
    out_bias,
    norm_gain,
    norm_bias,
    stored_rows,
    row_owner,
    row_slot,
    centroids,
):
    peer_count = lax.axis_size("dp")
    half = peer_count // 2
    width = word_table.shape[1]
    vocab_rows = word_table.shape[0]
    passes, seq_len = token_ids.shape
    token_count = passes * seq_len
    row_count = row_slot.shape[0]
    store_count = stored_rows.shape[0]
    token_cap = max(2, 3 * token_count // peer_count)
    row_cap = max(2, 3 * row_count // peer_count)

    across = [(i, i ^ half) for i in range(peer_count)]
    beside = [(i, i ^ 1) for i in range(peer_count)]

    def hand_on(blocks):
        got = [blocks[0]]
        for step in range(1, len(blocks)):
            moves = [(i, i ^ (2 * step)) for i in range(peer_count)]
            got.append(lax.ppermute(blocks[step], "dp", moves))
        return got

    ahead = store_count * 3 // 4 // 16 * 16
    sibling_rows = lax.ppermute(stored_rows, "dp", beside)
    first_rows = lax.ppermute(stored_rows[:ahead], "dp", across)
    sizes = (peer_count, vocab_rows, token_cap, row_cap, row_count - store_count)
    owners = row_owner.reshape(1, row_count)
    sibling_owners = lax.ppermute(owners, "dp", beside)
    plan, token_slot, code, sibling_code = route(
        token_ids, owners, row_slot[None], sibling_owners, sizes
    )
    plan, sibling_rows = lax.optimization_barrier((plan, sibling_rows))
    codes = lax.all_to_all(plan, "dp", split_axis=0, concat_axis=0, tiled=True)
    *blocks, last_rows = pack_rows(
        code,
        sibling_code,
        [stored_rows],
        [sibling_rows],
        half,
        row_cap,
        row_count,
        rest=store_count - ahead,
    )
    codes, last_rows = lax.optimization_barrier((codes, last_rows))
    last_rows = lax.ppermute(last_rows, "dp", across)
    own_half = hand_on(blocks)
    plan = codes[:, 0, row_count:]
    wanted = plan[:, :token_cap].reshape(peer_count * token_cap)
    chosen = wanted[:, None] == jnp.arange(vocab_rows, dtype=jnp.int32)[None, :]
    found = jnp.dot(
        chosen.astype(jnp.bfloat16), word_table, preferred_element_type=jnp.float32
    ).astype(jnp.bfloat16)
    found, first_rows, own_half[:2] = lax.optimization_barrier(
        (found, first_rows, own_half[:2])
    )
    plan_behind, last_rows = lax.optimization_barrier((plan, last_rows))
    fetched = lax.all_to_all(
        found.reshape(peer_count, token_cap, width), "dp", split_axis=0, concat_axis=0, tiled=True
    ).reshape(peer_count * token_cap, width)

    sources = lax.axis_index("dp") ^ jnp.arange(peer_count, dtype=jnp.int32)
    got_places = plan_behind[:, token_cap : token_cap + row_cap][sources].reshape(half, 2 * row_cap)
    spare = padded(2 * row_cap) - 2 * row_cap
    got_places = jnp.pad(got_places, ((0, 0), (0, spare)), constant_values=-1).reshape(1, -1)
    near_rows, last_rows = lax.optimization_barrier((own_half, last_rows))
    means, share = early_update(got_places, centroids, near_rows)
    first_rows, last_rows, means = lax.optimization_barrier((first_rows, last_rows, means))
    partner_rows = [first_rows, last_rows]
    far_rows = [lax.ppermute(rows, "dp", beside) for rows in partner_rows]
    picks = (half, half ^ 1)
    blocks = pack_rows(codes, codes, partner_rows, far_rows, half, row_cap, row_count, picks)
    other_half = hand_on(blocks)
    late_places = plan[:, token_cap + row_cap :].reshape(1, -1)
    fetched, means, share, got_places = lax.optimization_barrier(
        (fetched, means, share, got_places)
    )

    passage_embed, spread = encode(
        peer_count,
        token_slot,
        fetched,
        lengths,
        pos_table,
        emb_gain,
        emb_bias,
        w_qkv,
        w_out,
        out_bias,
        norm_gain,
        norm_bias,
    )
    all_embeds = lax.all_to_all(
        spread, "dp", split_axis=0, concat_axis=0, tiled=True
    )
    new_centroids = late_update(got_places, late_places, all_embeds, share, means, other_half)
    return (passage_embed, new_centroids)


def solution(mesh):
    return jax.shard_map(
        shards,
        mesh=mesh,
        in_specs=(
            P(("groups", "dp"), None),
            P(("groups", "dp")),
            P("dp", None),
            P(),
            P(),
            P(),
            P(),
            P(),
            P(),
            P(),
            P(),
            P(("groups", "dp"), None),
            P(("groups", "dp"), None),
            P(("groups", "dp")),
            P(("groups", "dp"), None),
        ),
        out_specs=(P(("groups", "dp"), None), P(("groups", "dp"), None)),
        check_vma=False,
    )
```
